128 devices in a mesh: leaf: 16 (over z_hi, x, core), col: 8 (over y, z_lo).
Axes of the slice: x: 4, y: 4, z: 4 (z_hi: 2, z_lo: 2; z = z_hi * 2 + z_lo), core: 2. Of those that a mesh axis runs over, the one named last changes fastest.
Arguments:
- features: bfloat16 [48, 1048576], P(None, ('leaf', 'col')), may hold values from -12 to 12
- targets: bfloat16 [1048576], P(('leaf', 'col')), may hold values from -6 to 6
- owner: int32 [1048576], P(('leaf', 'col')), may hold values from 0 to 127, as said below
- length_scales: float32 [48], replicated, may hold values from 4 to 12
- ridge: float32 [1], replicated, may hold values from 0.0005 to 2
- leaf_pivots: int32 [16, 256], P('leaf'), may hold values from 0 to 65535, as said below
- parent_pivots: int32 [8, 256], replicated, may hold values from 0 to 511, as said below
- top_pivots: int32 [4, 256], replicated, may hold values from 0 to 511, as said below
Outputs:
- leaf_reduced: float32 [16, 256, 512], P('leaf', 'col')
- top_reduced: float32 [16, 256, 256], P('leaf', 'col')
- top_rhs: float32 [16, 256], P('leaf')
The draws below stay inside these ranges and needn't reach their ends.
Inputs may be any that keep to these rules, and one draw needn't show every extreme that they name: `owner`: each block of 8192 consecutive samples names every block exactly 64 times. `leaf_pivots`: entries of a row are distinct. `parent_pivots`: entries of a row are distinct. `top_pivots`: entries of a row are distinct.
All inputs are finite; a program needn't handle non-finite values.
Results may differ from the reference program's by a relative error of at most 0.0029.
Values may be sent and summed in bfloat16 or wider, within the bound.
A program may use at most 64 MiB of HBM per device.

```python
import math
import jax
import jax.numpy as jnp
from jax import lax

F = 48
RANK = 256
ROWS = 8192
SHARDS = 128
PACKET = 64
LEAVES = 16
NODE_ROWS = 65536
SAMPLES = 1048576


def draw_features(key, part):
    key = jax.random.fold_in(key, 21)
    noise_key = jax.random.fold_in(key, 0)
    return jnp.clip(jax.random.normal(noise_key, (F, SAMPLES), jnp.float32), -6.0, 6.0).astype(jnp.bfloat16)


def draw_ridge(key, part):
    key = jax.random.fold_in(key, 22)
    return jnp.exp(jax.random.uniform(key, (1,), jnp.float32, jnp.log(0.5), jnp.log(2.0)))


def draw_owner(key, part):
    key = jax.random.fold_in(key, 11)
    keys = jax.random.split(key, SHARDS)
    orders = jax.vmap(lambda k: jax.random.permutation(k, ROWS))(keys)
    return (orders % SHARDS).reshape(-1).astype(jnp.int32)


def draw_leaf_pivots(key, part):
    key = jax.random.fold_in(key, 12)
    keys = jax.random.split(key, LEAVES)
    return jax.vmap(lambda k: jax.random.permutation(k, NODE_ROWS)[:RANK])(keys).astype(jnp.int32)


def draw_parent_pivots(key, part):
    key = jax.random.fold_in(key, 13)
    keys = jax.random.split(key, LEAVES // 2)
    return jax.vmap(lambda k: jax.random.permutation(k, 2 * RANK)[:RANK])(keys).astype(jnp.int32)


def draw_top_pivots(key, part):
    key = jax.random.fold_in(key, 14)
    keys = jax.random.split(key, LEAVES // 4)
    return jax.vmap(lambda k: jax.random.permutation(k, 2 * RANK)[:RANK])(keys).astype(jnp.int32)


def block_levels(stream_key, shape, cuts, smallest, top_value):
    gain = 1.0
    for position, shards_of in cuts:
        draws = jax.random.uniform(jax.random.fold_in(jax.random.fold_in(stream_key, 6), position), (shards_of,), jnp.float32, smallest / len(cuts), top_value / len(cuts))
        gain = gain * jnp.repeat(jnp.exp(draws), shape[position] // shards_of).reshape((-1,) + (1,) * (len(shape) - 1 - position))
    return gain


def gaussian(own_key, extent, deviation, reach, cuts=(), kind=jnp.bfloat16):
    values = deviation * jax.random.normal(own_key, extent, jnp.float32)
    if cuts:
        values = values * block_levels(own_key, extent, cuts, -0.22, 0.18)
    return jnp.clip(values, -reach, reach).astype(kind)


def setup_inputs(seed: int = 0) -> dict:
    splits = jax.random.split(jax.random.key(seed), 9)
    return {
        "features": draw_features(jax.random.fold_in(splits[8], 71), 0),
        "targets": gaussian(splits[1], (SAMPLES,), 1.0, 6.0, ((0, 128),)),
        "owner": draw_owner(jax.random.fold_in(splits[8], 71), 0),
        "length_scales": jnp.clip(jnp.exp(jax.random.uniform(splits[3], (F,), jnp.float32, math.log(4.0), math.log(12.0))), 4.0, 12.0),
        "ridge": draw_ridge(jax.random.fold_in(splits[8], 71), 0),
        "leaf_pivots": draw_leaf_pivots(jax.random.fold_in(splits[8], 71), 0),
        "parent_pivots": draw_parent_pivots(jax.random.fold_in(splits[8], 71), 0),
        "top_pivots": draw_top_pivots(jax.random.fold_in(splits[8], 71), 0),
    }


def kernel(points, skel, inverse):
    left = points.astype(jnp.float32) * inverse[:, None]
    right = skel.astype(jnp.float32) * inverse[:, None]
    cross = lax.dot_general(left, right, (((0,), (0,)), ((), ())), precision=lax.Precision.HIGHEST)
    dist = jnp.sum(left * left, 0)[:, None] + jnp.sum(right * right, 0)[None, :] - 2.0 * cross
    return jnp.exp(-0.5 * jnp.maximum(dist, 0.0))


def accumulate(points, values, own_skel, other_skel, inverse, width):
    count = points.shape[1] // width
    rank = own_skel.shape[1]
    contract = (((0,), (0,)), ((), ()))

    def step(index, carry):
        gram, couple, rhs = carry
        block = lax.dynamic_slice_in_dim(points, index * width, width, 1)
        target = lax.dynamic_slice_in_dim(values, index * width, width, 0)
        basis = kernel(block, own_skel, inverse).astype(jnp.bfloat16)
        across = kernel(block, other_skel, inverse).astype(jnp.bfloat16)
        gram = gram + lax.dot_general(basis, basis, contract, preferred_element_type=jnp.float32)
        couple = couple + lax.dot_general(basis, across, contract, preferred_element_type=jnp.float32)
        rhs = rhs + jnp.dot(target[None, :], basis, preferred_element_type=jnp.float32)[0]
        return gram, couple, rhs

    zero = jnp.zeros((rank, rank), jnp.float32)
    return lax.fori_loop(0, count, step, (zero, zero, jnp.zeros((rank,), jnp.float32)))


def merge_pair(first, second, first_rhs, second_rhs, first_skel, second_skel, pivots):
    rank = first.shape[0]
    lower = jnp.concatenate([second[:, rank:], second[:, :rank]], 1)
    whole = jnp.concatenate([first, lower], 0)
    chosen = jnp.take(jnp.take(whole, pivots, 0), pivots, 1)
    rhs = jnp.take(jnp.concatenate([first_rhs, second_rhs]), pivots)
    skel = jnp.take(jnp.concatenate([first_skel, second_skel], 1), pivots, 1)
    return chosen, rhs, skel


def merge_top(first, second, first_rhs, second_rhs, first_skel, second_skel, pivots, inverse):
    cross = kernel(first_skel, second_skel, inverse)
    whole = jnp.concatenate([jnp.concatenate([first, cross], 1), jnp.concatenate([cross.T, second], 1)], 0)
    chosen = jnp.take(jnp.take(whole, pivots, 0), pivots, 1)
    rhs = jnp.take(jnp.concatenate([first_rhs, second_rhs]), pivots)
    return chosen, rhs


def reference(features, targets, owner, length_scales, ridge, leaf_pivots, parent_pivots, top_pivots):
    inverse = 1.0 / length_scales
    order = jnp.argsort(owner.reshape(SHARDS, ROWS), axis=1, stable=True).astype(jnp.int32)
    order = order + (jnp.arange(SHARDS, dtype=jnp.int32) * ROWS)[:, None]
    permute = order.reshape(SHARDS, SHARDS, PACKET).transpose(1, 0, 2).reshape(-1)
    placed = jnp.take(features, permute, axis=1)
    values = jnp.take(targets, permute)
    nodes = placed.reshape(F, LEAVES, NODE_ROWS).transpose(1, 0, 2)
    node_values = values.reshape(LEAVES, NODE_ROWS)
    skel = jax.vmap(lambda pts, piv: jnp.take(pts, piv, axis=1).astype(jnp.float32))(nodes, leaf_pivots)
    sibling = skel.reshape(LEAVES // 2, 2, F, RANK)[:, ::-1].reshape(LEAVES, F, RANK)
    width = math.gcd(NODE_ROWS, 4096)
    gram, couple, rhs = lax.map(lambda item: accumulate(item[0], item[1], item[2], item[3], inverse, width), (nodes, node_values, skel, sibling))
    eye = jnp.eye(RANK, 2 * RANK, dtype=jnp.float32)
    stacked = jnp.concatenate([gram, couple], 2) / NODE_ROWS + ridge[0] * eye[None]
    rhs = rhs / NODE_ROWS
    par_m, par_r, par_s = jax.vmap(merge_pair)(stacked[0::2], stacked[1::2], rhs[0::2], rhs[1::2], skel[0::2], skel[1::2], parent_pivots)
    top_m, top_r = jax.vmap(lambda a, b, c, d, e, f, g: merge_top(a, b, c, d, e, f, g, inverse))(par_m[0::2], par_m[1::2], par_r[0::2], par_r[1::2], par_s[0::2], par_s[1::2], top_pivots)
    return stacked, jnp.repeat(top_m, 4, axis=0), jnp.repeat(top_r, 4, axis=0)
```

```python
import functools
import math

import jax
import jax.numpy as jnp
from jax import lax
from jax.experimental import pallas as pl
from jax.experimental.pallas import tpu as pltpu
from jax.sharding import PartitionSpec as P

F = 48
RANK = 256
ROWS = 8192
LEAVES = 16
COLS = 8
OWNERS = 128
PACKET = 64
PER = ROWS // LEAVES
CHUNK = 256
CHUNKS = ROWS // CHUNK
WINDOW = 40
REGION = PER + WINDOW
WIDE = 64
SLAB = RANK // COLS
NODE = ROWS * COLS
LOG2E = math.log2(math.e)
BF = jnp.bfloat16
F32 = jnp.float32
NT = (((1,), (1,)), ((), ()))
MESH = pl.DeviceIdType.MESH


def dma(count):
    return [pltpu.SemaphoreType.DMA((count,))] * 2


def params(number=None, limit=24):
    if number is None:
        return pltpu.CompilerParams(vmem_limit_bytes=limit * 2**20)
    return pltpu.CompilerParams(
        collective_id=number, has_side_effects=True, vmem_limit_bytes=limit * 2**20
    )


ANYWHERE = pl.BlockSpec(memory_space=pl.ANY)
VMEM = pl.BlockSpec(memory_space=pltpu.VMEM)


def iota(shape, axis):
    return lax.broadcasted_iota(jnp.int32, shape, axis)


def dot(a, b):
    return jnp.dot(a, b, preferred_element_type=F32)


def dot_nt(a, b):
    return lax.dot_general(a, b, NT, preferred_element_type=F32)


def row_pair(two):
    return jnp.concatenate([two[0:1], two[1:2]], 1)


def pack_kernel(
    feat_hbm, target, owner, out_feat, out_aux,
    feat, goals, rows, ybuf, zbuf, table, scal, sem, feat_sem,
):
    bring = pltpu.make_async_copy(feat_hbm, feat, feat_sem)
    bring.start()
    goals[...] = target[...].astype(F32)
    before = (iota((CHUNK, CHUNK), 0) < iota((CHUNK, CHUNK), 1)).astype(F32).astype(BF)
    weights = jnp.concatenate([before, jnp.ones((CHUNK, 128), BF)], 1)
    lane = iota((LEAVES, 128), 1)

    def ranks(t, carry):
        seen, seen_leaf, most = carry
        own = row_pair(owner[pl.ds(2 * t, 2), :])
        leaf = own // 8
        is_own = iota((OWNERS, CHUNK), 0) == own
        is_leaf = iota((LEAVES, CHUNK), 0) == leaf
        is_after = iota((LEAVES, CHUNK), 0) > leaf
        marks = jnp.concatenate(
            [m.astype(F32).astype(BF) for m in (is_own, is_leaf, is_after)], 0
        )
        sums = dot(marks, weights)
        counts = sums[:OWNERS, CHUNK:]
        leaf_counts = sums[OWNERS : OWNERS + LEAVES, CHUNK:]
        base = sums[OWNERS + LEAVES :, CHUNK:]
        prior = sums[:OWNERS, :CHUNK] + jnp.concatenate([seen, seen], 1)
        rank = jnp.sum(jnp.where(is_own, prior, 0.0), 0, keepdims=True)
        place = sums[OWNERS : OWNERS + LEAVES, :CHUNK] + jnp.concatenate([base, base], 1)
        place = jnp.sum(jnp.where(is_leaf, place, 0.0), 0, keepdims=True)
        tag = (own % 8).astype(F32) * PACKET + rank - (PER // 2)
        rows[t, 0:1, :] = place
        rows[t, 1:2, :] = row_pair(goals[pl.ds(2 * t, 2), :])
        rows[t, 2:3, :] = tag
        here = lane == t
        table[0:LEAVES, :] = jnp.where(here, seen_leaf.astype(jnp.int32), table[0:LEAVES, :])
        table[LEAVES : 2 * LEAVES, :] = jnp.where(
            here, base.astype(jnp.int32), table[LEAVES : 2 * LEAVES, :]
        )
        return seen + counts, seen_leaf + leaf_counts, jnp.maximum(most, leaf_counts)

    table[0:LEAVES, :] = jnp.full((LEAVES, 128), PER, jnp.int32)
    zero = jnp.zeros((LEAVES, 128), F32)
    _, _, most = lax.fori_loop(
        0, CHUNKS, ranks, (jnp.zeros((OWNERS, 128), F32), zero, zero), unroll=8
    )
    most = jnp.broadcast_to(jnp.max(most, 0, keepdims=True), (8, 128))
    table[2 * LEAVES :, :] = most.astype(jnp.int32)
    move = pltpu.make_async_copy(table, scal, sem)
    move.start()
    bring.wait()

    def sort(t, _):
        start = pl.multiple_of(t * CHUNK, CHUNK)
        row = iota((16, CHUNK), 0)
        place, goal, tag = rows[t, 0:1, :], rows[t, 1:2, :], rows[t, 2:3, :]
        extra = jnp.where(row == 0, goal, jnp.where(row == 1, tag, 0.0)).astype(BF)
        joined = jnp.concatenate([feat[:, pl.ds(start, CHUNK)], extra], 0)
        chosen = (iota((CHUNK, CHUNK), 0) == place.astype(jnp.int32)).astype(F32).astype(BF)
        ybuf[pl.ds(start, CHUNK), :] = dot_nt(chosen, joined)
        return 0

    lax.fori_loop(0, CHUNKS, sort, 0, unroll=8)
    move.wait()
    widest = scal[2 * LEAVES, 0]

    @pl.when(widest <= WINDOW)
    def quick():
        def merge(t, _):
            for i in range(LEAVES):
                source = t * CHUNK + scal[LEAVES + i, t]
                goal = i * REGION + scal[i, t]
                zbuf[pl.ds(goal, WINDOW), :] = ybuf[pl.ds(source, WINDOW), :]
            return 0

        lax.fori_loop(0, CHUNKS, merge, 0, unroll=2)

    @pl.when(widest > WINDOW)
    def slow():
        def merge(index, _):
            t = index // LEAVES
            i = index % LEAVES
            source = t * CHUNK + scal[LEAVES + i, t]
            first = scal[i, t]
            count = scal[i, t + 1] - first

            def part(k, _):
                rows = ybuf[pl.ds(source + 8 * k, 8), :]
                zbuf[pl.ds(i * REGION + first + 8 * k, 8), :] = rows
                return 0

            lax.fori_loop(0, (count + 7) // 8, part, 0)
            return 0

        lax.fori_loop(0, CHUNKS * LEAVES, merge, 0)

    eye = (iota((WIDE, WIDE), 0) == iota((WIDE, WIDE), 1)).astype(F32).astype(BF)
    for i in range(LEAVES):
        turned = dot_nt(eye, zbuf[i * REGION : i * REGION + PER, :].astype(BF))
        out_feat[i] = turned[:F].astype(BF)
        out_aux[i] = jnp.concatenate(
            [turned[F + r : F + r + 1, 128 * k : 128 * k + 128] for r in range(2) for k in range(4)], 0
        )


def in_hbm(*arrays):
    return [pltpu.with_memory_space_constraint(a, pltpu.HBM) for a in arrays]


def pack(features, targets, owner):
    return pl.pallas_call(
        pack_kernel,
        out_shape=(pltpu.VMEM((LEAVES, F, PER), BF), pltpu.VMEM((LEAVES, 8, 128), F32)),
        in_specs=[ANYWHERE, VMEM, VMEM],
        out_specs=[VMEM] * 2,
        scratch_shapes=[
            pltpu.VMEM((F, ROWS), BF),
            pltpu.VMEM((ROWS // 128, 128), F32),
            pltpu.VMEM((CHUNKS, 8, CHUNK), F32),
            pltpu.VMEM((ROWS + WINDOW, WIDE), F32),
            pltpu.VMEM((LEAVES * REGION, WIDE), F32),
            pltpu.VMEM((40, 128), jnp.int32),
            pltpu.SMEM((40, 128), jnp.int32),
            pltpu.SemaphoreType.DMA,
            pltpu.SemaphoreType.DMA,
        ],
        compiler_params=params(),
        name="pack",
    )(*in_hbm(features, targets, owner))


def split3(x):
    high = x.astype(BF)
    rest = x - high.astype(F32)
    mid = rest.astype(BF)
    return high, mid, (rest - mid.astype(F32)).astype(BF)


def stack16(parts, width):
    row = iota((16, width), 0)
    block = jnp.zeros((16, width), F32)
    for k, part in enumerate(parts):
        block = jnp.where(row == k, part if isinstance(part, float) else part.astype(F32), block)
    return block.astype(BF)


def half_norm(points, scale):
    return jnp.sum(points * points * (0.5 * scale), 0, keepdims=True)


def point_side(points, scale):
    high, mid, low = split3(-half_norm(points, scale))
    return stack16([high, mid, low, 1.0, 1.0, 1.0], points.shape[1])


def skel_side(skel, scale):
    width = skel.shape[1]
    high, mid, low = split3(skel * scale)
    extra = stack16([1.0, 1.0, 1.0, *split3(-half_norm(skel, scale))], width)
    parts = [p.astype(F32) for p in (high, mid, low, extra)]
    fill = jnp.zeros((256 - 3 * F - 16, width), F32)
    return jnp.concatenate([*parts, fill], 0).T.astype(BF)


def select_row(table, row):
    hit = iota(table.shape, 0) == row
    return jnp.sum(jnp.where(hit, table.astype(F32), 0.0), 0, keepdims=True)


def to_column(row):
    return jnp.broadcast_to(row, (128, row.shape[1])).T


def across(column, width):
    return jnp.concatenate([column] * (width // 128), 1)


def place_of(leaf, col):
    return dict(device_id=(leaf, col), device_id_type=MESH)


def mate(k):
    leaf, col = lax.axis_index("leaf"), lax.axis_index("col")
    to = (leaf + k) % LEAVES
    cross = (to // 8 + leaf // 8) % 2
    return place_of(to, col + cross * (1 - 2 * (col % 2)))


def beside(k):
    leaf, col = lax.axis_index("leaf"), lax.axis_index("col")
    return place_of(leaf, (col + k) % COLS)


def cousin(k):
    leaf, col = lax.axis_index("leaf"), lax.axis_index("col")
    return place_of(leaf - leaf % 4 + (leaf + k) % 4, col)


def greet(peers):
    barrier = pltpu.get_barrier_semaphore()
    for peer in peers:
        pl.semaphore_signal(barrier, inc=1, **peer)
    return lambda: pl.semaphore_wait(barrier, len(peers))


def remote(src, dst, sems, k, peer):
    return pltpu.make_async_remote_copy(src, dst, sems[0].at[k], sems[1].at[k], **peer)


def top_index(parent, top, group):
    top_row = select_row(top[...], group)
    below = jnp.concatenate([select_row(parent[...], 2 * group + r) for r in range(2)], 1)
    number = iota((RANK, 2 * RANK), 1)
    below = below + jnp.where(iota((1, 2 * RANK), 1) >= RANK, 2.0 * RANK, 0.0)
    hit = across(to_column(top_row), 2 * RANK) == number.astype(F32)
    index = jnp.sum(jnp.where(hit, below, 0.0), 1, keepdims=True)
    return jnp.broadcast_to(index, (RANK, 128))


def exchange_kernel(
    feat, aux, ridge, pivots_hbm, scales_hbm, parent_hbm, top_hbm, out_share, out_top, out_rhs,
    pivots, scales, parent, top, spare, rx, ra, hot, side, sk, mine, sk4, left, basis, acc,
    rows, columns, fours, index, tops, ps, pr, rs, rr, t4, r4,
    s_f, r_f, s_a, r_a, s_k, r_k, s_4, r_4, s_p, r_p, s_r, r_r, s_t, r_t, s_q, r_q, local,
):
    leaf = lax.axis_index("leaf")
    col = lax.axis_index("col")
    quarter = leaf % 4
    sibling = quarter + 1 - 2 * (quarter % 2)
    ready = greet([mate(k) for k in range(1, LEAVES)] + [beside(k) for k in range(1, COLS)])
    smalls = [
        pltpu.make_async_copy(a, b, local.at[k])
        for k, (a, b) in enumerate(
            [(pivots_hbm, pivots), (scales_hbm, scales), (parent_hbm, parent), (top_hbm, top)]
        )
    ]
    for copy in smalls:
        copy.start()

    def send_feat(k):
        return remote(feat.at[(leaf + k) % LEAVES], rx.at[k], (s_f, r_f), k, mate(k))

    def send_aux(k):
        return remote(aux.at[(leaf + k) % LEAVES], ra.at[k], (s_a, r_a), k, mate(k))

    def begin_aux(k, _):
        send_aux(k).start()
        return 0

    def begin_feat(k, _):
        send_feat(k).start()
        return 0

    rx[0] = feat[leaf]
    ra[0] = aux[leaf]
    ready()
    lax.fori_loop(1, LEAVES, begin_aux, 0)
    lax.fori_loop(1, LEAVES, begin_feat, 0)

    for copy in smalls:
        copy.wait()
    spare[...] = jnp.ones((8, 128), F32)
    spare[0:1, 0:F] = scales[...]
    inverse = 1.0 / to_column(spare[0:1, :])[:F]
    scale = inverse * inverse * LOG2E
    scale2 = across(scale, RANK)
    scale4 = across(scale, PER)

    place = pivots[...]
    within = place % ROWS
    block = within // PACKET
    key = (block // COLS) * PER + (place // ROWS) * PACKET + within % PACKET
    holder = block % COLS
    crossed = (block // COLS) // 8 != leaf // 8
    holder = jnp.where(crossed, holder + 1 - 2 * (holder % 2), holder)
    key = jnp.where(holder == col, key, -PER)
    key = across(to_column(key.astype(F32)), PER)

    def mark(k):
        source = (leaf + LEAVES - k) % LEAVES
        tags = ra[k, 4:8, :]
        tag = jnp.concatenate([tags[r : r + 1] for r in range(4)], 1)
        wanted = tag + (PER // 2 + source * PER).astype(F32)
        hot[k] = (key == wanted).astype(F32).astype(BF)

    def mark_next(k, _):
        send_aux(k).wait_recv()
        mark(k)
        return 0

    mark(0)
    lax.fori_loop(1, LEAVES, mark_next, 0)

    index[...] = top_index(parent, top, leaf // 4)
    index2 = across(index[...], 2 * RANK)
    number = iota((RANK, 2 * RANK), 1)
    base = (quarter * RANK).astype(F32)
    other = (sibling * RANK).astype(F32)
    chosen = index2[:, :RANK] == iota((RANK, RANK), 1).astype(F32) + base
    rows[...] = chosen.astype(F32).astype(BF)
    lanes = number.astype(F32) + jnp.where(number < RANK, base, other - RANK)
    columns[...] = (index2 == lanes).astype(F32).astype(BF)
    chosen = across(index[...], 4 * RANK) == iota((RANK, 4 * RANK), 1).astype(F32)
    fours[...] = chosen.astype(F32).astype(BF)

    def pick(k, total):
        send_feat(k).wait_recv()
        return total + dot_nt(hot[k], rx[k])

    picked = lax.fori_loop(1, LEAVES, pick, dot_nt(hot[0], rx[0]))
    picked = jnp.concatenate([picked, jnp.zeros((RANK, 128 - F), F32)], 1).T[:F]
    sk[0] = picked.astype(BF)

    def send_skel(k):
        return remote(sk.at[0], sk.at[k], (s_k, r_k), k, beside(k))

    for k in range(1, COLS):
        send_skel(k).start()

    def norms(k, _):
        side[k] = point_side(rx[k].astype(F32), scale4)
        return 0

    lax.fori_loop(0, LEAVES, norms, 0, unroll=2)
    for k in range(1, COLS):
        send_skel(k).wait_recv()
        picked = picked + sk[k].astype(F32)
    mine[...] = picked.astype(BF)
    sk4[quarter] = picked.astype(BF)

    def send_four(k):
        return remote(mine, sk4.at[quarter], (s_4, r_4), k, cousin(k))

    for k in (1, 3, 2):
        send_four(k).start()
    left[0:RANK, :] = skel_side(picked, scale2)
    for k in range(1, 4):
        remote(mine, sk4.at[(quarter + 4 - k) % 4], (s_4, r_4), k, cousin(k)).wait_recv()
    left[RANK:, :] = skel_side(sk4[sibling].astype(F32), scale2)

    def block_of(k, slot):
        p = rx[k]
        fill = jnp.zeros((256 - 3 * F - 16, PER), BF)
        right = jnp.concatenate([p, p, p, side[k], fill], 0)
        power = dot(left[...], right)
        basis[slot, 0 : 2 * RANK, :] = jnp.exp2(jnp.minimum(power, 0.0)).astype(BF)
        value = jnp.concatenate([ra[k, r : r + 1, :] for r in range(4)], 1)
        basis[slot, 2 * RANK :, :] = jnp.broadcast_to(value, (16, PER)).astype(BF)

    def gram_of(slot):
        acc[...] += dot_nt(basis[slot], basis[slot, 0:RANK, :])

    acc[...] = jnp.zeros_like(acc)
    block_of(0, 0)

    def two(step, _):
        block_of(2 * step + 1, 1)
        gram_of(0)
        block_of(2 * step + 2, 0)
        gram_of(1)
        return 0

    lax.fori_loop(0, LEAVES // 2 - 1, two, 0)
    block_of(LEAVES - 1, 1)
    gram_of(0)
    gram_of(1)

    gram = acc[0:RANK, :].astype(BF)
    couple = acc[RANK : 2 * RANK, :].T.astype(BF)
    part = jnp.concatenate([gram, couple], 1)
    chosen = dot_nt(dot(rows[...], part).astype(BF), columns[...]).astype(BF)
    rhs = acc[2 * RANK : 2 * RANK + 1, :]
    rhs = jnp.sum(dot_nt(stack16(split3(rhs), RANK), rows[...]), 0, keepdims=True)
    for k in range(COLS):
        cut = slice(k * SLAB, (k + 1) * SLAB)
        ps[k, :, 0 : 2 * RANK] = part[cut]
        ps[k, :, 2 * RANK :] = chosen[cut]
    rs[...] = jnp.zeros_like(rs)
    rs[0:1, :] = rhs[:, :128]
    rs[1:2, :] = rhs[:, 128:]

    def send_part(k):
        return remote(ps.at[(col + k) % COLS], pr.at[k], (s_p, r_p), k, beside(k))

    def send_rhs(k):
        return remote(rs, rr.at[k], (s_r, r_r), k, beside(k))

    for k in range(1, COLS):
        send_part(k).start()
        send_rhs(k).start()

    whole = jnp.concatenate([sk4[k] for k in range(4)], 1)
    points = dot_nt(whole, fours[...])
    fill = jnp.zeros((256 - 3 * F - 16, RANK), BF)
    points_b = points.astype(BF)
    right = jnp.concatenate([points_b, points_b, points_b, point_side(points, scale2), fill], 0)
    value = jnp.exp2(jnp.minimum(dot(skel_side(points, scale2), right), 0.0))
    crossing = (across(index[...], RANK) >= 2.0 * RANK) != (index[...].T[0:1, :] >= 2.0 * RANK)
    square = iota((RANK, RANK), 0) == iota((RANK, RANK), 1)
    tops[...] = jnp.where(crossing, value, 0.0) + jnp.where(square, ridge[0], 0.0)

    total = ps[col].astype(F32)
    rhs = rs[...]
    for k in range(1, COLS):
        send_part(k).wait_recv()
        total = total + pr[k].astype(F32)
    for k in range(1, COLS):
        send_rhs(k).wait_recv()
        rhs = rhs + rr[k]
    total = total * (1.0 / NODE)
    t4[0] = total[:, 2 * RANK :].astype(BF)
    r4[0] = rhs * (1.0 / NODE)

    def send_top(k):
        return remote(t4.at[0], t4.at[k], (s_t, r_t), k, cousin(k))

    def send_top_rhs(k):
        return remote(r4.at[0], r4.at[k], (s_q, r_q), k, cousin(k))

    for k in range(1, 4):
        send_top(k).start()
        send_top_rhs(k).start()
    diagonal = iota((SLAB, 2 * RANK), 0) + col * SLAB == iota((SLAB, 2 * RANK), 1)
    out_share[0] = total[:, : 2 * RANK] + jnp.where(diagonal, ridge[0], 0.0)
    result = total[:, 2 * RANK :] + tops[pl.ds(pl.multiple_of(col * SLAB, SLAB), SLAB), :]
    rhs = r4[0]
    for k in range(1, 4):
        send_top(k).wait_recv()
        send_top_rhs(k).wait_recv()
        result = result + t4[k].astype(F32)
        rhs = rhs + r4[k]
    out_top[0] = result
    out_rhs[...] = jnp.concatenate([rhs[0:1], rhs[1:2]], 1)

    def finish(k, _):
        send_aux(k).wait_send()
        send_feat(k).wait_send()
        return 0

    lax.fori_loop(1, LEAVES, finish, 0)
    for k in range(1, COLS):
        send_skel(k).wait_send()
        send_part(k).wait_send()
        send_rhs(k).wait_send()
    for k in range(1, 4):
        send_four(k).wait_send()
        send_top(k).wait_send()
        send_top_rhs(k).wait_send()


SHAPES = ((1, SLAB, 2 * RANK), (1, SLAB, RANK), (1, RANK))


def exchange(feat, aux, ridge, *smalls):
    return pl.pallas_call(
        exchange_kernel,
        out_shape=tuple(pltpu.VMEM(shape, F32) for shape in SHAPES),
        in_specs=[VMEM, VMEM, pl.BlockSpec(memory_space=pltpu.SMEM)] + [ANYWHERE] * 4,
        out_specs=[VMEM] * 3,
        scratch_shapes=[
            pltpu.VMEM((1, RANK), jnp.int32),
            pltpu.VMEM((1, F), F32),
            pltpu.VMEM((8, RANK), jnp.int32),
            pltpu.VMEM((4, RANK), jnp.int32),
            pltpu.VMEM((8, 128), F32),
            pltpu.VMEM((LEAVES, F, PER), BF),
            pltpu.VMEM((LEAVES, 8, 128), F32),
            pltpu.VMEM((LEAVES, RANK, PER), BF),
            pltpu.VMEM((LEAVES, 16, PER), BF),
            pltpu.VMEM((COLS, F, RANK), BF),
            pltpu.VMEM((F, RANK), BF),
            pltpu.VMEM((4, F, RANK), BF),
            pltpu.VMEM((2 * RANK, 256), BF),
            pltpu.VMEM((2, 2 * RANK + 16, PER), BF),
            pltpu.VMEM((2 * RANK + 16, RANK), F32),
            pltpu.VMEM((RANK, RANK), BF),
            pltpu.VMEM((RANK, 2 * RANK), BF),
            pltpu.VMEM((RANK, 4 * RANK), BF),
            pltpu.VMEM((RANK, 128), F32),
            pltpu.VMEM((RANK, RANK), F32),
            pltpu.VMEM((COLS, SLAB, 3 * RANK), BF),
            pltpu.VMEM((COLS, SLAB, 3 * RANK), BF),
            pltpu.VMEM((8, 128), F32),
            pltpu.VMEM((COLS, 8, 128), F32),
            pltpu.VMEM((4, SLAB, RANK), BF),
            pltpu.VMEM((4, 8, 128), F32),
            *dma(LEAVES),
            *dma(LEAVES),
            *dma(COLS),
            *dma(4),
            *dma(COLS),
            *dma(COLS),
            *dma(4),
            *dma(4),
            pltpu.SemaphoreType.DMA((4,)),
        ],
        compiler_params=params(0, 40),
        name="exchange",
    )(feat, aux, ridge, *in_hbm(*smalls))


def emit_kernel(*refs):
    ins, outs, sem = refs[:3], refs[3:6], refs[6]
    copies = [pltpu.make_async_copy(a, b, sem.at[k]) for k, (a, b) in enumerate(zip(ins, outs))]
    for copy in copies:
        copy.start()
    for copy in copies:
        copy.wait()


def emit(results):
    return pl.pallas_call(
        emit_kernel,
        out_shape=tuple(jax.ShapeDtypeStruct(shape, F32) for shape in SHAPES),
        in_specs=[VMEM] * 3,
        out_specs=[ANYWHERE] * 3,
        scratch_shapes=[pltpu.SemaphoreType.DMA((3,))],
        compiler_params=params(),
        name="emit",
    )(*results)


def local(features, targets, owner, length_scales, ridge, leaf_pivots, parent_pivots, top_pivots):
    feat, aux = pack(
        features, targets.reshape(ROWS // 128, 128), owner.reshape(ROWS // 128, 128)
    )
    return tuple(
        emit(
            exchange(
                feat, aux, ridge, leaf_pivots, length_scales.reshape(1, F), parent_pivots, top_pivots
            )
        )
    )


def solution(mesh):
    return jax.shard_map(
        local,
        mesh=mesh,
        in_specs=(
            P(None, ("leaf", "col")),
            P(("leaf", "col")),
            P(("leaf", "col")),
            P(),
            P(),
            P("leaf", None),
            P(),
            P(),
        ),
        out_specs=(P("leaf", "col", None), P("leaf", "col", None), P("leaf", None)),
        check_vma=False,
    )
```

```python
import functools
import math

import jax
import jax.numpy as jnp
from jax import lax
from jax.experimental import pallas as pl
from jax.experimental.pallas import tpu as pltpu
from jax.sharding import PartitionSpec as P

F = 48
RANK = 256
ROWS = 8192
LEAVES = 16
COLS = 8
OWNERS = 128
PACKET = 64
PER = ROWS // LEAVES
CHUNK = 256
CHUNKS = ROWS // CHUNK
WINDOW = 40
REGION = PER + WINDOW
WIDE = 64
SLAB = RANK // COLS
NODE = ROWS * COLS
LOG2E = math.log2(math.e)
BF = jnp.bfloat16
F32 = jnp.float32
NT = (((1,), (1,)), ((), ()))
MESH = pl.DeviceIdType.MESH


def dma(count):
    return [pltpu.SemaphoreType.DMA((count,))] * 2


def params(number=None, limit=24):
    if number is None:
        return pltpu.CompilerParams(vmem_limit_bytes=limit * 2**20)
    return pltpu.CompilerParams(
        collective_id=number, has_side_effects=True, vmem_limit_bytes=limit * 2**20
    )


ANYWHERE = pl.BlockSpec(memory_space=pl.ANY)
VMEM = pl.BlockSpec(memory_space=pltpu.VMEM)


def iota(shape, axis):
    return lax.broadcasted_iota(jnp.int32, shape, axis)


def dot(a, b):
    return jnp.dot(a, b, preferred_element_type=F32)


def dot_nt(a, b):
    return lax.dot_general(a, b, NT, preferred_element_type=F32)


def row_pair(two):
    return jnp.concatenate([two[0:1], two[1:2]], 1)


def pack_kernel(
    feat_hbm, target, owner, zbuf, feat, goals, rows, ybuf, table, scal, sem, feat_sem
):
    bring = pltpu.make_async_copy(feat_hbm, feat, feat_sem)
    bring.start()
    goals[...] = target[...].astype(F32)
    before = (iota((CHUNK, CHUNK), 0) < iota((CHUNK, CHUNK), 1)).astype(F32).astype(BF)
    weights = jnp.concatenate([before, jnp.ones((CHUNK, 128), BF)], 1)
    lane = iota((LEAVES, 128), 1)

    def ranks(t, carry):
        seen, seen_leaf, most = carry
        own = row_pair(owner[pl.ds(2 * t, 2), :])
        leaf = own // 8
        is_own = iota((OWNERS, CHUNK), 0) == own
        is_leaf = iota((LEAVES, CHUNK), 0) == leaf
        is_after = iota((LEAVES, CHUNK), 0) > leaf
        marks = jnp.concatenate(
            [m.astype(F32).astype(BF) for m in (is_own, is_leaf, is_after)], 0
        )
        sums = dot(marks, weights)
        counts = sums[:OWNERS, CHUNK:]
        leaf_counts = sums[OWNERS : OWNERS + LEAVES, CHUNK:]
        base = sums[OWNERS + LEAVES :, CHUNK:]
        prior = sums[:OWNERS, :CHUNK] + jnp.concatenate([seen, seen], 1)
        rank = jnp.sum(jnp.where(is_own, prior, 0.0), 0, keepdims=True)
        place = sums[OWNERS : OWNERS + LEAVES, :CHUNK] + jnp.concatenate([base, base], 1)
        place = jnp.sum(jnp.where(is_leaf, place, 0.0), 0, keepdims=True)
        tag = (own % 8).astype(F32) * PACKET + rank - (PER // 2)
        rows[t, 0:1, :] = place
        rows[t, 1:2, :] = row_pair(goals[pl.ds(2 * t, 2), :])
        rows[t, 2:3, :] = tag
        here = lane == t
        table[0:LEAVES, :] = jnp.where(here, seen_leaf.astype(jnp.int32), table[0:LEAVES, :])
        table[LEAVES : 2 * LEAVES, :] = jnp.where(
            here, base.astype(jnp.int32), table[LEAVES : 2 * LEAVES, :]
        )
        return seen + counts, seen_leaf + leaf_counts, jnp.maximum(most, leaf_counts)

    table[0:LEAVES, :] = jnp.full((LEAVES, 128), PER, jnp.int32)
    zero = jnp.zeros((LEAVES, 128), F32)
    _, _, most = lax.fori_loop(
        0, CHUNKS, ranks, (jnp.zeros((OWNERS, 128), F32), zero, zero), unroll=4
    )
    most = jnp.broadcast_to(jnp.max(most, 0, keepdims=True), (8, 128))
    table[2 * LEAVES :, :] = most.astype(jnp.int32)
    move = pltpu.make_async_copy(table, scal, sem)
    move.start()
    bring.wait()

    def sort(t, _):
        start = pl.multiple_of(t * CHUNK, CHUNK)
        row = iota((16, CHUNK), 0)
        place, goal, tag = rows[t, 0:1, :], rows[t, 1:2, :], rows[t, 2:3, :]
        extra = jnp.where(row == 0, goal, jnp.where(row == 1, tag, 0.0)).astype(BF)
        joined = jnp.concatenate([feat[:, pl.ds(start, CHUNK)], extra], 0)
        chosen = (iota((CHUNK, CHUNK), 0) == place.astype(jnp.int32)).astype(F32).astype(BF)
        ybuf[pl.ds(start, CHUNK), :] = dot_nt(chosen, joined)
        return 0

    lax.fori_loop(0, CHUNKS, sort, 0, unroll=4)
    move.wait()
    widest = scal[2 * LEAVES, 0]

    @pl.when(widest <= WINDOW)
    def quick():
        def merge(t, _):
            for i in range(LEAVES):
                source = t * CHUNK + scal[LEAVES + i, t]
                goal = i * REGION + scal[i, t]
                zbuf[pl.ds(goal, WINDOW), :] = ybuf[pl.ds(source, WINDOW), :]
            return 0

        lax.fori_loop(0, CHUNKS, merge, 0, unroll=2)

    @pl.when(widest > WINDOW)
    def slow():
        def merge(index, _):
            t = index // LEAVES
            i = index % LEAVES
            source = t * CHUNK + scal[LEAVES + i, t]
            first = scal[i, t]
            count = scal[i, t + 1] - first

            def part(k, _):
                rows = ybuf[pl.ds(source + 8 * k, 8), :]
                zbuf[pl.ds(i * REGION + first + 8 * k, 8), :] = rows
                return 0

            lax.fori_loop(0, (count + 7) // 8, part, 0)
            return 0

        lax.fori_loop(0, CHUNKS * LEAVES, merge, 0)


def in_hbm(*arrays):
    return [pltpu.with_memory_space_constraint(a, pltpu.HBM) for a in arrays]


def pack(features, targets, owner):
    return pl.pallas_call(
        pack_kernel,
        out_shape=pltpu.VMEM((LEAVES * REGION, WIDE), F32),
        in_specs=[ANYWHERE, VMEM, VMEM],
        out_specs=VMEM,
        scratch_shapes=[
            pltpu.VMEM((F, ROWS), BF),
            pltpu.VMEM((ROWS // 128, 128), F32),
            pltpu.VMEM((CHUNKS, 8, CHUNK), F32),
            pltpu.VMEM((ROWS + WINDOW, WIDE), F32),
            pltpu.VMEM((40, 128), jnp.int32),
            pltpu.SMEM((40, 128), jnp.int32),
            pltpu.SemaphoreType.DMA,
            pltpu.SemaphoreType.DMA,
        ],
        compiler_params=params(),
        name="pack",
    )(*in_hbm(features, targets, owner))


def split3(x):
    high = x.astype(BF)
    rest = x - high.astype(F32)
    mid = rest.astype(BF)
    return high, mid, (rest - mid.astype(F32)).astype(BF)


def stack16(parts, width):
    row = iota((16, width), 0)
    block = jnp.zeros((16, width), F32)
    for k, part in enumerate(parts):
        block = jnp.where(row == k, part if isinstance(part, float) else part.astype(F32), block)
    return block.astype(BF)


def half_norm(points, scale):
    return jnp.sum(points * points * (0.5 * scale), 0, keepdims=True)


def point_side(points, scale):
    high, mid, low = split3(-half_norm(points, scale))
    return stack16([high, mid, low, 1.0, 1.0, 1.0], points.shape[1])


def skel_side(skel, scale):
    width = skel.shape[1]
    high, mid, low = split3(skel * scale)
    extra = stack16([1.0, 1.0, 1.0, *split3(-half_norm(skel, scale))], width)
    parts = [p.astype(F32) for p in (high, mid, low, extra)]
    fill = jnp.zeros((256 - 3 * F - 16, width), F32)
    return jnp.concatenate([*parts, fill], 0).T.astype(BF)


def select_row(table, row):
    hit = iota(table.shape, 0) == row
    return jnp.sum(jnp.where(hit, table.astype(F32), 0.0), 0, keepdims=True)


def to_column(row):
    return jnp.broadcast_to(row, (128, row.shape[1])).T


def across(column, width):
    return jnp.concatenate([column] * (width // 128), 1)


def place_of(leaf, col):
    return dict(device_id=(leaf, col), device_id_type=MESH)


def mate(k):
    leaf, col = lax.axis_index("leaf"), lax.axis_index("col")
    to = (leaf + k) % LEAVES
    cross = (to // 8 + leaf // 8) % 2
    return place_of(to, col + cross * (1 - 2 * (col % 2)))


def beside(k):
    leaf, col = lax.axis_index("leaf"), lax.axis_index("col")
    return place_of(leaf, (col + k) % COLS)


def cousin(k):
    leaf, col = lax.axis_index("leaf"), lax.axis_index("col")
    return place_of(leaf - leaf % 4 + (leaf + k) % 4, col)


def each(count, step, unroll=1):
    lax.fori_loop(1, count, lambda k, _: (step(k), 0)[1], 0, unroll=unroll)


def remote(src, dst, sems, k, peer):
    return pltpu.make_async_remote_copy(src, dst, sems[0].at[k], sems[1].at[k], **peer)


def top_index(parent, top, group):
    top_row = select_row(top[...], group)
    below = jnp.concatenate([select_row(parent[...], 2 * group + r) for r in range(2)], 1)
    number = iota((RANK, 2 * RANK), 1)
    below = below + jnp.where(iota((1, 2 * RANK), 1) >= RANK, 2.0 * RANK, 0.0)
    hit = across(to_column(top_row), 2 * RANK) == number.astype(F32)
    index = jnp.sum(jnp.where(hit, below, 0.0), 1, keepdims=True)
    return jnp.broadcast_to(index, (RANK, 128))


def exchange_kernel(
    merged, ridge, pivots_hbm, scales_hbm, parent_hbm, top_hbm, out_share, out_top, out_rhs,
    pivots, scales, parent, top, spare, feat, aux, rx, ra, hot, side, sk, mine, sk4, left,
    even, odd, acc, rows, columns, fours, index, tops, ps, pr, pt, qr, rs, rr, t4, r4,
    s_f, r_f, s_a, r_a, s_k, r_k, s_4, r_4, s_p, r_p, s_o, r_o, s_r, r_r, s_t, r_t, s_q, r_q, local,
):
    leaf = lax.axis_index("leaf")
    col = lax.axis_index("col")
    quarter = leaf % 4
    sibling = quarter + 1 - 2 * (quarter % 2)
    barrier = pltpu.get_barrier_semaphore()
    each(LEAVES, lambda k: pl.semaphore_signal(barrier, inc=1, **mate(k)))
    each(COLS, lambda k: pl.semaphore_signal(barrier, inc=1, **beside(k)))
    smalls = [
        pltpu.make_async_copy(a, b, local.at[k])
        for k, (a, b) in enumerate(
            [(pivots_hbm, pivots), (scales_hbm, scales), (parent_hbm, parent), (top_hbm, top)]
        )
    ]
    for copy in smalls:
        copy.start()

    eye = (iota((WIDE, WIDE), 0) == iota((WIDE, WIDE), 1)).astype(F32).astype(BF)

    def turn(k, _):
        start = pl.multiple_of((leaf + k) % LEAVES * REGION, 8)
        turned = dot_nt(eye, merged[pl.ds(start, PER), :].astype(BF))
        feat[k] = turned[:F].astype(BF)
        aux[k] = jnp.concatenate(
            [turned[F + r : F + r + 1, 128 * k : 128 * k + 128] for r in range(2) for k in range(4)], 0
        )
        return 0

    def send_feat(k):
        return remote(feat.at[k], rx.at[k], (s_f, r_f), k, mate(k))

    def send_aux(k):
        return remote(aux.at[k], ra.at[k], (s_a, r_a), k, mate(k))

    lax.fori_loop(0, LEAVES, turn, 0, unroll=4)
    rx[0] = feat[0]
    ra[0] = aux[0]
    pl.semaphore_wait(barrier, LEAVES + COLS - 2)
    each(LEAVES, lambda k: send_aux(k).start())
    each(LEAVES, lambda k: send_feat(k).start())

    for copy in smalls:
        copy.wait()
    spare[...] = jnp.ones((8, 128), F32)
    spare[0:1, 0:F] = scales[...]
    inverse = 1.0 / to_column(spare[0:1, :])[:F]
    scale = inverse * inverse * LOG2E
    scale2 = across(scale, RANK)
    scale4 = across(scale, PER)

    place = pivots[...]
    within = place % ROWS
    block = within // PACKET
    key = (block // COLS) * PER + (place // ROWS) * PACKET + within % PACKET
    holder = block % COLS
    crossed = (block // COLS) // 8 != leaf // 8
    holder = jnp.where(crossed, holder + 1 - 2 * (holder % 2), holder)
    key = jnp.where(holder == col, key, -PER)
    key = across(to_column(key.astype(F32)), PER)

    def mark(k):
        source = (leaf + LEAVES - k) % LEAVES
        tags = ra[k, 4:8, :]
        tag = jnp.concatenate([tags[r : r + 1] for r in range(4)], 1)
        wanted = tag + (PER // 2 + source * PER).astype(F32)
        hot[k] = (key == wanted).astype(F32).astype(BF)

    def mark_next(k, _):
        pl.when(k > 0)(lambda: send_aux(k).wait_recv())
        mark(k)
        return 0

    lax.fori_loop(0, LEAVES, mark_next, 0)

    index[...] = top_index(parent, top, leaf // 4)
    index2 = across(index[...], 2 * RANK)
    number = iota((RANK, 2 * RANK), 1)
    base = (quarter * RANK).astype(F32)
    other = (sibling * RANK).astype(F32)
    chosen = index2[:, :RANK] == iota((RANK, RANK), 1).astype(F32) + base
    rows[...] = chosen.astype(F32).astype(BF)
    lanes = number.astype(F32) + jnp.where(number < RANK, base, other - RANK)
    columns[...] = (index2 == lanes).astype(F32).astype(BF)
    chosen = across(index[...], 4 * RANK) == iota((RANK, 4 * RANK), 1).astype(F32)
    fours[...] = chosen.astype(F32).astype(BF)

    def pick(j, total):
        for r in range(4):
            k = 4 * j + r
            if r:
                send_feat(k).wait_recv()
            else:
                pl.when(k > 0)(lambda: send_feat(k).wait_recv())
        for r in range(4):
            total = total + dot_nt(hot[4 * j + r], rx[4 * j + r])
        return total

    picked = lax.fori_loop(0, LEAVES // 4, pick, jnp.zeros((RANK, F), F32))
    picked = jnp.concatenate([picked, jnp.zeros((RANK, 128 - F), F32)], 1).T[:F]
    sk[0] = picked.astype(BF)

    def send_skel(k):
        return remote(sk.at[0], sk.at[k], (s_k, r_k), k, beside(k))

    each(COLS, lambda k: send_skel(k).start())

    def norms(k, _):
        side[k] = point_side(rx[k].astype(F32), scale4)
        return 0

    lax.fori_loop(0, LEAVES, norms, 0)

    def add_skel(k, total):
        send_skel(k).wait_recv()
        return total + sk[k].astype(F32)

    picked = lax.fori_loop(1, COLS, add_skel, picked)
    mine[...] = picked.astype(BF)
    sk4[quarter] = picked.astype(BF)

    def send_four(k):
        return remote(mine, sk4.at[quarter], (s_4, r_4), k, cousin(k))

    each(4, lambda k: send_four(k).start())
    left[0:RANK, :] = skel_side(picked, scale2)
    each(4, lambda k: remote(mine, sk4.at[(quarter + 4 - k) % 4], (s_4, r_4), k, cousin(k)).wait_recv())
    left[RANK:, :] = skel_side(sk4[sibling].astype(F32), scale2)

    def block_of(k, half):
        p = rx[k]
        fill = jnp.zeros((256 - 3 * F - 16, PER), BF)
        power = dot(left[...], jnp.concatenate([p, p, p, side[k], fill], 0))
        half[0 : 2 * RANK, :] = jnp.exp2(jnp.minimum(power, 0.0)).astype(BF)
        value = jnp.concatenate([ra[k, r : r + 1, :] for r in range(4)], 1)
        half[2 * RANK :, :] = jnp.broadcast_to(value, (16, PER)).astype(BF)

    def gram_of(half):
        acc[...] += dot_nt(half[...], half[0:RANK, :])

    def two(j, _):
        block_of(2 * j, even)
        gram_of(odd)
        block_of(2 * j + 1, odd)
        gram_of(even)
        return 0

    acc[...] = jnp.zeros_like(acc)
    odd[...] = jnp.zeros_like(odd)
    lax.fori_loop(0, LEAVES // 2, two, 0)
    gram_of(odd)

    gram = acc[0:RANK, :].astype(BF)
    couple = acc[RANK : 2 * RANK, :].T.astype(BF)
    part = jnp.concatenate([gram, couple], 1)
    for k in range(COLS):
        ps[k] = part[k * SLAB : (k + 1) * SLAB]

    def send_part(k):
        return remote(ps.at[(col + k) % COLS], pr.at[k], (s_p, r_p), k, beside(k))

    def send_chosen(k):
        return remote(pt.at[(col + k) % COLS], qr.at[k], (s_o, r_o), k, beside(k))

    def send_rhs(k):
        return remote(rs, rr.at[k], (s_r, r_r), k, beside(k))

    each(COLS, lambda k: send_part(k).start())
    rhs = acc[2 * RANK : 2 * RANK + 1, :]
    rhs = jnp.sum(dot_nt(stack16(split3(rhs), RANK), rows[...]), 0, keepdims=True)
    rs[...] = jnp.zeros_like(rs)
    rs[0:1, :] = rhs[:, :128]
    rs[1:2, :] = rhs[:, 128:]
    chosen = dot_nt(dot(rows[...], part).astype(BF), columns[...]).astype(BF)
    for k in range(COLS):
        pt[k] = chosen[k * SLAB : (k + 1) * SLAB]
    each(COLS, lambda k: send_chosen(k).start())
    each(COLS, lambda k: send_rhs(k).start())

    whole = jnp.concatenate([sk4[k] for k in range(4)], 1)
    points = dot_nt(whole, fours[...])
    fill = jnp.zeros((256 - 3 * F - 16, RANK), BF)
    points_b = points.astype(BF)
    right = jnp.concatenate([points_b, points_b, points_b, point_side(points, scale2), fill], 0)
    value = jnp.exp2(jnp.minimum(dot(skel_side(points, scale2), right), 0.0))
    crossing = (across(index[...], RANK) >= 2.0 * RANK) != (index[...].T[0:1, :] >= 2.0 * RANK)
    square = iota((RANK, RANK), 0) == iota((RANK, RANK), 1)
    tops[...] = jnp.where(crossing, value, 0.0) + jnp.where(square, ridge[0], 0.0)

    def add_part(k, total):
        send_part(k).wait_recv()
        return total + pr[k].astype(F32)

    def add_chosen(k, totals):
        send_chosen(k).wait_recv()
        send_rhs(k).wait_recv()
        return totals[0] + qr[k].astype(F32), totals[1] + rr[k]

    total = lax.fori_loop(1, COLS, add_part, ps[col].astype(F32))
    diagonal = iota((SLAB, 2 * RANK), 0) + col * SLAB == iota((SLAB, 2 * RANK), 1)
    out_share[0] = total * (1.0 / NODE) + jnp.where(diagonal, ridge[0], 0.0)
    chosen, rhs = lax.fori_loop(1, COLS, add_chosen, (pt[col].astype(F32), rs[...]))
    chosen = chosen * (1.0 / NODE)
    t4[0] = chosen.astype(BF)
    r4[0] = rhs * (1.0 / NODE)

    def send_top(k):
        return remote(t4.at[0], t4.at[k], (s_t, r_t), k, cousin(k))

    def send_top_rhs(k):
        return remote(r4.at[0], r4.at[k], (s_q, r_q), k, cousin(k))

    each(4, lambda k: send_top(k).start())
    each(4, lambda k: send_top_rhs(k).start())
    result = chosen + tops[pl.ds(pl.multiple_of(col * SLAB, SLAB), SLAB), :]

    def add_top(k, totals):
        send_top(k).wait_recv()
        send_top_rhs(k).wait_recv()
        return totals[0] + t4[k].astype(F32), totals[1] + r4[k]

    result, rhs = lax.fori_loop(1, 4, add_top, (result, r4[0]))
    out_top[0] = result
    out_rhs[...] = jnp.concatenate([rhs[0:1], rhs[1:2]], 1)

    def finish(sends):
        return lambda k: [send(k).wait_send() for send in sends]

    each(LEAVES, finish((send_aux, send_feat)))
    each(COLS, finish((send_skel, send_part, send_chosen, send_rhs)))
    each(4, finish((send_four, send_top, send_top_rhs)))


SHAPES = ((1, SLAB, 2 * RANK), (1, SLAB, RANK), (1, RANK))


def exchange(merged, ridge, *smalls):
    return pl.pallas_call(
        exchange_kernel,
        out_shape=tuple(pltpu.VMEM(shape, F32) for shape in SHAPES),
        in_specs=[VMEM, pl.BlockSpec(memory_space=pltpu.SMEM)] + [ANYWHERE] * 4,
        out_specs=[VMEM] * 3,
        scratch_shapes=[
            pltpu.VMEM((1, RANK), jnp.int32),
            pltpu.VMEM((1, F), F32),
            pltpu.VMEM((8, RANK), jnp.int32),
            pltpu.VMEM((4, RANK), jnp.int32),
            pltpu.VMEM((8, 128), F32),
            pltpu.VMEM((LEAVES, F, PER), BF),
            pltpu.VMEM((LEAVES, 8, 128), F32),
            pltpu.VMEM((LEAVES, F, PER), BF),
            pltpu.VMEM((LEAVES, 8, 128), F32),
            pltpu.VMEM((LEAVES, RANK, PER), BF),
            pltpu.VMEM((LEAVES, 16, PER), BF),
            pltpu.VMEM((COLS, F, RANK), BF),
            pltpu.VMEM((F, RANK), BF),
            pltpu.VMEM((4, F, RANK), BF),
            pltpu.VMEM((2 * RANK, 256), BF),
            pltpu.VMEM((2 * RANK + 16, PER), BF),
            pltpu.VMEM((2 * RANK + 16, PER), BF),
            pltpu.VMEM((2 * RANK + 16, RANK), F32),
            pltpu.VMEM((RANK, RANK), BF),
            pltpu.VMEM((RANK, 2 * RANK), BF),
            pltpu.VMEM((RANK, 4 * RANK), BF),
            pltpu.VMEM((RANK, 128), F32),
            pltpu.VMEM((RANK, RANK), F32),
            pltpu.VMEM((COLS, SLAB, 2 * RANK), BF),
            pltpu.VMEM((COLS, SLAB, 2 * RANK), BF),
            pltpu.VMEM((COLS, SLAB, RANK), BF),
            pltpu.VMEM((COLS, SLAB, RANK), BF),
            pltpu.VMEM((8, 128), F32),
            pltpu.VMEM((COLS, 8, 128), F32),
            pltpu.VMEM((4, SLAB, RANK), BF),
            pltpu.VMEM((4, 8, 128), F32),
            *dma(LEAVES),
            *dma(LEAVES),
            *dma(COLS),
            *dma(4),
            *dma(COLS),
            *dma(COLS),
            *dma(COLS),
            *dma(4),
            *dma(4),
            pltpu.SemaphoreType.DMA((4,)),
        ],
        compiler_params=params(0, 40),
        name="exchange",
    )(merged, ridge, *in_hbm(*smalls))


def emit_kernel(*refs):
    ins, outs, sem = refs[:3], refs[3:6], refs[6]
    copies = [pltpu.make_async_copy(a, b, sem.at[k]) for k, (a, b) in enumerate(zip(ins, outs))]
    for copy in copies:
        copy.start()
    for copy in copies:
        copy.wait()


def emit(results):
    return pl.pallas_call(
        emit_kernel,
        out_shape=tuple(jax.ShapeDtypeStruct(shape, F32) for shape in SHAPES),
        in_specs=[VMEM] * 3,
        out_specs=[ANYWHERE] * 3,
        scratch_shapes=[pltpu.SemaphoreType.DMA((3,))],
        compiler_params=params(),
        name="emit",
    )(*results)


def local(features, targets, owner, length_scales, ridge, leaf_pivots, parent_pivots, top_pivots):
    merged = pack(features, targets.reshape(ROWS // 128, 128), owner.reshape(ROWS // 128, 128))
    smalls = (leaf_pivots, length_scales.reshape(1, F), parent_pivots, top_pivots)
    return tuple(emit(exchange(merged, ridge, *smalls)))


def solution(mesh):
    return jax.shard_map(
        local,
        mesh=mesh,
        in_specs=(
            P(None, ("leaf", "col")),
            P(("leaf", "col")),
            P(("leaf", "col")),
            P(),
            P(),
            P("leaf", None),
            P(),
            P(),
        ),
        out_specs=(P("leaf", "col", None), P("leaf", "col", None), P("leaf", None)),
        check_vma=False,
    )
```

```python
import functools
import math

import jax
import jax.numpy as jnp
from jax import lax
from jax.experimental import pallas as pl
from jax.experimental.pallas import tpu as pltpu
from jax.sharding import PartitionSpec as P

F = 48
RANK = 256
ROWS = 8192
LEAVES = 16
COLS = 8
OWNERS = 128
PACKET = 64
PER = ROWS // LEAVES
CHUNK = 256
CHUNKS = ROWS // CHUNK
WINDOW = 40
REGION = PER + WINDOW
WIDE = 64
SLAB = RANK // COLS
NODE = ROWS * COLS
LOG2E = math.log2(math.e)
BF = jnp.bfloat16
F32 = jnp.float32
NT = (((1,), (1,)), ((), ()))
MESH = pl.DeviceIdType.MESH


def dma(count):
    return [pltpu.SemaphoreType.DMA((count,))] * 2


def params(number=None, limit=24):
    if number is None:
        return pltpu.CompilerParams(vmem_limit_bytes=limit * 2**20)
    return pltpu.CompilerParams(
        collective_id=number, has_side_effects=True, vmem_limit_bytes=limit * 2**20
    )


ANYWHERE = pl.BlockSpec(memory_space=pl.ANY)
VMEM = pl.BlockSpec(memory_space=pltpu.VMEM)


def iota(shape, axis):
    return lax.broadcasted_iota(jnp.int32, shape, axis)


def dot(a, b):
    return jnp.dot(a, b, preferred_element_type=F32)


def dot_nt(a, b):
    return lax.dot_general(a, b, NT, preferred_element_type=F32)


def row_pair(two):
    return jnp.concatenate([two[0:1], two[1:2]], 1)


def pack_kernel(
    feat_hbm, target, owner, zbuf, feat, goals, rows, ybuf, table, scal, sem, feat_sem
):
    bring = pltpu.make_async_copy(feat_hbm, feat, feat_sem)
    bring.start()
    goals[...] = target[...].astype(F32)
    before = (iota((CHUNK, CHUNK), 0) < iota((CHUNK, CHUNK), 1)).astype(F32).astype(BF)
    weights = jnp.concatenate([before, jnp.ones((CHUNK, 128), BF)], 1)
    lane = iota((LEAVES, 128), 1)

    def ranks(t, carry):
        seen, seen_leaf, most = carry
        own = row_pair(owner[pl.ds(2 * t, 2), :])
        leaf = own // 8
        is_own = iota((OWNERS, CHUNK), 0) == own
        is_leaf = iota((LEAVES, CHUNK), 0) == leaf
        is_after = iota((LEAVES, CHUNK), 0) > leaf
        marks = jnp.concatenate(
            [m.astype(F32).astype(BF) for m in (is_own, is_leaf, is_after)], 0
        )
        sums = dot(marks, weights)
        counts = sums[:OWNERS, CHUNK:]
        leaf_counts = sums[OWNERS : OWNERS + LEAVES, CHUNK:]
        base = sums[OWNERS + LEAVES :, CHUNK:]
        prior = sums[:OWNERS, :CHUNK] + jnp.concatenate([seen, seen], 1)
        rank = jnp.sum(jnp.where(is_own, prior, 0.0), 0, keepdims=True)
        place = sums[OWNERS : OWNERS + LEAVES, :CHUNK] + jnp.concatenate([base, base], 1)
        place = jnp.sum(jnp.where(is_leaf, place, 0.0), 0, keepdims=True)
        tag = (own % 8).astype(F32) * PACKET + rank - (PER // 2)
        rows[t, 0:1, :] = place
        rows[t, 1:2, :] = row_pair(goals[pl.ds(2 * t, 2), :])
        rows[t, 2:3, :] = tag
        here = lane == t
        table[0:LEAVES, :] = jnp.where(here, seen_leaf.astype(jnp.int32), table[0:LEAVES, :])
        table[LEAVES : 2 * LEAVES, :] = jnp.where(
            here, base.astype(jnp.int32), table[LEAVES : 2 * LEAVES, :]
        )
        return seen + counts, seen_leaf + leaf_counts, jnp.maximum(most, leaf_counts)

    table[0:LEAVES, :] = jnp.full((LEAVES, 128), PER, jnp.int32)
    zero = jnp.zeros((LEAVES, 128), F32)
    _, _, most = lax.fori_loop(
        0, CHUNKS, ranks, (jnp.zeros((OWNERS, 128), F32), zero, zero), unroll=16
    )
    most = jnp.broadcast_to(jnp.max(most, 0, keepdims=True), (8, 128))
    table[2 * LEAVES :, :] = most.astype(jnp.int32)
    move = pltpu.make_async_copy(table, scal, sem)
    move.start()
    bring.wait()

    def sort(t, _):
        start = pl.multiple_of(t * CHUNK, CHUNK)
        row = iota((16, CHUNK), 0)
        place, goal, tag = rows[t, 0:1, :], rows[t, 1:2, :], rows[t, 2:3, :]
        extra = jnp.where(row == 0, goal, jnp.where(row == 1, tag, 0.0)).astype(BF)
        joined = jnp.concatenate([feat[:, pl.ds(start, CHUNK)], extra], 0)
        chosen = (iota((CHUNK, CHUNK), 0) == place.astype(jnp.int32)).astype(F32).astype(BF)
        ybuf[pl.ds(start, CHUNK), :] = dot_nt(chosen, joined)
        return 0

    lax.fori_loop(0, CHUNKS, sort, 0, unroll=8)
    move.wait()
    widest = scal[2 * LEAVES, 0]

    @pl.when(widest <= WINDOW)
    def quick():
        def merge(t, _):
            for i in range(LEAVES):
                source = t * CHUNK + scal[LEAVES + i, t]
                goal = i * REGION + scal[i, t]
                zbuf[pl.ds(goal, WINDOW), :] = ybuf[pl.ds(source, WINDOW), :]
            return 0

        lax.fori_loop(0, CHUNKS, merge, 0, unroll=4)

    @pl.when(widest > WINDOW)
    def slow():
        def merge(index, _):
            t = index // LEAVES
            i = index % LEAVES
            source = t * CHUNK + scal[LEAVES + i, t]
            first = scal[i, t]
            count = scal[i, t + 1] - first

            def part(k, _):
                rows = ybuf[pl.ds(source + 8 * k, 8), :]
                zbuf[pl.ds(i * REGION + first + 8 * k, 8), :] = rows
                return 0

            lax.fori_loop(0, (count + 7) // 8, part, 0)
            return 0

        lax.fori_loop(0, CHUNKS * LEAVES, merge, 0)


def in_hbm(*arrays):
    return [pltpu.with_memory_space_constraint(a, pltpu.HBM) for a in arrays]


def pack(features, targets, owner):
    return pl.pallas_call(
        pack_kernel,
        out_shape=pltpu.VMEM((LEAVES * REGION, WIDE), F32),
        in_specs=[ANYWHERE, VMEM, VMEM],
        out_specs=VMEM,
        scratch_shapes=[
            pltpu.VMEM((F, ROWS), BF),
            pltpu.VMEM((ROWS // 128, 128), F32),
            pltpu.VMEM((CHUNKS, 8, CHUNK), F32),
            pltpu.VMEM((ROWS + WINDOW, WIDE), F32),
            pltpu.VMEM((40, 128), jnp.int32),
            pltpu.SMEM((40, 128), jnp.int32),
            pltpu.SemaphoreType.DMA,
            pltpu.SemaphoreType.DMA,
        ],
        compiler_params=params(),
        name="pack",
    )(*in_hbm(features, targets, owner))


def split3(x):
    high = x.astype(BF)
    rest = x - high.astype(F32)
    mid = rest.astype(BF)
    return high, mid, (rest - mid.astype(F32)).astype(BF)


def stack16(parts, width):
    row = iota((16, width), 0)
    block = jnp.zeros((16, width), F32)
    for k, part in enumerate(parts):
        block = jnp.where(row == k, part if isinstance(part, float) else part.astype(F32), block)
    return block.astype(BF)


def half_norm(points, scale):
    return jnp.sum(points * points * (0.5 * scale), 0, keepdims=True)


def point_side(points, scale):
    high, mid, low = split3(-half_norm(points, scale))
    return stack16([high, mid, low, 1.0, 1.0, 1.0], points.shape[1])


def skel_side(skel, scale):
    width = skel.shape[1]
    high, mid, low = split3(skel * scale)
    extra = stack16([1.0, 1.0, 1.0, *split3(-half_norm(skel, scale))], width)
    parts = [p.astype(F32) for p in (high, mid, low, extra)]
    fill = jnp.zeros((256 - 3 * F - 16, width), F32)
    return jnp.concatenate([*parts, fill], 0).T.astype(BF)


def select_row(table, row):
    hit = iota(table.shape, 0) == row
    return jnp.sum(jnp.where(hit, table.astype(F32), 0.0), 0, keepdims=True)


def to_column(row):
    return jnp.broadcast_to(row, (128, row.shape[1])).T


def across(column, width):
    return jnp.concatenate([column] * (width // 128), 1)


def place_of(leaf, col):
    return dict(device_id=(leaf, col), device_id_type=MESH)


def mate(k):
    leaf, col = lax.axis_index("leaf"), lax.axis_index("col")
    to = (leaf + k) % LEAVES
    cross = (to // 8 + leaf // 8) % 2
    return place_of(to, col + cross * (1 - 2 * (col % 2)))


def beside(k):
    leaf, col = lax.axis_index("leaf"), lax.axis_index("col")
    return place_of(leaf, (col + k) % COLS)


def cousin(k):
    leaf, col = lax.axis_index("leaf"), lax.axis_index("col")
    return place_of(leaf - leaf % 4 + (leaf + k) % 4, col)


def each(count, step, unroll=1):
    lax.fori_loop(1, count, lambda k, _: (step(k), 0)[1], 0, unroll=unroll)


def remote(src, dst, sems, k, peer):
    return pltpu.make_async_remote_copy(src, dst, sems[0].at[k], sems[1].at[k], **peer)


def top_index(parent, top, group):
    top_row = select_row(top[...], group)
    below = jnp.concatenate([select_row(parent[...], 2 * group + r) for r in range(2)], 1)
    number = iota((RANK, 2 * RANK), 1)
    below = below + jnp.where(iota((1, 2 * RANK), 1) >= RANK, 2.0 * RANK, 0.0)
    hit = across(to_column(top_row), 2 * RANK) == number.astype(F32)
    index = jnp.sum(jnp.where(hit, below, 0.0), 1, keepdims=True)
    return jnp.broadcast_to(index, (RANK, 128))


def exchange_kernel(
    merged, ridge, pivots_hbm, scales_hbm, parent_hbm, top_hbm, out_share, out_top, out_rhs,
    pivots, scales, parent, top, spare, feat, aux, rx, ra, hot, side, sk, mine, sk4, left,
    even, odd, other_even, other_odd, gram, couple, rows, columns, fours, index, tops,
    pg, gr, pc, cr, pt, qr, rs, rr, t4, r4,
    s_f, r_f, s_a, r_a, s_k, r_k, s_4, r_4, s_p, r_p, s_c, r_c, s_o, r_o, s_r, r_r, s_t, r_t, s_q, r_q, local,
):
    leaf = lax.axis_index("leaf")
    col = lax.axis_index("col")
    quarter = leaf % 4
    sibling = quarter + 1 - 2 * (quarter % 2)
    barrier = pltpu.get_barrier_semaphore()
    each(LEAVES, lambda k: pl.semaphore_signal(barrier, inc=1, **mate(k)))
    each(COLS, lambda k: pl.semaphore_signal(barrier, inc=1, **beside(k)))
    smalls = [
        pltpu.make_async_copy(a, b, local.at[k])
        for k, (a, b) in enumerate(
            [(pivots_hbm, pivots), (scales_hbm, scales), (parent_hbm, parent), (top_hbm, top)]
        )
    ]
    for copy in smalls:
        copy.start()

    eye = (iota((WIDE, WIDE), 0) == iota((WIDE, WIDE), 1)).astype(F32).astype(BF)

    def turn(k):
        start = pl.multiple_of((leaf + k) % LEAVES * REGION, 8)
        turned = dot_nt(eye, merged[pl.ds(start, PER), :].astype(BF))
        feat[k] = turned[:F].astype(BF)
        aux[k] = jnp.concatenate(
            [turned[F + r : F + r + 1, 128 * c : 128 * c + 128] for r in range(2) for c in range(4)], 0
        )

    def send_feat(k):
        return remote(feat.at[k], rx.at[k], (s_f, r_f), k, mate(k))

    def send_aux(k):
        return remote(aux.at[k], ra.at[k], (s_a, r_a), k, mate(k))

    def four(j, _):
        for r in range(1, 5):
            turn((4 * j + r) % LEAVES)
        pl.when(j == 0)(lambda: pl.semaphore_wait(barrier, LEAVES + COLS - 2))
        for send in (send_aux, send_feat):
            for r in range(1, 4):
                send(4 * j + r).start()
            pl.when(j < 3)(lambda: send(4 * j + 4).start())
        return 0

    lax.fori_loop(0, LEAVES // 4, four, 0)
    rx[0] = feat[0]
    ra[0] = aux[0]

    for copy in smalls:
        copy.wait()
    spare[...] = jnp.ones((8, 128), F32)
    spare[0:1, 0:F] = scales[...]
    inverse = 1.0 / to_column(spare[0:1, :])[:F]
    scale = inverse * inverse * LOG2E
    scale2 = across(scale, RANK)
    scale4 = across(scale, PER)

    place = pivots[...]
    within = place % ROWS
    block = within // PACKET
    key = (block // COLS) * PER + (place // ROWS) * PACKET + within % PACKET
    holder = block % COLS
    crossed = (block // COLS) // 8 != leaf // 8
    holder = jnp.where(crossed, holder + 1 - 2 * (holder % 2), holder)
    key = jnp.where(holder == col, key, -PER)
    key = across(to_column(key.astype(F32)), PER)

    def mark(k):
        source = (leaf + LEAVES - k) % LEAVES
        tags = ra[k, 4:8, :]
        tag = jnp.concatenate([tags[r : r + 1] for r in range(4)], 1)
        wanted = tag + (PER // 2 + source * PER).astype(F32)
        hot[k] = (key == wanted).astype(F32).astype(BF)

    def mark_next(k, _):
        pl.when(k > 0)(lambda: send_aux(k).wait_recv())
        mark(k)
        return 0

    lax.fori_loop(0, LEAVES, mark_next, 0)

    index[...] = top_index(parent, top, leaf // 4)
    index2 = across(index[...], 2 * RANK)
    number = iota((RANK, 2 * RANK), 1)
    base = (quarter * RANK).astype(F32)
    other = (sibling * RANK).astype(F32)
    chosen = index2[:, :RANK] == iota((RANK, RANK), 1).astype(F32) + base
    rows[...] = chosen.astype(F32).astype(BF)
    lanes = number.astype(F32) + jnp.where(number < RANK, base, other - RANK)
    columns[...] = (index2 == lanes).astype(F32).astype(BF)
    chosen = across(index[...], 4 * RANK) == iota((RANK, 4 * RANK), 1).astype(F32)
    fours[...] = chosen.astype(F32).astype(BF)

    def pick(j, total):
        for r in range(4):
            k = 4 * j + r
            if r:
                send_feat(k).wait_recv()
            else:
                pl.when(k > 0)(lambda: send_feat(k).wait_recv())
        for r in range(4):
            total = total + dot_nt(hot[4 * j + r], rx[4 * j + r])
        return total

    picked = lax.fori_loop(0, LEAVES // 4, pick, jnp.zeros((RANK, F), F32))
    picked = jnp.concatenate([picked, jnp.zeros((RANK, 128 - F), F32)], 1).T[:F]
    sk[0] = picked.astype(BF)

    def send_skel(k):
        return remote(sk.at[0], sk.at[k], (s_k, r_k), k, beside(k))

    each(COLS, lambda k: send_skel(k).start())

    def norms(k, _):
        side[k] = point_side(rx[k].astype(F32), scale4)
        return 0

    lax.fori_loop(0, LEAVES, norms, 0)

    def add_skel(k, total):
        send_skel(k).wait_recv()
        return total + sk[k].astype(F32)

    picked = lax.fori_loop(1, COLS, add_skel, picked)
    mine[...] = picked.astype(BF)
    sk4[quarter] = picked.astype(BF)

    def send_four(k):
        return remote(mine, sk4.at[quarter], (s_4, r_4), k, cousin(k))

    each(4, lambda k: send_four(k).start())
    left[0:RANK, :] = skel_side(picked, scale2)

    def block_of(k, out, begin):
        p = rx[k]
        fill = jnp.zeros((256 - 3 * F - 16, PER), BF)
        right = jnp.concatenate([p, p, p, side[k], fill], 0)
        power = dot(left[begin : begin + RANK, :], right)
        out[0:RANK, :] = jnp.exp2(jnp.minimum(power, 0.0)).astype(BF)

    def own_of(k, out):
        block_of(k, out, 0)
        value = jnp.concatenate([ra[k, r : r + 1, :] for r in range(4)], 1)
        out[RANK:, :] = jnp.broadcast_to(value, (16, PER)).astype(BF)

    def gram_of(u):
        gram[...] += dot_nt(u[...], u[0:RANK, :])

    def couple_of(v, u):
        couple[...] += dot_nt(v[...], u[0:RANK, :])

    last = LEAVES // 2 - 1

    def own_two(j, _):
        own_of(2 * j, even.at[j])
        gram_of(odd.at[(j + last) % (last + 1)])
        own_of(2 * j + 1, odd.at[j])
        gram_of(even.at[j])
        return 0

    def other_two(j, _):
        block_of(2 * j, other_even, RANK)
        couple_of(other_odd, odd.at[(j + last) % (last + 1)])
        block_of(2 * j + 1, other_odd, RANK)
        couple_of(other_even, even.at[j])
        return 0

    gram[...] = jnp.zeros_like(gram)
    couple[...] = jnp.zeros_like(couple)
    odd[last] = jnp.zeros((RANK + 16, PER), BF)
    other_odd[...] = jnp.zeros_like(other_odd)
    lax.fori_loop(0, last + 1, own_two, 0)
    gram_of(odd.at[last])

    def send_gram(k):
        return remote(pg.at[(col + k) % COLS], gr.at[k], (s_p, r_p), k, beside(k))

    def send_couple(k):
        return remote(pc.at[(col + k) % COLS], cr.at[k], (s_c, r_c), k, beside(k))

    def send_chosen(k):
        return remote(pt.at[(col + k) % COLS], qr.at[k], (s_o, r_o), k, beside(k))

    def send_rhs(k):
        return remote(rs, rr.at[k], (s_r, r_r), k, beside(k))

    part = gram[0:RANK, :].astype(BF)
    for k in range(COLS):
        pg[k] = part[k * SLAB : (k + 1) * SLAB]
    rhs = gram[RANK : RANK + 1, :]
    rhs = jnp.sum(dot_nt(stack16(split3(rhs), RANK), rows[...]), 0, keepdims=True)
    rs[...] = jnp.zeros_like(rs)
    rs[0:1, :] = rhs[:, :128]
    rs[1:2, :] = rhs[:, 128:]
    each(COLS, lambda k: send_gram(k).start())
    each(COLS, lambda k: send_rhs(k).start())
    tops[...] = dot_nt(dot(rows[...], part).astype(BF), columns[:, 0:RANK])

    each(4, lambda k: remote(mine, sk4.at[(quarter + 4 - k) % 4], (s_4, r_4), k, cousin(k)).wait_recv())
    left[RANK:, :] = skel_side(sk4[sibling].astype(F32), scale2)
    lax.fori_loop(0, last + 1, other_two, 0)
    couple_of(other_odd, odd.at[last])

    part = couple[...].astype(BF)
    chosen = dot_nt(dot_nt(rows[...], part).astype(BF), columns[:, RANK:]) + tops[...]
    chosen = chosen.astype(BF)
    for k in range(COLS):
        pt[k] = chosen[k * SLAB : (k + 1) * SLAB]
    each(COLS, lambda k: send_chosen(k).start())
    part = couple[...].T.astype(BF)
    for k in range(COLS):
        pc[k] = part[k * SLAB : (k + 1) * SLAB]
    each(COLS, lambda k: send_couple(k).start())

    whole = jnp.concatenate([sk4[k] for k in range(4)], 1)
    points = dot_nt(whole, fours[...])
    fill = jnp.zeros((256 - 3 * F - 16, RANK), BF)
    points_b = points.astype(BF)
    right = jnp.concatenate([points_b, points_b, points_b, point_side(points, scale2), fill], 0)
    value = jnp.exp2(jnp.minimum(dot(skel_side(points, scale2), right), 0.0))
    crossing = (across(index[...], RANK) >= 2.0 * RANK) != (index[...].T[0:1, :] >= 2.0 * RANK)
    square = iota((RANK, RANK), 0) == iota((RANK, RANK), 1)
    tops[...] = jnp.where(crossing, value, 0.0) + jnp.where(square, ridge[0], 0.0)

    def add_chosen(k, totals):
        send_chosen(k).wait_recv()
        send_rhs(k).wait_recv()
        return totals[0] + qr[k].astype(F32), totals[1] + rr[k]

    chosen, rhs = lax.fori_loop(1, COLS, add_chosen, (pt[col].astype(F32), rs[...]))
    chosen = chosen * (1.0 / NODE)
    t4[0] = chosen.astype(BF)
    r4[0] = rhs * (1.0 / NODE)

    def send_top(k):
        return remote(t4.at[0], t4.at[k], (s_t, r_t), k, cousin(k))

    def send_top_rhs(k):
        return remote(r4.at[0], r4.at[k], (s_q, r_q), k, cousin(k))

    each(4, lambda k: send_top(k).start())
    each(4, lambda k: send_top_rhs(k).start())

    def add_gram(k, total):
        send_gram(k).wait_recv()
        return total + gr[k].astype(F32)

    def add_couple(k, total):
        send_couple(k).wait_recv()
        return total + cr[k].astype(F32)

    total = lax.fori_loop(1, COLS, add_gram, pg[col].astype(F32))
    diagonal = iota((SLAB, RANK), 0) + col * SLAB == iota((SLAB, RANK), 1)
    out_share[0, :, 0:RANK] = total * (1.0 / NODE) + jnp.where(diagonal, ridge[0], 0.0)
    total = lax.fori_loop(1, COLS, add_couple, pc[col].astype(F32))
    out_share[0, :, RANK:] = total * (1.0 / NODE)
    result = chosen + tops[pl.ds(pl.multiple_of(col * SLAB, SLAB), SLAB), :]

    def add_top(k, totals):
        send_top(k).wait_recv()
        send_top_rhs(k).wait_recv()
        return totals[0] + t4[k].astype(F32), totals[1] + r4[k]

    result, rhs = lax.fori_loop(1, 4, add_top, (result, r4[0]))
    out_top[0] = result
    out_rhs[...] = jnp.concatenate([rhs[0:1], rhs[1:2]], 1)

    def finish(sends):
        return lambda k: [send(k).wait_send() for send in sends]

    each(LEAVES, finish((send_aux, send_feat)))
    each(COLS, finish((send_skel, send_gram, send_couple, send_chosen, send_rhs)))
    each(4, finish((send_four, send_top, send_top_rhs)))


SHAPES = ((1, SLAB, 2 * RANK), (1, SLAB, RANK), (1, RANK))


def exchange(merged, ridge, *smalls):
    return pl.pallas_call(
        exchange_kernel,
        out_shape=tuple(pltpu.VMEM(shape, F32) for shape in SHAPES),
        in_specs=[VMEM, pl.BlockSpec(memory_space=pltpu.SMEM)] + [ANYWHERE] * 4,
        out_specs=[VMEM] * 3,
        scratch_shapes=[
            pltpu.VMEM((1, RANK), jnp.int32),
            pltpu.VMEM((1, F), F32),
            pltpu.VMEM((8, RANK), jnp.int32),
            pltpu.VMEM((4, RANK), jnp.int32),
            pltpu.VMEM((8, 128), F32),
            pltpu.VMEM((LEAVES, F, PER), BF),
            pltpu.VMEM((LEAVES, 8, 128), F32),
            pltpu.VMEM((LEAVES, F, PER), BF),
            pltpu.VMEM((LEAVES, 8, 128), F32),
            pltpu.VMEM((LEAVES, RANK, PER), BF),
            pltpu.VMEM((LEAVES, 16, PER), BF),
            pltpu.VMEM((COLS, F, RANK), BF),
            pltpu.VMEM((F, RANK), BF),
            pltpu.VMEM((4, F, RANK), BF),
            pltpu.VMEM((2 * RANK, 256), BF),
            pltpu.VMEM((LEAVES // 2, RANK + 16, PER), BF),
            pltpu.VMEM((LEAVES // 2, RANK + 16, PER), BF),
            pltpu.VMEM((RANK, PER), BF),
            pltpu.VMEM((RANK, PER), BF),
            pltpu.VMEM((RANK + 16, RANK), F32),
            pltpu.VMEM((RANK, RANK), F32),
            pltpu.VMEM((RANK, RANK), BF),
            pltpu.VMEM((RANK, 2 * RANK), BF),
            pltpu.VMEM((RANK, 4 * RANK), BF),
            pltpu.VMEM((RANK, 128), F32),
            pltpu.VMEM((RANK, RANK), F32),
            pltpu.VMEM((COLS, SLAB, RANK), BF),
            pltpu.VMEM((COLS, SLAB, RANK), BF),
            pltpu.VMEM((COLS, SLAB, RANK), BF),
            pltpu.VMEM((COLS, SLAB, RANK), BF),
            pltpu.VMEM((COLS, SLAB, RANK), BF),
            pltpu.VMEM((COLS, SLAB, RANK), BF),
            pltpu.VMEM((8, 128), F32),
            pltpu.VMEM((COLS, 8, 128), F32),
            pltpu.VMEM((4, SLAB, RANK), BF),
            pltpu.VMEM((4, 8, 128), F32),
            *dma(LEAVES),
            *dma(LEAVES),
            *dma(COLS),
            *dma(4),
            *dma(COLS),
            *dma(COLS),
            *dma(COLS),
            *dma(COLS),
            *dma(4),
            *dma(4),
            pltpu.SemaphoreType.DMA((4,)),
        ],
        compiler_params=params(0, 40),
        name="exchange",
    )(merged, ridge, *in_hbm(*smalls))


def emit_kernel(*refs):
    ins, outs, sem = refs[:3], refs[3:6], refs[6]
    copies = [pltpu.make_async_copy(a, b, sem.at[k]) for k, (a, b) in enumerate(zip(ins, outs))]
    for copy in copies:
        copy.start()
    for copy in copies:
        copy.wait()


def emit(results):
    return pl.pallas_call(
        emit_kernel,
        out_shape=tuple(jax.ShapeDtypeStruct(shape, F32) for shape in SHAPES),
        in_specs=[VMEM] * 3,
        out_specs=[ANYWHERE] * 3,
        scratch_shapes=[pltpu.SemaphoreType.DMA((3,))],
        compiler_params=params(),
        name="emit",
    )(*results)


def local(features, targets, owner, length_scales, ridge, leaf_pivots, parent_pivots, top_pivots):
    merged = pack(features, targets.reshape(ROWS // 128, 128), owner.reshape(ROWS // 128, 128))
    smalls = (leaf_pivots, length_scales.reshape(1, F), parent_pivots, top_pivots)
    return tuple(emit(exchange(merged, ridge, *smalls)))


def solution(mesh):
    return jax.shard_map(
        local,
        mesh=mesh,
        in_specs=(
            P(None, ("leaf", "col")),
            P(("leaf", "col")),
            P(("leaf", "col")),
            P(),
            P(),
            P("leaf", None),
            P(),
            P(),
        ),
        out_specs=(P("leaf", "col", None), P("leaf", "col", None), P("leaf", None)),
        check_vma=False,
    )
```

```python
import functools
import math

import jax
import jax.numpy as jnp
from jax import lax
from jax.experimental import pallas as pl
from jax.experimental.pallas import tpu as pltpu
from jax.sharding import PartitionSpec as P

F = 48
RANK = 256
ROWS = 8192
LEAVES = 16
COLS = 8
OWNERS = 128
PACKET = 64
PER = ROWS // LEAVES
CHUNK = 256
CHUNKS = ROWS // CHUNK
WINDOW = 40
REGION = PER + WINDOW
SLOTS = 16
WHICH = 50
WIDE = 64
SLAB = RANK // COLS
NODE = ROWS * COLS
LOG2E = math.log2(math.e)
BF = jnp.bfloat16
F32 = jnp.float32
NT = (((1,), (1,)), ((), ()))
MESH = pl.DeviceIdType.MESH


def dma(count):
    return [pltpu.SemaphoreType.DMA((count,))] * 2


def params(number=None, limit=24):
    if number is None:
        return pltpu.CompilerParams(vmem_limit_bytes=limit * 2**20)
    return pltpu.CompilerParams(
        collective_id=number, has_side_effects=True, vmem_limit_bytes=limit * 2**20
    )


ANYWHERE = pl.BlockSpec(memory_space=pl.ANY)
VMEM = pl.BlockSpec(memory_space=pltpu.VMEM)


def iota(shape, axis):
    return lax.broadcasted_iota(jnp.int32, shape, axis)


def dot(a, b):
    return jnp.dot(a, b, preferred_element_type=F32)


def dot_nt(a, b):
    return lax.dot_general(a, b, NT, preferred_element_type=F32)


def row_pair(two):
    return jnp.concatenate([two[0:1], two[1:2]], 1)


def ordering():
    return (iota((CHUNK, CHUNK), 0) < iota((CHUNK, CHUNK), 1)).astype(F32).astype(BF)


def rank_all(target, owner, goals, rows, table):
    goals[...] = target[...].astype(F32)
    weights = jnp.concatenate([ordering(), jnp.ones((CHUNK, 128), BF)], 1)
    lane = iota((LEAVES, 128), 1)

    def ranks(t, carry):
        seen, seen_leaf, most = carry
        own = row_pair(owner[pl.ds(2 * t, 2), :])
        leaf = own // 8
        is_own = iota((OWNERS, CHUNK), 0) == own
        is_leaf = iota((LEAVES, CHUNK), 0) == leaf
        is_after = iota((LEAVES, CHUNK), 0) > leaf
        marks = jnp.concatenate(
            [m.astype(F32).astype(BF) for m in (is_own, is_leaf, is_after)], 0
        )
        sums = dot(marks, weights)
        counts = sums[:OWNERS, CHUNK:]
        leaf_counts = sums[OWNERS : OWNERS + LEAVES, CHUNK:]
        base = sums[OWNERS + LEAVES :, CHUNK:]
        prior = sums[:OWNERS, :CHUNK] + jnp.concatenate([seen, seen], 1)
        rank = jnp.sum(jnp.where(is_own, prior, 0.0), 0, keepdims=True)
        place = sums[OWNERS : OWNERS + LEAVES, :CHUNK] + jnp.concatenate([base, base], 1)
        place = jnp.sum(jnp.where(is_leaf, place, 0.0), 0, keepdims=True)
        tag = (own % 8).astype(F32) * PACKET + rank - (PER // 2)
        rows[t, 0:1, :] = place
        rows[t, 1:2, :] = row_pair(goals[pl.ds(2 * t, 2), :])
        rows[t, 2:3, :] = tag
        rows[t, 3:4, :] = own.astype(F32) * PACKET + rank
        here = lane == t
        table[0:LEAVES, :] = jnp.where(here, seen_leaf.astype(jnp.int32), table[0:LEAVES, :])
        table[LEAVES : 2 * LEAVES, :] = jnp.where(
            here, base.astype(jnp.int32), table[LEAVES : 2 * LEAVES, :]
        )
        return seen + counts, seen_leaf + leaf_counts, jnp.maximum(most, leaf_counts)

    table[0:LEAVES, :] = jnp.full((LEAVES, 128), PER, jnp.int32)
    zero = jnp.zeros((LEAVES, 128), F32)
    _, _, most = lax.fori_loop(
        0, CHUNKS, ranks, (jnp.zeros((OWNERS, 128), F32), zero, zero), unroll=16
    )
    most = jnp.broadcast_to(jnp.max(most, 0, keepdims=True), (8, 128))
    table[2 * LEAVES :, :] = most.astype(jnp.int32)


def joined_of(feat, rows, t):
    row = iota((16, CHUNK), 0)
    goal, tag = rows[t, 1:2, :], rows[t, 2:3, :]
    extra = jnp.where(row == 0, goal, jnp.where(row == 1, tag, 0.0)).astype(BF)
    return jnp.concatenate([feat[:, pl.ds(pl.multiple_of(t * CHUNK, CHUNK), CHUNK)], extra], 0)


def sort_all(feat, rows, ybuf):
    def sort(t, _):
        place = rows[t, 0:1, :].astype(jnp.int32)
        chosen = (iota((CHUNK, CHUNK), 0) == place).astype(F32).astype(BF)
        start = pl.multiple_of(t * CHUNK, CHUNK)
        ybuf[pl.ds(start, CHUNK), :] = dot_nt(chosen, joined_of(feat, rows, t))
        return 0

    lax.fori_loop(0, CHUNKS, sort, 0, unroll=8)


def merge_all(scal, ybuf, zbuf):
    widest = scal[2 * LEAVES, 0]

    @pl.when(widest <= WINDOW)
    def quick():
        def merge(t, _):
            for i in range(LEAVES):
                source = t * CHUNK + scal[LEAVES + i, t]
                goal = i * REGION + scal[i, t]
                zbuf[pl.ds(goal, WINDOW), :] = ybuf[pl.ds(source, WINDOW), :]
            return 0

        lax.fori_loop(0, CHUNKS, merge, 0, unroll=4)

    @pl.when(widest > WINDOW)
    def slow():
        def merge(index, _):
            t = index // LEAVES
            i = index % LEAVES
            source = t * CHUNK + scal[LEAVES + i, t]
            first = scal[i, t]
            count = scal[i, t + 1] - first

            def part(k, _):
                rows = ybuf[pl.ds(source + 8 * k, 8), :]
                zbuf[pl.ds(i * REGION + first + 8 * k, 8), :] = rows
                return 0

            lax.fori_loop(0, (count + 7) // 8, part, 0)
            return 0

        lax.fori_loop(0, CHUNKS * LEAVES, merge, 0)


def pack_kernel(
    feat_hbm, target, owner, zbuf, feat, goals, rows, ybuf, table, scal, sem, feat_sem
):
    bring = pltpu.make_async_copy(feat_hbm, feat, feat_sem)
    bring.start()
    rank_all(target, owner, goals, rows, table)
    move = pltpu.make_async_copy(table, scal, sem)
    move.start()
    bring.wait()
    sort_all(feat, rows, ybuf)
    move.wait()
    merge_all(scal, ybuf, zbuf)


def merge_kernel(ybuf, table, zbuf, scal, sem):
    move = pltpu.make_async_copy(table, scal, sem)
    move.start()
    move.wait()
    merge_all(scal, ybuf, zbuf)


def prepare_kernel(
    feat_hbm, target, owner, pivots, ybuf, table, slots, most,
    feat, goals, rows, held, picks, feat_sem, s_v, r_v, s_s, r_s,
):
    leaf = lax.axis_index("leaf")
    block = leaf * COLS + lax.axis_index("col")
    barrier = pltpu.get_barrier_semaphore()
    each(LEAVES, lambda k: pl.semaphore_signal(barrier, inc=1, **mate(k)))
    bring = pltpu.make_async_copy(feat_hbm, feat, feat_sem)
    bring.start()
    rank_all(target, owner, goals, rows, table)

    def send_pivots(k):
        return remote(pivots, held.at[k], (s_v, r_v), k, mate(k))

    def send_slots(k):
        return remote(picks.at[k], slots.at[k], (s_s, r_s), k, mate(k))

    held[0] = pivots[...]
    pl.semaphore_wait(barrier, LEAVES - 1)
    each(LEAVES, lambda k: send_pivots(k).start())
    each(LEAVES, lambda k: send_pivots(k).wait_recv())

    place = jnp.concatenate([held[(LEAVES - b) % LEAVES] for b in range(LEAVES)], 0)
    home = place % ROWS // PACKET
    number = ((leaf + iota((LEAVES, RANK), 0)) % LEAVES) * 8 + place // ROWS
    number = (number * PACKET + place % PACKET).astype(F32)
    valid = home == block
    order = dot(valid.astype(F32).astype(BF), ordering())
    order = jnp.where(valid, order, -1.0)

    def spread(table):
        return jnp.concatenate(
            [jnp.broadcast_to(table[b : b + 1], (SLOTS, RANK)) for b in range(LEAVES)], 0
        )

    shape = (LEAVES * SLOTS, RANK)
    hit = spread(order) == (iota(shape, 0) % SLOTS).astype(F32)
    wanted = jnp.sum(jnp.where(hit, spread(number) + 1.0, 0.0), 1, keepdims=True) - 1.0
    which = jnp.sum(jnp.where(hit, iota(shape, 1).astype(F32) + 1.0, 0.0), 1, keepdims=True) - 1.0
    wanted = jnp.broadcast_to(wanted, (LEAVES * SLOTS, CHUNK))
    bring.wait()

    def take(t, total):
        chosen = (wanted == rows[t, 3:4, :]).astype(F32).astype(BF)
        fill = jnp.zeros((128 - WIDE, CHUNK), BF)
        return total + dot_nt(chosen, jnp.concatenate([joined_of(feat, rows, t), fill], 0))

    shape = (LEAVES * SLOTS, 128)
    taken = lax.fori_loop(0, CHUNKS, take, jnp.zeros(shape, F32), unroll=4)
    taken = jnp.where(iota(shape, 1) == WHICH, which, taken).astype(BF)
    for b in range(LEAVES):
        picks[b] = taken[b * SLOTS : (b + 1) * SLOTS]
    slots[0] = picks[0]
    each(LEAVES, lambda k: send_slots(k).start())
    sort_all(feat, rows, ybuf)

    largest = jnp.zeros((OWNERS, 1), F32)
    for b in range(LEAVES):
        inside = (iota((OWNERS, RANK), 0) == home[b : b + 1]).astype(F32)
        largest = jnp.maximum(largest, jnp.sum(inside, 1, keepdims=True))
    most[...] = jnp.broadcast_to(jnp.max(largest, 0, keepdims=True), (8, 128))
    each(LEAVES, lambda k: send_slots(k).wait_recv())
    each(LEAVES, lambda k: (send_pivots(k).wait_send(), send_slots(k).wait_send()))


def in_hbm(*arrays):
    return [pltpu.with_memory_space_constraint(a, pltpu.HBM) for a in arrays]


def pack(features, targets, owner):
    return pl.pallas_call(
        pack_kernel,
        out_shape=pltpu.VMEM((LEAVES * REGION, WIDE), F32),
        in_specs=[ANYWHERE, VMEM, VMEM],
        out_specs=VMEM,
        scratch_shapes=[
            pltpu.VMEM((F, ROWS), BF),
            pltpu.VMEM((ROWS // 128, 128), F32),
            pltpu.VMEM((CHUNKS, 8, CHUNK), F32),
            pltpu.VMEM((ROWS + WINDOW, WIDE), F32),
            pltpu.VMEM((40, 128), jnp.int32),
            pltpu.SMEM((40, 128), jnp.int32),
            pltpu.SemaphoreType.DMA,
            pltpu.SemaphoreType.DMA,
        ],
        compiler_params=params(),
        name="pack",
    )(*in_hbm(features, targets, owner))


def prepare(features, targets, owner, pivots):
    return pl.pallas_call(
        prepare_kernel,
        out_shape=(
            pltpu.VMEM((ROWS + WINDOW, WIDE), F32),
            pltpu.VMEM((40, 128), jnp.int32),
            pltpu.VMEM((LEAVES, SLOTS, 128), BF),
            jax.ShapeDtypeStruct((8, 128), F32),
        ),
        in_specs=[ANYWHERE, VMEM, VMEM, VMEM],
        out_specs=[VMEM] * 4,
        scratch_shapes=[
            pltpu.VMEM((F, ROWS), BF),
            pltpu.VMEM((ROWS // 128, 128), F32),
            pltpu.VMEM((CHUNKS, 8, CHUNK), F32),
            pltpu.VMEM((LEAVES, 1, RANK), jnp.int32),
            pltpu.VMEM((LEAVES, SLOTS, 128), BF),
            pltpu.SemaphoreType.DMA,
            *dma(LEAVES),
            *dma(LEAVES),
        ],
        compiler_params=params(0),
        name="prepare",
    )(*in_hbm(features, targets, owner, pivots))


def merge(ybuf, table):
    return pl.pallas_call(
        merge_kernel,
        out_shape=pltpu.VMEM((LEAVES * REGION, WIDE), F32),
        in_specs=[VMEM] * 2,
        out_specs=VMEM,
        scratch_shapes=[pltpu.SMEM((40, 128), jnp.int32), pltpu.SemaphoreType.DMA],
        compiler_params=params(),
        name="merge",
    )(ybuf, table)


def split3(x):
    high = x.astype(BF)
    rest = x - high.astype(F32)
    mid = rest.astype(BF)
    return high, mid, (rest - mid.astype(F32)).astype(BF)


def stack16(parts, width):
    row = iota((16, width), 0)
    block = jnp.zeros((16, width), F32)
    for k, part in enumerate(parts):
        block = jnp.where(row == k, part if isinstance(part, float) else part.astype(F32), block)
    return block.astype(BF)


def half_norm(points, scale):
    return jnp.sum(points * points * (0.5 * scale), 0, keepdims=True)


def point_side(points, scale):
    high, mid, low = split3(-half_norm(points, scale))
    return stack16([high, mid, low, 1.0, 1.0, 1.0], points.shape[1])


def skel_side(skel, scale):
    width = skel.shape[1]
    high, mid, low = split3(skel * scale)
    extra = stack16([1.0, 1.0, 1.0, *split3(-half_norm(skel, scale))], width)
    parts = [p.astype(F32) for p in (high, mid, low, extra)]
    fill = jnp.zeros((256 - 3 * F - 16, width), F32)
    return jnp.concatenate([*parts, fill], 0).T.astype(BF)


def select_row(table, row):
    hit = iota(table.shape, 0) == row
    return jnp.sum(jnp.where(hit, table.astype(F32), 0.0), 0, keepdims=True)


def to_column(row):
    return jnp.broadcast_to(row, (128, row.shape[1])).T


def across(column, width):
    return jnp.concatenate([column] * (width // 128), 1)


def place_of(leaf, col):
    return dict(device_id=(leaf, col), device_id_type=MESH)


def mate(k):
    leaf, col = lax.axis_index("leaf"), lax.axis_index("col")
    to = (leaf + k) % LEAVES
    cross = (to // 8 + leaf // 8) % 2
    return place_of(to, col + cross * (1 - 2 * (col % 2)))


def beside(k):
    leaf, col = lax.axis_index("leaf"), lax.axis_index("col")
    return place_of(leaf, (col + k) % COLS)


def cousin(k):
    leaf, col = lax.axis_index("leaf"), lax.axis_index("col")
    return place_of(leaf - leaf % 4 + (leaf + k) % 4, col)


def each(count, step, unroll=1):
    lax.fori_loop(1, count, lambda k, _: (step(k), 0)[1], 0, unroll=unroll)


def remote(src, dst, sems, k, peer):
    return pltpu.make_async_remote_copy(src, dst, sems[0].at[k], sems[1].at[k], **peer)


def top_index(parent, top, group):
    top_row = select_row(top[...], group)
    below = jnp.concatenate([select_row(parent[...], 2 * group + r) for r in range(2)], 1)
    number = iota((RANK, 2 * RANK), 1)
    below = below + jnp.where(iota((1, 2 * RANK), 1) >= RANK, 2.0 * RANK, 0.0)
    hit = across(to_column(top_row), 2 * RANK) == number.astype(F32)
    index = jnp.sum(jnp.where(hit, below, 0.0), 1, keepdims=True)
    return jnp.broadcast_to(index, (RANK, 128))


def exchange_kernel(
    early, merged, slots, ridge, pivots_hbm, scales_hbm, parent_hbm, top_hbm, out_share, out_top, out_rhs,
    pivots, scales, parent, top, spare, feat, aux, rx, ra, hot, side, sk, mine, sk4, left,
    even, odd, other_even, other_odd, gram, couple, rows, columns, fours, index, tops,
    pg, gr, pc, cr, pt, qr, rs, rr, t4, r4,
    s_f, r_f, s_a, r_a, s_k, r_k, s_4, r_4, s_p, r_p, s_c, r_c, s_o, r_o, s_r, r_r, s_t, r_t, s_q, r_q, local,
):
    leaf = lax.axis_index("leaf")
    col = lax.axis_index("col")
    quarter = leaf % 4
    sibling = quarter + 1 - 2 * (quarter % 2)
    barrier = pltpu.get_barrier_semaphore()
    each(LEAVES, lambda k: pl.semaphore_signal(barrier, inc=1, **mate(k)))
    each(COLS, lambda k: pl.semaphore_signal(barrier, inc=1, **beside(k)))
    smalls = [
        pltpu.make_async_copy(a, b, local.at[k])
        for k, (a, b) in enumerate(
            [(pivots_hbm, pivots), (scales_hbm, scales), (parent_hbm, parent), (top_hbm, top)]
        )
    ]
    for copy in smalls:
        copy.start()

    eye = (iota((WIDE, WIDE), 0) == iota((WIDE, WIDE), 1)).astype(F32).astype(BF)

    def turn(k):
        start = pl.multiple_of((leaf + k) % LEAVES * REGION, 8)
        turned = dot_nt(eye, merged[pl.ds(start, PER), :].astype(BF))
        feat[k] = turned[:F].astype(BF)
        aux[k] = jnp.concatenate(
            [turned[F + r : F + r + 1, 128 * c : 128 * c + 128] for r in range(2) for c in range(4)], 0
        )

    def send_feat(k):
        return remote(feat.at[k], rx.at[k], (s_f, r_f), k, mate(k))

    def send_aux(k):
        return remote(aux.at[k], ra.at[k], (s_a, r_a), k, mate(k))

    def send_skel(k):
        return remote(sk.at[0], sk.at[k], (s_k, r_k), k, beside(k))

    if early:
        came = jnp.concatenate([slots[b] for b in range(LEAVES)], 0).astype(F32)
        chosen = came[:, WHICH : WHICH + 1] == iota((LEAVES * SLOTS, RANK), 1).astype(F32)
        picked = dot(came.T[:F].astype(BF), chosen.astype(F32).astype(BF))
        sk[0] = picked.astype(BF)

    def four(j, _):
        for r in range(1, 5):
            turn((4 * j + r) % LEAVES)

        @pl.when(j == 0)
        def begin():
            pl.semaphore_wait(barrier, LEAVES + COLS - 2)
            if early:
                each(COLS, lambda k: send_skel(k).start())

        for send in (send_aux, send_feat):
            for r in range(1, 4):
                send(4 * j + r).start()
            pl.when(j < 3)(lambda: send(4 * j + 4).start())
        return 0

    lax.fori_loop(0, LEAVES // 4, four, 0)
    rx[0] = feat[0]
    ra[0] = aux[0]

    for copy in smalls:
        copy.wait()
    spare[...] = jnp.ones((8, 128), F32)
    spare[0:1, 0:F] = scales[...]
    inverse = 1.0 / to_column(spare[0:1, :])[:F]
    scale = inverse * inverse * LOG2E
    scale2 = across(scale, RANK)
    scale4 = across(scale, PER)

    index[...] = top_index(parent, top, leaf // 4)
    index2 = across(index[...], 2 * RANK)
    number = iota((RANK, 2 * RANK), 1)
    base = (quarter * RANK).astype(F32)
    other = (sibling * RANK).astype(F32)
    chosen = index2[:, :RANK] == iota((RANK, RANK), 1).astype(F32) + base
    rows[...] = chosen.astype(F32).astype(BF)
    lanes = number.astype(F32) + jnp.where(number < RANK, base, other - RANK)
    columns[...] = (index2 == lanes).astype(F32).astype(BF)
    chosen = across(index[...], 4 * RANK) == iota((RANK, 4 * RANK), 1).astype(F32)
    fours[...] = chosen.astype(F32).astype(BF)

    def norms(k, _):
        side[k] = point_side(rx[k].astype(F32), scale4)
        return 0

    if not early:
        place = pivots[...]
        within = place % ROWS
        block = within // PACKET
        key = (block // COLS) * PER + (place // ROWS) * PACKET + within % PACKET
        holder = block % COLS
        crossed = (block // COLS) // 8 != leaf // 8
        holder = jnp.where(crossed, holder + 1 - 2 * (holder % 2), holder)
        key = jnp.where(holder == col, key, -PER)
        key = across(to_column(key.astype(F32)), PER)

        def mark(k):
            source = (leaf + LEAVES - k) % LEAVES
            tags = ra[k, 4:8, :]
            tag = jnp.concatenate([tags[r : r + 1] for r in range(4)], 1)
            wanted = tag + (PER // 2 + source * PER).astype(F32)
            hot[k] = (key == wanted).astype(F32).astype(BF)

        def mark_next(k, _):
            pl.when(k > 0)(lambda: send_aux(k).wait_recv())
            mark(k)
            return 0

        lax.fori_loop(0, LEAVES, mark_next, 0)

        def pick(j, total):
            for r in range(4):
                k = 4 * j + r
                if r:
                    send_feat(k).wait_recv()
                else:
                    pl.when(k > 0)(lambda: send_feat(k).wait_recv())
            for r in range(4):
                total = total + dot_nt(hot[4 * j + r], rx[4 * j + r])
            return total

        picked = lax.fori_loop(0, LEAVES // 4, pick, jnp.zeros((RANK, F), F32))
        picked = jnp.concatenate([picked, jnp.zeros((RANK, 128 - F), F32)], 1).T[:F]
        sk[0] = picked.astype(BF)

        each(COLS, lambda k: send_skel(k).start())

        lax.fori_loop(0, LEAVES, norms, 0)

    def add_skel(k, total):
        send_skel(k).wait_recv()
        return total + sk[k].astype(F32)

    picked = lax.fori_loop(1, COLS, add_skel, picked)
    mine[...] = picked.astype(BF)
    sk4[quarter] = picked.astype(BF)

    def send_four(k):
        return remote(mine, sk4.at[quarter], (s_4, r_4), k, cousin(k))

    each(4, lambda k: send_four(k).start())
    left[0:RANK, :] = skel_side(picked, scale2)

    def block_of(k, out, begin):
        p = rx[k]
        fill = jnp.zeros((256 - 3 * F - 16, PER), BF)
        right = jnp.concatenate([p, p, p, side[k], fill], 0)
        power = dot(left[begin : begin + RANK, :], right)
        out[0:RANK, :] = jnp.exp2(jnp.minimum(power, 0.0)).astype(BF)

    def own_of(k, out):
        block_of(k, out, 0)
        value = jnp.concatenate([ra[k, r : r + 1, :] for r in range(4)], 1)
        out[RANK:, :] = jnp.broadcast_to(value, (16, PER)).astype(BF)

    def gram_of(u):
        gram[...] += dot_nt(u[...], u[0:RANK, :])

    def couple_of(v, u):
        couple[...] += dot_nt(v[...], u[0:RANK, :])

    last = LEAVES // 2 - 1

    def own_two(j, _):
        if early:
            pl.when(j > 0)(lambda: receive(2 * j))
            receive(2 * j + 1)
            norms(2 * j, 0)
            norms(2 * j + 1, 0)
        own_of(2 * j, even.at[j])
        gram_of(odd.at[(j + last) % (last + 1)])
        own_of(2 * j + 1, odd.at[j])
        gram_of(even.at[j])
        return 0

    def receive(k):
        send_aux(k).wait_recv()
        send_feat(k).wait_recv()

    def other_two(j, _):
        block_of(2 * j, other_even, RANK)
        couple_of(other_odd, odd.at[(j + last) % (last + 1)])
        block_of(2 * j + 1, other_odd, RANK)
        couple_of(other_even, even.at[j])
        return 0

    gram[...] = jnp.zeros_like(gram)
    couple[...] = jnp.zeros_like(couple)
    odd[last] = jnp.zeros((RANK + 16, PER), BF)
    other_odd[...] = jnp.zeros_like(other_odd)
    def send_gram(k):
        return remote(pg.at[(col + k) % COLS], gr.at[k], (s_p, r_p), k, beside(k))

    def send_couple(k):
        return remote(pc.at[(col + k) % COLS], cr.at[k], (s_c, r_c), k, beside(k))

    def send_chosen(k):
        return remote(pt.at[(col + k) % COLS], qr.at[k], (s_o, r_o), k, beside(k))

    def send_rhs(k):
        return remote(rs, rr.at[k], (s_r, r_r), k, beside(k))

    def sibling_side():
        each(4, lambda k: remote(mine, sk4.at[(quarter + 4 - k) % 4], (s_4, r_4), k, cousin(k)).wait_recv())
        left[RANK:, :] = skel_side(sk4[sibling].astype(F32), scale2)

    def give_gram():
        gram_of(odd.at[last])
        part = gram[0:RANK, :].astype(BF)
        for k in range(COLS):
            pg[k] = part[k * SLAB : (k + 1) * SLAB]
        rhs = gram[RANK : RANK + 1, :]
        rhs = jnp.sum(dot_nt(stack16(split3(rhs), RANK), rows[...]), 0, keepdims=True)
        rs[...] = jnp.zeros_like(rs)
        rs[0:1, :] = rhs[:, :128]
        rs[1:2, :] = rhs[:, 128:]
        each(COLS, lambda k: send_gram(k).start())
        each(COLS, lambda k: send_rhs(k).start())
        tops[...] = dot_nt(dot(rows[...], part).astype(BF), columns[:, 0:RANK])

    def half(h, _):
        pairs = LEAVES // 4
        lax.fori_loop(pairs * h, pairs * (h + 1), own_two, 0)
        pl.when(h == 0)(sibling_side)
        pl.when(h == 1)(give_gram)
        lax.fori_loop(pairs * h, pairs * (h + 1), other_two, 0)
        return 0

    lax.fori_loop(0, 2, half, 0)
    couple_of(other_odd, odd.at[last])

    part = couple[...].astype(BF)
    chosen = dot_nt(dot_nt(rows[...], part).astype(BF), columns[:, RANK:]) + tops[...]
    chosen = chosen.astype(BF)
    for k in range(COLS):
        pt[k] = chosen[k * SLAB : (k + 1) * SLAB]
    each(COLS, lambda k: send_chosen(k).start())
    part = couple[...].T.astype(BF)
    for k in range(COLS):
        pc[k] = part[k * SLAB : (k + 1) * SLAB]
    each(COLS, lambda k: send_couple(k).start())

    whole = jnp.concatenate([sk4[k] for k in range(4)], 1)
    points = dot_nt(whole, fours[...])
    fill = jnp.zeros((256 - 3 * F - 16, RANK), BF)
    points_b = points.astype(BF)
    right = jnp.concatenate([points_b, points_b, points_b, point_side(points, scale2), fill], 0)
    value = jnp.exp2(jnp.minimum(dot(skel_side(points, scale2), right), 0.0))
    crossing = (across(index[...], RANK) >= 2.0 * RANK) != (index[...].T[0:1, :] >= 2.0 * RANK)
    square = iota((RANK, RANK), 0) == iota((RANK, RANK), 1)
    tops[...] = jnp.where(crossing, value, 0.0) + jnp.where(square, ridge[0], 0.0)

    def add_chosen(k, totals):
        send_chosen(k).wait_recv()
        send_rhs(k).wait_recv()
        return totals[0] + qr[k].astype(F32), totals[1] + rr[k]

    chosen, rhs = lax.fori_loop(1, COLS, add_chosen, (pt[col].astype(F32), rs[...]))
    chosen = chosen * (1.0 / NODE)
    t4[0] = chosen.astype(BF)
    r4[0] = rhs * (1.0 / NODE)

    def send_top(k):
        return remote(t4.at[0], t4.at[k], (s_t, r_t), k, cousin(k))

    def send_top_rhs(k):
        return remote(r4.at[0], r4.at[k], (s_q, r_q), k, cousin(k))

    each(4, lambda k: send_top(k).start())
    each(4, lambda k: send_top_rhs(k).start())

    def add_gram(k, total):
        send_gram(k).wait_recv()
        return total + gr[k].astype(F32)

    def add_couple(k, total):
        send_couple(k).wait_recv()
        return total + cr[k].astype(F32)

    total = lax.fori_loop(1, COLS, add_gram, pg[col].astype(F32))
    diagonal = iota((SLAB, RANK), 0) + col * SLAB == iota((SLAB, RANK), 1)
    out_share[0, :, 0:RANK] = total * (1.0 / NODE) + jnp.where(diagonal, ridge[0], 0.0)
    total = lax.fori_loop(1, COLS, add_couple, pc[col].astype(F32))
    out_share[0, :, RANK:] = total * (1.0 / NODE)
    result = chosen + tops[pl.ds(pl.multiple_of(col * SLAB, SLAB), SLAB), :]

    def add_top(k, totals):
        send_top(k).wait_recv()
        send_top_rhs(k).wait_recv()
        return totals[0] + t4[k].astype(F32), totals[1] + r4[k]

    result, rhs = lax.fori_loop(1, 4, add_top, (result, r4[0]))
    out_top[0] = result
    out_rhs[...] = jnp.concatenate([rhs[0:1], rhs[1:2]], 1)

    def finish(sends):
        return lambda k: [send(k).wait_send() for send in sends]

    each(LEAVES, finish((send_aux, send_feat)))
    each(COLS, finish((send_skel, send_gram, send_couple, send_chosen, send_rhs)))
    each(4, finish((send_four, send_top, send_top_rhs)))


SHAPES = ((1, SLAB, 2 * RANK), (1, SLAB, RANK), (1, RANK))


def exchange(early, number, merged, slots, ridge, *smalls):
    return pl.pallas_call(
        functools.partial(exchange_kernel, early),
        out_shape=tuple(pltpu.VMEM(shape, F32) for shape in SHAPES),
        in_specs=[VMEM, VMEM, pl.BlockSpec(memory_space=pltpu.SMEM)] + [ANYWHERE] * 4,
        out_specs=[VMEM] * 3,
        scratch_shapes=[
            pltpu.VMEM((1, RANK), jnp.int32),
            pltpu.VMEM((1, F), F32),
            pltpu.VMEM((8, RANK), jnp.int32),
            pltpu.VMEM((4, RANK), jnp.int32),
            pltpu.VMEM((8, 128), F32),
            pltpu.VMEM((LEAVES, F, PER), BF),
            pltpu.VMEM((LEAVES, 8, 128), F32),
            pltpu.VMEM((LEAVES, F, PER), BF),
            pltpu.VMEM((LEAVES, 8, 128), F32),
            pltpu.VMEM((LEAVES, RANK, PER), BF),
            pltpu.VMEM((LEAVES, 16, PER), BF),
            pltpu.VMEM((COLS, F, RANK), BF),
            pltpu.VMEM((F, RANK), BF),
            pltpu.VMEM((4, F, RANK), BF),
            pltpu.VMEM((2 * RANK, 256), BF),
            pltpu.VMEM((LEAVES // 2, RANK + 16, PER), BF),
            pltpu.VMEM((LEAVES // 2, RANK + 16, PER), BF),
            pltpu.VMEM((RANK, PER), BF),
            pltpu.VMEM((RANK, PER), BF),
            pltpu.VMEM((RANK + 16, RANK), F32),
            pltpu.VMEM((RANK, RANK), F32),
            pltpu.VMEM((RANK, RANK), BF),
            pltpu.VMEM((RANK, 2 * RANK), BF),
            pltpu.VMEM((RANK, 4 * RANK), BF),
            pltpu.VMEM((RANK, 128), F32),
            pltpu.VMEM((RANK, RANK), F32),
            pltpu.VMEM((COLS, SLAB, RANK), BF),
            pltpu.VMEM((COLS, SLAB, RANK), BF),
            pltpu.VMEM((COLS, SLAB, RANK), BF),
            pltpu.VMEM((COLS, SLAB, RANK), BF),
            pltpu.VMEM((COLS, SLAB, RANK), BF),
            pltpu.VMEM((COLS, SLAB, RANK), BF),
            pltpu.VMEM((8, 128), F32),
            pltpu.VMEM((COLS, 8, 128), F32),
            pltpu.VMEM((4, SLAB, RANK), BF),
            pltpu.VMEM((4, 8, 128), F32),
            *dma(LEAVES),
            *dma(LEAVES),
            *dma(COLS),
            *dma(4),
            *dma(COLS),
            *dma(COLS),
            *dma(COLS),
            *dma(COLS),
            *dma(4),
            *dma(4),
            pltpu.SemaphoreType.DMA((4,)),
        ],
        compiler_params=params(number, 40),
        name="exchange",
    )(merged, slots, ridge, *in_hbm(*smalls))


def emit_kernel(*refs):
    ins, outs, sem = refs[:3], refs[3:6], refs[6]
    copies = [pltpu.make_async_copy(a, b, sem.at[k]) for k, (a, b) in enumerate(zip(ins, outs))]
    for copy in copies:
        copy.start()
    for copy in copies:
        copy.wait()


def emit(results):
    return pl.pallas_call(
        emit_kernel,
        out_shape=tuple(jax.ShapeDtypeStruct(shape, F32) for shape in SHAPES),
        in_specs=[VMEM] * 3,
        out_specs=[ANYWHERE] * 3,
        scratch_shapes=[pltpu.SemaphoreType.DMA((3,))],
        compiler_params=params(),
        name="emit",
    )(*results)


def local(features, targets, owner, length_scales, ridge, leaf_pivots, parent_pivots, top_pivots):
    samples = (features, targets.reshape(ROWS // 128, 128), owner.reshape(ROWS // 128, 128))
    smalls = (leaf_pivots, length_scales.reshape(1, F), parent_pivots, top_pivots)
    ybuf, table, slots, most = prepare(*samples, leaf_pivots)
    results = exchange(True, 1, merge(ybuf, table), slots, ridge, *smalls)

    def again():
        none = jnp.zeros((LEAVES, SLOTS, 128), BF)
        return tuple(emit(exchange(False, 2, pack(*samples), none, ridge, *smalls)))

    return lax.cond(most[0, 0] > SLOTS, again, lambda: tuple(emit(results)))


def solution(mesh):
    return jax.shard_map(
        local,
        mesh=mesh,
        in_specs=(
            P(None, ("leaf", "col")),
            P(("leaf", "col")),
            P(("leaf", "col")),
            P(),
            P(),
            P("leaf", None),
            P(),
            P(),
        ),
        out_specs=(P("leaf", "col", None), P("leaf", "col", None), P("leaf", None)),
        check_vma=False,
    )
```

```python
import functools
import math

import jax
import jax.numpy as jnp
from jax import lax
from jax.experimental import pallas as pl
from jax.experimental.pallas import tpu as pltpu
from jax.sharding import PartitionSpec as P

F = 48
RANK = 256
ROWS = 8192
LEAVES = 16
COLS = 8
OWNERS = 128
PACKET = 64
PER = ROWS // LEAVES
CHUNK = 256
CHUNKS = ROWS // CHUNK
GROUP = 8
WINDOW = 40
REGION = PER + WINDOW
WIDE = 64
SLAB = RANK // COLS
NODE = ROWS * COLS
LOG2E = math.log2(math.e)
BF = jnp.bfloat16
F32 = jnp.float32
NT = (((1,), (1,)), ((), ()))
MESH = pl.DeviceIdType.MESH


def dma(count):
    return [pltpu.SemaphoreType.DMA((count,))] * 2


def params(number=None, limit=24):
    if number is None:
        return pltpu.CompilerParams(vmem_limit_bytes=limit * 2**20)
    return pltpu.CompilerParams(
        collective_id=number, has_side_effects=True, vmem_limit_bytes=limit * 2**20
    )


ANYWHERE = pl.BlockSpec(memory_space=pl.ANY)
VMEM = pl.BlockSpec(memory_space=pltpu.VMEM)


def iota(shape, axis):
    return lax.broadcasted_iota(jnp.int32, shape, axis)


def dot(a, b):
    return jnp.dot(a, b, preferred_element_type=F32)


def dot_nt(a, b):
    return lax.dot_general(a, b, NT, preferred_element_type=F32)


def row_pair(two):
    return jnp.concatenate([two[0:1], two[1:2]], 1)


def pack_kernel(
    feat_hbm, target, owner, zbuf, feat, goals, rows, cums, ybuf, table, scal, sem, feat_sem
):
    bring = pltpu.make_async_copy(feat_hbm, feat, feat_sem)
    bring.start()
    goals[...] = target[...].astype(F32)
    before = (iota((CHUNK, CHUNK), 0) < iota((CHUNK, CHUNK), 1)).astype(F32).astype(BF)
    lane = iota((LEAVES, 128), 1)
    kinds = OWNERS + 2 * LEAVES

    def ranks(group, carry):
        seen, seen_leaf, most = carry
        owners = []
        marks = []
        for r in range(GROUP):
            own = row_pair(owner[pl.ds(2 * (group * GROUP + r), 2), :])
            leaf = own // 8
            owners.append(own)
            marks.append((iota((OWNERS, CHUNK), 0) == own).astype(F32).astype(BF))
            marks.append((iota((LEAVES, CHUNK), 0) == leaf).astype(F32).astype(BF))
            marks.append((iota((LEAVES, CHUNK), 0) > leaf).astype(F32).astype(BF))
        cums[...] = dot(jnp.concatenate(marks, 0), before)
        for r in range(GROUP):
            t = group * GROUP + r
            own = owners[r]
            leaf = own // 8
            sums = cums[kinds * r : kinds * (r + 1), :]
            final = jnp.concatenate([m[:, CHUNK - 1 :].astype(F32) for m in marks[3 * r : 3 * r + 3]], 0)
            totals = sums[:, CHUNK - 1 :] + final
            leaf_counts = totals[OWNERS : OWNERS + LEAVES]
            base = totals[OWNERS + LEAVES :]
            rank = jnp.where(iota((OWNERS, CHUNK), 0) == own, sums[:OWNERS] + seen, 0.0)
            rank = jnp.sum(rank, 0, keepdims=True)
            place = sums[OWNERS : OWNERS + LEAVES] + base
            place = jnp.where(iota((LEAVES, CHUNK), 0) == leaf, place, 0.0)
            rows[t, 0:1, :] = jnp.sum(place, 0, keepdims=True)
            rows[t, 1:2, :] = row_pair(goals[pl.ds(2 * t, 2), :])
            rows[t, 2:3, :] = (own % 8).astype(F32) * PACKET + rank - (PER // 2)
            here = lane == t
            table[0:LEAVES, :] = jnp.where(here, seen_leaf.astype(jnp.int32), table[0:LEAVES, :])
            table[LEAVES : 2 * LEAVES, :] = jnp.where(
                here, base.astype(jnp.int32), table[LEAVES : 2 * LEAVES, :]
            )
            seen = seen + totals[:OWNERS]
            seen_leaf = seen_leaf + leaf_counts
            most = jnp.maximum(most, leaf_counts)
        return seen, seen_leaf, most

    table[0:LEAVES, :] = jnp.full((LEAVES, 128), PER, jnp.int32)
    start = goals[0:16, 0:1] * 0.0
    _, _, most = lax.fori_loop(
        0, CHUNKS // GROUP, ranks, (jnp.concatenate([start] * 8, 0), start, start), unroll=2
    )
    most = jnp.broadcast_to(jnp.max(most, 0, keepdims=True), (8, 128))
    table[2 * LEAVES :, :] = most.astype(jnp.int32)
    move = pltpu.make_async_copy(table, scal, sem)
    move.start()
    bring.wait()

    def sort(t, _):
        start = pl.multiple_of(t * CHUNK, CHUNK)
        row = iota((16, CHUNK), 0)
        place, goal, tag = rows[t, 0:1, :], rows[t, 1:2, :], rows[t, 2:3, :]
        extra = jnp.where(row == 0, goal, jnp.where(row == 1, tag, 0.0)).astype(BF)
        joined = jnp.concatenate([feat[:, pl.ds(start, CHUNK)], extra], 0)
        chosen = (iota((CHUNK, CHUNK), 0) == place.astype(jnp.int32)).astype(F32).astype(BF)
        ybuf[pl.ds(start, CHUNK), :] = dot_nt(chosen, joined)
        return 0

    lax.fori_loop(0, CHUNKS, sort, 0, unroll=8)
    move.wait()
    widest = scal[2 * LEAVES, 0]

    @pl.when(widest <= WINDOW)
    def quick():
        def merge(t, _):
            for i in range(LEAVES):
                source = t * CHUNK + scal[LEAVES + i, t]
                goal = i * REGION + scal[i, t]
                zbuf[pl.ds(goal, WINDOW), :] = ybuf[pl.ds(source, WINDOW), :]
            return 0

        lax.fori_loop(0, CHUNKS, merge, 0, unroll=4)

    @pl.when(widest > WINDOW)
    def slow():
        def merge(index, _):
            t = index // LEAVES
            i = index % LEAVES
            source = t * CHUNK + scal[LEAVES + i, t]
            first = scal[i, t]
            count = scal[i, t + 1] - first

            def part(k, _):
                rows = ybuf[pl.ds(source + 8 * k, 8), :]
                zbuf[pl.ds(i * REGION + first + 8 * k, 8), :] = rows
                return 0

            lax.fori_loop(0, (count + 7) // 8, part, 0)
            return 0

        lax.fori_loop(0, CHUNKS * LEAVES, merge, 0)


def in_hbm(*arrays):
    return [pltpu.with_memory_space_constraint(a, pltpu.HBM) for a in arrays]


def pack(features, targets, owner):
    return pl.pallas_call(
        pack_kernel,
        out_shape=pltpu.VMEM((LEAVES * REGION, WIDE), F32),
        in_specs=[ANYWHERE, VMEM, VMEM],
        out_specs=VMEM,
        scratch_shapes=[
            pltpu.VMEM((F, ROWS), BF),
            pltpu.VMEM((ROWS // 128, 128), F32),
            pltpu.VMEM((CHUNKS, 8, CHUNK), F32),
            pltpu.VMEM((GROUP * (OWNERS + 2 * LEAVES), CHUNK), F32),
            pltpu.VMEM((ROWS + WINDOW, WIDE), F32),
            pltpu.VMEM((40, 128), jnp.int32),
            pltpu.SMEM((40, 128), jnp.int32),
            pltpu.SemaphoreType.DMA,
            pltpu.SemaphoreType.DMA,
        ],
        compiler_params=params(),
        name="pack",
    )(*in_hbm(features, targets, owner))


def split3(x):
    high = x.astype(BF)
    rest = x - high.astype(F32)
    mid = rest.astype(BF)
    return high, mid, (rest - mid.astype(F32)).astype(BF)


def stack16(parts, width):
    row = iota((16, width), 0)
    block = jnp.zeros((16, width), F32)
    for k, part in enumerate(parts):
        block = jnp.where(row == k, part if isinstance(part, float) else part.astype(F32), block)
    return block.astype(BF)


def half_norm(points, scale):
    return jnp.sum(points * points * (0.5 * scale), 0, keepdims=True)


def point_side(points, scale):
    high, mid, low = split3(-half_norm(points, scale))
    return stack16([high, mid, low, 1.0, 1.0, 1.0], points.shape[1])


def skel_side(skel, scale):
    width = skel.shape[1]
    high, mid, low = split3(skel * scale)
    extra = stack16([1.0, 1.0, 1.0, *split3(-half_norm(skel, scale))], width)
    parts = [p.astype(F32) for p in (high, mid, low, extra)]
    fill = jnp.zeros((256 - 3 * F - 16, width), F32)
    return jnp.concatenate([*parts, fill], 0).T.astype(BF)


def select_row(table, row):
    hit = iota(table.shape, 0) == row
    return jnp.sum(jnp.where(hit, table.astype(F32), 0.0), 0, keepdims=True)


def to_column(row):
    return jnp.broadcast_to(row, (128, row.shape[1])).T


def across(column, width):
    return jnp.concatenate([column] * (width // 128), 1)


def place_of(leaf, col):
    return dict(device_id=(leaf, col), device_id_type=MESH)


def mate(k):
    leaf, col = lax.axis_index("leaf"), lax.axis_index("col")
    to = (leaf + k) % LEAVES
    cross = (to // 8 + leaf // 8) % 2
    return place_of(to, col + cross * (1 - 2 * (col % 2)))


def beside(k):
    leaf, col = lax.axis_index("leaf"), lax.axis_index("col")
    return place_of(leaf, (col + k) % COLS)


def cousin(k):
    leaf, col = lax.axis_index("leaf"), lax.axis_index("col")
    return place_of(leaf - leaf % 4 + (leaf + k) % 4, col)


def each(count, step, unroll=1):
    lax.fori_loop(1, count, lambda k, _: (step(k), 0)[1], 0, unroll=unroll)


def remote(src, dst, sems, k, peer):
    return pltpu.make_async_remote_copy(src, dst, sems[0].at[k], sems[1].at[k], **peer)


def top_index(parent, top, group):
    top_row = select_row(top[...], group)
    below = jnp.concatenate([select_row(parent[...], 2 * group + r) for r in range(2)], 1)
    number = iota((RANK, 2 * RANK), 1)
    below = below + jnp.where(iota((1, 2 * RANK), 1) >= RANK, 2.0 * RANK, 0.0)
    hit = across(to_column(top_row), 2 * RANK) == number.astype(F32)
    index = jnp.sum(jnp.where(hit, below, 0.0), 1, keepdims=True)
    return jnp.broadcast_to(index, (RANK, 128))


def exchange_kernel(
    merged, ridge, pivots_hbm, scales_hbm, parent_hbm, top_hbm, out_share, out_top, out_rhs,
    pivots, scales, parent, top, spare, feat, aux, rx, ra, hot, side, sk, mine, sk4, left,
    own_even, own_odd, even, odd, other_even, other_odd, gram, couple, rows, columns, fours, index, tops,
    pg, gr, pc, cr, pt, qr, rs, rr, t4, r4,
    s_f, r_f, s_a, r_a, s_k, r_k, s_4, r_4, s_p, r_p, s_c, r_c, s_o, r_o, s_r, r_r, s_t, r_t, s_q, r_q, local,
):
    leaf = lax.axis_index("leaf")
    col = lax.axis_index("col")
    quarter = leaf % 4
    sibling = quarter + 1 - 2 * (quarter % 2)
    barrier = pltpu.get_barrier_semaphore()
    each(LEAVES, lambda k: pl.semaphore_signal(barrier, inc=1, **mate(k)))
    each(COLS, lambda k: pl.semaphore_signal(barrier, inc=1, **beside(k)))
    smalls = [
        pltpu.make_async_copy(a, b, local.at[k])
        for k, (a, b) in enumerate(
            [(pivots_hbm, pivots), (scales_hbm, scales), (parent_hbm, parent), (top_hbm, top)]
        )
    ]
    for copy in smalls:
        copy.start()

    eye = (iota((WIDE, WIDE), 0) == iota((WIDE, WIDE), 1)).astype(F32).astype(BF)

    def turn(k):
        start = pl.multiple_of((leaf + k) % LEAVES * REGION, 8)
        turned = dot_nt(eye, merged[pl.ds(start, PER), :].astype(BF))
        feat[k] = turned[:F].astype(BF)
        aux[k] = jnp.concatenate(
            [turned[F + r : F + r + 1, 128 * c : 128 * c + 128] for r in range(2) for c in range(4)], 0
        )

    def send_feat(k):
        return remote(feat.at[k], rx.at[k], (s_f, r_f), k, mate(k))

    def send_aux(k):
        return remote(aux.at[k], ra.at[k], (s_a, r_a), k, mate(k))

    def four(j, _):
        for r in range(1, 5):
            turn((4 * j + r) % LEAVES)
        pl.when(j == 0)(lambda: pl.semaphore_wait(barrier, LEAVES + COLS - 2))
        for send in (send_aux, send_feat):
            for r in range(1, 4):
                send(4 * j + r).start()
            pl.when(j < 3)(lambda: send(4 * j + 4).start())
        return 0

    lax.fori_loop(0, LEAVES // 4, four, 0)
    rx[0] = feat[0]
    ra[0] = aux[0]

    for copy in smalls:
        copy.wait()
    spare[...] = jnp.ones((8, 128), F32)
    spare[0:1, 0:F] = scales[...]
    inverse = 1.0 / to_column(spare[0:1, :])[:F]
    scale = inverse * inverse * LOG2E
    scale2 = across(scale, RANK)
    scale4 = across(scale, PER)

    place = pivots[...]
    within = place % ROWS
    block = within // PACKET
    key = (block // COLS) * PER + (place // ROWS) * PACKET + within % PACKET
    holder = block % COLS
    crossed = (block // COLS) // 8 != leaf // 8
    holder = jnp.where(crossed, holder + 1 - 2 * (holder % 2), holder)
    key = jnp.where(holder == col, key, -PER)
    key = across(to_column(key.astype(F32)), PER)

    def mark(k):
        source = (leaf + LEAVES - k) % LEAVES
        tags = ra[k, 4:8, :]
        tag = jnp.concatenate([tags[r : r + 1] for r in range(4)], 1)
        wanted = tag + (PER // 2 + source * PER).astype(F32)
        hot[k] = (key == wanted).astype(F32).astype(BF)

    def mark_next(k, _):
        pl.when(k > 0)(lambda: send_aux(k).wait_recv())
        mark(k)
        return 0

    lax.fori_loop(0, LEAVES, mark_next, 0)

    index[...] = top_index(parent, top, leaf // 4)
    index2 = across(index[...], 2 * RANK)
    number = iota((RANK, 2 * RANK), 1)
    base = (quarter * RANK).astype(F32)
    other = (sibling * RANK).astype(F32)
    chosen = index2[:, :RANK] == iota((RANK, RANK), 1).astype(F32) + base
    rows[...] = chosen.astype(F32).astype(BF)
    lanes = number.astype(F32) + jnp.where(number < RANK, base, other - RANK)
    columns[...] = (index2 == lanes).astype(F32).astype(BF)
    chosen = across(index[...], 4 * RANK) == iota((RANK, 4 * RANK), 1).astype(F32)
    fours[...] = chosen.astype(F32).astype(BF)

    def pick(j, total):
        for r in range(4):
            k = 4 * j + r
            if r:
                send_feat(k).wait_recv()
            else:
                pl.when(k > 0)(lambda: send_feat(k).wait_recv())
        for r in range(4):
            total = total + dot_nt(hot[4 * j + r], rx[4 * j + r])
        return total

    picked = lax.fori_loop(0, LEAVES // 4, pick, jnp.zeros((RANK, F), F32))
    picked = jnp.concatenate([picked, jnp.zeros((RANK, 128 - F), F32)], 1).T[:F]
    sk[0] = picked.astype(BF)

    def send_skel(k):
        return remote(sk.at[0], sk.at[k], (s_k, r_k), k, beside(k))

    each(COLS, lambda k: send_skel(k).start())

    def norms(k, _):
        side[k] = point_side(rx[k].astype(F32), scale4)
        return 0

    lax.fori_loop(0, LEAVES, norms, 0)

    def add_skel(k, total):
        send_skel(k).wait_recv()
        return total + sk[k].astype(F32)

    picked = lax.fori_loop(1, COLS, add_skel, picked)
    mine[...] = picked.astype(BF)
    sk4[quarter] = picked.astype(BF)

    def send_four(k):
        return remote(mine, sk4.at[quarter], (s_4, r_4), k, cousin(k))

    each(4, lambda k: send_four(k).start())
    left[0:RANK, :] = skel_side(picked, scale2)

    def block_of(k, out, begin):
        p = rx[k]
        fill = jnp.zeros((256 - 3 * F - 16, PER), BF)
        right = jnp.concatenate([p, p, p, side[k], fill], 0)
        power = dot(left[begin : begin + RANK, :], right)
        out[0:RANK, :] = jnp.exp2(jnp.minimum(power, 0.0)).astype(BF)

    def own_of(k, out, turned):
        block_of(k, out, 0)
        turned[...] = out[0:RANK, :].T
        value = jnp.concatenate([ra[k, r : r + 1, :] for r in range(4)], 1)
        out[RANK:, :] = jnp.broadcast_to(value, (16, PER)).astype(BF)

    def gram_of(u, turned):
        gram[...] += dot(u[...], turned[...])

    def couple_of(v, turned):
        couple[...] += dot(v[...], turned[...])

    last = LEAVES // 2 - 1

    def own_two(j, _):
        own_of(2 * j, own_even, even.at[j])
        gram_of(own_odd, odd.at[(j + last) % (last + 1)])
        own_of(2 * j + 1, own_odd, odd.at[j])
        gram_of(own_even, even.at[j])
        return 0

    def other_two(j, _):
        block_of(2 * j, other_even, RANK)
        couple_of(other_odd, odd.at[(j + last) % (last + 1)])
        block_of(2 * j + 1, other_odd, RANK)
        couple_of(other_even, even.at[j])
        return 0

    gram[...] = jnp.zeros_like(gram)
    couple[...] = jnp.zeros_like(couple)
    odd[last] = jnp.zeros((PER, RANK), BF)
    own_odd[...] = jnp.zeros_like(own_odd)
    other_odd[...] = jnp.zeros_like(other_odd)
    lax.fori_loop(0, last + 1, own_two, 0)
    gram_of(own_odd, odd.at[last])

    def send_gram(k):
        return remote(pg.at[(col + k) % COLS], gr.at[k], (s_p, r_p), k, beside(k))

    def send_couple(k):
        return remote(pc.at[(col + k) % COLS], cr.at[k], (s_c, r_c), k, beside(k))

    def send_chosen(k):
        return remote(pt.at[(col + k) % COLS], qr.at[k], (s_o, r_o), k, beside(k))

    def send_rhs(k):
        return remote(rs, rr.at[k], (s_r, r_r), k, beside(k))

    part = gram[0:RANK, :].astype(BF)
    for k in range(COLS):
        pg[k] = part[k * SLAB : (k + 1) * SLAB]
    rhs = gram[RANK : RANK + 1, :]
    rhs = jnp.sum(dot_nt(stack16(split3(rhs), RANK), rows[...]), 0, keepdims=True)
    rs[...] = jnp.zeros_like(rs)
    rs[0:1, :] = rhs[:, :128]
    rs[1:2, :] = rhs[:, 128:]
    each(COLS, lambda k: send_gram(k).start())
    each(COLS, lambda k: send_rhs(k).start())
    tops[...] = dot_nt(dot(rows[...], part).astype(BF), columns[:, 0:RANK])

    each(4, lambda k: remote(mine, sk4.at[(quarter + 4 - k) % 4], (s_4, r_4), k, cousin(k)).wait_recv())
    left[RANK:, :] = skel_side(sk4[sibling].astype(F32), scale2)
    lax.fori_loop(0, last + 1, other_two, 0)
    couple_of(other_odd, odd.at[last])

    part = couple[...].astype(BF)
    chosen = dot_nt(dot_nt(rows[...], part).astype(BF), columns[:, RANK:]) + tops[...]
    chosen = chosen.astype(BF)
    for k in range(COLS):
        pt[k] = chosen[k * SLAB : (k + 1) * SLAB]
    each(COLS, lambda k: send_chosen(k).start())
    part = couple[...].T.astype(BF)
    for k in range(COLS):
        pc[k] = part[k * SLAB : (k + 1) * SLAB]
    each(COLS, lambda k: send_couple(k).start())

    whole = jnp.concatenate([sk4[k] for k in range(4)], 1)
    points = dot_nt(whole, fours[...])
    fill = jnp.zeros((256 - 3 * F - 16, RANK), BF)
    points_b = points.astype(BF)
    right = jnp.concatenate([points_b, points_b, points_b, point_side(points, scale2), fill], 0)
    value = jnp.exp2(jnp.minimum(dot(skel_side(points, scale2), right), 0.0))
    crossing = (across(index[...], RANK) >= 2.0 * RANK) != (index[...].T[0:1, :] >= 2.0 * RANK)
    square = iota((RANK, RANK), 0) == iota((RANK, RANK), 1)
    tops[...] = jnp.where(crossing, value, 0.0) + jnp.where(square, ridge[0], 0.0)

    def finish(sends):
        return lambda k: [send(k).wait_send() for send in sends]

    each(LEAVES, finish((send_aux, send_feat)))
    each(COLS, finish((send_skel, send_gram, send_rhs)))
    each(4, finish((send_four,)))

    def add_chosen(k, totals):
        send_chosen(k).wait_recv()
        send_rhs(k).wait_recv()
        return totals[0] + qr[k].astype(F32), totals[1] + rr[k]

    chosen, rhs = lax.fori_loop(1, COLS, add_chosen, (pt[col].astype(F32), rs[...]))
    chosen = chosen * (1.0 / NODE)
    t4[0] = chosen.astype(BF)
    r4[0] = rhs * (1.0 / NODE)

    def send_top(k):
        return remote(t4.at[0], t4.at[k], (s_t, r_t), k, cousin(k))

    def send_top_rhs(k):
        return remote(r4.at[0], r4.at[k], (s_q, r_q), k, cousin(k))

    each(4, lambda k: send_top(k).start())
    each(4, lambda k: send_top_rhs(k).start())

    def add_gram(k, total):
        send_gram(k).wait_recv()
        return total + gr[k].astype(F32)

    def add_couple(k, total):
        send_couple(k).wait_recv()
        return total + cr[k].astype(F32)

    total = lax.fori_loop(1, COLS, add_gram, pg[col].astype(F32))
    diagonal = iota((SLAB, RANK), 0) + col * SLAB == iota((SLAB, RANK), 1)
    out_share[0, :, 0:RANK] = total * (1.0 / NODE) + jnp.where(diagonal, ridge[0], 0.0)
    total = lax.fori_loop(1, COLS, add_couple, pc[col].astype(F32))
    out_share[0, :, RANK:] = total * (1.0 / NODE)
    result = chosen + tops[pl.ds(pl.multiple_of(col * SLAB, SLAB), SLAB), :]

    def add_top(k, totals):
        send_top(k).wait_recv()
        send_top_rhs(k).wait_recv()
        return totals[0] + t4[k].astype(F32), totals[1] + r4[k]

    result, rhs = lax.fori_loop(1, 4, add_top, (result, r4[0]))
    out_top[0] = result
    out_rhs[...] = jnp.concatenate([rhs[0:1], rhs[1:2]], 1)

    each(COLS, finish((send_couple, send_chosen)))
    each(4, finish((send_top, send_top_rhs)))


SHAPES = ((1, SLAB, 2 * RANK), (1, SLAB, RANK), (1, RANK))


def exchange(merged, ridge, *smalls):
    return pl.pallas_call(
        exchange_kernel,
        out_shape=tuple(pltpu.VMEM(shape, F32) for shape in SHAPES),
        in_specs=[VMEM, pl.BlockSpec(memory_space=pltpu.SMEM)] + [ANYWHERE] * 4,
        out_specs=[VMEM] * 3,
        scratch_shapes=[
            pltpu.VMEM((1, RANK), jnp.int32),
            pltpu.VMEM((1, F), F32),
            pltpu.VMEM((8, RANK), jnp.int32),
            pltpu.VMEM((4, RANK), jnp.int32),
            pltpu.VMEM((8, 128), F32),
            pltpu.VMEM((LEAVES, F, PER), BF),
            pltpu.VMEM((LEAVES, 8, 128), F32),
            pltpu.VMEM((LEAVES, F, PER), BF),
            pltpu.VMEM((LEAVES, 8, 128), F32),
            pltpu.VMEM((LEAVES, RANK, PER), BF),
            pltpu.VMEM((LEAVES, 16, PER), BF),
            pltpu.VMEM((COLS, F, RANK), BF),
            pltpu.VMEM((F, RANK), BF),
            pltpu.VMEM((4, F, RANK), BF),
            pltpu.VMEM((2 * RANK, 256), BF),
            pltpu.VMEM((RANK + 16, PER), BF),
            pltpu.VMEM((RANK + 16, PER), BF),
            pltpu.VMEM((LEAVES // 2, PER, RANK), BF),
            pltpu.VMEM((LEAVES // 2, PER, RANK), BF),
            pltpu.VMEM((RANK, PER), BF),
            pltpu.VMEM((RANK, PER), BF),
            pltpu.VMEM((RANK + 16, RANK), F32),
            pltpu.VMEM((RANK, RANK), F32),
            pltpu.VMEM((RANK, RANK), BF),
            pltpu.VMEM((RANK, 2 * RANK), BF),
            pltpu.VMEM((RANK, 4 * RANK), BF),
            pltpu.VMEM((RANK, 128), F32),
            pltpu.VMEM((RANK, RANK), F32),
            pltpu.VMEM((COLS, SLAB, RANK), BF),
            pltpu.VMEM((COLS, SLAB, RANK), BF),
            pltpu.VMEM((COLS, SLAB, RANK), BF),
            pltpu.VMEM((COLS, SLAB, RANK), BF),
            pltpu.VMEM((COLS, SLAB, RANK), BF),
            pltpu.VMEM((COLS, SLAB, RANK), BF),
            pltpu.VMEM((8, 128), F32),
            pltpu.VMEM((COLS, 8, 128), F32),
            pltpu.VMEM((4, SLAB, RANK), BF),
            pltpu.VMEM((4, 8, 128), F32),
            *dma(LEAVES),
            *dma(LEAVES),
            *dma(COLS),
            *dma(4),
            *dma(COLS),
            *dma(COLS),
            *dma(COLS),
            *dma(COLS),
            *dma(4),
            *dma(4),
            pltpu.SemaphoreType.DMA((4,)),
        ],
        compiler_params=params(0, 40),
        name="exchange",
    )(merged, ridge, *in_hbm(*smalls))


def emit_kernel(*refs):
    ins, outs, sem = refs[:3], refs[3:6], refs[6]
    copies = [pltpu.make_async_copy(a, b, sem.at[k]) for k, (a, b) in enumerate(zip(ins, outs))]
    for copy in copies:
        copy.start()
    for copy in copies:
        copy.wait()


def emit(results):
    return pl.pallas_call(
        emit_kernel,
        out_shape=tuple(jax.ShapeDtypeStruct(shape, F32) for shape in SHAPES),
        in_specs=[VMEM] * 3,
        out_specs=[ANYWHERE] * 3,
        scratch_shapes=[pltpu.SemaphoreType.DMA((3,))],
        compiler_params=params(),
        name="emit",
    )(*results)


def local(features, targets, owner, length_scales, ridge, leaf_pivots, parent_pivots, top_pivots):
    merged = pack(features, targets.reshape(ROWS // 128, 128), owner.reshape(ROWS // 128, 128))
    smalls = (leaf_pivots, length_scales.reshape(1, F), parent_pivots, top_pivots)
    return tuple(emit(exchange(merged, ridge, *smalls)))


def solution(mesh):
    return jax.shard_map(
        local,
        mesh=mesh,
        in_specs=(
            P(None, ("leaf", "col")),
            P(("leaf", "col")),
            P(("leaf", "col")),
            P(),
            P(),
            P("leaf", None),
            P(),
            P(),
        ),
        out_specs=(P("leaf", "col", None), P("leaf", "col", None), P("leaf", None)),
        check_vma=False,
    )
```

```python
import functools
import math

import jax
import jax.numpy as jnp
from jax import lax
from jax.experimental import pallas as pl
from jax.experimental.pallas import tpu as pltpu
from jax.sharding import PartitionSpec as P

F = 48
RANK = 256
ROWS = 8192
LEAVES = 16
COLS = 8
OWNERS = 128
PACKET = 64
PER = ROWS // LEAVES
CHUNK = 256
CHUNKS = ROWS // CHUNK
WINDOW = 40
REGION = PER + WINDOW
SLOTS = 16
WHICH = 50
WIDE = 64
SLAB = RANK // COLS
NODE = ROWS * COLS
LOG2E = math.log2(math.e)
BF = jnp.bfloat16
F32 = jnp.float32
NT = (((1,), (1,)), ((), ()))
MESH = pl.DeviceIdType.MESH


def dma(count):
    return [pltpu.SemaphoreType.DMA((count,))] * 2


def params(number=None, limit=24):
    if number is None:
        return pltpu.CompilerParams(vmem_limit_bytes=limit * 2**20)
    return pltpu.CompilerParams(
        collective_id=number, has_side_effects=True, vmem_limit_bytes=limit * 2**20
    )


ANYWHERE = pl.BlockSpec(memory_space=pl.ANY)
VMEM = pl.BlockSpec(memory_space=pltpu.VMEM)


def iota(shape, axis):
    return lax.broadcasted_iota(jnp.int32, shape, axis)


def dot(a, b):
    return jnp.dot(a, b, preferred_element_type=F32)


def dot_nt(a, b):
    return lax.dot_general(a, b, NT, preferred_element_type=F32)


def row_pair(two):
    return jnp.concatenate([two[0:1], two[1:2]], 1)


def ordering():
    return (iota((CHUNK, CHUNK), 0) < iota((CHUNK, CHUNK), 1)).astype(F32).astype(BF)


def rank_all(target, owner, goals, rows, table):
    goals[...] = target[...].astype(F32)
    weights = jnp.concatenate([ordering(), jnp.ones((CHUNK, 128), BF)], 1)
    lane = iota((LEAVES, 128), 1)

    def ranks(t, carry):
        seen, seen_leaf, most = carry
        own = row_pair(owner[pl.ds(2 * t, 2), :])
        leaf = own // 8
        is_own = iota((OWNERS, CHUNK), 0) == own
        is_leaf = iota((LEAVES, CHUNK), 0) == leaf
        is_after = iota((LEAVES, CHUNK), 0) > leaf
        marks = jnp.concatenate(
            [m.astype(F32).astype(BF) for m in (is_own, is_leaf, is_after)], 0
        )
        sums = dot(marks, weights)
        counts = sums[:OWNERS, CHUNK:]
        leaf_counts = sums[OWNERS : OWNERS + LEAVES, CHUNK:]
        base = sums[OWNERS + LEAVES :, CHUNK:]
        prior = sums[:OWNERS, :CHUNK] + jnp.concatenate([seen, seen], 1)
        rank = jnp.sum(jnp.where(is_own, prior, 0.0), 0, keepdims=True)
        place = sums[OWNERS : OWNERS + LEAVES, :CHUNK] + jnp.concatenate([base, base], 1)
        place = jnp.sum(jnp.where(is_leaf, place, 0.0), 0, keepdims=True)
        tag = (own % 8).astype(F32) * PACKET + rank - (PER // 2)
        rows[t, 0:1, :] = place
        rows[t, 1:2, :] = row_pair(goals[pl.ds(2 * t, 2), :])
        rows[t, 2:3, :] = tag
        rows[t, 3:4, :] = own.astype(F32) * PACKET + rank
        here = lane == t
        table[0:LEAVES, :] = jnp.where(here, seen_leaf.astype(jnp.int32), table[0:LEAVES, :])
        table[LEAVES : 2 * LEAVES, :] = jnp.where(
            here, base.astype(jnp.int32), table[LEAVES : 2 * LEAVES, :]
        )
        return seen + counts, seen_leaf + leaf_counts, jnp.maximum(most, leaf_counts)

    table[0:LEAVES, :] = jnp.full((LEAVES, 128), PER, jnp.int32)
    zero = jnp.zeros((LEAVES, 128), F32)
    _, _, most = lax.fori_loop(
        0, CHUNKS, ranks, (jnp.zeros((OWNERS, 128), F32), zero, zero), unroll=16
    )
    most = jnp.broadcast_to(jnp.max(most, 0, keepdims=True), (8, 128))
    table[2 * LEAVES :, :] = most.astype(jnp.int32)


def joined_of(feat, rows, t):
    row = iota((16, CHUNK), 0)
    goal, tag = rows[t, 1:2, :], rows[t, 2:3, :]
    extra = jnp.where(row == 0, goal, jnp.where(row == 1, tag, 0.0)).astype(BF)
    return jnp.concatenate([feat[:, pl.ds(pl.multiple_of(t * CHUNK, CHUNK), CHUNK)], extra], 0)


def sort_all(feat, rows, ybuf):
    def sort(t, _):
        place = rows[t, 0:1, :].astype(jnp.int32)
        chosen = (iota((CHUNK, CHUNK), 0) == place).astype(F32).astype(BF)
        start = pl.multiple_of(t * CHUNK, CHUNK)
        ybuf[pl.ds(start, CHUNK), :] = dot_nt(chosen, joined_of(feat, rows, t))
        return 0

    lax.fori_loop(0, CHUNKS, sort, 0, unroll=8)


def merge_all(scal, ybuf, zbuf):
    widest = scal[2 * LEAVES, 0]

    @pl.when(widest <= WINDOW)
    def quick():
        def merge(t, _):
            for i in range(LEAVES):
                source = t * CHUNK + scal[LEAVES + i, t]
                goal = i * REGION + scal[i, t]
                zbuf[pl.ds(goal, WINDOW), :] = ybuf[pl.ds(source, WINDOW), :]
            return 0

        lax.fori_loop(0, CHUNKS, merge, 0, unroll=4)

    @pl.when(widest > WINDOW)
    def slow():
        def merge(index, _):
            t = index // LEAVES
            i = index % LEAVES
            source = t * CHUNK + scal[LEAVES + i, t]
            first = scal[i, t]
            count = scal[i, t + 1] - first

            def part(k, _):
                rows = ybuf[pl.ds(source + 8 * k, 8), :]
                zbuf[pl.ds(i * REGION + first + 8 * k, 8), :] = rows
                return 0

            lax.fori_loop(0, (count + 7) // 8, part, 0)
            return 0

        lax.fori_loop(0, CHUNKS * LEAVES, merge, 0)


def pack_kernel(
    feat_hbm, target, owner, zbuf, feat, goals, rows, ybuf, table, scal, sem, feat_sem
):
    bring = pltpu.make_async_copy(feat_hbm, feat, feat_sem)
    bring.start()
    rank_all(target, owner, goals, rows, table)
    move = pltpu.make_async_copy(table, scal, sem)
    move.start()
    bring.wait()
    sort_all(feat, rows, ybuf)
    move.wait()
    merge_all(scal, ybuf, zbuf)


def merge_kernel(ybuf, table, zbuf, scal, sem):
    move = pltpu.make_async_copy(table, scal, sem)
    move.start()
    move.wait()
    merge_all(scal, ybuf, zbuf)


def prepare_kernel(
    feat_hbm, target, owner, pivots, ybuf, table, held, feat, goals, rows, feat_sem, s_v, r_v
):
    barrier = pltpu.get_barrier_semaphore()
    each(LEAVES, lambda k: pl.semaphore_signal(barrier, inc=1, **mate(k)))
    bring = pltpu.make_async_copy(feat_hbm, feat, feat_sem)
    bring.start()
    rank_all(target, owner, goals, rows, table)

    def send_pivots(k):
        return remote(pivots, held.at[k], (s_v, r_v), k, mate(k))

    held[0] = pivots[...]
    pl.semaphore_wait(barrier, LEAVES - 1)
    each(LEAVES, lambda k: send_pivots(k).start())
    bring.wait()
    sort_all(feat, rows, ybuf)
    each(LEAVES, lambda k: (send_pivots(k).wait_send(), send_pivots(k).wait_recv()))


def in_hbm(*arrays):
    return [pltpu.with_memory_space_constraint(a, pltpu.HBM) for a in arrays]


def pack(features, targets, owner):
    return pl.pallas_call(
        pack_kernel,
        out_shape=pltpu.VMEM((LEAVES * REGION, WIDE), F32),
        in_specs=[ANYWHERE, VMEM, VMEM],
        out_specs=VMEM,
        scratch_shapes=[
            pltpu.VMEM((F, ROWS), BF),
            pltpu.VMEM((ROWS // 128, 128), F32),
            pltpu.VMEM((CHUNKS, 8, CHUNK), F32),
            pltpu.VMEM((ROWS + WINDOW, WIDE), F32),
            pltpu.VMEM((40, 128), jnp.int32),
            pltpu.SMEM((40, 128), jnp.int32),
            pltpu.SemaphoreType.DMA,
            pltpu.SemaphoreType.DMA,
        ],
        compiler_params=params(),
        name="pack",
    )(*in_hbm(features, targets, owner))


def prepare(features, targets, owner, pivots):
    return pl.pallas_call(
        prepare_kernel,
        out_shape=(
            pltpu.VMEM((ROWS + WINDOW, WIDE), F32),
            pltpu.VMEM((40, 128), jnp.int32),
            pltpu.VMEM((LEAVES, 1, RANK), jnp.int32),
        ),
        in_specs=[ANYWHERE, VMEM, VMEM, VMEM],
        out_specs=[VMEM] * 3,
        scratch_shapes=[
            pltpu.VMEM((F, ROWS), BF),
            pltpu.VMEM((ROWS // 128, 128), F32),
            pltpu.VMEM((CHUNKS, 8, CHUNK), F32),
            pltpu.SemaphoreType.DMA,
            *dma(LEAVES),
        ],
        compiler_params=params(0),
        name="prepare",
    )(*in_hbm(features, targets, owner, pivots))


def merge(ybuf, table):
    return pl.pallas_call(
        merge_kernel,
        out_shape=pltpu.VMEM((LEAVES * REGION, WIDE), F32),
        in_specs=[VMEM] * 2,
        out_specs=VMEM,
        scratch_shapes=[pltpu.SMEM((40, 128), jnp.int32), pltpu.SemaphoreType.DMA],
        compiler_params=params(),
        name="merge",
    )(ybuf, table)


def split3(x):
    high = x.astype(BF)
    rest = x - high.astype(F32)
    mid = rest.astype(BF)
    return high, mid, (rest - mid.astype(F32)).astype(BF)


def stack16(parts, width):
    row = iota((16, width), 0)
    block = jnp.zeros((16, width), F32)
    for k, part in enumerate(parts):
        block = jnp.where(row == k, part if isinstance(part, float) else part.astype(F32), block)
    return block.astype(BF)


def half_norm(points, scale):
    return jnp.sum(points * points * (0.5 * scale), 0, keepdims=True)


def point_side(points, scale):
    high, mid, low = split3(-half_norm(points, scale))
    return stack16([high, mid, low, 1.0, 1.0, 1.0], points.shape[1])


def skel_side(skel, scale):
    width = skel.shape[1]
    high, mid, low = split3(skel * scale)
    extra = stack16([1.0, 1.0, 1.0, *split3(-half_norm(skel, scale))], width)
    parts = [p.astype(F32) for p in (high, mid, low, extra)]
    fill = jnp.zeros((256 - 3 * F - 16, width), F32)
    return jnp.concatenate([*parts, fill], 0).T.astype(BF)


def select_row(table, row):
    hit = iota(table.shape, 0) == row
    return jnp.sum(jnp.where(hit, table.astype(F32), 0.0), 0, keepdims=True)


def to_column(row):
    return jnp.broadcast_to(row, (128, row.shape[1])).T


def across(column, width):
    return jnp.concatenate([column] * (width // 128), 1)


def place_of(leaf, col):
    return dict(device_id=(leaf, col), device_id_type=MESH)


def rem(a, b):
    return lax.rem(jnp.int32(a), jnp.int32(b))


def div(a, b):
    return lax.div(jnp.int32(a), jnp.int32(b))


def mate(k):
    leaf, col = lax.axis_index("leaf"), lax.axis_index("col")
    to = rem(leaf + k, LEAVES)
    cross = rem(div(to, 8) + div(leaf, 8), 2)
    return place_of(to, col + cross * (1 - 2 * rem(col, 2)))


def beside(k):
    leaf, col = lax.axis_index("leaf"), lax.axis_index("col")
    return place_of(leaf, rem(col + k, COLS))


def cousin(k):
    leaf, col = lax.axis_index("leaf"), lax.axis_index("col")
    return place_of(leaf - rem(leaf, 4) + rem(leaf + k, 4), col)


def each(count, step, unroll=1):
    lax.fori_loop(1, count, lambda k, _: (step(k), 0)[1], 0, unroll=unroll)


def turn_of(n):
    odd = rem(n, 2)
    return rem(odd * div(n + 1, 2) + (1 - odd) * (LEAVES - div(n, 2)), LEAVES)


def remote(src, dst, sems, k, peer):
    return pltpu.make_async_remote_copy(src, dst, sems[0].at[k], sems[1].at[k], **peer)


def top_index(parent, top, group):
    top_row = select_row(top[...], group)
    below = jnp.concatenate([select_row(parent[...], 2 * group + r) for r in range(2)], 1)
    number = iota((RANK, 2 * RANK), 1)
    below = below + jnp.where(iota((1, 2 * RANK), 1) >= RANK, 2.0 * RANK, 0.0)
    hit = across(to_column(top_row), 2 * RANK) == number.astype(F32)
    index = jnp.sum(jnp.where(hit, below, 0.0), 1, keepdims=True)
    return jnp.broadcast_to(index, (RANK, 128))


def exchange_kernel(
    early, merged, held, ridge, pivots_hbm, scales_hbm, parent_hbm, top_hbm, out_share, out_top, out_rhs, most,
    pivots, scales, parent, top, spare, feat, aux, rx, ra, wants, small, got, hot, side, sk, mine, sk4, left,
    even, odd, other_even, other_odd, gram, couple, rows, columns, fours, index, tops,
    pg, gr, pc, cr, pt, qr, rs, rr, t4, r4,
    s_f, r_f, s_a, r_a, s_k, r_k, s_4, r_4, s_p, r_p, s_c, r_c, s_o, r_o, s_r, r_r, s_t, r_t, s_q, r_q, local,
):
    leaf = lax.axis_index("leaf")
    col = lax.axis_index("col")
    quarter = leaf % 4
    sibling = quarter + 1 - 2 * (quarter % 2)
    barrier = pltpu.get_barrier_semaphore()
    each(LEAVES, lambda k: pl.semaphore_signal(barrier, inc=1, **mate(k)))
    each(COLS, lambda k: pl.semaphore_signal(barrier, inc=1, **beside(k)))
    smalls = [
        pltpu.make_async_copy(a, b, local.at[k])
        for k, (a, b) in enumerate(
            [(pivots_hbm, pivots), (scales_hbm, scales), (parent_hbm, parent), (top_hbm, top)]
        )
    ]
    for copy in smalls:
        copy.start()

    eye = (iota((WIDE, WIDE), 0) == iota((WIDE, WIDE), 1)).astype(F32).astype(BF)

    if early:
        place = jnp.concatenate([held[(LEAVES - b) % LEAVES] for b in range(LEAVES)], 0)
        home = place % ROWS // PACKET
        valid = home == leaf * COLS + col
        number = (place // ROWS * PACKET + place % PACKET - PER // 2).astype(F32)
        order = dot(valid.astype(F32).astype(BF), ordering())
        order = jnp.where(valid, order, -1.0)

        def spread(table):
            return jnp.concatenate(
                [jnp.broadcast_to(table[b : b + 1], (SLOTS, RANK)) for b in range(LEAVES)], 0
            )

        shape = (LEAVES * SLOTS, RANK)
        hit = spread(order) == (iota(shape, 0) % SLOTS).astype(F32)
        wanted = jnp.where(hit, spread(number) + PER, 0.0)
        which = jnp.where(hit, iota(shape, 1).astype(F32) + 1.0, 0.0)
        shape = (LEAVES * SLOTS, 128)
        wants[0] = jnp.broadcast_to(jnp.sum(wanted, 1, keepdims=True) - PER, shape)
        wants[1] = jnp.broadcast_to(jnp.sum(which, 1, keepdims=True) - 1.0, shape)

    def turn(k):
        start = pl.multiple_of((leaf + k) % LEAVES * REGION, 8)
        turned = dot_nt(eye, merged[pl.ds(start, PER), :].astype(BF))
        feat[k] = turned[:F].astype(BF)
        goals, tags = (
            [turned[F + r : F + r + 1, 128 * c : 128 * c + 128] for c in range(4)] for r in range(2)
        )
        if early:
            slots = pl.ds(pl.multiple_of(k * SLOTS, SLOTS), SLOTS)
            chosen = (across(wants[0, slots, :], PER) == turned[F + 1 : F + 2]).astype(F32).astype(BF)
            taken = dot_nt(chosen, jnp.concatenate([turned, turned], 0).astype(BF))
            taken = jnp.where(iota((SLOTS, 128), 1) == WHICH, wants[1, slots, :], taken)
            zero = jnp.zeros((12, 128), F32)
            small[k] = jnp.concatenate([taken, *goals, zero], 0).astype(BF)
        else:
            aux[k] = jnp.concatenate(goals + tags, 0)

    def send_feat(k):
        return remote(feat.at[k], rx.at[k], (s_f, r_f), k, mate(k))

    def send_aux(k):
        return remote(aux.at[k], ra.at[k], (s_a, r_a), k, mate(k))

    def send_skel(k):
        return remote(sk.at[0], sk.at[k], (s_k, r_k), k, beside(k))

    def send_small(k):
        return remote(small.at[k], got.at[k], (s_a, r_a), k, mate(k))

    def turn_four(j, _):
        for r in range(4):
            turn(4 * j + r)
        return 0

    lax.fori_loop(0, LEAVES // 4, turn_four, 0)
    rx[0] = feat[0]
    if early:
        got[0] = small[0]
    else:
        ra[0] = aux[0]
    pl.semaphore_wait(barrier, LEAVES + COLS - 2)
    each(LEAVES, lambda n: (send_small if early else send_aux)(turn_of(n)).start())
    lax.fori_loop(1, 9 if early else LEAVES, lambda n, _: (send_feat(turn_of(n)).start(), 0)[1], 0)

    for copy in smalls:
        copy.wait()
    spare[...] = jnp.ones((8, 128), F32)
    spare[0:1, 0:F] = scales[...]
    inverse = 1.0 / to_column(spare[0:1, :])[:F]
    scale = inverse * inverse * LOG2E
    scale2 = across(scale, RANK)
    scale4 = across(scale, PER)

    index[...] = top_index(parent, top, leaf // 4)
    index2 = across(index[...], 2 * RANK)
    number = iota((RANK, 2 * RANK), 1)
    base = (quarter * RANK).astype(F32)
    other = (sibling * RANK).astype(F32)
    chosen = index2[:, :RANK] == iota((RANK, RANK), 1).astype(F32) + base
    rows[...] = chosen.astype(F32).astype(BF)
    lanes = number.astype(F32) + jnp.where(number < RANK, base, other - RANK)
    columns[...] = (index2 == lanes).astype(F32).astype(BF)
    chosen = across(index[...], 4 * RANK) == iota((RANK, 4 * RANK), 1).astype(F32)
    fours[...] = chosen.astype(F32).astype(BF)

    def norms(k, _):
        side[k] = point_side(rx[k].astype(F32), scale4)
        return 0

    if not early:
        place = pivots[...]
        within = place % ROWS
        block = within // PACKET
        key = (block // COLS) * PER + (place // ROWS) * PACKET + within % PACKET
        holder = block % COLS
        crossed = (block // COLS) // 8 != leaf // 8
        holder = jnp.where(crossed, holder + 1 - 2 * (holder % 2), holder)
        key = jnp.where(holder == col, key, -PER)
        key = across(to_column(key.astype(F32)), PER)

        def mark(k):
            source = (leaf + LEAVES - k) % LEAVES
            tags = ra[k, 4:8, :]
            tag = jnp.concatenate([tags[r : r + 1] for r in range(4)], 1)
            wanted = tag + (PER // 2 + source * PER).astype(F32)
            hot[k] = (key == wanted).astype(F32).astype(BF)

        def mark_next(k, _):
            pl.when(k > 0)(lambda: send_aux(k).wait_recv())
            mark(k)
            return 0

        lax.fori_loop(0, LEAVES, mark_next, 0)

        def pick(j, total):
            for r in range(4):
                k = 4 * j + r
                if r:
                    send_feat(k).wait_recv()
                else:
                    pl.when(k > 0)(lambda: send_feat(k).wait_recv())
            for r in range(4):
                total = total + dot_nt(hot[4 * j + r], rx[4 * j + r])
            return total

        picked = lax.fori_loop(0, LEAVES // 4, pick, jnp.zeros((RANK, F), F32))
        picked = jnp.concatenate([picked, jnp.zeros((RANK, 128 - F), F32)], 1).T[:F]
        sk[0] = picked.astype(BF)

        each(COLS, lambda k: send_skel(k).start())
        lax.fori_loop(0, LEAVES, norms, 0)
    else:
        each(LEAVES, lambda n: send_small(turn_of(n)).wait_recv())
        came = jnp.concatenate([got[k, 0:SLOTS, :] for k in range(LEAVES)], 0).astype(F32)
        chosen = came[:, WHICH : WHICH + 1] == iota((LEAVES * SLOTS, RANK), 1).astype(F32)
        picked = dot(came.T[:F].astype(BF), chosen.astype(F32).astype(BF))
        sk[0] = picked.astype(BF)
        each(COLS, lambda k: send_skel(k).start())
        lax.fori_loop(9, LEAVES, lambda n, _: (send_feat(turn_of(n)).start(), 0)[1], 0)

        largest = jnp.zeros((OWNERS, 1), F32)
        for b in range(LEAVES):
            inside = (iota((OWNERS, RANK), 0) == home[b : b + 1]).astype(F32)
            largest = jnp.maximum(largest, jnp.sum(inside, 1, keepdims=True))
    most[0] = jnp.max(largest).astype(jnp.int32) if early else 0

    def add_skel(k, total):
        send_skel(k).wait_recv()
        return total + sk[k].astype(F32)

    picked = lax.fori_loop(1, COLS, add_skel, picked)
    mine[...] = picked.astype(BF)
    sk4[quarter] = picked.astype(BF)

    def send_four(k):
        return remote(mine, sk4.at[quarter], (s_4, r_4), k, cousin(k))

    each(4, lambda k: send_four(k).start())
    left[0:RANK, :] = skel_side(picked, scale2)

    def block_of(k, out, begin):
        p = rx[k]
        fill = jnp.zeros((256 - 3 * F - 16, PER), BF)
        right = jnp.concatenate([p, p, p, side[k], fill], 0)
        power = dot(left[begin : begin + RANK, :], right)
        out[0:RANK, :] = jnp.exp2(jnp.minimum(power, 0.0)).astype(BF)

    def own_of(k, out):
        block_of(k, out, 0)
        value = got[k, SLOTS : 2 * SLOTS, :].astype(F32) if early else ra[k]
        value = jnp.concatenate([value[r : r + 1] for r in range(4)], 1)
        out[RANK:, :] = jnp.broadcast_to(value, (16, PER)).astype(BF)

    def gram_of(u):
        gram[...] += dot_nt(u[...], u[0:RANK, :])

    def couple_of(v, u):
        couple[...] += dot_nt(v[...], u[0:RANK, :])

    last = LEAVES // 2 - 1

    def own_two(j, _):
        k, l = turn_of(2 * j), turn_of(2 * j + 1)
        if early:
            pl.when(j > 0)(lambda: send_feat(k).wait_recv())
            send_feat(l).wait_recv()
            norms(k, 0)
            norms(l, 0)
        own_of(k, even.at[j])
        gram_of(odd.at[rem(j + last, last + 1)])
        own_of(l, odd.at[j])
        gram_of(even.at[j])
        return 0

    def other_two(j, _):
        block_of(turn_of(2 * j), other_even, RANK)
        couple_of(other_odd, odd.at[rem(j + last, last + 1)])
        block_of(turn_of(2 * j + 1), other_odd, RANK)
        couple_of(other_even, even.at[j])
        return 0

    gram[...] = jnp.zeros_like(gram)
    couple[...] = jnp.zeros_like(couple)
    odd[last] = jnp.zeros((RANK + 16, PER), BF)
    other_odd[...] = jnp.zeros_like(other_odd)
    def send_gram(k):
        return remote(pg.at[(col + k) % COLS], gr.at[k], (s_p, r_p), k, beside(k))

    def send_couple(k):
        return remote(pc.at[(col + k) % COLS], cr.at[k], (s_c, r_c), k, beside(k))

    def send_chosen(k):
        return remote(pt.at[(col + k) % COLS], qr.at[k], (s_o, r_o), k, beside(k))

    def send_rhs(k):
        return remote(rs, rr.at[k], (s_r, r_r), k, beside(k))

    def sibling_side():
        each(4, lambda k: remote(mine, sk4.at[(quarter + 4 - k) % 4], (s_4, r_4), k, cousin(k)).wait_recv())
        left[RANK:, :] = skel_side(sk4[sibling].astype(F32), scale2)

    def give_gram():
        gram_of(odd.at[last])
        part = gram[0:RANK, :].astype(BF)
        for k in range(COLS):
            pg[k] = part[k * SLAB : (k + 1) * SLAB]
        rhs = gram[RANK : RANK + 1, :]
        rhs = jnp.sum(dot_nt(stack16(split3(rhs), RANK), rows[...]), 0, keepdims=True)
        rs[...] = jnp.zeros_like(rs)
        rs[0:1, :] = rhs[:, :128]
        rs[1:2, :] = rhs[:, 128:]
        each(COLS, lambda k: send_gram(k).start())
        each(COLS, lambda k: send_rhs(k).start())
        tops[...] = dot_nt(dot(rows[...], part).astype(BF), columns[:, 0:RANK])

    def half(h, _):
        pairs = LEAVES // 4
        lax.fori_loop(pairs * h, pairs * (h + 1), own_two, 0)
        pl.when(h == 0)(sibling_side)
        pl.when(h == 1)(give_gram)
        lax.fori_loop(pairs * h, pairs * (h + 1), other_two, 0)
        return 0

    lax.fori_loop(0, 2, half, 0)
    couple_of(other_odd, odd.at[last])

    part = couple[...].astype(BF)
    chosen = dot_nt(dot_nt(rows[...], part).astype(BF), columns[:, RANK:]) + tops[...]
    chosen = chosen.astype(BF)
    for k in range(COLS):
        pt[k] = chosen[k * SLAB : (k + 1) * SLAB]
    each(COLS, lambda k: send_chosen(k).start())
    part = couple[...].T.astype(BF)
    for k in range(COLS):
        pc[k] = part[k * SLAB : (k + 1) * SLAB]
    each(COLS, lambda k: send_couple(k).start())

    whole = jnp.concatenate([sk4[k] for k in range(4)], 1)
    points = dot_nt(whole, fours[...])
    fill = jnp.zeros((256 - 3 * F - 16, RANK), BF)
    points_b = points.astype(BF)
    right = jnp.concatenate([points_b, points_b, points_b, point_side(points, scale2), fill], 0)
    value = jnp.exp2(jnp.minimum(dot(skel_side(points, scale2), right), 0.0))
    crossing = (across(index[...], RANK) >= 2.0 * RANK) != (index[...].T[0:1, :] >= 2.0 * RANK)
    square = iota((RANK, RANK), 0) == iota((RANK, RANK), 1)
    tops[...] = jnp.where(crossing, value, 0.0) + jnp.where(square, ridge[0], 0.0)

    def finish(sends):
        return lambda k: [send(k).wait_send() for send in sends]

    each(LEAVES, finish((send_small if early else send_aux, send_feat)))
    each(COLS, finish((send_skel, send_gram, send_rhs)))
    each(4, finish((send_four,)))

    def add_chosen(k, totals):
        send_chosen(k).wait_recv()
        send_rhs(k).wait_recv()
        return totals[0] + qr[k].astype(F32), totals[1] + rr[k]

    chosen, rhs = lax.fori_loop(1, COLS, add_chosen, (pt[col].astype(F32), rs[...]))
    chosen = chosen * (1.0 / NODE)
    t4[0] = chosen.astype(BF)
    r4[0] = rhs * (1.0 / NODE)

    def send_top(k):
        return remote(t4.at[0], t4.at[k], (s_t, r_t), k, cousin(k))

    def send_top_rhs(k):
        return remote(r4.at[0], r4.at[k], (s_q, r_q), k, cousin(k))

    each(4, lambda k: send_top(k).start())
    each(4, lambda k: send_top_rhs(k).start())

    def add_gram(k, total):
        send_gram(k).wait_recv()
        return total + gr[k].astype(F32)

    def add_couple(k, total):
        send_couple(k).wait_recv()
        return total + cr[k].astype(F32)

    total = lax.fori_loop(1, COLS, add_gram, pg[col].astype(F32))
    diagonal = iota((SLAB, RANK), 0) + col * SLAB == iota((SLAB, RANK), 1)
    out_share[0, :, 0:RANK] = total * (1.0 / NODE) + jnp.where(diagonal, ridge[0], 0.0)
    total = lax.fori_loop(1, COLS, add_couple, pc[col].astype(F32))
    out_share[0, :, RANK:] = total * (1.0 / NODE)
    result = chosen + tops[pl.ds(pl.multiple_of(col * SLAB, SLAB), SLAB), :]

    def add_top(k, totals):
        send_top(k).wait_recv()
        send_top_rhs(k).wait_recv()
        return totals[0] + t4[k].astype(F32), totals[1] + r4[k]

    result, rhs = lax.fori_loop(1, 4, add_top, (result, r4[0]))
    out_top[0] = result
    out_rhs[...] = jnp.concatenate([rhs[0:1], rhs[1:2]], 1)

    each(COLS, finish((send_couple, send_chosen)))
    each(4, finish((send_top, send_top_rhs)))


SHAPES = ((1, SLAB, 2 * RANK), (1, SLAB, RANK), (1, RANK))


def exchange(early, number, merged, held, ridge, *smalls):
    return pl.pallas_call(
        functools.partial(exchange_kernel, early),
        out_shape=(
            *(pltpu.VMEM(shape, F32) for shape in SHAPES),
            jax.ShapeDtypeStruct((1,), jnp.int32),
        ),
        in_specs=[VMEM, VMEM, pl.BlockSpec(memory_space=pltpu.SMEM)] + [ANYWHERE] * 4,
        out_specs=[VMEM] * 3 + [pl.BlockSpec(memory_space=pltpu.SMEM)],
        scratch_shapes=[
            pltpu.VMEM((1, RANK), jnp.int32),
            pltpu.VMEM((1, F), F32),
            pltpu.VMEM((8, RANK), jnp.int32),
            pltpu.VMEM((4, RANK), jnp.int32),
            pltpu.VMEM((8, 128), F32),
            pltpu.VMEM((LEAVES, F, PER), BF),
            pltpu.VMEM((LEAVES, 8, 128), F32),
            pltpu.VMEM((LEAVES, F, PER), BF),
            pltpu.VMEM((LEAVES, 8, 128), F32),
            pltpu.VMEM((2, LEAVES * SLOTS, 128), F32),
            pltpu.VMEM((LEAVES, 2 * SLOTS, 128), BF),
            pltpu.VMEM((LEAVES, 2 * SLOTS, 128), BF),
            pltpu.VMEM((LEAVES, RANK, PER), BF),
            pltpu.VMEM((LEAVES, 16, PER), BF),
            pltpu.VMEM((COLS, F, RANK), BF),
            pltpu.VMEM((F, RANK), BF),
            pltpu.VMEM((4, F, RANK), BF),
            pltpu.VMEM((2 * RANK, 256), BF),
            pltpu.VMEM((LEAVES // 2, RANK + 16, PER), BF),
            pltpu.VMEM((LEAVES // 2, RANK + 16, PER), BF),
            pltpu.VMEM((RANK, PER), BF),
            pltpu.VMEM((RANK, PER), BF),
            pltpu.VMEM((RANK + 16, RANK), F32),
            pltpu.VMEM((RANK, RANK), F32),
            pltpu.VMEM((RANK, RANK), BF),
            pltpu.VMEM((RANK, 2 * RANK), BF),
            pltpu.VMEM((RANK, 4 * RANK), BF),
            pltpu.VMEM((RANK, 128), F32),
            pltpu.VMEM((RANK, RANK), F32),
            pltpu.VMEM((COLS, SLAB, RANK), BF),
            pltpu.VMEM((COLS, SLAB, RANK), BF),
            pltpu.VMEM((COLS, SLAB, RANK), BF),
            pltpu.VMEM((COLS, SLAB, RANK), BF),
            pltpu.VMEM((COLS, SLAB, RANK), BF),
            pltpu.VMEM((COLS, SLAB, RANK), BF),
            pltpu.VMEM((8, 128), F32),
            pltpu.VMEM((COLS, 8, 128), F32),
            pltpu.VMEM((4, SLAB, RANK), BF),
            pltpu.VMEM((4, 8, 128), F32),
            *dma(LEAVES),
            *dma(LEAVES),
            *dma(COLS),
            *dma(4),
            *dma(COLS),
            *dma(COLS),
            *dma(COLS),
            *dma(COLS),
            *dma(4),
            *dma(4),
            pltpu.SemaphoreType.DMA((4,)),
        ],
        compiler_params=params(number, 40),
        name="exchange",
    )(merged, held, ridge, *in_hbm(*smalls))


def emit_kernel(*refs):
    ins, outs, sem = refs[:3], refs[3:6], refs[6]
    copies = [pltpu.make_async_copy(a, b, sem.at[k]) for k, (a, b) in enumerate(zip(ins, outs))]
    for copy in copies:
        copy.start()
    for copy in copies:
        copy.wait()


def emit(results):
    return pl.pallas_call(
        emit_kernel,
        out_shape=tuple(jax.ShapeDtypeStruct(shape, F32) for shape in SHAPES),
        in_specs=[VMEM] * 3,
        out_specs=[ANYWHERE] * 3,
        scratch_shapes=[pltpu.SemaphoreType.DMA((3,))],
        compiler_params=params(),
        name="emit",
    )(*results)


def local(features, targets, owner, length_scales, ridge, leaf_pivots, parent_pivots, top_pivots):
    samples = (features, targets.reshape(ROWS // 128, 128), owner.reshape(ROWS // 128, 128))
    smalls = (leaf_pivots, length_scales.reshape(1, F), parent_pivots, top_pivots)
    ybuf, table, held = prepare(*samples, leaf_pivots)
    *results, most = exchange(True, 1, merge(ybuf, table), held, ridge, *smalls)

    def again():
        none = jnp.zeros((LEAVES, 1, RANK), jnp.int32)
        return tuple(emit(exchange(False, 2, pack(*samples), none, ridge, *smalls)[:3]))

    return lax.cond(most[0] > SLOTS, again, lambda: tuple(emit(results)))


def solution(mesh):
    return jax.shard_map(
        local,
        mesh=mesh,
        in_specs=(
            P(None, ("leaf", "col")),
            P(("leaf", "col")),
            P(("leaf", "col")),
            P(),
            P(),
            P("leaf", None),
            P(),
            P(),
        ),
        out_specs=(P("leaf", "col", None), P("leaf", "col", None), P("leaf", None)),
        check_vma=False,
    )
```

```python
import functools
import math

import jax
import jax.numpy as jnp
from jax import lax
from jax.experimental import pallas as pl
from jax.experimental.pallas import tpu as pltpu
from jax.sharding import PartitionSpec as P

F = 48
RANK = 256
ROWS = 8192
LEAVES = 16
COLS = 8
OWNERS = 128
PACKET = 64
PER = ROWS // LEAVES
CHUNK = 256
CHUNKS = ROWS // CHUNK
WINDOW = 40
REGION = PER + WINDOW
WIDE = 64
SLAB = RANK // COLS
NODE = ROWS * COLS
LOG2E = math.log2(math.e)
BF = jnp.bfloat16
F32 = jnp.float32
NT = (((1,), (1,)), ((), ()))
MESH = pl.DeviceIdType.MESH


def dma(count):
    return [pltpu.SemaphoreType.DMA((count,))] * 2


def params(number=None, limit=24):
    if number is None:
        return pltpu.CompilerParams(vmem_limit_bytes=limit * 2**20)
    return pltpu.CompilerParams(
        collective_id=number, has_side_effects=True, vmem_limit_bytes=limit * 2**20
    )


ANYWHERE = pl.BlockSpec(memory_space=pl.ANY)
VMEM = pl.BlockSpec(memory_space=pltpu.VMEM)


def iota(shape, axis):
    return lax.broadcasted_iota(jnp.int32, shape, axis)


def dot(a, b):
    return jnp.dot(a, b, preferred_element_type=F32)


def dot_nt(a, b):
    return lax.dot_general(a, b, NT, preferred_element_type=F32)


def row_pair(two):
    return jnp.concatenate([two[0:1], two[1:2]], 1)


def pack_kernel(
    feat_hbm, target, owner, zbuf, feat, goals, rows, ybuf, table, scal, sem, feat_sem
):
    bring = pltpu.make_async_copy(feat_hbm, feat, feat_sem)
    bring.start()
    goals[...] = target[...].astype(F32)
    before = (iota((CHUNK, CHUNK), 0) < iota((CHUNK, CHUNK), 1)).astype(F32).astype(BF)
    weights = jnp.concatenate([before, jnp.ones((CHUNK, 128), BF)], 1)
    lane = iota((LEAVES, 128), 1)

    def ranks(t, carry):
        seen, seen_leaf, most = carry
        own = row_pair(owner[pl.ds(2 * t, 2), :])
        leaf = own // 8
        is_own = iota((OWNERS, CHUNK), 0) == own
        is_leaf = iota((LEAVES, CHUNK), 0) == leaf
        is_after = iota((LEAVES, CHUNK), 0) > leaf
        marks = jnp.concatenate(
            [m.astype(F32).astype(BF) for m in (is_own, is_leaf, is_after)], 0
        )
        sums = dot(marks, weights)
        counts = sums[:OWNERS, CHUNK:]
        leaf_counts = sums[OWNERS : OWNERS + LEAVES, CHUNK:]
        base = sums[OWNERS + LEAVES :, CHUNK:]
        prior = sums[:OWNERS, :CHUNK] + jnp.concatenate([seen, seen], 1)
        rank = jnp.sum(jnp.where(is_own, prior, 0.0), 0, keepdims=True)
        place = sums[OWNERS : OWNERS + LEAVES, :CHUNK] + jnp.concatenate([base, base], 1)
        place = jnp.sum(jnp.where(is_leaf, place, 0.0), 0, keepdims=True)
        tag = (own % 8).astype(F32) * PACKET + rank - (PER // 2)
        rows[t, 0:1, :] = place
        rows[t, 1:2, :] = row_pair(goals[pl.ds(2 * t, 2), :])
        rows[t, 2:3, :] = tag
        here = lane == t
        table[0:LEAVES, :] = jnp.where(here, seen_leaf.astype(jnp.int32), table[0:LEAVES, :])
        table[LEAVES : 2 * LEAVES, :] = jnp.where(
            here, base.astype(jnp.int32), table[LEAVES : 2 * LEAVES, :]
        )
        return seen + counts, seen_leaf + leaf_counts, jnp.maximum(most, leaf_counts)

    table[0:LEAVES, :] = jnp.full((LEAVES, 128), PER, jnp.int32)
    zero = jnp.zeros((LEAVES, 128), F32)
    _, _, most = lax.fori_loop(
        0, CHUNKS, ranks, (jnp.zeros((OWNERS, 128), F32), zero, zero), unroll=16
    )
    most = jnp.broadcast_to(jnp.max(most, 0, keepdims=True), (8, 128))
    table[2 * LEAVES :, :] = most.astype(jnp.int32)
    move = pltpu.make_async_copy(table, scal, sem)
    move.start()
    bring.wait()

    def sort(t, _):
        start = pl.multiple_of(t * CHUNK, CHUNK)
        row = iota((16, CHUNK), 0)
        place, goal, tag = rows[t, 0:1, :], rows[t, 1:2, :], rows[t, 2:3, :]
        extra = jnp.where(row == 0, goal, jnp.where(row == 1, tag, 0.0)).astype(BF)
        joined = jnp.concatenate([feat[:, pl.ds(start, CHUNK)], extra], 0)
        chosen = (iota((CHUNK, CHUNK), 0) == place.astype(jnp.int32)).astype(F32).astype(BF)
        ybuf[pl.ds(start, CHUNK), :] = dot_nt(chosen, joined)
        return 0

    lax.fori_loop(0, CHUNKS, sort, 0, unroll=8)
    move.wait()
    widest = scal[2 * LEAVES, 0]

    @pl.when(widest <= WINDOW)
    def quick():
        def merge(t, _):
            for i in range(LEAVES):
                source = t * CHUNK + scal[LEAVES + i, t]
                goal = i * REGION + scal[i, t]
                zbuf[pl.ds(goal, WINDOW), :] = ybuf[pl.ds(source, WINDOW), :]
            return 0

        lax.fori_loop(0, CHUNKS, merge, 0, unroll=4)

    @pl.when(widest > WINDOW)
    def slow():
        def merge(index, _):
            t = index // LEAVES
            i = index % LEAVES
            source = t * CHUNK + scal[LEAVES + i, t]
            first = scal[i, t]
            count = scal[i, t + 1] - first

            def part(k, _):
                rows = ybuf[pl.ds(source + 8 * k, 8), :]
                zbuf[pl.ds(i * REGION + first + 8 * k, 8), :] = rows
                return 0

            lax.fori_loop(0, (count + 7) // 8, part, 0)
            return 0

        lax.fori_loop(0, CHUNKS * LEAVES, merge, 0)


def in_hbm(*arrays):
    return [pltpu.with_memory_space_constraint(a, pltpu.HBM) for a in arrays]


def pack(features, targets, owner):
    return pl.pallas_call(
        pack_kernel,
        out_shape=pltpu.VMEM((LEAVES * REGION, WIDE), F32),
        in_specs=[ANYWHERE, VMEM, VMEM],
        out_specs=VMEM,
        scratch_shapes=[
            pltpu.VMEM((F, ROWS), BF),
            pltpu.VMEM((ROWS // 128, 128), F32),
            pltpu.VMEM((CHUNKS, 8, CHUNK), F32),
            pltpu.VMEM((ROWS + WINDOW, WIDE), F32),
            pltpu.VMEM((40, 128), jnp.int32),
            pltpu.SMEM((40, 128), jnp.int32),
            pltpu.SemaphoreType.DMA,
            pltpu.SemaphoreType.DMA,
        ],
        compiler_params=params(),
        name="pack",
    )(*in_hbm(features, targets, owner))


def split3(x):
    high = x.astype(BF)
    rest = x - high.astype(F32)
    mid = rest.astype(BF)
    return high, mid, (rest - mid.astype(F32)).astype(BF)


def stack16(parts, width):
    row = iota((16, width), 0)
    block = jnp.zeros((16, width), F32)
    for k, part in enumerate(parts):
        block = jnp.where(row == k, part if isinstance(part, float) else part.astype(F32), block)
    return block.astype(BF)


def half_norm(points, scale):
    return jnp.sum(points * points * (0.5 * scale), 0, keepdims=True)


def point_side(points, scale):
    high, mid, low = split3(-half_norm(points, scale))
    return stack16([high, mid, low, 1.0, 1.0, 1.0], points.shape[1])


def skel_side(skel, scale):
    width = skel.shape[1]
    high, mid, low = split3(skel * scale)
    extra = stack16([1.0, 1.0, 1.0, *split3(-half_norm(skel, scale))], width)
    parts = [p.astype(F32) for p in (high, mid, low, extra)]
    fill = jnp.zeros((256 - 3 * F - 16, width), F32)
    return jnp.concatenate([*parts, fill], 0).T.astype(BF)


def select_row(table, row):
    hit = iota(table.shape, 0) == row
    return jnp.sum(jnp.where(hit, table.astype(F32), 0.0), 0, keepdims=True)


def to_column(row):
    return jnp.broadcast_to(row, (128, row.shape[1])).T


def across(column, width):
    return jnp.concatenate([column] * (width // 128), 1)


def place_of(leaf, col):
    return dict(device_id=(leaf, col), device_id_type=MESH)


def mate(k):
    leaf, col = lax.axis_index("leaf"), lax.axis_index("col")
    to = (leaf + k) % LEAVES
    cross = (to // 8 + leaf // 8) % 2
    return place_of(to, col + cross * (1 - 2 * (col % 2)))


def beside(k):
    leaf, col = lax.axis_index("leaf"), lax.axis_index("col")
    return place_of(leaf, (col + k) % COLS)


def cousin(k):
    leaf, col = lax.axis_index("leaf"), lax.axis_index("col")
    return place_of(leaf - leaf % 4 + (leaf + k) % 4, col)


def each(count, step, unroll=1):
    lax.fori_loop(1, count, lambda k, _: (step(k), 0)[1], 0, unroll=unroll)


def turn_of(n):
    n = jnp.int32(n)
    odd = lax.rem(n, jnp.int32(2))
    half = lax.div(n + odd, jnp.int32(2))
    return lax.rem(odd * half + (1 - odd) * (LEAVES - half), jnp.int32(LEAVES))


def remote(src, dst, sems, k, peer):
    return pltpu.make_async_remote_copy(src, dst, sems[0].at[k], sems[1].at[k], **peer)


def top_index(parent, top, group):
    top_row = select_row(top[...], group)
    below = jnp.concatenate([select_row(parent[...], 2 * group + r) for r in range(2)], 1)
    number = iota((RANK, 2 * RANK), 1)
    below = below + jnp.where(iota((1, 2 * RANK), 1) >= RANK, 2.0 * RANK, 0.0)
    hit = across(to_column(top_row), 2 * RANK) == number.astype(F32)
    index = jnp.sum(jnp.where(hit, below, 0.0), 1, keepdims=True)
    return jnp.broadcast_to(index, (RANK, 128))


def exchange_kernel(
    merged, ridge, pivots_hbm, scales_hbm, parent_hbm, top_hbm, out_share, out_top, out_rhs,
    pivots, scales, parent, top, spare, feat, aux, rx, ra, hot, side, sk, mine, sk4, left,
    even, odd, other_even, other_odd, gram, couple, rows, columns, fours, index, tops,
    pg, gr, pc, cr, pt, qr, rs, rr, t4, r4,
    s_f, r_f, s_a, r_a, s_k, r_k, s_4, r_4, s_p, r_p, s_c, r_c, s_o, r_o, s_r, r_r, s_t, r_t, s_q, r_q, local,
):
    leaf = lax.axis_index("leaf")
    col = lax.axis_index("col")
    quarter = leaf % 4
    sibling = quarter + 1 - 2 * (quarter % 2)
    barrier = pltpu.get_barrier_semaphore()
    each(LEAVES, lambda k: pl.semaphore_signal(barrier, inc=1, **mate(k)))
    each(COLS, lambda k: pl.semaphore_signal(barrier, inc=1, **beside(k)))
    smalls = [
        pltpu.make_async_copy(a, b, local.at[k])
        for k, (a, b) in enumerate(
            [(pivots_hbm, pivots), (scales_hbm, scales), (parent_hbm, parent), (top_hbm, top)]
        )
    ]
    for copy in smalls:
        copy.start()

    eye = (iota((WIDE, WIDE), 0) == iota((WIDE, WIDE), 1)).astype(F32).astype(BF)

    def turn(k):
        start = pl.multiple_of((leaf + k) % LEAVES * REGION, 8)
        turned = dot_nt(eye, merged[pl.ds(start, PER), :].astype(BF))
        feat[k] = turned[:F].astype(BF)
        aux[k] = jnp.concatenate(
            [turned[F + r : F + r + 1, 128 * c : 128 * c + 128] for r in range(2) for c in range(4)], 0
        )

    def send_feat(k):
        return remote(feat.at[k], rx.at[k], (s_f, r_f), k, mate(k))

    def send_aux(k):
        return remote(aux.at[k], ra.at[k], (s_a, r_a), k, mate(k))

    def four(j, _):
        steps = [turn_of(lax.rem(4 * j + r, LEAVES)) for r in range(1, 5)]
        for k in steps:
            turn(k)
        pl.when(j == 0)(lambda: pl.semaphore_wait(barrier, LEAVES + COLS - 2))
        for send in (send_aux, send_feat):
            for k in steps[:3]:
                send(k).start()
            pl.when(j < 3)(lambda: send(steps[3]).start())
        return 0

    lax.fori_loop(0, LEAVES // 4, four, 0)
    rx[0] = feat[0]
    ra[0] = aux[0]

    for copy in smalls:
        copy.wait()
    spare[...] = jnp.ones((8, 128), F32)
    spare[0:1, 0:F] = scales[...]
    inverse = 1.0 / to_column(spare[0:1, :])[:F]
    scale = inverse * inverse * LOG2E
    scale2 = across(scale, RANK)
    scale4 = across(scale, PER)

    place = pivots[...]
    within = place % ROWS
    block = within // PACKET
    key = (block // COLS) * PER + (place // ROWS) * PACKET + within % PACKET
    holder = block % COLS
    crossed = (block // COLS) // 8 != leaf // 8
    holder = jnp.where(crossed, holder + 1 - 2 * (holder % 2), holder)
    key = jnp.where(holder == col, key, -PER)
    key = across(to_column(key.astype(F32)), PER)

    def mark(k):
        source = (leaf + LEAVES - k) % LEAVES
        tags = ra[k, 4:8, :]
        tag = jnp.concatenate([tags[r : r + 1] for r in range(4)], 1)
        wanted = tag + (PER // 2 + source * PER).astype(F32)
        hot[k] = (key == wanted).astype(F32).astype(BF)

    def mark_next(n, _):
        k = turn_of(n)
        pl.when(n > 0)(lambda: send_aux(k).wait_recv())
        mark(k)
        return 0

    lax.fori_loop(0, LEAVES, mark_next, 0)

    index[...] = top_index(parent, top, leaf // 4)
    index2 = across(index[...], 2 * RANK)
    number = iota((RANK, 2 * RANK), 1)
    base = (quarter * RANK).astype(F32)
    other = (sibling * RANK).astype(F32)
    chosen = index2[:, :RANK] == iota((RANK, RANK), 1).astype(F32) + base
    rows[...] = chosen.astype(F32).astype(BF)
    lanes = number.astype(F32) + jnp.where(number < RANK, base, other - RANK)
    columns[...] = (index2 == lanes).astype(F32).astype(BF)
    chosen = across(index[...], 4 * RANK) == iota((RANK, 4 * RANK), 1).astype(F32)
    fours[...] = chosen.astype(F32).astype(BF)

    def pick(j, total):
        steps = [turn_of(4 * j + r) for r in range(4)]
        pl.when(j > 0)(lambda: send_feat(steps[0]).wait_recv())
        for k in steps[1:]:
            send_feat(k).wait_recv()
        for k in steps:
            total = total + dot_nt(hot[k], rx[k])
        return total

    picked = lax.fori_loop(0, LEAVES // 4, pick, jnp.zeros((RANK, F), F32))
    picked = jnp.concatenate([picked, jnp.zeros((RANK, 128 - F), F32)], 1).T[:F]
    sk[0] = picked.astype(BF)

    def send_skel(k):
        return remote(sk.at[0], sk.at[k], (s_k, r_k), k, beside(k))

    each(COLS, lambda k: send_skel(k).start())

    def norms(k, _):
        side[k] = point_side(rx[k].astype(F32), scale4)
        return 0

    lax.fori_loop(0, LEAVES, norms, 0)

    def add_skel(k, total):
        send_skel(k).wait_recv()
        return total + sk[k].astype(F32)

    picked = lax.fori_loop(1, COLS, add_skel, picked)
    mine[...] = picked.astype(BF)
    sk4[quarter] = picked.astype(BF)

    def send_four(k):
        return remote(mine, sk4.at[quarter], (s_4, r_4), k, cousin(k))

    each(4, lambda k: send_four(k).start())
    left[0:RANK, :] = skel_side(picked, scale2)

    def block_of(k, out, begin):
        p = rx[k]
        fill = jnp.zeros((256 - 3 * F - 16, PER), BF)
        right = jnp.concatenate([p, p, p, side[k], fill], 0)
        power = dot(left[begin : begin + RANK, :], right)
        out[0:RANK, :] = jnp.exp2(jnp.minimum(power, 0.0)).astype(BF)

    def own_of(k, out):
        block_of(k, out, 0)
        value = jnp.concatenate([ra[k, r : r + 1, :] for r in range(4)], 1)
        out[RANK:, :] = jnp.broadcast_to(value, (16, PER)).astype(BF)

    def gram_of(u):
        gram[...] += dot_nt(u[...], u[0:RANK, :])

    def couple_of(v, u):
        couple[...] += dot_nt(v[...], u[0:RANK, :])

    last = LEAVES // 2 - 1

    def own_two(j, _):
        own_of(2 * j, even.at[j])
        gram_of(odd.at[(j + last) % (last + 1)])
        own_of(2 * j + 1, odd.at[j])
        gram_of(even.at[j])
        return 0

    def other_two(j, _):
        block_of(2 * j, other_even, RANK)
        couple_of(other_odd, odd.at[(j + last) % (last + 1)])
        block_of(2 * j + 1, other_odd, RANK)
        couple_of(other_even, even.at[j])
        return 0

    gram[...] = jnp.zeros_like(gram)
    couple[...] = jnp.zeros_like(couple)
    odd[last] = jnp.zeros((RANK + 16, PER), BF)
    other_odd[...] = jnp.zeros_like(other_odd)
    lax.fori_loop(0, last + 1, own_two, 0)
    gram_of(odd.at[last])

    def send_gram(k):
        return remote(pg.at[(col + k) % COLS], gr.at[k], (s_p, r_p), k, beside(k))

    def send_couple(k):
        return remote(pc.at[(col + k) % COLS], cr.at[k], (s_c, r_c), k, beside(k))

    def send_chosen(k):
        return remote(pt.at[(col + k) % COLS], qr.at[k], (s_o, r_o), k, beside(k))

    def send_rhs(k):
        return remote(rs, rr.at[k], (s_r, r_r), k, beside(k))

    part = gram[0:RANK, :].astype(BF)
    for k in range(COLS):
        pg[k] = part[k * SLAB : (k + 1) * SLAB]
    rhs = gram[RANK : RANK + 1, :]
    rhs = jnp.sum(dot_nt(stack16(split3(rhs), RANK), rows[...]), 0, keepdims=True)
    rs[...] = jnp.zeros_like(rs)
    rs[0:1, :] = rhs[:, :128]
    rs[1:2, :] = rhs[:, 128:]
    each(COLS, lambda k: send_gram(k).start())
    each(COLS, lambda k: send_rhs(k).start())
    tops[...] = dot_nt(dot(rows[...], part).astype(BF), columns[:, 0:RANK])

    each(4, lambda k: remote(mine, sk4.at[(quarter + 4 - k) % 4], (s_4, r_4), k, cousin(k)).wait_recv())
    left[RANK:, :] = skel_side(sk4[sibling].astype(F32), scale2)
    lax.fori_loop(0, last + 1, other_two, 0)
    couple_of(other_odd, odd.at[last])

    part = couple[...].astype(BF)
    chosen = dot_nt(dot_nt(rows[...], part).astype(BF), columns[:, RANK:]) + tops[...]
    chosen = chosen.astype(BF)
    for k in range(COLS):
        pt[k] = chosen[k * SLAB : (k + 1) * SLAB]
    each(COLS, lambda k: send_chosen(k).start())
    part = couple[...].T.astype(BF)
    for k in range(COLS):
        pc[k] = part[k * SLAB : (k + 1) * SLAB]
    each(COLS, lambda k: send_couple(k).start())

    whole = jnp.concatenate([sk4[k] for k in range(4)], 1)
    points = dot_nt(whole, fours[...])
    fill = jnp.zeros((256 - 3 * F - 16, RANK), BF)
    points_b = points.astype(BF)
    right = jnp.concatenate([points_b, points_b, points_b, point_side(points, scale2), fill], 0)
    value = jnp.exp2(jnp.minimum(dot(skel_side(points, scale2), right), 0.0))
    crossing = (across(index[...], RANK) >= 2.0 * RANK) != (index[...].T[0:1, :] >= 2.0 * RANK)
    square = iota((RANK, RANK), 0) == iota((RANK, RANK), 1)
    tops[...] = jnp.where(crossing, value, 0.0) + jnp.where(square, ridge[...], 0.0)

    def finish(sends):
        return lambda k: [send(k).wait_send() for send in sends]

    each(LEAVES, finish((send_aux, send_feat)))
    each(COLS, finish((send_skel, send_gram, send_rhs)))
    each(4, finish((send_four,)))

    def add_chosen(k, totals):
        send_chosen(k).wait_recv()
        send_rhs(k).wait_recv()
        return totals[0] + qr[k].astype(F32), totals[1] + rr[k]

    chosen, rhs = lax.fori_loop(1, COLS, add_chosen, (pt[col].astype(F32), rs[...]))
    chosen = chosen * (1.0 / NODE)
    t4[0] = chosen.astype(BF)
    r4[0] = rhs * (1.0 / NODE)

    def send_top(k):
        return remote(t4.at[0], t4.at[k], (s_t, r_t), k, cousin(k))

    def send_top_rhs(k):
        return remote(r4.at[0], r4.at[k], (s_q, r_q), k, cousin(k))

    each(4, lambda k: send_top(k).start())
    each(4, lambda k: send_top_rhs(k).start())

    def add_gram(k, total):
        send_gram(k).wait_recv()
        return total + gr[k].astype(F32)

    def add_couple(k, total):
        send_couple(k).wait_recv()
        return total + cr[k].astype(F32)

    total = lax.fori_loop(1, COLS, add_gram, pg[col].astype(F32))
    diagonal = iota((SLAB, RANK), 0) + col * SLAB == iota((SLAB, RANK), 1)
    out_share[0, :, 0:RANK] = total * (1.0 / NODE) + jnp.where(diagonal, ridge[...], 0.0)
    total = lax.fori_loop(1, COLS, add_couple, pc[col].astype(F32))
    out_share[0, :, RANK:] = total * (1.0 / NODE)
    result = chosen + tops[pl.ds(pl.multiple_of(col * SLAB, SLAB), SLAB), :]

    def add_top(k, totals):
        send_top(k).wait_recv()
        send_top_rhs(k).wait_recv()
        return totals[0] + t4[k].astype(F32), totals[1] + r4[k]

    result, rhs = lax.fori_loop(1, 4, add_top, (result, r4[0]))
    out_top[0] = result
    out_rhs[...] = jnp.concatenate([rhs[0:1], rhs[1:2]], 1)

    each(COLS, finish((send_couple, send_chosen)))
    each(4, finish((send_top, send_top_rhs)))


SHAPES = ((1, SLAB, 2 * RANK), (1, SLAB, RANK), (1, RANK))


def exchange(merged, ridge, *smalls):
    return pl.pallas_call(
        exchange_kernel,
        out_shape=tuple(pltpu.VMEM(shape, F32) for shape in SHAPES),
        in_specs=[VMEM, VMEM] + [ANYWHERE] * 4,
        out_specs=[VMEM] * 3,
        scratch_shapes=[
            pltpu.VMEM((1, RANK), jnp.int32),
            pltpu.VMEM((1, F), F32),
            pltpu.VMEM((8, RANK), jnp.int32),
            pltpu.VMEM((4, RANK), jnp.int32),
            pltpu.VMEM((8, 128), F32),
            pltpu.VMEM((LEAVES, F, PER), BF),
            pltpu.VMEM((LEAVES, 8, 128), F32),
            pltpu.VMEM((LEAVES, F, PER), BF),
            pltpu.VMEM((LEAVES, 8, 128), F32),
            pltpu.VMEM((LEAVES, RANK, PER), BF),
            pltpu.VMEM((LEAVES, 16, PER), BF),
            pltpu.VMEM((COLS, F, RANK), BF),
            pltpu.VMEM((F, RANK), BF),
            pltpu.VMEM((4, F, RANK), BF),
            pltpu.VMEM((2 * RANK, 256), BF),
            pltpu.VMEM((LEAVES // 2, RANK + 16, PER), BF),
            pltpu.VMEM((LEAVES // 2, RANK + 16, PER), BF),
            pltpu.VMEM((RANK, PER), BF),
            pltpu.VMEM((RANK, PER), BF),
            pltpu.VMEM((RANK + 16, RANK), F32),
            pltpu.VMEM((RANK, RANK), F32),
            pltpu.VMEM((RANK, RANK), BF),
            pltpu.VMEM((RANK, 2 * RANK), BF),
            pltpu.VMEM((RANK, 4 * RANK), BF),
            pltpu.VMEM((RANK, 128), F32),
            pltpu.VMEM((RANK, RANK), F32),
            pltpu.VMEM((COLS, SLAB, RANK), BF),
            pltpu.VMEM((COLS, SLAB, RANK), BF),
            pltpu.VMEM((COLS, SLAB, RANK), BF),
            pltpu.VMEM((COLS, SLAB, RANK), BF),
            pltpu.VMEM((COLS, SLAB, RANK), BF),
            pltpu.VMEM((COLS, SLAB, RANK), BF),
            pltpu.VMEM((8, 128), F32),
            pltpu.VMEM((COLS, 8, 128), F32),
            pltpu.VMEM((4, SLAB, RANK), BF),
            pltpu.VMEM((4, 8, 128), F32),
            *dma(LEAVES),
            *dma(LEAVES),
            *dma(COLS),
            *dma(4),
            *dma(COLS),
            *dma(COLS),
            *dma(COLS),
            *dma(COLS),
            *dma(4),
            *dma(4),
            pltpu.SemaphoreType.DMA((4,)),
        ],
        compiler_params=params(0, 40),
        name="exchange",
    )(merged, ridge, *in_hbm(*smalls))


def emit_kernel(*refs):
    ins, outs, sem = refs[:3], refs[3:6], refs[6]
    copies = [pltpu.make_async_copy(a, b, sem.at[k]) for k, (a, b) in enumerate(zip(ins, outs))]
    for copy in copies:
        copy.start()
    for copy in copies:
        copy.wait()


def emit(results):
    return pl.pallas_call(
        emit_kernel,
        out_shape=tuple(jax.ShapeDtypeStruct(shape, F32) for shape in SHAPES),
        in_specs=[VMEM] * 3,
        out_specs=[ANYWHERE] * 3,
        scratch_shapes=[pltpu.SemaphoreType.DMA((3,))],
        compiler_params=params(),
        name="emit",
    )(*results)


def local(features, targets, owner, length_scales, ridge, leaf_pivots, parent_pivots, top_pivots):
    merged = pack(features, targets.reshape(ROWS // 128, 128), owner.reshape(ROWS // 128, 128))
    smalls = (leaf_pivots, length_scales.reshape(1, F), parent_pivots, top_pivots)
    return tuple(emit(exchange(merged, ridge.reshape(1, 1), *smalls)))


def solution(mesh):
    return jax.shard_map(
        local,
        mesh=mesh,
        in_specs=(
            P(None, ("leaf", "col")),
            P(("leaf", "col")),
            P(("leaf", "col")),
            P(),
            P(),
            P("leaf", None),
            P(),
            P(),
        ),
        out_specs=(P("leaf", "col", None), P("leaf", "col", None), P("leaf", None)),
        check_vma=False,
    )
```

```python
import functools
import math

import jax
import jax.numpy as jnp
from jax import lax
from jax.experimental import pallas as pl
from jax.experimental.pallas import tpu as pltpu
from jax.sharding import PartitionSpec as P

F = 48
RANK = 256
ROWS = 8192
LEAVES = 16
COLS = 8
OWNERS = 128
PACKET = 64
PER = ROWS // LEAVES
CHUNK = 256
CHUNKS = ROWS // CHUNK
WINDOW = 40
REGION = PER + WINDOW
BIN = 40
BINS = BIN * CHUNKS
SLOTS = 16
WHICH = 50
FULL = 51
WIDE = 64
SLAB = RANK // COLS
NODE = ROWS * COLS
LOG2E = math.log2(math.e)
BF = jnp.bfloat16
F32 = jnp.float32
NT = (((1,), (1,)), ((), ()))
MESH = pl.DeviceIdType.MESH


def dma(count):
    return [pltpu.SemaphoreType.DMA((count,))] * 2


def params(number=None, limit=24):
    if number is None:
        return pltpu.CompilerParams(vmem_limit_bytes=limit * 2**20)
    return pltpu.CompilerParams(
        collective_id=number, has_side_effects=True, vmem_limit_bytes=limit * 2**20
    )


ANYWHERE = pl.BlockSpec(memory_space=pl.ANY)
VMEM = pl.BlockSpec(memory_space=pltpu.VMEM)


def iota(shape, axis):
    return lax.broadcasted_iota(jnp.int32, shape, axis)


def dot(a, b):
    return jnp.dot(a, b, preferred_element_type=F32)


def dot_nt(a, b):
    return lax.dot_general(a, b, NT, preferred_element_type=F32)


def row_pair(two):
    return jnp.concatenate([two[0:1], two[1:2]], 1)


def pack_kernel(
    feat_hbm, target, owner, zbuf, feat, goals, rows, ybuf, table, scal, sem, feat_sem
):
    bring = pltpu.make_async_copy(feat_hbm, feat, feat_sem)
    bring.start()
    goals[...] = target[...].astype(F32)
    before = (iota((CHUNK, CHUNK), 0) < iota((CHUNK, CHUNK), 1)).astype(F32).astype(BF)
    weights = jnp.concatenate([before, jnp.ones((CHUNK, 128), BF)], 1)
    lane = iota((LEAVES, 128), 1)

    def ranks(t, carry):
        seen, seen_leaf, most = carry
        own = row_pair(owner[pl.ds(2 * t, 2), :])
        leaf = own // 8
        is_own = iota((OWNERS, CHUNK), 0) == own
        is_leaf = iota((LEAVES, CHUNK), 0) == leaf
        is_after = iota((LEAVES, CHUNK), 0) > leaf
        marks = jnp.concatenate(
            [m.astype(F32).astype(BF) for m in (is_own, is_leaf, is_after)], 0
        )
        sums = dot(marks, weights)
        counts = sums[:OWNERS, CHUNK:]
        leaf_counts = sums[OWNERS : OWNERS + LEAVES, CHUNK:]
        base = sums[OWNERS + LEAVES :, CHUNK:]
        prior = sums[:OWNERS, :CHUNK] + jnp.concatenate([seen, seen], 1)
        rank = jnp.sum(jnp.where(is_own, prior, 0.0), 0, keepdims=True)
        place = sums[OWNERS : OWNERS + LEAVES, :CHUNK] + jnp.concatenate([base, base], 1)
        place = jnp.sum(jnp.where(is_leaf, place, 0.0), 0, keepdims=True)
        tag = (own % 8).astype(F32) * PACKET + rank - (PER // 2)
        rows[t, 0:1, :] = place
        rows[t, 1:2, :] = row_pair(goals[pl.ds(2 * t, 2), :])
        rows[t, 2:3, :] = tag
        here = lane == t
        table[0:LEAVES, :] = jnp.where(here, seen_leaf.astype(jnp.int32), table[0:LEAVES, :])
        table[LEAVES : 2 * LEAVES, :] = jnp.where(
            here, base.astype(jnp.int32), table[LEAVES : 2 * LEAVES, :]
        )
        return seen + counts, seen_leaf + leaf_counts, jnp.maximum(most, leaf_counts)

    table[0:LEAVES, :] = jnp.full((LEAVES, 128), PER, jnp.int32)
    zero = jnp.zeros((LEAVES, 128), F32)
    _, _, most = lax.fori_loop(
        0, CHUNKS, ranks, (jnp.zeros((OWNERS, 128), F32), zero, zero), unroll=16
    )
    most = jnp.broadcast_to(jnp.max(most, 0, keepdims=True), (8, 128))
    table[2 * LEAVES :, :] = most.astype(jnp.int32)
    move = pltpu.make_async_copy(table, scal, sem)
    move.start()
    bring.wait()

    def sort(t, _):
        start = pl.multiple_of(t * CHUNK, CHUNK)
        row = iota((16, CHUNK), 0)
        place, goal, tag = rows[t, 0:1, :], rows[t, 1:2, :], rows[t, 2:3, :]
        extra = jnp.where(row == 0, goal, jnp.where(row == 1, tag, 0.0)).astype(BF)
        joined = jnp.concatenate([feat[:, pl.ds(start, CHUNK)], extra], 0)
        chosen = (iota((CHUNK, CHUNK), 0) == place.astype(jnp.int32)).astype(F32).astype(BF)
        ybuf[pl.ds(start, CHUNK), :] = dot_nt(chosen, joined)
        return 0

    lax.fori_loop(0, CHUNKS, sort, 0, unroll=8)
    move.wait()
    widest = scal[2 * LEAVES, 0]

    @pl.when(widest <= WINDOW)
    def quick():
        def merge(t, _):
            for i in range(LEAVES):
                source = t * CHUNK + scal[LEAVES + i, t]
                goal = i * REGION + scal[i, t]
                zbuf[pl.ds(goal, WINDOW), :] = ybuf[pl.ds(source, WINDOW), :]
            return 0

        lax.fori_loop(0, CHUNKS, merge, 0, unroll=4)

    @pl.when(widest > WINDOW)
    def slow():
        def merge(index, _):
            t = index // LEAVES
            i = index % LEAVES
            source = t * CHUNK + scal[LEAVES + i, t]
            first = scal[i, t]
            count = scal[i, t + 1] - first

            def part(k, _):
                rows = ybuf[pl.ds(source + 8 * k, 8), :]
                zbuf[pl.ds(i * REGION + first + 8 * k, 8), :] = rows
                return 0

            lax.fori_loop(0, (count + 7) // 8, part, 0)
            return 0

        lax.fori_loop(0, CHUNKS * LEAVES, merge, 0)


def in_hbm(*arrays):
    return [pltpu.with_memory_space_constraint(a, pltpu.HBM) for a in arrays]


def pack(features, targets, owner):
    return pl.pallas_call(
        pack_kernel,
        out_shape=pltpu.VMEM((LEAVES * REGION, WIDE), F32),
        in_specs=[ANYWHERE, VMEM, VMEM],
        out_specs=VMEM,
        scratch_shapes=[
            pltpu.VMEM((F, ROWS), BF),
            pltpu.VMEM((ROWS // 128, 128), F32),
            pltpu.VMEM((CHUNKS, 8, CHUNK), F32),
            pltpu.VMEM((ROWS + WINDOW, WIDE), F32),
            pltpu.VMEM((40, 128), jnp.int32),
            pltpu.SMEM((40, 128), jnp.int32),
            pltpu.SemaphoreType.DMA,
            pltpu.SemaphoreType.DMA,
        ],
        compiler_params=params(),
        name="pack",
    )(*in_hbm(features, targets, owner))


def split3(x):
    high = x.astype(BF)
    rest = x - high.astype(F32)
    mid = rest.astype(BF)
    return high, mid, (rest - mid.astype(F32)).astype(BF)


def stack16(parts, width):
    row = iota((16, width), 0)
    block = jnp.zeros((16, width), F32)
    for k, part in enumerate(parts):
        block = jnp.where(row == k, part if isinstance(part, float) else part.astype(F32), block)
    return block.astype(BF)


def half_norm(points, scale):
    return jnp.sum(points * points * (0.5 * scale), 0, keepdims=True)


def point_side(points, scale):
    high, mid, low = split3(-half_norm(points, scale))
    return stack16([high, mid, low, 1.0, 1.0, 1.0], points.shape[1])


def skel_side(skel, scale):
    width = skel.shape[1]
    high, mid, low = split3(skel * scale)
    extra = stack16([1.0, 1.0, 1.0, *split3(-half_norm(skel, scale))], width)
    parts = [p.astype(F32) for p in (high, mid, low, extra)]
    fill = jnp.zeros((256 - 3 * F - 16, width), F32)
    return jnp.concatenate([*parts, fill], 0).T.astype(BF)


def select_row(table, row):
    hit = iota(table.shape, 0) == row
    return jnp.sum(jnp.where(hit, table.astype(F32), 0.0), 0, keepdims=True)


def to_column(row):
    return jnp.broadcast_to(row, (128, row.shape[1])).T


def across(column, width):
    return jnp.concatenate([column] * (width // 128), 1)


def place_of(leaf, col):
    return dict(device_id=(leaf, col), device_id_type=MESH)


def mate(k):
    leaf, col = lax.axis_index("leaf"), lax.axis_index("col")
    to = (leaf + k) % LEAVES
    cross = (to // 8 + leaf // 8) % 2
    return place_of(to, col + cross * (1 - 2 * (col % 2)))


def beside(k):
    leaf, col = lax.axis_index("leaf"), lax.axis_index("col")
    return place_of(leaf, (col + k) % COLS)


def cousin(k):
    leaf, col = lax.axis_index("leaf"), lax.axis_index("col")
    return place_of(leaf - leaf % 4 + (leaf + k) % 4, col)


def each(count, step, unroll=1):
    lax.fori_loop(1, count, lambda k, _: (step(k), 0)[1], 0, unroll=unroll)


def rem(a, b):
    return lax.rem(jnp.int32(a), jnp.int32(b))


def turn_of(n):
    n = jnp.int32(n)
    odd = lax.rem(n, jnp.int32(2))
    half = lax.div(n + odd, jnp.int32(2))
    return lax.rem(odd * half + (1 - odd) * (LEAVES - half), jnp.int32(LEAVES))


def remote(src, dst, sems, k, peer):
    return pltpu.make_async_remote_copy(src, dst, sems[0].at[k], sems[1].at[k], **peer)


def top_index(parent, top, group):
    top_row = select_row(top[...], group)
    below = jnp.concatenate([select_row(parent[...], 2 * group + r) for r in range(2)], 1)
    number = iota((RANK, 2 * RANK), 1)
    below = below + jnp.where(iota((1, 2 * RANK), 1) >= RANK, 2.0 * RANK, 0.0)
    hit = across(to_column(top_row), 2 * RANK) == number.astype(F32)
    index = jnp.sum(jnp.where(hit, below, 0.0), 1, keepdims=True)
    return jnp.broadcast_to(index, (RANK, 128))


def exchange_kernel(
    merged, ridge, pivots_hbm, scales_hbm, parent_hbm, top_hbm, out_share, out_top, out_rhs,
    pivots, scales, parent, top, spare, feat, aux, rx, ra, hot, side, sk, mine, sk4, left,
    even, odd, other_even, other_odd, gram, couple, rows, columns, fours, index, tops,
    pg, gr, pc, cr, pt, qr, rs, rr, t4, r4,
    s_f, r_f, s_a, r_a, s_k, r_k, s_4, r_4, s_p, r_p, s_c, r_c, s_o, r_o, s_r, r_r, s_t, r_t, s_q, r_q, local,
):
    leaf = lax.axis_index("leaf")
    col = lax.axis_index("col")
    quarter = leaf % 4
    sibling = quarter + 1 - 2 * (quarter % 2)
    barrier = pltpu.get_barrier_semaphore()
    each(LEAVES, lambda k: pl.semaphore_signal(barrier, inc=1, **mate(k)))
    each(COLS, lambda k: pl.semaphore_signal(barrier, inc=1, **beside(k)))
    smalls = [
        pltpu.make_async_copy(a, b, local.at[k])
        for k, (a, b) in enumerate(
            [(pivots_hbm, pivots), (scales_hbm, scales), (parent_hbm, parent), (top_hbm, top)]
        )
    ]
    for copy in smalls:
        copy.start()

    eye = (iota((WIDE, WIDE), 0) == iota((WIDE, WIDE), 1)).astype(F32).astype(BF)

    def turn(k):
        start = pl.multiple_of((leaf + k) % LEAVES * REGION, 8)
        turned = dot_nt(eye, merged[pl.ds(start, PER), :].astype(BF))
        feat[k] = turned[:F].astype(BF)
        aux[k] = jnp.concatenate(
            [turned[F + r : F + r + 1, 128 * c : 128 * c + 128] for r in range(2) for c in range(4)], 0
        )

    def send_feat(k):
        return remote(feat.at[k], rx.at[k], (s_f, r_f), k, mate(k))

    def send_aux(k):
        return remote(aux.at[k], ra.at[k], (s_a, r_a), k, mate(k))

    def four(j, _):
        steps = [turn_of(lax.rem(4 * j + r, LEAVES)) for r in range(1, 5)]
        for k in steps:
            turn(k)
        pl.when(j == 0)(lambda: pl.semaphore_wait(barrier, LEAVES + COLS - 2))
        for send in (send_aux, send_feat):
            for k in steps[:3]:
                send(k).start()
            pl.when(j < 3)(lambda: send(steps[3]).start())
        return 0

    lax.fori_loop(0, LEAVES // 4, four, 0)
    rx[0] = feat[0]
    ra[0] = aux[0]

    for copy in smalls:
        copy.wait()
    spare[...] = jnp.ones((8, 128), F32)
    spare[0:1, 0:F] = scales[...]
    inverse = 1.0 / to_column(spare[0:1, :])[:F]
    scale = inverse * inverse * LOG2E
    scale2 = across(scale, RANK)
    scale4 = across(scale, PER)

    place = pivots[...]
    within = place % ROWS
    block = within // PACKET
    key = (block // COLS) * PER + (place // ROWS) * PACKET + within % PACKET
    holder = block % COLS
    crossed = (block // COLS) // 8 != leaf // 8
    holder = jnp.where(crossed, holder + 1 - 2 * (holder % 2), holder)
    key = jnp.where(holder == col, key, -PER)
    key = across(to_column(key.astype(F32)), PER)

    def mark(k):
        source = (leaf + LEAVES - k) % LEAVES
        tags = ra[k, 4:8, :]
        tag = jnp.concatenate([tags[r : r + 1] for r in range(4)], 1)
        wanted = tag + (PER // 2 + source * PER).astype(F32)
        hot[k] = (key == wanted).astype(F32).astype(BF)

    def mark_next(n, _):
        k = turn_of(n)
        pl.when(n > 0)(lambda: send_aux(k).wait_recv())
        mark(k)
        return 0

    lax.fori_loop(0, LEAVES, mark_next, 0)

    index[...] = top_index(parent, top, leaf // 4)
    index2 = across(index[...], 2 * RANK)
    number = iota((RANK, 2 * RANK), 1)
    base = (quarter * RANK).astype(F32)
    other = (sibling * RANK).astype(F32)
    chosen = index2[:, :RANK] == iota((RANK, RANK), 1).astype(F32) + base
    rows[...] = chosen.astype(F32).astype(BF)
    lanes = number.astype(F32) + jnp.where(number < RANK, base, other - RANK)
    columns[...] = (index2 == lanes).astype(F32).astype(BF)
    chosen = across(index[...], 4 * RANK) == iota((RANK, 4 * RANK), 1).astype(F32)
    fours[...] = chosen.astype(F32).astype(BF)

    def pick(j, total):
        steps = [turn_of(4 * j + r) for r in range(4)]
        pl.when(j > 0)(lambda: send_feat(steps[0]).wait_recv())
        for k in steps[1:]:
            send_feat(k).wait_recv()
        for k in steps:
            total = total + dot_nt(hot[k], rx[k])
        return total

    picked = lax.fori_loop(0, LEAVES // 4, pick, jnp.zeros((RANK, F), F32))
    picked = jnp.concatenate([picked, jnp.zeros((RANK, 128 - F), F32)], 1).T[:F]
    sk[0] = picked.astype(BF)

    def send_skel(k):
        return remote(sk.at[0], sk.at[k], (s_k, r_k), k, beside(k))

    each(COLS, lambda k: send_skel(k).start())

    def norms(k, _):
        side[k] = point_side(rx[k].astype(F32), scale4)
        return 0

    lax.fori_loop(0, LEAVES, norms, 0)

    def add_skel(k, total):
        send_skel(k).wait_recv()
        return total + sk[k].astype(F32)

    picked = lax.fori_loop(1, COLS, add_skel, picked)
    mine[...] = picked.astype(BF)
    sk4[quarter] = picked.astype(BF)

    def send_four(k):
        return remote(mine, sk4.at[quarter], (s_4, r_4), k, cousin(k))

    each(4, lambda k: send_four(k).start())
    left[0:RANK, :] = skel_side(picked, scale2)

    def block_of(k, out, begin):
        p = rx[k]
        fill = jnp.zeros((256 - 3 * F - 16, PER), BF)
        right = jnp.concatenate([p, p, p, side[k], fill], 0)
        power = dot(left[begin : begin + RANK, :], right)
        out[0:RANK, :] = jnp.exp2(jnp.minimum(power, 0.0)).astype(BF)

    def own_of(k, out):
        block_of(k, out, 0)
        value = jnp.concatenate([ra[k, r : r + 1, :] for r in range(4)], 1)
        out[RANK:, :] = jnp.broadcast_to(value, (16, PER)).astype(BF)

    def gram_of(u):
        gram[...] += dot_nt(u[...], u[0:RANK, :])

    def couple_of(v, u):
        couple[...] += dot_nt(v[...], u[0:RANK, :])

    last = LEAVES // 2 - 1

    def own_two(j, _):
        own_of(2 * j, even.at[j])
        gram_of(odd.at[(j + last) % (last + 1)])
        own_of(2 * j + 1, odd.at[j])
        gram_of(even.at[j])
        return 0

    def other_two(j, _):
        block_of(2 * j, other_even, RANK)
        couple_of(other_odd, odd.at[(j + last) % (last + 1)])
        block_of(2 * j + 1, other_odd, RANK)
        couple_of(other_even, even.at[j])
        return 0

    gram[...] = jnp.zeros_like(gram)
    couple[...] = jnp.zeros_like(couple)
    odd[last] = jnp.zeros((RANK + 16, PER), BF)
    other_odd[...] = jnp.zeros_like(other_odd)
    lax.fori_loop(0, last + 1, own_two, 0)
    gram_of(odd.at[last])

    def send_gram(k):
        return remote(pg.at[(col + k) % COLS], gr.at[k], (s_p, r_p), k, beside(k))

    def send_couple(k):
        return remote(pc.at[(col + k) % COLS], cr.at[k], (s_c, r_c), k, beside(k))

    def send_chosen(k):
        return remote(pt.at[(col + k) % COLS], qr.at[k], (s_o, r_o), k, beside(k))

    def send_rhs(k):
        return remote(rs, rr.at[k], (s_r, r_r), k, beside(k))

    part = gram[0:RANK, :].astype(BF)
    for k in range(COLS):
        pg[k] = part[k * SLAB : (k + 1) * SLAB]
    rhs = gram[RANK : RANK + 1, :]
    rhs = jnp.sum(dot_nt(stack16(split3(rhs), RANK), rows[...]), 0, keepdims=True)
    rs[...] = jnp.zeros_like(rs)
    rs[0:1, :] = rhs[:, :128]
    rs[1:2, :] = rhs[:, 128:]
    each(COLS, lambda k: send_gram(k).start())
    each(COLS, lambda k: send_rhs(k).start())
    tops[...] = dot_nt(dot(rows[...], part).astype(BF), columns[:, 0:RANK])

    each(4, lambda k: remote(mine, sk4.at[(quarter + 4 - k) % 4], (s_4, r_4), k, cousin(k)).wait_recv())
    left[RANK:, :] = skel_side(sk4[sibling].astype(F32), scale2)
    lax.fori_loop(0, last + 1, other_two, 0)
    couple_of(other_odd, odd.at[last])

    part = couple[...].astype(BF)
    chosen = dot_nt(dot_nt(rows[...], part).astype(BF), columns[:, RANK:]) + tops[...]
    chosen = chosen.astype(BF)
    for k in range(COLS):
        pt[k] = chosen[k * SLAB : (k + 1) * SLAB]
    each(COLS, lambda k: send_chosen(k).start())
    part = couple[...].T.astype(BF)
    for k in range(COLS):
        pc[k] = part[k * SLAB : (k + 1) * SLAB]
    each(COLS, lambda k: send_couple(k).start())

    whole = jnp.concatenate([sk4[k] for k in range(4)], 1)
    points = dot_nt(whole, fours[...])
    fill = jnp.zeros((256 - 3 * F - 16, RANK), BF)
    points_b = points.astype(BF)
    right = jnp.concatenate([points_b, points_b, points_b, point_side(points, scale2), fill], 0)
    value = jnp.exp2(jnp.minimum(dot(skel_side(points, scale2), right), 0.0))
    crossing = (across(index[...], RANK) >= 2.0 * RANK) != (index[...].T[0:1, :] >= 2.0 * RANK)
    square = iota((RANK, RANK), 0) == iota((RANK, RANK), 1)
    tops[...] = jnp.where(crossing, value, 0.0) + jnp.where(square, ridge[...], 0.0)

    def finish(sends):
        return lambda k: [send(k).wait_send() for send in sends]

    each(LEAVES, finish((send_aux, send_feat)))
    each(COLS, finish((send_skel, send_gram, send_rhs)))
    each(4, finish((send_four,)))

    def add_chosen(k, totals):
        send_chosen(k).wait_recv()
        send_rhs(k).wait_recv()
        return totals[0] + qr[k].astype(F32), totals[1] + rr[k]

    chosen, rhs = lax.fori_loop(1, COLS, add_chosen, (pt[col].astype(F32), rs[...]))
    chosen = chosen * (1.0 / NODE)
    t4[0] = chosen.astype(BF)
    r4[0] = rhs * (1.0 / NODE)

    def send_top(k):
        return remote(t4.at[0], t4.at[k], (s_t, r_t), k, cousin(k))

    def send_top_rhs(k):
        return remote(r4.at[0], r4.at[k], (s_q, r_q), k, cousin(k))

    each(4, lambda k: send_top(k).start())
    each(4, lambda k: send_top_rhs(k).start())

    def add_gram(k, total):
        send_gram(k).wait_recv()
        return total + gr[k].astype(F32)

    def add_couple(k, total):
        send_couple(k).wait_recv()
        return total + cr[k].astype(F32)

    total = lax.fori_loop(1, COLS, add_gram, pg[col].astype(F32))
    diagonal = iota((SLAB, RANK), 0) + col * SLAB == iota((SLAB, RANK), 1)
    out_share[0, :, 0:RANK] = total * (1.0 / NODE) + jnp.where(diagonal, ridge[...], 0.0)
    total = lax.fori_loop(1, COLS, add_couple, pc[col].astype(F32))
    out_share[0, :, RANK:] = total * (1.0 / NODE)
    result = chosen + tops[pl.ds(pl.multiple_of(col * SLAB, SLAB), SLAB), :]

    def add_top(k, totals):
        send_top(k).wait_recv()
        send_top_rhs(k).wait_recv()
        return totals[0] + t4[k].astype(F32), totals[1] + r4[k]

    result, rhs = lax.fori_loop(1, 4, add_top, (result, r4[0]))
    out_top[0] = result
    out_rhs[...] = jnp.concatenate([rhs[0:1], rhs[1:2]], 1)

    each(COLS, finish((send_couple, send_chosen)))
    each(4, finish((send_top, send_top_rhs)))


def stream_kernel(
    feat_hbm, target, owner, pivots, ridge, scales_hbm, parent_hbm, top_hbm,
    out_share, out_top, out_rhs, flag,
    feat_in, goals, ranked, starts, counts, places, bins, held, slots, came, scales, parent, top, spare,
    feat, aux, rx, ra, side, sk, mine, sk4, left, even, odd, other_even, other_odd, gram, couple,
    rows, columns, fours, index, tops, pg, gr, pc, cr, pt, qr, rs, rr, t4, r4,
    s_v, r_v, s_s, r_s, s_f, r_f, s_a, r_a, s_k, r_k, s_4, r_4, s_p, r_p, s_c, r_c, s_o, r_o,
    s_r, r_r, s_t, r_t, s_q, r_q, local,
):
    leaf = lax.axis_index("leaf")
    col = lax.axis_index("col")
    quarter = leaf % 4
    sibling = quarter + 1 - 2 * (quarter % 2)
    barrier = pltpu.get_barrier_semaphore()
    each(LEAVES, lambda k: pl.semaphore_signal(barrier, inc=1, **mate(k)))
    each(COLS, lambda k: pl.semaphore_signal(barrier, inc=1, **beside(k)))
    bring = pltpu.make_async_copy(feat_hbm, feat_in, local.at[3])
    bring.start()
    smalls = [
        pltpu.make_async_copy(a, b, local.at[k])
        for k, (a, b) in enumerate([(scales_hbm, scales), (parent_hbm, parent), (top_hbm, top)])
    ]
    for copy in smalls:
        copy.start()

    def send_pivots(k):
        return remote(pivots, held.at[k], (s_v, r_v), k, mate(k))

    def send_slots(k):
        return remote(slots.at[k], came.at[k], (s_s, r_s), k, mate(k))

    def send_feat(k):
        return remote(feat.at[k], rx.at[k], (s_f, r_f), k, mate(k))

    def send_aux(k):
        return remote(aux.at[k], ra.at[k], (s_a, r_a), k, mate(k))

    def send_skel(k):
        return remote(sk.at[0], sk.at[k], (s_k, r_k), k, beside(k))

    goals[...] = target[...].astype(F32)
    before = (iota((CHUNK, CHUNK), 0) < iota((CHUNK, CHUNK), 1)).astype(F32).astype(BF)
    weights = jnp.concatenate([before, jnp.ones((CHUNK, 128), BF)], 1)
    lane = iota((LEAVES, 128), 1)

    def rank(t, carry):
        seen, seen_leaf, most = carry
        own = row_pair(owner[pl.ds(2 * t, 2), :])
        group = own // 8
        is_own = iota((OWNERS, CHUNK), 0) == own
        is_leaf = iota((LEAVES, CHUNK), 0) == group
        marks = jnp.concatenate([m.astype(F32).astype(BF) for m in (is_own, is_leaf)], 0)
        sums = dot(marks, weights)
        leaf_counts = sums[OWNERS:, CHUNK:]
        prior = sums[:OWNERS, :CHUNK] + jnp.concatenate([seen, seen], 1)
        place = jnp.sum(jnp.where(is_own, prior, 0.0), 0, keepdims=True)
        ranked[t, 0:1, :] = (group * BIN).astype(F32) + jnp.sum(
            jnp.where(is_leaf, sums[OWNERS:, :CHUNK], 0.0), 0, keepdims=True
        )
        ranked[t, 1:2, :] = row_pair(goals[pl.ds(2 * t, 2), :])
        ranked[t, 2:3, :] = own.astype(F32) * PACKET + place
        starts[...] = jnp.where(lane == t, seen_leaf, starts[...])
        counts[...] = jnp.where(lane == t, leaf_counts, counts[...])
        return seen + sums[:OWNERS, CHUNK:], seen_leaf + leaf_counts, jnp.maximum(most, leaf_counts)

    starts[...] = jnp.zeros_like(starts)
    counts[...] = jnp.zeros_like(counts)
    zero = jnp.zeros((LEAVES, 128), F32)
    _, _, most = lax.fori_loop(
        0, CHUNKS, rank, (jnp.zeros((OWNERS, 128), F32), zero, zero), unroll=16
    )
    full = jnp.maximum(jnp.max(most, 0, keepdims=True) - BIN, 0.0)

    held[0] = pivots[...]
    pl.semaphore_wait(barrier, LEAVES + COLS - 2)
    each(LEAVES, lambda k: send_pivots(k).start())

    def joined_of(t):
        row = iota((16, CHUNK), 0)
        extra = jnp.where(row == 0, ranked[t, 1:2, :], 0.0).astype(BF)
        return jnp.concatenate([feat_in[:, pl.ds(pl.multiple_of(t * CHUNK, CHUNK), CHUNK)], extra], 0)

    def fill_bins(t, _):
        place = ranked[t, 0:1, :].astype(jnp.int32)
        chosen = (iota((LEAVES * BIN, CHUNK), 0) == place).astype(F32).astype(BF)
        binned = dot_nt(chosen, joined_of(t))
        for i in range(LEAVES):
            bins[i, pl.ds(pl.multiple_of(t * BIN, 8), BIN), :] = binned[i * BIN : (i + 1) * BIN]
        return 0

    bring.wait()
    lax.fori_loop(0, CHUNKS, fill_bins, 0, unroll=4)

    spot, chunk = iota((128, BINS), 1), iota((128, BINS), 0)
    inside = (spot >= chunk * BIN) & (spot < chunk * BIN + BIN)
    offset = spot[0:1] - jnp.sum(jnp.where(inside, chunk * BIN, 0), 0, keepdims=True)
    offset = offset.astype(F32)
    high = jnp.where(starts[...] >= 256.0, 256.0, 0.0)
    parts = jnp.concatenate([high, starts[...] - high, counts[...]], 0).astype(BF)
    parts = dot(parts, inside.astype(F32).astype(BF))
    table = parts[:LEAVES] + parts[LEAVES : 2 * LEAVES] + offset
    table = jnp.where(offset < parts[2 * LEAVES :], table, -1.0)
    for i in range(LEAVES):
        places[i] = table[i : i + 1]

    eye = (iota((WIDE, WIDE), 0) == iota((WIDE, WIDE), 1)).astype(F32).astype(BF)

    def packet(k):
        to = lax.rem(leaf + k, jnp.int32(LEAVES))
        chosen = (iota((PER, BINS), 0).astype(F32) == places[to]).astype(F32).astype(BF)
        packed = dot(chosen, bins[to].astype(BF)).astype(BF)
        turned = dot_nt(eye, packed)
        feat[k] = turned[:F].astype(BF)
        aux[k] = jnp.concatenate([turned[F : F + 1, 128 * c : 128 * c + 128] for c in range(4)] * 2, 0)

    def give(n, _):
        k = turn_of(n)
        packet(k)
        send_aux(k).start()
        send_feat(k).start()
        return 0

    lax.fori_loop(1, 4, give, 0)

    each(LEAVES, lambda k: send_pivots(k).wait_recv())
    place = jnp.concatenate([held[(LEAVES - b) % LEAVES] for b in range(LEAVES)], 0)
    home = place % ROWS // PACKET
    number = ((leaf + iota((LEAVES, RANK), 0)) % LEAVES) * 8 + place // ROWS
    number = (number * PACKET + place % PACKET).astype(F32)
    valid = home == leaf * COLS + col
    order = dot(valid.astype(F32).astype(BF), before)
    order = jnp.where(valid, order, -1.0)

    def spread(table):
        return jnp.concatenate(
            [jnp.broadcast_to(table[b : b + 1], (SLOTS, RANK)) for b in range(LEAVES)], 0
        )

    shape = (LEAVES * SLOTS, RANK)
    hit = spread(order) == (iota(shape, 0) % SLOTS).astype(F32)
    wanted = jnp.sum(jnp.where(hit, spread(number) + 1.0, 0.0), 1, keepdims=True) - 1.0
    which = jnp.sum(jnp.where(hit, iota(shape, 1).astype(F32) + 1.0, 0.0), 1, keepdims=True) - 1.0
    wanted = jnp.broadcast_to(wanted, (LEAVES * SLOTS, CHUNK))

    def take(t, total):
        chosen = (wanted == ranked[t, 2:3, :]).astype(F32).astype(BF)
        rest = jnp.zeros((128 - WIDE, CHUNK), BF)
        return total + dot_nt(chosen, jnp.concatenate([joined_of(t), rest], 0))

    shape = (LEAVES * SLOTS, 128)
    taken = lax.fori_loop(0, CHUNKS, take, jnp.zeros(shape, F32), unroll=4)
    taken = jnp.where(iota(shape, 1) == WHICH, which, taken)
    taken = jnp.where(iota(shape, 1) == FULL, full, taken).astype(BF)
    for b in range(LEAVES):
        slots[b] = taken[b * SLOTS : (b + 1) * SLOTS]
    came[0] = slots[0]
    each(LEAVES, lambda k: send_slots(k).start())
    lax.fori_loop(4, 11, give, 0)

    each(LEAVES, lambda k: send_slots(k).wait_recv())
    got = jnp.concatenate([came[b] for b in range(LEAVES)], 0).astype(F32)
    chosen = got[:, WHICH : WHICH + 1] == iota((LEAVES * SLOTS, RANK), 1).astype(F32)
    picked = dot(got.T[:F].astype(BF), chosen.astype(F32).astype(BF))
    full = jnp.broadcast_to(jnp.max(got[:, FULL : FULL + 1], 0, keepdims=True), (1, 128))
    sk[0] = picked.astype(BF)
    each(COLS, lambda k: send_skel(k).start())
    lax.fori_loop(11, LEAVES, give, 0)
    packet(0)
    rx[0] = feat[0]
    ra[0] = aux[0]

    largest = jnp.zeros((OWNERS, 1), F32)
    for b in range(LEAVES):
        held_here = (iota((OWNERS, RANK), 0) == home[b : b + 1]).astype(F32)
        largest = jnp.maximum(largest, jnp.sum(held_here, 1, keepdims=True))

    for copy in smalls:
        copy.wait()
    spare[...] = jnp.ones((8, 128), F32)
    spare[0:1, 0:F] = scales[...]
    inverse = 1.0 / to_column(spare[0:1, :])[:F]
    scale = inverse * inverse * LOG2E
    scale2 = across(scale, RANK)
    scale4 = across(scale, PER)

    index[...] = top_index(parent, top, leaf // 4)
    index2 = across(index[...], 2 * RANK)
    number = iota((RANK, 2 * RANK), 1)
    base = (quarter * RANK).astype(F32)
    other = (sibling * RANK).astype(F32)
    chosen = index2[:, :RANK] == iota((RANK, RANK), 1).astype(F32) + base
    rows[...] = chosen.astype(F32).astype(BF)
    lanes = number.astype(F32) + jnp.where(number < RANK, base, other - RANK)
    columns[...] = (index2 == lanes).astype(F32).astype(BF)
    chosen = across(index[...], 4 * RANK) == iota((RANK, 4 * RANK), 1).astype(F32)
    fours[...] = chosen.astype(F32).astype(BF)

    def norms(k):
        side[k] = point_side(rx[k].astype(F32), scale4)

    def add_skel(k, total):
        send_skel(k).wait_recv()
        return total + sk[k].astype(F32)

    picked = lax.fori_loop(1, COLS, add_skel, picked)
    mine[...] = picked.astype(BF)
    sk4[quarter] = picked.astype(BF)

    def send_four(k):
        return remote(mine, sk4.at[quarter], (s_4, r_4), k, cousin(k))

    each(4, lambda k: send_four(k).start())
    left[0:RANK, :] = skel_side(picked, scale2)

    def block_of(k, out, begin):
        p = rx[k]
        fill = jnp.zeros((256 - 3 * F - 16, PER), BF)
        right = jnp.concatenate([p, p, p, side[k], fill], 0)
        power = dot(left[begin : begin + RANK, :], right)
        out[0:RANK, :] = jnp.exp2(jnp.minimum(power, 0.0)).astype(BF)

    def own_of(k, out):
        block_of(k, out, 0)
        value = ra[k]
        value = jnp.concatenate([value[r : r + 1] for r in range(4)], 1)
        out[RANK:, :] = jnp.broadcast_to(value, (16, PER)).astype(BF)

    def gram_of(u):
        gram[...] += dot_nt(u[...], u[0:RANK, :])

    def couple_of(v, u):
        couple[...] += dot_nt(v[...], u[0:RANK, :])

    last = LEAVES // 2 - 1

    def own_two(j, _):
        k, l = turn_of(2 * j), turn_of(2 * j + 1)
        pl.when(j > 0)(lambda: receive(k))
        receive(l)
        norms(k)
        norms(l)
        own_of(k, even.at[j])
        gram_of(odd.at[rem(j + last, last + 1)])
        own_of(l, odd.at[j])
        gram_of(even.at[j])
        return 0

    def receive(k):
        send_aux(k).wait_recv()
        send_feat(k).wait_recv()

    def other_two(j, _):
        block_of(turn_of(2 * j), other_even, RANK)
        couple_of(other_odd, odd.at[rem(j + last, last + 1)])
        block_of(turn_of(2 * j + 1), other_odd, RANK)
        couple_of(other_even, even.at[j])
        return 0

    gram[...] = jnp.zeros_like(gram)
    couple[...] = jnp.zeros_like(couple)
    odd[last] = jnp.zeros((RANK + 16, PER), BF)
    other_odd[...] = jnp.zeros_like(other_odd)
    def send_gram(k):
        return remote(pg.at[(col + k) % COLS], gr.at[k], (s_p, r_p), k, beside(k))

    def send_couple(k):
        return remote(pc.at[(col + k) % COLS], cr.at[k], (s_c, r_c), k, beside(k))

    def send_chosen(k):
        return remote(pt.at[(col + k) % COLS], qr.at[k], (s_o, r_o), k, beside(k))

    def send_rhs(k):
        return remote(rs, rr.at[k], (s_r, r_r), k, beside(k))

    def sibling_side():
        each(4, lambda k: remote(mine, sk4.at[(quarter + 4 - k) % 4], (s_4, r_4), k, cousin(k)).wait_recv())
        left[RANK:, :] = skel_side(sk4[sibling].astype(F32), scale2)

    def give_gram():
        gram_of(odd.at[last])
        part = gram[0:RANK, :].astype(BF)
        for k in range(COLS):
            pg[k] = part[k * SLAB : (k + 1) * SLAB]
        rhs = gram[RANK : RANK + 1, :]
        rhs = jnp.sum(dot_nt(stack16(split3(rhs), RANK), rows[...]), 0, keepdims=True)
        rs[...] = jnp.zeros_like(rs)
        rs[0:1, :] = rhs[:, :128]
        rs[1:2, :] = rhs[:, 128:]
        rs[2:3, :] = full
        each(COLS, lambda k: send_gram(k).start())
        each(COLS, lambda k: send_rhs(k).start())
        tops[...] = dot_nt(dot(rows[...], part).astype(BF), columns[:, 0:RANK])

    def half(h, _):
        pairs = LEAVES // 4
        lax.fori_loop(pairs * h, pairs * (h + 1), own_two, 0)
        pl.when(h == 0)(sibling_side)
        pl.when(h == 1)(give_gram)
        lax.fori_loop(pairs * h, pairs * (h + 1), other_two, 0)
        return 0

    lax.fori_loop(0, 2, half, 0)
    couple_of(other_odd, odd.at[last])

    part = couple[...].astype(BF)
    chosen = dot_nt(dot_nt(rows[...], part).astype(BF), columns[:, RANK:]) + tops[...]
    chosen = chosen.astype(BF)
    for k in range(COLS):
        pt[k] = chosen[k * SLAB : (k + 1) * SLAB]
    each(COLS, lambda k: send_chosen(k).start())
    part = couple[...].T.astype(BF)
    for k in range(COLS):
        pc[k] = part[k * SLAB : (k + 1) * SLAB]
    each(COLS, lambda k: send_couple(k).start())

    whole = jnp.concatenate([sk4[k] for k in range(4)], 1)
    points = dot_nt(whole, fours[...])
    fill = jnp.zeros((256 - 3 * F - 16, RANK), BF)
    points_b = points.astype(BF)
    right = jnp.concatenate([points_b, points_b, points_b, point_side(points, scale2), fill], 0)
    value = jnp.exp2(jnp.minimum(dot(skel_side(points, scale2), right), 0.0))
    crossing = (across(index[...], RANK) >= 2.0 * RANK) != (index[...].T[0:1, :] >= 2.0 * RANK)
    square = iota((RANK, RANK), 0) == iota((RANK, RANK), 1)
    tops[...] = jnp.where(crossing, value, 0.0) + jnp.where(square, ridge[...], 0.0)

    def finish(sends):
        return lambda k: [send(k).wait_send() for send in sends]

    each(LEAVES, finish((send_pivots, send_slots, send_aux, send_feat)))
    each(COLS, finish((send_skel, send_gram, send_rhs)))
    each(4, finish((send_four,)))

    def add_chosen(k, totals):
        send_chosen(k).wait_recv()
        send_rhs(k).wait_recv()
        return totals[0] + qr[k].astype(F32), totals[1] + rr[k]

    chosen, rhs = lax.fori_loop(1, COLS, add_chosen, (pt[col].astype(F32), rs[...]))
    over = jnp.maximum(jnp.max(rhs[2:3, :]), jnp.max(largest) - SLOTS)
    flag[0] = (over > 0.0).astype(jnp.int32)
    chosen = chosen * (1.0 / NODE)
    t4[0] = chosen.astype(BF)
    r4[0] = rhs * (1.0 / NODE)

    def send_top(k):
        return remote(t4.at[0], t4.at[k], (s_t, r_t), k, cousin(k))

    def send_top_rhs(k):
        return remote(r4.at[0], r4.at[k], (s_q, r_q), k, cousin(k))

    each(4, lambda k: send_top(k).start())
    each(4, lambda k: send_top_rhs(k).start())

    def add_gram(k, total):
        send_gram(k).wait_recv()
        return total + gr[k].astype(F32)

    def add_couple(k, total):
        send_couple(k).wait_recv()
        return total + cr[k].astype(F32)

    total = lax.fori_loop(1, COLS, add_gram, pg[col].astype(F32))
    diagonal = iota((SLAB, RANK), 0) + col * SLAB == iota((SLAB, RANK), 1)
    out_share[0, :, 0:RANK] = total * (1.0 / NODE) + jnp.where(diagonal, ridge[...], 0.0)
    total = lax.fori_loop(1, COLS, add_couple, pc[col].astype(F32))
    out_share[0, :, RANK:] = total * (1.0 / NODE)
    result = chosen + tops[pl.ds(pl.multiple_of(col * SLAB, SLAB), SLAB), :]

    def add_top(k, totals):
        send_top(k).wait_recv()
        send_top_rhs(k).wait_recv()
        return totals[0] + t4[k].astype(F32), totals[1] + r4[k]

    result, rhs = lax.fori_loop(1, 4, add_top, (result, r4[0]))
    out_top[0] = result
    out_rhs[...] = jnp.concatenate([rhs[0:1], rhs[1:2]], 1)

    each(COLS, finish((send_couple, send_chosen)))
    each(4, finish((send_top, send_top_rhs)))


SHAPES = ((1, SLAB, 2 * RANK), (1, SLAB, RANK), (1, RANK))


def exchange(merged, ridge, *smalls):
    return pl.pallas_call(
        exchange_kernel,
        out_shape=tuple(pltpu.VMEM(shape, F32) for shape in SHAPES),
        in_specs=[VMEM, VMEM] + [ANYWHERE] * 4,
        out_specs=[VMEM] * 3,
        scratch_shapes=[
            pltpu.VMEM((1, RANK), jnp.int32),
            pltpu.VMEM((1, F), F32),
            pltpu.VMEM((8, RANK), jnp.int32),
            pltpu.VMEM((4, RANK), jnp.int32),
            pltpu.VMEM((8, 128), F32),
            pltpu.VMEM((LEAVES, F, PER), BF),
            pltpu.VMEM((LEAVES, 8, 128), F32),
            pltpu.VMEM((LEAVES, F, PER), BF),
            pltpu.VMEM((LEAVES, 8, 128), F32),
            pltpu.VMEM((LEAVES, RANK, PER), BF),
            pltpu.VMEM((LEAVES, 16, PER), BF),
            pltpu.VMEM((COLS, F, RANK), BF),
            pltpu.VMEM((F, RANK), BF),
            pltpu.VMEM((4, F, RANK), BF),
            pltpu.VMEM((2 * RANK, 256), BF),
            pltpu.VMEM((LEAVES // 2, RANK + 16, PER), BF),
            pltpu.VMEM((LEAVES // 2, RANK + 16, PER), BF),
            pltpu.VMEM((RANK, PER), BF),
            pltpu.VMEM((RANK, PER), BF),
            pltpu.VMEM((RANK + 16, RANK), F32),
            pltpu.VMEM((RANK, RANK), F32),
            pltpu.VMEM((RANK, RANK), BF),
            pltpu.VMEM((RANK, 2 * RANK), BF),
            pltpu.VMEM((RANK, 4 * RANK), BF),
            pltpu.VMEM((RANK, 128), F32),
            pltpu.VMEM((RANK, RANK), F32),
            pltpu.VMEM((COLS, SLAB, RANK), BF),
            pltpu.VMEM((COLS, SLAB, RANK), BF),
            pltpu.VMEM((COLS, SLAB, RANK), BF),
            pltpu.VMEM((COLS, SLAB, RANK), BF),
            pltpu.VMEM((COLS, SLAB, RANK), BF),
            pltpu.VMEM((COLS, SLAB, RANK), BF),
            pltpu.VMEM((8, 128), F32),
            pltpu.VMEM((COLS, 8, 128), F32),
            pltpu.VMEM((4, SLAB, RANK), BF),
            pltpu.VMEM((4, 8, 128), F32),
            *dma(LEAVES),
            *dma(LEAVES),
            *dma(COLS),
            *dma(4),
            *dma(COLS),
            *dma(COLS),
            *dma(COLS),
            *dma(COLS),
            *dma(4),
            *dma(4),
            pltpu.SemaphoreType.DMA((4,)),
        ],
        compiler_params=params(0, 40),
        name="exchange",
    )(merged, ridge, *in_hbm(*smalls))


def stream(samples, pivots, ridge, *smalls):
    return pl.pallas_call(
        stream_kernel,
        out_shape=(
            *(pltpu.VMEM(shape, F32) for shape in SHAPES),
            jax.ShapeDtypeStruct((1,), jnp.int32),
        ),
        in_specs=[ANYWHERE, VMEM, VMEM, VMEM, VMEM] + [ANYWHERE] * 3,
        out_specs=[VMEM] * 3 + [pl.BlockSpec(memory_space=pltpu.SMEM)],
        scratch_shapes=[
            pltpu.VMEM((F, ROWS), BF),
            pltpu.VMEM((ROWS // 128, 128), F32),
            pltpu.VMEM((CHUNKS, 8, CHUNK), F32),
            pltpu.VMEM((LEAVES, 128), F32),
            pltpu.VMEM((LEAVES, 128), F32),
            pltpu.VMEM((LEAVES, 1, BINS), F32),
            pltpu.VMEM((LEAVES, BINS, WIDE), F32),
            pltpu.VMEM((LEAVES, 1, RANK), jnp.int32),
            pltpu.VMEM((LEAVES, SLOTS, 128), BF),
            pltpu.VMEM((LEAVES, SLOTS, 128), BF),
            pltpu.VMEM((1, F), F32),
            pltpu.VMEM((8, RANK), jnp.int32),
            pltpu.VMEM((4, RANK), jnp.int32),
            pltpu.VMEM((8, 128), F32),
            pltpu.VMEM((LEAVES, F, PER), BF),
            pltpu.VMEM((LEAVES, 8, 128), F32),
            pltpu.VMEM((LEAVES, F, PER), BF),
            pltpu.VMEM((LEAVES, 8, 128), F32),
            pltpu.VMEM((LEAVES, 16, PER), BF),
            pltpu.VMEM((COLS, F, RANK), BF),
            pltpu.VMEM((F, RANK), BF),
            pltpu.VMEM((4, F, RANK), BF),
            pltpu.VMEM((2 * RANK, 256), BF),
            pltpu.VMEM((LEAVES // 2, RANK + 16, PER), BF),
            pltpu.VMEM((LEAVES // 2, RANK + 16, PER), BF),
            pltpu.VMEM((RANK, PER), BF),
            pltpu.VMEM((RANK, PER), BF),
            pltpu.VMEM((RANK + 16, RANK), F32),
            pltpu.VMEM((RANK, RANK), F32),
            pltpu.VMEM((RANK, RANK), BF),
            pltpu.VMEM((RANK, 2 * RANK), BF),
            pltpu.VMEM((RANK, 4 * RANK), BF),
            pltpu.VMEM((RANK, 128), F32),
            pltpu.VMEM((RANK, RANK), F32),
            pltpu.VMEM((COLS, SLAB, RANK), BF),
            pltpu.VMEM((COLS, SLAB, RANK), BF),
            pltpu.VMEM((COLS, SLAB, RANK), BF),
            pltpu.VMEM((COLS, SLAB, RANK), BF),
            pltpu.VMEM((COLS, SLAB, RANK), BF),
            pltpu.VMEM((COLS, SLAB, RANK), BF),
            pltpu.VMEM((8, 128), F32),
            pltpu.VMEM((COLS, 8, 128), F32),
            pltpu.VMEM((4, SLAB, RANK), BF),
            pltpu.VMEM((4, 8, 128), F32),
            *dma(LEAVES),
            *dma(LEAVES),
            *dma(LEAVES),
            *dma(LEAVES),
            *dma(COLS),
            *dma(4),
            *dma(COLS),
            *dma(COLS),
            *dma(COLS),
            *dma(COLS),
            *dma(4),
            *dma(4),
            pltpu.SemaphoreType.DMA((4,)),
        ],
        compiler_params=params(1, 40),
        name="stream",
    )(*in_hbm(*samples, pivots), ridge, *in_hbm(*smalls))


def emit_kernel(*refs):
    ins, outs, sem = refs[:3], refs[3:6], refs[6]
    copies = [pltpu.make_async_copy(a, b, sem.at[k]) for k, (a, b) in enumerate(zip(ins, outs))]
    for copy in copies:
        copy.start()
    for copy in copies:
        copy.wait()


def emit(results):
    return pl.pallas_call(
        emit_kernel,
        out_shape=tuple(jax.ShapeDtypeStruct(shape, F32) for shape in SHAPES),
        in_specs=[VMEM] * 3,
        out_specs=[ANYWHERE] * 3,
        scratch_shapes=[pltpu.SemaphoreType.DMA((3,))],
        compiler_params=params(),
        name="emit",
    )(*results)


def local(features, targets, owner, length_scales, ridge, leaf_pivots, parent_pivots, top_pivots):
    samples = (features, targets.reshape(ROWS // 128, 128), owner.reshape(ROWS // 128, 128))
    ridge = ridge.reshape(1, 1)
    smalls = (length_scales.reshape(1, F), parent_pivots, top_pivots)
    *results, flag = stream(samples, leaf_pivots, ridge, *smalls)

    def again():
        return tuple(emit(exchange(pack(*samples), ridge, leaf_pivots, *smalls)))

    return lax.switch(flag[0], [lambda: tuple(emit(results)), again])


def solution(mesh):
    return jax.shard_map(
        local,
        mesh=mesh,
        in_specs=(
            P(None, ("leaf", "col")),
            P(("leaf", "col")),
            P(("leaf", "col")),
            P(),
            P(),
            P("leaf", None),
            P(),
            P(),
        ),
        out_specs=(P("leaf", "col", None), P("leaf", "col", None), P("leaf", None)),
        check_vma=False,
    )
```

```python
import functools
import math

import jax
import jax.numpy as jnp
from jax import lax
from jax.experimental import pallas as pl
from jax.experimental.pallas import tpu as pltpu
from jax.sharding import PartitionSpec as P

F = 48
RANK = 256
ROWS = 8192
LEAVES = 16
COLS = 8
OWNERS = 128
PACKET = 64
PER = ROWS // LEAVES
CHUNK = 256
CHUNKS = ROWS // CHUNK
WINDOW = 40
REGION = PER + WINDOW
TILES = PER // 8
SLOTS = 16
WHICH = 50
FULL = 51
WIDE = 64
SLAB = RANK // COLS
NODE = ROWS * COLS
LOG2E = math.log2(math.e)
BF = jnp.bfloat16
F32 = jnp.float32
NT = (((1,), (1,)), ((), ()))
MESH = pl.DeviceIdType.MESH


def dma(count):
    return [pltpu.SemaphoreType.DMA((count,))] * 2


def params(number=None, limit=24):
    if number is None:
        return pltpu.CompilerParams(vmem_limit_bytes=limit * 2**20)
    return pltpu.CompilerParams(
        collective_id=number, has_side_effects=True, vmem_limit_bytes=limit * 2**20
    )


ANYWHERE = pl.BlockSpec(memory_space=pl.ANY)
VMEM = pl.BlockSpec(memory_space=pltpu.VMEM)


def iota(shape, axis):
    return lax.broadcasted_iota(jnp.int32, shape, axis)


def dot(a, b):
    return jnp.dot(a, b, preferred_element_type=F32)


def dot_nt(a, b):
    return lax.dot_general(a, b, NT, preferred_element_type=F32)


def row_pair(two):
    return jnp.concatenate([two[0:1], two[1:2]], 1)


def pack_kernel(
    feat_hbm, target, owner, zbuf, feat, goals, rows, ybuf, table, scal, sem, feat_sem
):
    bring = pltpu.make_async_copy(feat_hbm, feat, feat_sem)
    bring.start()
    goals[...] = target[...].astype(F32)
    before = (iota((CHUNK, CHUNK), 0) < iota((CHUNK, CHUNK), 1)).astype(F32).astype(BF)
    weights = jnp.concatenate([before, jnp.ones((CHUNK, 128), BF)], 1)
    lane = iota((LEAVES, 128), 1)

    def ranks(t, carry):
        seen, seen_leaf, most = carry
        own = row_pair(owner[pl.ds(2 * t, 2), :])
        leaf = own // 8
        is_own = iota((OWNERS, CHUNK), 0) == own
        is_leaf = iota((LEAVES, CHUNK), 0) == leaf
        is_after = iota((LEAVES, CHUNK), 0) > leaf
        marks = jnp.concatenate(
            [m.astype(F32).astype(BF) for m in (is_own, is_leaf, is_after)], 0
        )
        sums = dot(marks, weights)
        counts = sums[:OWNERS, CHUNK:]
        leaf_counts = sums[OWNERS : OWNERS + LEAVES, CHUNK:]
        base = sums[OWNERS + LEAVES :, CHUNK:]
        prior = sums[:OWNERS, :CHUNK] + jnp.concatenate([seen, seen], 1)
        rank = jnp.sum(jnp.where(is_own, prior, 0.0), 0, keepdims=True)
        place = sums[OWNERS : OWNERS + LEAVES, :CHUNK] + jnp.concatenate([base, base], 1)
        place = jnp.sum(jnp.where(is_leaf, place, 0.0), 0, keepdims=True)
        tag = (own % 8).astype(F32) * PACKET + rank - (PER // 2)
        rows[t, 0:1, :] = place
        rows[t, 1:2, :] = row_pair(goals[pl.ds(2 * t, 2), :])
        rows[t, 2:3, :] = tag
        here = lane == t
        table[0:LEAVES, :] = jnp.where(here, seen_leaf.astype(jnp.int32), table[0:LEAVES, :])
        table[LEAVES : 2 * LEAVES, :] = jnp.where(
            here, base.astype(jnp.int32), table[LEAVES : 2 * LEAVES, :]
        )
        return seen + counts, seen_leaf + leaf_counts, jnp.maximum(most, leaf_counts)

    table[0:LEAVES, :] = jnp.full((LEAVES, 128), PER, jnp.int32)
    zero = jnp.zeros((LEAVES, 128), F32)
    _, _, most = lax.fori_loop(
        0, CHUNKS, ranks, (jnp.zeros((OWNERS, 128), F32), zero, zero), unroll=16
    )
    most = jnp.broadcast_to(jnp.max(most, 0, keepdims=True), (8, 128))
    table[2 * LEAVES :, :] = most.astype(jnp.int32)
    move = pltpu.make_async_copy(table, scal, sem)
    move.start()
    bring.wait()

    def sort(t, _):
        start = pl.multiple_of(t * CHUNK, CHUNK)
        row = iota((16, CHUNK), 0)
        place, goal, tag = rows[t, 0:1, :], rows[t, 1:2, :], rows[t, 2:3, :]
        extra = jnp.where(row == 0, goal, jnp.where(row == 1, tag, 0.0)).astype(BF)
        joined = jnp.concatenate([feat[:, pl.ds(start, CHUNK)], extra], 0)
        chosen = (iota((CHUNK, CHUNK), 0) == place.astype(jnp.int32)).astype(F32).astype(BF)
        ybuf[pl.ds(start, CHUNK), :] = dot_nt(chosen, joined)
        return 0

    lax.fori_loop(0, CHUNKS, sort, 0, unroll=8)
    move.wait()
    widest = scal[2 * LEAVES, 0]

    @pl.when(widest <= WINDOW)
    def quick():
        def merge(t, _):
            for i in range(LEAVES):
                source = t * CHUNK + scal[LEAVES + i, t]
                goal = i * REGION + scal[i, t]
                zbuf[pl.ds(goal, WINDOW), :] = ybuf[pl.ds(source, WINDOW), :]
            return 0

        lax.fori_loop(0, CHUNKS, merge, 0, unroll=4)

    @pl.when(widest > WINDOW)
    def slow():
        def merge(index, _):
            t = index // LEAVES
            i = index % LEAVES
            source = t * CHUNK + scal[LEAVES + i, t]
            first = scal[i, t]
            count = scal[i, t + 1] - first

            def part(k, _):
                rows = ybuf[pl.ds(source + 8 * k, 8), :]
                zbuf[pl.ds(i * REGION + first + 8 * k, 8), :] = rows
                return 0

            lax.fori_loop(0, (count + 7) // 8, part, 0)
            return 0

        lax.fori_loop(0, CHUNKS * LEAVES, merge, 0)


def in_hbm(*arrays):
    return [pltpu.with_memory_space_constraint(a, pltpu.HBM) for a in arrays]


def pack(features, targets, owner):
    return pl.pallas_call(
        pack_kernel,
        out_shape=pltpu.VMEM((LEAVES * REGION, WIDE), F32),
        in_specs=[ANYWHERE, VMEM, VMEM],
        out_specs=VMEM,
        scratch_shapes=[
            pltpu.VMEM((F, ROWS), BF),
            pltpu.VMEM((ROWS // 128, 128), F32),
            pltpu.VMEM((CHUNKS, 8, CHUNK), F32),
            pltpu.VMEM((ROWS + WINDOW, WIDE), F32),
            pltpu.VMEM((40, 128), jnp.int32),
            pltpu.SMEM((40, 128), jnp.int32),
            pltpu.SemaphoreType.DMA,
            pltpu.SemaphoreType.DMA,
        ],
        compiler_params=params(),
        name="pack",
    )(*in_hbm(features, targets, owner))


def split3(x):
    high = x.astype(BF)
    rest = x - high.astype(F32)
    mid = rest.astype(BF)
    return high, mid, (rest - mid.astype(F32)).astype(BF)


def stack16(parts, width):
    row = iota((16, width), 0)
    block = jnp.zeros((16, width), F32)
    for k, part in enumerate(parts):
        block = jnp.where(row == k, part if isinstance(part, float) else part.astype(F32), block)
    return block.astype(BF)


def half_norm(points, scale):
    return jnp.sum(points * points * (0.5 * scale), 0, keepdims=True)


def point_side(points, scale):
    high, mid, low = split3(-half_norm(points, scale))
    return stack16([high, mid, low, 1.0, 1.0, 1.0], points.shape[1])


def skel_side(skel, scale):
    width = skel.shape[1]
    high, mid, low = split3(skel * scale)
    extra = stack16([1.0, 1.0, 1.0, *split3(-half_norm(skel, scale))], width)
    parts = [p.astype(F32) for p in (high, mid, low, extra)]
    fill = jnp.zeros((256 - 3 * F - 16, width), F32)
    return jnp.concatenate([*parts, fill], 0).T.astype(BF)


def select_row(table, row):
    hit = iota(table.shape, 0) == row
    return jnp.sum(jnp.where(hit, table.astype(F32), 0.0), 0, keepdims=True)


def to_column(row):
    return jnp.broadcast_to(row, (128, row.shape[1])).T


def across(column, width):
    return jnp.concatenate([column] * (width // 128), 1)


def place_of(leaf, col):
    return dict(device_id=(leaf, col), device_id_type=MESH)


def mate(k):
    leaf, col = lax.axis_index("leaf"), lax.axis_index("col")
    to = (leaf + k) % LEAVES
    cross = (to // 8 + leaf // 8) % 2
    return place_of(to, col + cross * (1 - 2 * (col % 2)))


def beside(k):
    leaf, col = lax.axis_index("leaf"), lax.axis_index("col")
    return place_of(leaf, (col + k) % COLS)


def cousin(k):
    leaf, col = lax.axis_index("leaf"), lax.axis_index("col")
    return place_of(leaf - leaf % 4 + (leaf + k) % 4, col)


def each(count, step, unroll=1):
    lax.fori_loop(1, count, lambda k, _: (step(k), 0)[1], 0, unroll=unroll)


def rem(a, b):
    return lax.rem(jnp.int32(a), jnp.int32(b))


def turn_of(n):
    n = jnp.int32(n)
    odd = lax.rem(n, jnp.int32(2))
    half = lax.div(n + odd, jnp.int32(2))
    return lax.rem(odd * half + (1 - odd) * (LEAVES - half), jnp.int32(LEAVES))


def remote(src, dst, sems, k, peer):
    return pltpu.make_async_remote_copy(src, dst, sems[0].at[k], sems[1].at[k], **peer)


def top_index(parent, top, group):
    top_row = select_row(top[...], group)
    below = jnp.concatenate([select_row(parent[...], 2 * group + r) for r in range(2)], 1)
    number = iota((RANK, 2 * RANK), 1)
    below = below + jnp.where(iota((1, 2 * RANK), 1) >= RANK, 2.0 * RANK, 0.0)
    hit = across(to_column(top_row), 2 * RANK) == number.astype(F32)
    index = jnp.sum(jnp.where(hit, below, 0.0), 1, keepdims=True)
    return jnp.broadcast_to(index, (RANK, 128))


def exchange_kernel(
    merged, ridge, pivots_hbm, scales_hbm, parent_hbm, top_hbm, out_share, out_top, out_rhs,
    pivots, scales, parent, top, spare, feat, aux, rx, ra, hot, side, sk, mine, sk4, left,
    even, odd, other_even, other_odd, gram, couple, rows, columns, fours, index, tops,
    pg, gr, pc, cr, pt, qr, rs, rr, t4, r4,
    s_f, r_f, s_a, r_a, s_k, r_k, s_4, r_4, s_p, r_p, s_c, r_c, s_o, r_o, s_r, r_r, s_t, r_t, s_q, r_q, local,
):
    leaf = lax.axis_index("leaf")
    col = lax.axis_index("col")
    quarter = leaf % 4
    sibling = quarter + 1 - 2 * (quarter % 2)
    barrier = pltpu.get_barrier_semaphore()
    each(LEAVES, lambda k: pl.semaphore_signal(barrier, inc=1, **mate(k)))
    each(COLS, lambda k: pl.semaphore_signal(barrier, inc=1, **beside(k)))
    smalls = [
        pltpu.make_async_copy(a, b, local.at[k])
        for k, (a, b) in enumerate(
            [(pivots_hbm, pivots), (scales_hbm, scales), (parent_hbm, parent), (top_hbm, top)]
        )
    ]
    for copy in smalls:
        copy.start()

    eye = (iota((WIDE, WIDE), 0) == iota((WIDE, WIDE), 1)).astype(F32).astype(BF)

    def turn(k):
        start = pl.multiple_of((leaf + k) % LEAVES * REGION, 8)
        turned = dot_nt(eye, merged[pl.ds(start, PER), :].astype(BF))
        feat[k] = turned[:F].astype(BF)
        aux[k] = jnp.concatenate(
            [turned[F + r : F + r + 1, 128 * c : 128 * c + 128] for r in range(2) for c in range(4)], 0
        )

    def send_feat(k):
        return remote(feat.at[k], rx.at[k], (s_f, r_f), k, mate(k))

    def send_aux(k):
        return remote(aux.at[k], ra.at[k], (s_a, r_a), k, mate(k))

    def four(j, _):
        steps = [turn_of(lax.rem(4 * j + r, LEAVES)) for r in range(1, 5)]
        for k in steps:
            turn(k)
        pl.when(j == 0)(lambda: pl.semaphore_wait(barrier, LEAVES + COLS - 2))
        for send in (send_aux, send_feat):
            for k in steps[:3]:
                send(k).start()
            pl.when(j < 3)(lambda: send(steps[3]).start())
        return 0

    lax.fori_loop(0, LEAVES // 4, four, 0)
    rx[0] = feat[0]
    ra[0] = aux[0]

    for copy in smalls:
        copy.wait()
    spare[...] = jnp.ones((8, 128), F32)
    spare[0:1, 0:F] = scales[...]
    inverse = 1.0 / to_column(spare[0:1, :])[:F]
    scale = inverse * inverse * LOG2E
    scale2 = across(scale, RANK)
    scale4 = across(scale, PER)

    place = pivots[...]
    within = place % ROWS
    block = within // PACKET
    key = (block // COLS) * PER + (place // ROWS) * PACKET + within % PACKET
    holder = block % COLS
    crossed = (block // COLS) // 8 != leaf // 8
    holder = jnp.where(crossed, holder + 1 - 2 * (holder % 2), holder)
    key = jnp.where(holder == col, key, -PER)
    key = across(to_column(key.astype(F32)), PER)

    def mark(k):
        source = (leaf + LEAVES - k) % LEAVES
        tags = ra[k, 4:8, :]
        tag = jnp.concatenate([tags[r : r + 1] for r in range(4)], 1)
        wanted = tag + (PER // 2 + source * PER).astype(F32)
        hot[k] = (key == wanted).astype(F32).astype(BF)

    def mark_next(n, _):
        k = turn_of(n)
        pl.when(n > 0)(lambda: send_aux(k).wait_recv())
        mark(k)
        return 0

    lax.fori_loop(0, LEAVES, mark_next, 0)

    index[...] = top_index(parent, top, leaf // 4)
    index2 = across(index[...], 2 * RANK)
    number = iota((RANK, 2 * RANK), 1)
    base = (quarter * RANK).astype(F32)
    other = (sibling * RANK).astype(F32)
    chosen = index2[:, :RANK] == iota((RANK, RANK), 1).astype(F32) + base
    rows[...] = chosen.astype(F32).astype(BF)
    lanes = number.astype(F32) + jnp.where(number < RANK, base, other - RANK)
    columns[...] = (index2 == lanes).astype(F32).astype(BF)
    chosen = across(index[...], 4 * RANK) == iota((RANK, 4 * RANK), 1).astype(F32)
    fours[...] = chosen.astype(F32).astype(BF)

    def pick(j, total):
        steps = [turn_of(4 * j + r) for r in range(4)]
        pl.when(j > 0)(lambda: send_feat(steps[0]).wait_recv())
        for k in steps[1:]:
            send_feat(k).wait_recv()
        for k in steps:
            total = total + dot_nt(hot[k], rx[k])
        return total

    picked = lax.fori_loop(0, LEAVES // 4, pick, jnp.zeros((RANK, F), F32))
    picked = jnp.concatenate([picked, jnp.zeros((RANK, 128 - F), F32)], 1).T[:F]
    sk[0] = picked.astype(BF)

    def send_skel(k):
        return remote(sk.at[0], sk.at[k], (s_k, r_k), k, beside(k))

    each(COLS, lambda k: send_skel(k).start())

    def norms(k, _):
        side[k] = point_side(rx[k].astype(F32), scale4)
        return 0

    lax.fori_loop(0, LEAVES, norms, 0)

    def add_skel(k, total):
        send_skel(k).wait_recv()
        return total + sk[k].astype(F32)

    picked = lax.fori_loop(1, COLS, add_skel, picked)
    mine[...] = picked.astype(BF)
    sk4[quarter] = picked.astype(BF)

    def send_four(k):
        return remote(mine, sk4.at[quarter], (s_4, r_4), k, cousin(k))

    each(4, lambda k: send_four(k).start())
    left[0:RANK, :] = skel_side(picked, scale2)

    def block_of(k, out, begin):
        p = rx[k]
        fill = jnp.zeros((256 - 3 * F - 16, PER), BF)
        right = jnp.concatenate([p, p, p, side[k], fill], 0)
        power = dot(left[begin : begin + RANK, :], right)
        out[0:RANK, :] = jnp.exp2(jnp.minimum(power, 0.0)).astype(BF)

    def own_of(k, out):
        block_of(k, out, 0)
        value = jnp.concatenate([ra[k, r : r + 1, :] for r in range(4)], 1)
        out[RANK:, :] = jnp.broadcast_to(value, (16, PER)).astype(BF)

    def gram_of(u):
        gram[...] += dot_nt(u[...], u[0:RANK, :])

    def couple_of(v, u):
        couple[...] += dot_nt(v[...], u[0:RANK, :])

    last = LEAVES // 2 - 1

    def own_two(j, _):
        own_of(2 * j, even.at[j])
        gram_of(odd.at[(j + last) % (last + 1)])
        own_of(2 * j + 1, odd.at[j])
        gram_of(even.at[j])
        return 0

    def other_two(j, _):
        block_of(2 * j, other_even, RANK)
        couple_of(other_odd, odd.at[(j + last) % (last + 1)])
        block_of(2 * j + 1, other_odd, RANK)
        couple_of(other_even, even.at[j])
        return 0

    gram[...] = jnp.zeros_like(gram)
    couple[...] = jnp.zeros_like(couple)
    odd[last] = jnp.zeros((RANK + 16, PER), BF)
    other_odd[...] = jnp.zeros_like(other_odd)
    lax.fori_loop(0, last + 1, own_two, 0)
    gram_of(odd.at[last])

    def send_gram(k):
        return remote(pg.at[(col + k) % COLS], gr.at[k], (s_p, r_p), k, beside(k))

    def send_couple(k):
        return remote(pc.at[(col + k) % COLS], cr.at[k], (s_c, r_c), k, beside(k))

    def send_chosen(k):
        return remote(pt.at[(col + k) % COLS], qr.at[k], (s_o, r_o), k, beside(k))

    def send_rhs(k):
        return remote(rs, rr.at[k], (s_r, r_r), k, beside(k))

    part = gram[0:RANK, :].astype(BF)
    for k in range(COLS):
        pg[k] = part[k * SLAB : (k + 1) * SLAB]
    rhs = gram[RANK : RANK + 1, :]
    rhs = jnp.sum(dot_nt(stack16(split3(rhs), RANK), rows[...]), 0, keepdims=True)
    rs[...] = jnp.zeros_like(rs)
    rs[0:1, :] = rhs[:, :128]
    rs[1:2, :] = rhs[:, 128:]
    each(COLS, lambda k: send_gram(k).start())
    each(COLS, lambda k: send_rhs(k).start())
    tops[...] = dot_nt(dot(rows[...], part).astype(BF), columns[:, 0:RANK])

    each(4, lambda k: remote(mine, sk4.at[(quarter + 4 - k) % 4], (s_4, r_4), k, cousin(k)).wait_recv())
    left[RANK:, :] = skel_side(sk4[sibling].astype(F32), scale2)
    lax.fori_loop(0, last + 1, other_two, 0)
    couple_of(other_odd, odd.at[last])

    part = couple[...].astype(BF)
    chosen = dot_nt(dot_nt(rows[...], part).astype(BF), columns[:, RANK:]) + tops[...]
    chosen = chosen.astype(BF)
    for k in range(COLS):
        pt[k] = chosen[k * SLAB : (k + 1) * SLAB]
    each(COLS, lambda k: send_chosen(k).start())
    part = couple[...].T.astype(BF)
    for k in range(COLS):
        pc[k] = part[k * SLAB : (k + 1) * SLAB]
    each(COLS, lambda k: send_couple(k).start())

    whole = jnp.concatenate([sk4[k] for k in range(4)], 1)
    points = dot_nt(whole, fours[...])
    fill = jnp.zeros((256 - 3 * F - 16, RANK), BF)
    points_b = points.astype(BF)
    right = jnp.concatenate([points_b, points_b, points_b, point_side(points, scale2), fill], 0)
    value = jnp.exp2(jnp.minimum(dot(skel_side(points, scale2), right), 0.0))
    crossing = (across(index[...], RANK) >= 2.0 * RANK) != (index[...].T[0:1, :] >= 2.0 * RANK)
    square = iota((RANK, RANK), 0) == iota((RANK, RANK), 1)
    tops[...] = jnp.where(crossing, value, 0.0) + jnp.where(square, ridge[...], 0.0)

    def finish(sends):
        return lambda k: [send(k).wait_send() for send in sends]

    each(LEAVES, finish((send_aux, send_feat)))
    each(COLS, finish((send_skel, send_gram, send_rhs)))
    each(4, finish((send_four,)))

    def add_chosen(k, totals):
        send_chosen(k).wait_recv()
        send_rhs(k).wait_recv()
        return totals[0] + qr[k].astype(F32), totals[1] + rr[k]

    chosen, rhs = lax.fori_loop(1, COLS, add_chosen, (pt[col].astype(F32), rs[...]))
    chosen = chosen * (1.0 / NODE)
    t4[0] = chosen.astype(BF)
    r4[0] = rhs * (1.0 / NODE)

    def send_top(k):
        return remote(t4.at[0], t4.at[k], (s_t, r_t), k, cousin(k))

    def send_top_rhs(k):
        return remote(r4.at[0], r4.at[k], (s_q, r_q), k, cousin(k))

    each(4, lambda k: send_top(k).start())
    each(4, lambda k: send_top_rhs(k).start())

    def add_gram(k, total):
        send_gram(k).wait_recv()
        return total + gr[k].astype(F32)

    def add_couple(k, total):
        send_couple(k).wait_recv()
        return total + cr[k].astype(F32)

    total = lax.fori_loop(1, COLS, add_gram, pg[col].astype(F32))
    diagonal = iota((SLAB, RANK), 0) + col * SLAB == iota((SLAB, RANK), 1)
    out_share[0, :, 0:RANK] = total * (1.0 / NODE) + jnp.where(diagonal, ridge[...], 0.0)
    total = lax.fori_loop(1, COLS, add_couple, pc[col].astype(F32))
    out_share[0, :, RANK:] = total * (1.0 / NODE)
    result = chosen + tops[pl.ds(pl.multiple_of(col * SLAB, SLAB), SLAB), :]

    def add_top(k, totals):
        send_top(k).wait_recv()
        send_top_rhs(k).wait_recv()
        return totals[0] + t4[k].astype(F32), totals[1] + r4[k]

    result, rhs = lax.fori_loop(1, 4, add_top, (result, r4[0]))
    out_top[0] = result
    out_rhs[...] = jnp.concatenate([rhs[0:1], rhs[1:2]], 1)

    each(COLS, finish((send_couple, send_chosen)))
    each(4, finish((send_top, send_top_rhs)))


def stream_kernel(
    feat_hbm, target, owner, pivots, ridge, scales_hbm, parent_hbm, top_hbm,
    out_share, out_top, out_rhs, flag,
    feat_in, goals, ranked, starts, bases, ybuf, table, scal, held, slots, came, scales, parent, top, spare,
    feat, aux, rx, ra, side, sk, mine, sk4, left, even, odd, other_even, other_odd, gram, couple,
    rows, columns, fours, index, tops, pg, gr, pc, cr, pt, qr, rs, rr, t4, r4,
    s_v, r_v, s_s, r_s, s_f, r_f, s_a, r_a, s_k, r_k, s_4, r_4, s_p, r_p, s_c, r_c, s_o, r_o,
    s_r, r_r, s_t, r_t, s_q, r_q, local,
):
    leaf = lax.axis_index("leaf")
    col = lax.axis_index("col")
    quarter = leaf % 4
    sibling = quarter + 1 - 2 * (quarter % 2)
    barrier = pltpu.get_barrier_semaphore()
    each(LEAVES, lambda k: pl.semaphore_signal(barrier, inc=1, **mate(k)))
    each(COLS, lambda k: pl.semaphore_signal(barrier, inc=1, **beside(k)))
    bring = pltpu.make_async_copy(feat_hbm, feat_in, local.at[3])
    bring.start()
    smalls = [
        pltpu.make_async_copy(a, b, local.at[k])
        for k, (a, b) in enumerate([(scales_hbm, scales), (parent_hbm, parent), (top_hbm, top)])
    ]
    for copy in smalls:
        copy.start()

    def send_pivots(k):
        return remote(pivots, held.at[k], (s_v, r_v), k, mate(k))

    def send_slots(k):
        return remote(slots.at[k], came.at[k], (s_s, r_s), k, mate(k))

    def send_feat(k):
        return remote(feat.at[k], rx.at[k], (s_f, r_f), k, mate(k))

    def send_aux(k):
        return remote(aux.at[k], ra.at[k], (s_a, r_a), k, mate(k))

    def send_skel(k):
        return remote(sk.at[0], sk.at[k], (s_k, r_k), k, beside(k))

    goals[...] = target[...].astype(F32)
    before = (iota((CHUNK, CHUNK), 0) < iota((CHUNK, CHUNK), 1)).astype(F32).astype(BF)
    weights = jnp.concatenate([before, jnp.ones((CHUNK, 128), BF)], 1)
    lane = iota((LEAVES, 128), 1)

    def rank(t, carry):
        seen, seen_leaf = carry
        own = row_pair(owner[pl.ds(2 * t, 2), :])
        group = own // 8
        is_own = iota((OWNERS, CHUNK), 0) == own
        is_leaf = iota((LEAVES, CHUNK), 0) == group
        is_after = iota((LEAVES, CHUNK), 0) > group
        marks = jnp.concatenate([m.astype(F32).astype(BF) for m in (is_own, is_leaf, is_after)], 0)
        sums = dot(marks, weights)
        leaf_counts = sums[OWNERS : OWNERS + LEAVES, CHUNK:]
        base = sums[OWNERS + LEAVES :, CHUNK:]
        prior = sums[:OWNERS, :CHUNK] + jnp.concatenate([seen, seen], 1)
        place = jnp.sum(jnp.where(is_own, prior, 0.0), 0, keepdims=True)
        order = sums[OWNERS : OWNERS + LEAVES, :CHUNK] + jnp.concatenate([base, base], 1)
        ranked[t, 0:1, :] = jnp.sum(jnp.where(is_leaf, order, 0.0), 0, keepdims=True)
        ranked[t, 1:2, :] = row_pair(goals[pl.ds(2 * t, 2), :])
        ranked[t, 2:3, :] = own.astype(F32) * PACKET + place
        starts[...] = jnp.where(lane == t, seen_leaf, starts[...])
        bases[...] = jnp.where(lane == t, base, bases[...])
        return seen + sums[:OWNERS, CHUNK:], seen_leaf + leaf_counts

    starts[...] = jnp.zeros_like(starts)
    bases[...] = jnp.zeros_like(bases)
    lax.fori_loop(
        0, CHUNKS, rank, (jnp.zeros((OWNERS, 128), F32), jnp.zeros((LEAVES, 128), F32)), unroll=16
    )

    rest = jnp.zeros((128 - LEAVES, 128), F32)
    start_of = jnp.concatenate([starts[...], rest], 0).T[:CHUNKS]
    base_of = jnp.concatenate([bases[...], rest], 0).T[:CHUNKS]
    chunk = iota((CHUNKS, 128), 0)
    base_of = base_of + (chunk * CHUNK).astype(F32)
    chunk = chunk.astype(F32)
    first = 8.0 * iota((1, 128), 1).astype(F32)
    used = iota((1, 128), 1) < TILES
    full = jnp.zeros((1, 128), F32)
    table[...] = jnp.zeros_like(table)
    for i in range(LEAVES):
        begin = jnp.broadcast_to(start_of[:, i : i + 1], (CHUNKS, 128))
        place = jnp.broadcast_to(base_of[:, i : i + 1], (CHUNKS, 128))
        passed = (begin <= first) & (chunk > 0.0)
        current = jnp.sum(jnp.where(passed, 1.0, 0.0), 0, keepdims=True)
        for r in range(4):
            here = chunk == current + r
            row = jnp.sum(jnp.where(here, place, 0.0), 0, keepdims=True)
            edge = jnp.sum(jnp.where(here, begin, 0.0), 0, keepdims=True)
            edge = jnp.where(current + r < CHUNKS, edge, float(PER)) - first
            if r == 0:
                row = jnp.clip(jnp.where(used, row - edge, 0.0), 0.0, float(ROWS))
                table[i, 0:1, :] = row.astype(jnp.int32)
            elif r < 3:
                edge = jnp.where(used, jnp.clip(edge, 0.0, 8.0), 8.0)
                row = jnp.where(used & (current + r < CHUNKS), row - edge, 0.0)
                table[i, r : r + 1, :] = jnp.clip(row, 0.0, float(ROWS)).astype(jnp.int32)
                table[i, r + 2 : r + 3, :] = edge.astype(jnp.int32)
            else:
                full = jnp.maximum(full, jnp.where(used & (edge < 8.0), 1.0, 0.0))
    full = jnp.broadcast_to(jnp.max(full, 1, keepdims=True), (1, 128))
    tell = pltpu.make_async_copy(table, scal, local.at[4])
    tell.start()

    held[0] = pivots[...]
    pl.semaphore_wait(barrier, LEAVES + COLS - 2)
    each(LEAVES, lambda k: send_pivots(k).start())

    def joined_of(t):
        row = iota((16, CHUNK), 0)
        extra = jnp.where(row == 0, ranked[t, 1:2, :], 0.0).astype(BF)
        return jnp.concatenate([feat_in[:, pl.ds(pl.multiple_of(t * CHUNK, CHUNK), CHUNK)], extra], 0)

    def sort(t, _):
        place = ranked[t, 0:1, :].astype(jnp.int32)
        chosen = (iota((CHUNK, CHUNK), 0) == place).astype(F32).astype(BF)
        ybuf[pl.ds(pl.multiple_of(t * CHUNK, CHUNK), CHUNK), :] = dot_nt(chosen, joined_of(t))
        return 0

    bring.wait()
    lax.fori_loop(0, CHUNKS, sort, 0, unroll=8)
    ybuf[ROWS:, :] = jnp.zeros((16, WIDE), F32)
    tell.wait()

    eye = (iota((WIDE, WIDE), 0) == iota((WIDE, WIDE), 1)).astype(F32).astype(BF)
    sub = iota((8, WIDE), 0)

    def packet(k):
        to = lax.rem(leaf + k, jnp.int32(LEAVES))
        tiles = []
        for q in range(TILES):
            tile = ybuf[pl.ds(jnp.clip(scal[to, 0, q], 0, ROWS), 8), :]
            for r in (1, 2):
                later = ybuf[pl.ds(jnp.clip(scal[to, r, q], 0, ROWS), 8), :]
                tile = jnp.where(sub >= scal[to, r + 2, q], later, tile)
            tiles.append(tile)
        turned = dot_nt(eye, jnp.concatenate(tiles, 0).astype(BF))
        feat[k] = turned[:F].astype(BF)
        aux[k] = jnp.concatenate([turned[F : F + 1, 128 * c : 128 * c + 128] for c in range(4)] * 2, 0)

    def give(j, _):
        steps = turn_of(2 * j + 1), turn_of(rem(2 * j + 2, LEAVES))
        for k in steps:
            packet(k)
        send_aux(steps[0]).start()
        send_feat(steps[0]).start()

        @pl.when(j < LEAVES // 2 - 1)
        def second():
            send_aux(steps[1]).start()
            send_feat(steps[1]).start()

        return 0

    lax.fori_loop(0, 2, give, 0)

    each(LEAVES, lambda k: send_pivots(k).wait_recv())
    place = jnp.concatenate([held[(LEAVES - b) % LEAVES] for b in range(LEAVES)], 0)
    home = place % ROWS // PACKET
    number = ((leaf + iota((LEAVES, RANK), 0)) % LEAVES) * 8 + place // ROWS
    number = (number * PACKET + place % PACKET).astype(F32)
    valid = home == leaf * COLS + col
    order = dot(valid.astype(F32).astype(BF), before)
    order = jnp.where(valid, order, -1.0)

    def spread(table):
        return jnp.concatenate(
            [jnp.broadcast_to(table[b : b + 1], (SLOTS, RANK)) for b in range(LEAVES)], 0
        )

    shape = (LEAVES * SLOTS, RANK)
    hit = spread(order) == (iota(shape, 0) % SLOTS).astype(F32)
    wanted = jnp.sum(jnp.where(hit, spread(number) + 1.0, 0.0), 1, keepdims=True) - 1.0
    which = jnp.sum(jnp.where(hit, iota(shape, 1).astype(F32) + 1.0, 0.0), 1, keepdims=True) - 1.0
    wanted = jnp.broadcast_to(wanted, (LEAVES * SLOTS, CHUNK))

    def take(t, total):
        chosen = (wanted == ranked[t, 2:3, :]).astype(F32).astype(BF)
        rest = jnp.zeros((128 - WIDE, CHUNK), BF)
        return total + dot_nt(chosen, jnp.concatenate([joined_of(t), rest], 0))

    shape = (LEAVES * SLOTS, 128)
    taken = lax.fori_loop(0, CHUNKS, take, jnp.zeros(shape, F32), unroll=4)
    taken = jnp.where(iota(shape, 1) == WHICH, which, taken)
    taken = jnp.where(iota(shape, 1) == FULL, full, taken).astype(BF)
    for b in range(LEAVES):
        slots[b] = taken[b * SLOTS : (b + 1) * SLOTS]
    came[0] = slots[0]
    each(LEAVES, lambda k: send_slots(k).start())
    lax.fori_loop(2, 5, give, 0)

    each(LEAVES, lambda k: send_slots(k).wait_recv())
    got = jnp.concatenate([came[b] for b in range(LEAVES)], 0).astype(F32)
    chosen = got[:, WHICH : WHICH + 1] == iota((LEAVES * SLOTS, RANK), 1).astype(F32)
    picked = dot(got.T[:F].astype(BF), chosen.astype(F32).astype(BF))
    full = jnp.broadcast_to(jnp.max(got[:, FULL : FULL + 1], 0, keepdims=True), (1, 128))
    sk[0] = picked.astype(BF)
    each(COLS, lambda k: send_skel(k).start())
    lax.fori_loop(5, LEAVES // 2, give, 0)
    rx[0] = feat[0]
    ra[0] = aux[0]

    largest = jnp.zeros((OWNERS, 1), F32)
    for b in range(LEAVES):
        held_here = (iota((OWNERS, RANK), 0) == home[b : b + 1]).astype(F32)
        largest = jnp.maximum(largest, jnp.sum(held_here, 1, keepdims=True))

    for copy in smalls:
        copy.wait()
    spare[...] = jnp.ones((8, 128), F32)
    spare[0:1, 0:F] = scales[...]
    inverse = 1.0 / to_column(spare[0:1, :])[:F]
    scale = inverse * inverse * LOG2E
    scale2 = across(scale, RANK)
    scale4 = across(scale, PER)

    index[...] = top_index(parent, top, leaf // 4)
    index2 = across(index[...], 2 * RANK)
    number = iota((RANK, 2 * RANK), 1)
    base = (quarter * RANK).astype(F32)
    other = (sibling * RANK).astype(F32)
    chosen = index2[:, :RANK] == iota((RANK, RANK), 1).astype(F32) + base
    rows[...] = chosen.astype(F32).astype(BF)
    lanes = number.astype(F32) + jnp.where(number < RANK, base, other - RANK)
    columns[...] = (index2 == lanes).astype(F32).astype(BF)
    chosen = across(index[...], 4 * RANK) == iota((RANK, 4 * RANK), 1).astype(F32)
    fours[...] = chosen.astype(F32).astype(BF)

    def norms(k):
        side[k] = point_side(rx[k].astype(F32), scale4)

    def add_skel(k, total):
        send_skel(k).wait_recv()
        return total + sk[k].astype(F32)

    picked = lax.fori_loop(1, COLS, add_skel, picked)
    mine[...] = picked.astype(BF)
    sk4[quarter] = picked.astype(BF)

    def send_four(k):
        return remote(mine, sk4.at[quarter], (s_4, r_4), k, cousin(k))

    each(4, lambda k: send_four(k).start())
    left[0:RANK, :] = skel_side(picked, scale2)

    def block_of(k, out, begin):
        p = rx[k]
        fill = jnp.zeros((256 - 3 * F - 16, PER), BF)
        right = jnp.concatenate([p, p, p, side[k], fill], 0)
        power = dot(left[begin : begin + RANK, :], right)
        out[0:RANK, :] = jnp.exp2(jnp.minimum(power, 0.0)).astype(BF)

    def own_of(k, out):
        block_of(k, out, 0)
        value = ra[k]
        value = jnp.concatenate([value[r : r + 1] for r in range(4)], 1)
        out[RANK:, :] = jnp.broadcast_to(value, (16, PER)).astype(BF)

    def gram_of(u):
        gram[...] += dot_nt(u[...], u[0:RANK, :])

    def couple_of(v, u):
        couple[...] += dot_nt(v[...], u[0:RANK, :])

    last = LEAVES // 2 - 1

    def own_two(j, _):
        k, l = turn_of(2 * j), turn_of(2 * j + 1)
        pl.when(j > 0)(lambda: receive(k))
        receive(l)
        norms(k)
        norms(l)
        own_of(k, even.at[j])
        gram_of(odd.at[rem(j + last, last + 1)])
        own_of(l, odd.at[j])
        gram_of(even.at[j])
        return 0

    def receive(k):
        send_aux(k).wait_recv()
        send_feat(k).wait_recv()

    def other_two(j, _):
        block_of(turn_of(2 * j), other_even, RANK)
        couple_of(other_odd, odd.at[rem(j + last, last + 1)])
        block_of(turn_of(2 * j + 1), other_odd, RANK)
        couple_of(other_even, even.at[j])
        return 0

    gram[...] = jnp.zeros_like(gram)
    couple[...] = jnp.zeros_like(couple)
    odd[last] = jnp.zeros((RANK + 16, PER), BF)
    other_odd[...] = jnp.zeros_like(other_odd)
    def send_gram(k):
        return remote(pg.at[(col + k) % COLS], gr.at[k], (s_p, r_p), k, beside(k))

    def send_couple(k):
        return remote(pc.at[(col + k) % COLS], cr.at[k], (s_c, r_c), k, beside(k))

    def send_chosen(k):
        return remote(pt.at[(col + k) % COLS], qr.at[k], (s_o, r_o), k, beside(k))

    def send_rhs(k):
        return remote(rs, rr.at[k], (s_r, r_r), k, beside(k))

    def sibling_side():
        each(4, lambda k: remote(mine, sk4.at[(quarter + 4 - k) % 4], (s_4, r_4), k, cousin(k)).wait_recv())
        left[RANK:, :] = skel_side(sk4[sibling].astype(F32), scale2)

    def give_gram():
        gram_of(odd.at[last])
        part = gram[0:RANK, :].astype(BF)
        for k in range(COLS):
            pg[k] = part[k * SLAB : (k + 1) * SLAB]
        rhs = gram[RANK : RANK + 1, :]
        rhs = jnp.sum(dot_nt(stack16(split3(rhs), RANK), rows[...]), 0, keepdims=True)
        rs[...] = jnp.zeros_like(rs)
        rs[0:1, :] = rhs[:, :128]
        rs[1:2, :] = rhs[:, 128:]
        rs[2:3, :] = full
        each(COLS, lambda k: send_gram(k).start())
        each(COLS, lambda k: send_rhs(k).start())
        tops[...] = dot_nt(dot(rows[...], part).astype(BF), columns[:, 0:RANK])

    def half(h, _):
        pairs = LEAVES // 4
        lax.fori_loop(pairs * h, pairs * (h + 1), own_two, 0)
        pl.when(h == 0)(sibling_side)
        pl.when(h == 1)(give_gram)
        lax.fori_loop(pairs * h, pairs * (h + 1), other_two, 0)
        return 0

    lax.fori_loop(0, 2, half, 0)
    couple_of(other_odd, odd.at[last])

    part = couple[...].astype(BF)
    chosen = dot_nt(dot_nt(rows[...], part).astype(BF), columns[:, RANK:]) + tops[...]
    chosen = chosen.astype(BF)
    for k in range(COLS):
        pt[k] = chosen[k * SLAB : (k + 1) * SLAB]
    each(COLS, lambda k: send_chosen(k).start())
    part = couple[...].T.astype(BF)
    for k in range(COLS):
        pc[k] = part[k * SLAB : (k + 1) * SLAB]
    each(COLS, lambda k: send_couple(k).start())

    whole = jnp.concatenate([sk4[k] for k in range(4)], 1)
    points = dot_nt(whole, fours[...])
    fill = jnp.zeros((256 - 3 * F - 16, RANK), BF)
    points_b = points.astype(BF)
    right = jnp.concatenate([points_b, points_b, points_b, point_side(points, scale2), fill], 0)
    value = jnp.exp2(jnp.minimum(dot(skel_side(points, scale2), right), 0.0))
    crossing = (across(index[...], RANK) >= 2.0 * RANK) != (index[...].T[0:1, :] >= 2.0 * RANK)
    square = iota((RANK, RANK), 0) == iota((RANK, RANK), 1)
    tops[...] = jnp.where(crossing, value, 0.0) + jnp.where(square, ridge[...], 0.0)

    def finish(sends):
        return lambda k: [send(k).wait_send() for send in sends]

    each(LEAVES, finish((send_pivots, send_slots, send_aux, send_feat)))
    each(COLS, finish((send_skel, send_gram, send_rhs)))
    each(4, finish((send_four,)))

    def add_chosen(k, totals):
        send_chosen(k).wait_recv()
        send_rhs(k).wait_recv()
        return totals[0] + qr[k].astype(F32), totals[1] + rr[k]

    chosen, rhs = lax.fori_loop(1, COLS, add_chosen, (pt[col].astype(F32), rs[...]))
    over = jnp.maximum(jnp.max(rhs[2:3, :]), jnp.max(largest) - SLOTS)
    flag[0] = (over > 0.0).astype(jnp.int32)
    chosen = chosen * (1.0 / NODE)
    t4[0] = chosen.astype(BF)
    r4[0] = rhs * (1.0 / NODE)

    def send_top(k):
        return remote(t4.at[0], t4.at[k], (s_t, r_t), k, cousin(k))

    def send_top_rhs(k):
        return remote(r4.at[0], r4.at[k], (s_q, r_q), k, cousin(k))

    each(4, lambda k: send_top(k).start())
    each(4, lambda k: send_top_rhs(k).start())

    def add_gram(k, total):
        send_gram(k).wait_recv()
        return total + gr[k].astype(F32)

    def add_couple(k, total):
        send_couple(k).wait_recv()
        return total + cr[k].astype(F32)

    total = lax.fori_loop(1, COLS, add_gram, pg[col].astype(F32))
    diagonal = iota((SLAB, RANK), 0) + col * SLAB == iota((SLAB, RANK), 1)
    out_share[0, :, 0:RANK] = total * (1.0 / NODE) + jnp.where(diagonal, ridge[...], 0.0)
    total = lax.fori_loop(1, COLS, add_couple, pc[col].astype(F32))
    out_share[0, :, RANK:] = total * (1.0 / NODE)
    result = chosen + tops[pl.ds(pl.multiple_of(col * SLAB, SLAB), SLAB), :]

    def add_top(k, totals):
        send_top(k).wait_recv()
        send_top_rhs(k).wait_recv()
        return totals[0] + t4[k].astype(F32), totals[1] + r4[k]

    result, rhs = lax.fori_loop(1, 4, add_top, (result, r4[0]))
    out_top[0] = result
    out_rhs[...] = jnp.concatenate([rhs[0:1], rhs[1:2]], 1)

    each(COLS, finish((send_couple, send_chosen)))
    each(4, finish((send_top, send_top_rhs)))


SHAPES = ((1, SLAB, 2 * RANK), (1, SLAB, RANK), (1, RANK))


def exchange(merged, ridge, *smalls):
    return pl.pallas_call(
        exchange_kernel,
        out_shape=tuple(pltpu.VMEM(shape, F32) for shape in SHAPES),
        in_specs=[VMEM, VMEM] + [ANYWHERE] * 4,
        out_specs=[VMEM] * 3,
        scratch_shapes=[
            pltpu.VMEM((1, RANK), jnp.int32),
            pltpu.VMEM((1, F), F32),
            pltpu.VMEM((8, RANK), jnp.int32),
            pltpu.VMEM((4, RANK), jnp.int32),
            pltpu.VMEM((8, 128), F32),
            pltpu.VMEM((LEAVES, F, PER), BF),
            pltpu.VMEM((LEAVES, 8, 128), F32),
            pltpu.VMEM((LEAVES, F, PER), BF),
            pltpu.VMEM((LEAVES, 8, 128), F32),
            pltpu.VMEM((LEAVES, RANK, PER), BF),
            pltpu.VMEM((LEAVES, 16, PER), BF),
            pltpu.VMEM((COLS, F, RANK), BF),
            pltpu.VMEM((F, RANK), BF),
            pltpu.VMEM((4, F, RANK), BF),
            pltpu.VMEM((2 * RANK, 256), BF),
            pltpu.VMEM((LEAVES // 2, RANK + 16, PER), BF),
            pltpu.VMEM((LEAVES // 2, RANK + 16, PER), BF),
            pltpu.VMEM((RANK, PER), BF),
            pltpu.VMEM((RANK, PER), BF),
            pltpu.VMEM((RANK + 16, RANK), F32),
            pltpu.VMEM((RANK, RANK), F32),
            pltpu.VMEM((RANK, RANK), BF),
            pltpu.VMEM((RANK, 2 * RANK), BF),
            pltpu.VMEM((RANK, 4 * RANK), BF),
            pltpu.VMEM((RANK, 128), F32),
            pltpu.VMEM((RANK, RANK), F32),
            pltpu.VMEM((COLS, SLAB, RANK), BF),
            pltpu.VMEM((COLS, SLAB, RANK), BF),
            pltpu.VMEM((COLS, SLAB, RANK), BF),
            pltpu.VMEM((COLS, SLAB, RANK), BF),
            pltpu.VMEM((COLS, SLAB, RANK), BF),
            pltpu.VMEM((COLS, SLAB, RANK), BF),
            pltpu.VMEM((8, 128), F32),
            pltpu.VMEM((COLS, 8, 128), F32),
            pltpu.VMEM((4, SLAB, RANK), BF),
            pltpu.VMEM((4, 8, 128), F32),
            *dma(LEAVES),
            *dma(LEAVES),
            *dma(COLS),
            *dma(4),
            *dma(COLS),
            *dma(COLS),
            *dma(COLS),
            *dma(COLS),
            *dma(4),
            *dma(4),
            pltpu.SemaphoreType.DMA((5,)),
        ],
        compiler_params=params(0, 40),
        name="exchange",
    )(merged, ridge, *in_hbm(*smalls))


def stream(samples, pivots, ridge, *smalls):
    return pl.pallas_call(
        stream_kernel,
        out_shape=(
            *(pltpu.VMEM(shape, F32) for shape in SHAPES),
            jax.ShapeDtypeStruct((1,), jnp.int32),
        ),
        in_specs=[ANYWHERE, VMEM, VMEM, VMEM, VMEM] + [ANYWHERE] * 3,
        out_specs=[VMEM] * 3 + [pl.BlockSpec(memory_space=pltpu.SMEM)],
        scratch_shapes=[
            pltpu.VMEM((F, ROWS), BF),
            pltpu.VMEM((ROWS // 128, 128), F32),
            pltpu.VMEM((CHUNKS, 8, CHUNK), F32),
            pltpu.VMEM((LEAVES, 128), F32),
            pltpu.VMEM((LEAVES, 128), F32),
            pltpu.VMEM((ROWS + 16, WIDE), F32),
            pltpu.VMEM((LEAVES, 8, 128), jnp.int32),
            pltpu.SMEM((LEAVES, 8, 128), jnp.int32),
            pltpu.VMEM((LEAVES, 1, RANK), jnp.int32),
            pltpu.VMEM((LEAVES, SLOTS, 128), BF),
            pltpu.VMEM((LEAVES, SLOTS, 128), BF),
            pltpu.VMEM((1, F), F32),
            pltpu.VMEM((8, RANK), jnp.int32),
            pltpu.VMEM((4, RANK), jnp.int32),
            pltpu.VMEM((8, 128), F32),
            pltpu.VMEM((LEAVES, F, PER), BF),
            pltpu.VMEM((LEAVES, 8, 128), F32),
            pltpu.VMEM((LEAVES, F, PER), BF),
            pltpu.VMEM((LEAVES, 8, 128), F32),
            pltpu.VMEM((LEAVES, 16, PER), BF),
            pltpu.VMEM((COLS, F, RANK), BF),
            pltpu.VMEM((F, RANK), BF),
            pltpu.VMEM((4, F, RANK), BF),
            pltpu.VMEM((2 * RANK, 256), BF),
            pltpu.VMEM((LEAVES // 2, RANK + 16, PER), BF),
            pltpu.VMEM((LEAVES // 2, RANK + 16, PER), BF),
            pltpu.VMEM((RANK, PER), BF),
            pltpu.VMEM((RANK, PER), BF),
            pltpu.VMEM((RANK + 16, RANK), F32),
            pltpu.VMEM((RANK, RANK), F32),
            pltpu.VMEM((RANK, RANK), BF),
            pltpu.VMEM((RANK, 2 * RANK), BF),
            pltpu.VMEM((RANK, 4 * RANK), BF),
            pltpu.VMEM((RANK, 128), F32),
            pltpu.VMEM((RANK, RANK), F32),
            pltpu.VMEM((COLS, SLAB, RANK), BF),
            pltpu.VMEM((COLS, SLAB, RANK), BF),
            pltpu.VMEM((COLS, SLAB, RANK), BF),
            pltpu.VMEM((COLS, SLAB, RANK), BF),
            pltpu.VMEM((COLS, SLAB, RANK), BF),
            pltpu.VMEM((COLS, SLAB, RANK), BF),
            pltpu.VMEM((8, 128), F32),
            pltpu.VMEM((COLS, 8, 128), F32),
            pltpu.VMEM((4, SLAB, RANK), BF),
            pltpu.VMEM((4, 8, 128), F32),
            *dma(LEAVES),
            *dma(LEAVES),
            *dma(LEAVES),
            *dma(LEAVES),
            *dma(COLS),
            *dma(4),
            *dma(COLS),
            *dma(COLS),
            *dma(COLS),
            *dma(COLS),
            *dma(4),
            *dma(4),
            pltpu.SemaphoreType.DMA((5,)),
        ],
        compiler_params=params(1, 40),
        name="stream",
    )(*in_hbm(*samples, pivots), ridge, *in_hbm(*smalls))


def emit_kernel(*refs):
    ins, outs, sem = refs[:3], refs[3:6], refs[6]
    copies = [pltpu.make_async_copy(a, b, sem.at[k]) for k, (a, b) in enumerate(zip(ins, outs))]
    for copy in copies:
        copy.start()
    for copy in copies:
        copy.wait()


def emit(results):
    return pl.pallas_call(
        emit_kernel,
        out_shape=tuple(jax.ShapeDtypeStruct(shape, F32) for shape in SHAPES),
        in_specs=[VMEM] * 3,
        out_specs=[ANYWHERE] * 3,
        scratch_shapes=[pltpu.SemaphoreType.DMA((3,))],
        compiler_params=params(),
        name="emit",
    )(*results)


def local(features, targets, owner, length_scales, ridge, leaf_pivots, parent_pivots, top_pivots):
    samples = (features, targets.reshape(ROWS // 128, 128), owner.reshape(ROWS // 128, 128))
    ridge = ridge.reshape(1, 1)
    smalls = (length_scales.reshape(1, F), parent_pivots, top_pivots)
    *results, flag = stream(samples, leaf_pivots, ridge, *smalls)

    def again():
        return tuple(emit(exchange(pack(*samples), ridge, leaf_pivots, *smalls)))

    return lax.switch(flag[0], [lambda: tuple(emit(results)), again])


def solution(mesh):
    return jax.shard_map(
        local,
        mesh=mesh,
        in_specs=(
            P(None, ("leaf", "col")),
            P(("leaf", "col")),
            P(("leaf", "col")),
            P(),
            P(),
            P("leaf", None),
            P(),
            P(),
        ),
        out_specs=(P("leaf", "col", None), P("leaf", "col", None), P("leaf", None)),
        check_vma=False,
    )
```

```python
import functools
import math

import jax
import jax.numpy as jnp
from jax import lax
from jax.experimental import pallas as pl
from jax.experimental.pallas import tpu as pltpu
from jax.sharding import PartitionSpec as P

F = 48
RANK = 256
ROWS = 8192
LEAVES = 16
COLS = 8
OWNERS = 128
PACKET = 64
PER = ROWS // LEAVES
CHUNK = 256
CHUNKS = ROWS // CHUNK
WINDOW = 40
REGION = PER + WINDOW
TILE = 32
TILES = PER // TILE
PIECES = 6
AT_ONCE = 128 // TILES
SLOTS = 16
WHICH = 50
FULL = 51
WIDE = 64
SLAB = RANK // COLS
NODE = ROWS * COLS
LOG2E = math.log2(math.e)
BF = jnp.bfloat16
F32 = jnp.float32
NT = (((1,), (1,)), ((), ()))
MESH = pl.DeviceIdType.MESH


def dma(count):
    return [pltpu.SemaphoreType.DMA((count,))] * 2


def params(number=None, limit=24):
    if number is None:
        return pltpu.CompilerParams(vmem_limit_bytes=limit * 2**20)
    return pltpu.CompilerParams(
        collective_id=number, has_side_effects=True, vmem_limit_bytes=limit * 2**20
    )


ANYWHERE = pl.BlockSpec(memory_space=pl.ANY)
VMEM = pl.BlockSpec(memory_space=pltpu.VMEM)


def iota(shape, axis):
    return lax.broadcasted_iota(jnp.int32, shape, axis)


def dot(a, b):
    return jnp.dot(a, b, preferred_element_type=F32)


def dot_nt(a, b):
    return lax.dot_general(a, b, NT, preferred_element_type=F32)


def row_pair(two):
    return jnp.concatenate([two[0:1], two[1:2]], 1)


def pack_kernel(
    feat_hbm, target, owner, zbuf, feat, goals, rows, ybuf, table, scal, sem, feat_sem
):
    bring = pltpu.make_async_copy(feat_hbm, feat, feat_sem)
    bring.start()
    goals[...] = target[...].astype(F32)
    before = (iota((CHUNK, CHUNK), 0) < iota((CHUNK, CHUNK), 1)).astype(F32).astype(BF)
    weights = jnp.concatenate([before, jnp.ones((CHUNK, 128), BF)], 1)
    lane = iota((LEAVES, 128), 1)

    def ranks(t, carry):
        seen, seen_leaf, most = carry
        own = row_pair(owner[pl.ds(2 * t, 2), :])
        leaf = own // 8
        is_own = iota((OWNERS, CHUNK), 0) == own
        is_leaf = iota((LEAVES, CHUNK), 0) == leaf
        is_after = iota((LEAVES, CHUNK), 0) > leaf
        marks = jnp.concatenate(
            [m.astype(F32).astype(BF) for m in (is_own, is_leaf, is_after)], 0
        )
        sums = dot(marks, weights)
        counts = sums[:OWNERS, CHUNK:]
        leaf_counts = sums[OWNERS : OWNERS + LEAVES, CHUNK:]
        base = sums[OWNERS + LEAVES :, CHUNK:]
        prior = sums[:OWNERS, :CHUNK] + jnp.concatenate([seen, seen], 1)
        rank = jnp.sum(jnp.where(is_own, prior, 0.0), 0, keepdims=True)
        place = sums[OWNERS : OWNERS + LEAVES, :CHUNK] + jnp.concatenate([base, base], 1)
        place = jnp.sum(jnp.where(is_leaf, place, 0.0), 0, keepdims=True)
        tag = (own % 8).astype(F32) * PACKET + rank - (PER // 2)
        rows[t, 0:1, :] = place
        rows[t, 1:2, :] = row_pair(goals[pl.ds(2 * t, 2), :])
        rows[t, 2:3, :] = tag
        here = lane == t
        table[0:LEAVES, :] = jnp.where(here, seen_leaf.astype(jnp.int32), table[0:LEAVES, :])
        table[LEAVES : 2 * LEAVES, :] = jnp.where(
            here, base.astype(jnp.int32), table[LEAVES : 2 * LEAVES, :]
        )
        return seen + counts, seen_leaf + leaf_counts, jnp.maximum(most, leaf_counts)

    table[0:LEAVES, :] = jnp.full((LEAVES, 128), PER, jnp.int32)
    zero = jnp.zeros((LEAVES, 128), F32)
    _, _, most = lax.fori_loop(
        0, CHUNKS, ranks, (jnp.zeros((OWNERS, 128), F32), zero, zero), unroll=16
    )
    most = jnp.broadcast_to(jnp.max(most, 0, keepdims=True), (8, 128))
    table[2 * LEAVES :, :] = most.astype(jnp.int32)
    move = pltpu.make_async_copy(table, scal, sem)
    move.start()
    bring.wait()

    def sort(t, _):
        start = pl.multiple_of(t * CHUNK, CHUNK)
        row = iota((16, CHUNK), 0)
        place, goal, tag = rows[t, 0:1, :], rows[t, 1:2, :], rows[t, 2:3, :]
        extra = jnp.where(row == 0, goal, jnp.where(row == 1, tag, 0.0)).astype(BF)
        joined = jnp.concatenate([feat[:, pl.ds(start, CHUNK)], extra], 0)
        chosen = (iota((CHUNK, CHUNK), 0) == place.astype(jnp.int32)).astype(F32).astype(BF)
        ybuf[pl.ds(start, CHUNK), :] = dot_nt(chosen, joined)
        return 0

    lax.fori_loop(0, CHUNKS, sort, 0, unroll=8)
    move.wait()
    widest = scal[2 * LEAVES, 0]

    @pl.when(widest <= WINDOW)
    def quick():
        def merge(t, _):
            for i in range(LEAVES):
                source = t * CHUNK + scal[LEAVES + i, t]
                goal = i * REGION + scal[i, t]
                zbuf[pl.ds(goal, WINDOW), :] = ybuf[pl.ds(source, WINDOW), :]
            return 0

        lax.fori_loop(0, CHUNKS, merge, 0, unroll=4)

    @pl.when(widest > WINDOW)
    def slow():
        def merge(index, _):
            t = index // LEAVES
            i = index % LEAVES
            source = t * CHUNK + scal[LEAVES + i, t]
            first = scal[i, t]
            count = scal[i, t + 1] - first

            def part(k, _):
                rows = ybuf[pl.ds(source + 8 * k, 8), :]
                zbuf[pl.ds(i * REGION + first + 8 * k, 8), :] = rows
                return 0

            lax.fori_loop(0, (count + 7) // 8, part, 0)
            return 0

        lax.fori_loop(0, CHUNKS * LEAVES, merge, 0)


def in_hbm(*arrays):
    return [pltpu.with_memory_space_constraint(a, pltpu.HBM) for a in arrays]


def pack(features, targets, owner):
    return pl.pallas_call(
        pack_kernel,
        out_shape=pltpu.VMEM((LEAVES * REGION, WIDE), F32),
        in_specs=[ANYWHERE, VMEM, VMEM],
        out_specs=VMEM,
        scratch_shapes=[
            pltpu.VMEM((F, ROWS), BF),
            pltpu.VMEM((ROWS // 128, 128), F32),
            pltpu.VMEM((CHUNKS, 8, CHUNK), F32),
            pltpu.VMEM((ROWS + WINDOW, WIDE), F32),
            pltpu.VMEM((40, 128), jnp.int32),
            pltpu.SMEM((40, 128), jnp.int32),
            pltpu.SemaphoreType.DMA,
            pltpu.SemaphoreType.DMA,
        ],
        compiler_params=params(),
        name="pack",
    )(*in_hbm(features, targets, owner))


def split3(x):
    high = x.astype(BF)
    rest = x - high.astype(F32)
    mid = rest.astype(BF)
    return high, mid, (rest - mid.astype(F32)).astype(BF)


def stack16(parts, width):
    row = iota((16, width), 0)
    block = jnp.zeros((16, width), F32)
    for k, part in enumerate(parts):
        block = jnp.where(row == k, part if isinstance(part, float) else part.astype(F32), block)
    return block.astype(BF)


def half_norm(points, scale):
    return jnp.sum(points * points * (0.5 * scale), 0, keepdims=True)


def point_side(points, scale):
    high, mid, low = split3(-half_norm(points, scale))
    return stack16([high, mid, low, 1.0, 1.0, 1.0], points.shape[1])


def skel_side(skel, scale):
    width = skel.shape[1]
    high, mid, low = split3(skel * scale)
    extra = stack16([1.0, 1.0, 1.0, *split3(-half_norm(skel, scale))], width)
    parts = [p.astype(F32) for p in (high, mid, low, extra)]
    fill = jnp.zeros((256 - 3 * F - 16, width), F32)
    return jnp.concatenate([*parts, fill], 0).T.astype(BF)


def select_row(table, row):
    hit = iota(table.shape, 0) == row
    return jnp.sum(jnp.where(hit, table.astype(F32), 0.0), 0, keepdims=True)


def to_column(row):
    return jnp.broadcast_to(row, (128, row.shape[1])).T


def across(column, width):
    return jnp.concatenate([column] * (width // 128), 1)


def place_of(leaf, col):
    return dict(device_id=(leaf, col), device_id_type=MESH)


def mate(k):
    leaf, col = lax.axis_index("leaf"), lax.axis_index("col")
    to = (leaf + k) % LEAVES
    cross = (to // 8 + leaf // 8) % 2
    return place_of(to, col + cross * (1 - 2 * (col % 2)))


def beside(k):
    leaf, col = lax.axis_index("leaf"), lax.axis_index("col")
    return place_of(leaf, (col + k) % COLS)


def cousin(k):
    leaf, col = lax.axis_index("leaf"), lax.axis_index("col")
    return place_of(leaf - leaf % 4 + (leaf + k) % 4, col)


def each(count, step, unroll=1):
    lax.fori_loop(1, count, lambda k, _: (step(k), 0)[1], 0, unroll=unroll)


def rem(a, b):
    return lax.rem(jnp.int32(a), jnp.int32(b))


def turn_of(n):
    n = jnp.int32(n)
    odd = lax.rem(n, jnp.int32(2))
    half = lax.div(n + odd, jnp.int32(2))
    return lax.rem(odd * half + (1 - odd) * (LEAVES - half), jnp.int32(LEAVES))


def remote(src, dst, sems, k, peer):
    return pltpu.make_async_remote_copy(src, dst, sems[0].at[k], sems[1].at[k], **peer)


def top_index(parent, top, group):
    top_row = select_row(top[...], group)
    below = jnp.concatenate([select_row(parent[...], 2 * group + r) for r in range(2)], 1)
    number = iota((RANK, 2 * RANK), 1)
    below = below + jnp.where(iota((1, 2 * RANK), 1) >= RANK, 2.0 * RANK, 0.0)
    hit = across(to_column(top_row), 2 * RANK) == number.astype(F32)
    index = jnp.sum(jnp.where(hit, below, 0.0), 1, keepdims=True)
    return jnp.broadcast_to(index, (RANK, 128))


def exchange_kernel(
    merged, ridge, pivots_hbm, scales_hbm, parent_hbm, top_hbm, out_share, out_top, out_rhs,
    pivots, scales, parent, top, spare, feat, aux, rx, ra, hot, side, sk, mine, sk4, left,
    even, odd, other_even, other_odd, gram, couple, rows, columns, fours, index, tops,
    pg, gr, pc, cr, pt, qr, rs, rr, t4, r4,
    s_f, r_f, s_a, r_a, s_k, r_k, s_4, r_4, s_p, r_p, s_c, r_c, s_o, r_o, s_r, r_r, s_t, r_t, s_q, r_q, local,
):
    leaf = lax.axis_index("leaf")
    col = lax.axis_index("col")
    quarter = leaf % 4
    sibling = quarter + 1 - 2 * (quarter % 2)
    barrier = pltpu.get_barrier_semaphore()
    each(LEAVES, lambda k: pl.semaphore_signal(barrier, inc=1, **mate(k)))
    each(COLS, lambda k: pl.semaphore_signal(barrier, inc=1, **beside(k)))
    smalls = [
        pltpu.make_async_copy(a, b, local.at[k])
        for k, (a, b) in enumerate(
            [(pivots_hbm, pivots), (scales_hbm, scales), (parent_hbm, parent), (top_hbm, top)]
        )
    ]
    for copy in smalls:
        copy.start()

    eye = (iota((WIDE, WIDE), 0) == iota((WIDE, WIDE), 1)).astype(F32).astype(BF)

    def turn(k):
        start = pl.multiple_of((leaf + k) % LEAVES * REGION, 8)
        turned = dot_nt(eye, merged[pl.ds(start, PER), :].astype(BF))
        feat[k] = turned[:F].astype(BF)
        aux[k] = jnp.concatenate(
            [turned[F + r : F + r + 1, 128 * c : 128 * c + 128] for r in range(2) for c in range(4)], 0
        )

    def send_feat(k):
        return remote(feat.at[k], rx.at[k], (s_f, r_f), k, mate(k))

    def send_aux(k):
        return remote(aux.at[k], ra.at[k], (s_a, r_a), k, mate(k))

    def four(j, _):
        steps = [turn_of(lax.rem(4 * j + r, LEAVES)) for r in range(1, 5)]
        for k in steps:
            turn(k)
        pl.when(j == 0)(lambda: pl.semaphore_wait(barrier, LEAVES + COLS - 2))
        for send in (send_aux, send_feat):
            for k in steps[:3]:
                send(k).start()
            pl.when(j < 3)(lambda: send(steps[3]).start())
        return 0

    lax.fori_loop(0, LEAVES // 4, four, 0)
    rx[0] = feat[0]
    ra[0] = aux[0]

    for copy in smalls:
        copy.wait()
    spare[...] = jnp.ones((8, 128), F32)
    spare[0:1, 0:F] = scales[...]
    inverse = 1.0 / to_column(spare[0:1, :])[:F]
    scale = inverse * inverse * LOG2E
    scale2 = across(scale, RANK)
    scale4 = across(scale, PER)

    place = pivots[...]
    within = place % ROWS
    block = within // PACKET
    key = (block // COLS) * PER + (place // ROWS) * PACKET + within % PACKET
    holder = block % COLS
    crossed = (block // COLS) // 8 != leaf // 8
    holder = jnp.where(crossed, holder + 1 - 2 * (holder % 2), holder)
    key = jnp.where(holder == col, key, -PER)
    key = across(to_column(key.astype(F32)), PER)

    def mark(k):
        source = (leaf + LEAVES - k) % LEAVES
        tags = ra[k, 4:8, :]
        tag = jnp.concatenate([tags[r : r + 1] for r in range(4)], 1)
        wanted = tag + (PER // 2 + source * PER).astype(F32)
        hot[k] = (key == wanted).astype(F32).astype(BF)

    def mark_next(n, _):
        k = turn_of(n)
        pl.when(n > 0)(lambda: send_aux(k).wait_recv())
        mark(k)
        return 0

    lax.fori_loop(0, LEAVES, mark_next, 0)

    index[...] = top_index(parent, top, leaf // 4)
    index2 = across(index[...], 2 * RANK)
    number = iota((RANK, 2 * RANK), 1)
    base = (quarter * RANK).astype(F32)
    other = (sibling * RANK).astype(F32)
    chosen = index2[:, :RANK] == iota((RANK, RANK), 1).astype(F32) + base
    rows[...] = chosen.astype(F32).astype(BF)
    lanes = number.astype(F32) + jnp.where(number < RANK, base, other - RANK)
    columns[...] = (index2 == lanes).astype(F32).astype(BF)
    chosen = across(index[...], 4 * RANK) == iota((RANK, 4 * RANK), 1).astype(F32)
    fours[...] = chosen.astype(F32).astype(BF)

    def pick(j, total):
        steps = [turn_of(4 * j + r) for r in range(4)]
        pl.when(j > 0)(lambda: send_feat(steps[0]).wait_recv())
        for k in steps[1:]:
            send_feat(k).wait_recv()
        for k in steps:
            total = total + dot_nt(hot[k], rx[k])
        return total

    picked = lax.fori_loop(0, LEAVES // 4, pick, jnp.zeros((RANK, F), F32))
    picked = jnp.concatenate([picked, jnp.zeros((RANK, 128 - F), F32)], 1).T[:F]
    sk[0] = picked.astype(BF)

    def send_skel(k):
        return remote(sk.at[0], sk.at[k], (s_k, r_k), k, beside(k))

    each(COLS, lambda k: send_skel(k).start())

    def norms(k, _):
        side[k] = point_side(rx[k].astype(F32), scale4)
        return 0

    lax.fori_loop(0, LEAVES, norms, 0)

    def add_skel(k, total):
        send_skel(k).wait_recv()
        return total + sk[k].astype(F32)

    picked = lax.fori_loop(1, COLS, add_skel, picked)
    mine[...] = picked.astype(BF)
    sk4[quarter] = picked.astype(BF)

    def send_four(k):
        return remote(mine, sk4.at[quarter], (s_4, r_4), k, cousin(k))

    each(4, lambda k: send_four(k).start())
    left[0:RANK, :] = skel_side(picked, scale2)

    def block_of(k, out, begin):
        p = rx[k]
        fill = jnp.zeros((256 - 3 * F - 16, PER), BF)
        right = jnp.concatenate([p, p, p, side[k], fill], 0)
        power = dot(left[begin : begin + RANK, :], right)
        out[0:RANK, :] = jnp.exp2(jnp.minimum(power, 0.0)).astype(BF)

    def own_of(k, out):
        block_of(k, out, 0)
        value = jnp.concatenate([ra[k, r : r + 1, :] for r in range(4)], 1)
        out[RANK:, :] = jnp.broadcast_to(value, (16, PER)).astype(BF)

    def gram_of(u):
        gram[...] += dot_nt(u[...], u[0:RANK, :])

    def couple_of(v, u):
        couple[...] += dot_nt(v[...], u[0:RANK, :])

    last = LEAVES // 2 - 1

    def own_two(j, _):
        own_of(2 * j, even.at[j])
        gram_of(odd.at[(j + last) % (last + 1)])
        own_of(2 * j + 1, odd.at[j])
        gram_of(even.at[j])
        return 0

    def other_two(j, _):
        block_of(2 * j, other_even, RANK)
        couple_of(other_odd, odd.at[(j + last) % (last + 1)])
        block_of(2 * j + 1, other_odd, RANK)
        couple_of(other_even, even.at[j])
        return 0

    gram[...] = jnp.zeros_like(gram)
    couple[...] = jnp.zeros_like(couple)
    odd[last] = jnp.zeros((RANK + 16, PER), BF)
    other_odd[...] = jnp.zeros_like(other_odd)
    lax.fori_loop(0, last + 1, own_two, 0)
    gram_of(odd.at[last])

    def send_gram(k):
        return remote(pg.at[(col + k) % COLS], gr.at[k], (s_p, r_p), k, beside(k))

    def send_couple(k):
        return remote(pc.at[(col + k) % COLS], cr.at[k], (s_c, r_c), k, beside(k))

    def send_chosen(k):
        return remote(pt.at[(col + k) % COLS], qr.at[k], (s_o, r_o), k, beside(k))

    def send_rhs(k):
        return remote(rs, rr.at[k], (s_r, r_r), k, beside(k))

    part = gram[0:RANK, :].astype(BF)
    for k in range(COLS):
        pg[k] = part[k * SLAB : (k + 1) * SLAB]
    rhs = gram[RANK : RANK + 1, :]
    rhs = jnp.sum(dot_nt(stack16(split3(rhs), RANK), rows[...]), 0, keepdims=True)
    rs[...] = jnp.zeros_like(rs)
    rs[0:1, :] = rhs[:, :128]
    rs[1:2, :] = rhs[:, 128:]
    each(COLS, lambda k: send_gram(k).start())
    each(COLS, lambda k: send_rhs(k).start())
    tops[...] = dot_nt(dot(rows[...], part).astype(BF), columns[:, 0:RANK])

    each(4, lambda k: remote(mine, sk4.at[(quarter + 4 - k) % 4], (s_4, r_4), k, cousin(k)).wait_recv())
    left[RANK:, :] = skel_side(sk4[sibling].astype(F32), scale2)
    lax.fori_loop(0, last + 1, other_two, 0)
    couple_of(other_odd, odd.at[last])

    part = couple[...].astype(BF)
    chosen = dot_nt(dot_nt(rows[...], part).astype(BF), columns[:, RANK:]) + tops[...]
    chosen = chosen.astype(BF)
    for k in range(COLS):
        pt[k] = chosen[k * SLAB : (k + 1) * SLAB]
    each(COLS, lambda k: send_chosen(k).start())
    part = couple[...].T.astype(BF)
    for k in range(COLS):
        pc[k] = part[k * SLAB : (k + 1) * SLAB]
    each(COLS, lambda k: send_couple(k).start())

    whole = jnp.concatenate([sk4[k] for k in range(4)], 1)
    points = dot_nt(whole, fours[...])
    fill = jnp.zeros((256 - 3 * F - 16, RANK), BF)
    points_b = points.astype(BF)
    right = jnp.concatenate([points_b, points_b, points_b, point_side(points, scale2), fill], 0)
    value = jnp.exp2(jnp.minimum(dot(skel_side(points, scale2), right), 0.0))
    crossing = (across(index[...], RANK) >= 2.0 * RANK) != (index[...].T[0:1, :] >= 2.0 * RANK)
    square = iota((RANK, RANK), 0) == iota((RANK, RANK), 1)
    tops[...] = jnp.where(crossing, value, 0.0) + jnp.where(square, ridge[...], 0.0)

    def finish(sends):
        return lambda k: [send(k).wait_send() for send in sends]

    each(LEAVES, finish((send_aux, send_feat)))
    each(COLS, finish((send_skel, send_gram, send_rhs)))
    each(4, finish((send_four,)))

    def add_chosen(k, totals):
        send_chosen(k).wait_recv()
        send_rhs(k).wait_recv()
        return totals[0] + qr[k].astype(F32), totals[1] + rr[k]

    chosen, rhs = lax.fori_loop(1, COLS, add_chosen, (pt[col].astype(F32), rs[...]))
    chosen = chosen * (1.0 / NODE)
    t4[0] = chosen.astype(BF)
    r4[0] = rhs * (1.0 / NODE)

    def send_top(k):
        return remote(t4.at[0], t4.at[k], (s_t, r_t), k, cousin(k))

    def send_top_rhs(k):
        return remote(r4.at[0], r4.at[k], (s_q, r_q), k, cousin(k))

    each(4, lambda k: send_top(k).start())
    each(4, lambda k: send_top_rhs(k).start())

    def add_gram(k, total):
        send_gram(k).wait_recv()
        return total + gr[k].astype(F32)

    def add_couple(k, total):
        send_couple(k).wait_recv()
        return total + cr[k].astype(F32)

    total = lax.fori_loop(1, COLS, add_gram, pg[col].astype(F32))
    diagonal = iota((SLAB, RANK), 0) + col * SLAB == iota((SLAB, RANK), 1)
    out_share[0, :, 0:RANK] = total * (1.0 / NODE) + jnp.where(diagonal, ridge[...], 0.0)
    total = lax.fori_loop(1, COLS, add_couple, pc[col].astype(F32))
    out_share[0, :, RANK:] = total * (1.0 / NODE)
    result = chosen + tops[pl.ds(pl.multiple_of(col * SLAB, SLAB), SLAB), :]

    def add_top(k, totals):
        send_top(k).wait_recv()
        send_top_rhs(k).wait_recv()
        return totals[0] + t4[k].astype(F32), totals[1] + r4[k]

    result, rhs = lax.fori_loop(1, 4, add_top, (result, r4[0]))
    out_top[0] = result
    out_rhs[...] = jnp.concatenate([rhs[0:1], rhs[1:2]], 1)

    each(COLS, finish((send_couple, send_chosen)))
    each(4, finish((send_top, send_top_rhs)))


def stream_kernel(
    feat_hbm, target, owner, pivots, ridge, scales_hbm, parent_hbm, top_hbm,
    out_share, out_top, out_rhs, flag,
    feat_in, goals, ranked, starts, bases, ybuf, table, scal, held, slots, came, scales, parent, top, spare,
    feat, aux, rx, ra, side, sk, mine, sk4, left, even, odd, other_even, other_odd, gram, couple,
    rows, columns, fours, index, tops, pg, gr, pc, cr, pt, qr, rs, rr, t4, r4,
    s_v, r_v, s_s, r_s, s_f, r_f, s_a, r_a, s_k, r_k, s_4, r_4, s_p, r_p, s_c, r_c, s_o, r_o,
    s_r, r_r, s_t, r_t, s_q, r_q, local,
):
    leaf = lax.axis_index("leaf")
    col = lax.axis_index("col")
    quarter = leaf % 4
    sibling = quarter + 1 - 2 * (quarter % 2)
    barrier = pltpu.get_barrier_semaphore()
    each(LEAVES, lambda k: pl.semaphore_signal(barrier, inc=1, **mate(k)))
    each(COLS, lambda k: pl.semaphore_signal(barrier, inc=1, **beside(k)))
    bring = pltpu.make_async_copy(feat_hbm, feat_in, local.at[3])
    bring.start()
    smalls = [
        pltpu.make_async_copy(a, b, local.at[k])
        for k, (a, b) in enumerate([(scales_hbm, scales), (parent_hbm, parent), (top_hbm, top)])
    ]
    for copy in smalls:
        copy.start()

    def send_pivots(k):
        return remote(pivots, held.at[k], (s_v, r_v), k, mate(k))

    def send_slots(k):
        return remote(slots.at[k], came.at[k], (s_s, r_s), k, mate(k))

    def send_feat(k):
        return remote(feat.at[k], rx.at[k], (s_f, r_f), k, mate(k))

    def send_aux(k):
        return remote(aux.at[k], ra.at[k], (s_a, r_a), k, mate(k))

    def send_skel(k):
        return remote(sk.at[0], sk.at[k], (s_k, r_k), k, beside(k))

    goals[...] = target[...].astype(F32)
    before = (iota((CHUNK, CHUNK), 0) < iota((CHUNK, CHUNK), 1)).astype(F32).astype(BF)
    weights = jnp.concatenate([before, jnp.ones((CHUNK, 128), BF)], 1)
    lane = iota((LEAVES, 128), 1)

    def rank(t, carry):
        seen, seen_leaf = carry
        own = row_pair(owner[pl.ds(2 * t, 2), :])
        group = own // 8
        is_own = iota((OWNERS, CHUNK), 0) == own
        is_leaf = iota((LEAVES, CHUNK), 0) == group
        is_after = iota((LEAVES, CHUNK), 0) > group
        marks = jnp.concatenate([m.astype(F32).astype(BF) for m in (is_own, is_leaf, is_after)], 0)
        sums = dot(marks, weights)
        leaf_counts = sums[OWNERS : OWNERS + LEAVES, CHUNK:]
        base = sums[OWNERS + LEAVES :, CHUNK:]
        prior = sums[:OWNERS, :CHUNK] + jnp.concatenate([seen, seen], 1)
        place = jnp.sum(jnp.where(is_own, prior, 0.0), 0, keepdims=True)
        order = sums[OWNERS : OWNERS + LEAVES, :CHUNK] + jnp.concatenate([base, base], 1)
        ranked[t, 0:1, :] = jnp.sum(jnp.where(is_leaf, order, 0.0), 0, keepdims=True)
        ranked[t, 1:2, :] = row_pair(goals[pl.ds(2 * t, 2), :])
        ranked[t, 2:3, :] = own.astype(F32) * PACKET + place
        starts[...] = jnp.where(lane == t, seen_leaf, starts[...])
        bases[...] = jnp.where(lane == t, base, bases[...])
        return seen + sums[:OWNERS, CHUNK:], seen_leaf + leaf_counts

    starts[...] = jnp.zeros_like(starts)
    bases[...] = jnp.zeros_like(bases)
    lax.fori_loop(
        0, CHUNKS, rank, (jnp.zeros((OWNERS, 128), F32), jnp.zeros((LEAVES, 128), F32)), unroll=16
    )

    rest = jnp.zeros((128 - LEAVES, 128), F32)
    start_of = jnp.concatenate([starts[...], rest], 0).T[:CHUNKS]
    base_of = jnp.concatenate([bases[...], rest], 0).T[:CHUNKS]
    high = jnp.where(start_of >= 256.0, 256.0, 0.0)
    columns_of = jnp.concatenate([high, start_of - high, base_of], 0).astype(BF)
    chunk = iota((CHUNKS, 128), 0).astype(F32)
    first = (iota((1, 128), 1) % TILES * TILE).astype(F32)
    full = jnp.zeros((1, 128), F32)
    table[...] = jnp.zeros_like(table)
    for g in range(LEAVES // AT_ONCE):
        one = iota((128, 128), 0) == iota((128, 128), 1) // TILES + g * AT_ONCE
        spread_out = dot(columns_of, one.astype(F32).astype(BF))
        begin = spread_out[:CHUNKS] + spread_out[CHUNKS : 2 * CHUNKS]
        place = spread_out[2 * CHUNKS :] + chunk * CHUNK
        passed = (begin <= first) & (chunk > 0.0)
        current = jnp.sum(jnp.where(passed, 1.0, 0.0), 0, keepdims=True)
        for r in range(PIECES + 1):
            here = chunk == current + r
            row = jnp.sum(jnp.where(here, place, 0.0), 0, keepdims=True)
            edge = jnp.sum(jnp.where(here, begin, 0.0), 0, keepdims=True)
            edge = jnp.where(current + r < CHUNKS, edge, float(PER)) - first
            if r == PIECES:
                full = jnp.maximum(full, jnp.where(edge < TILE, 1.0, 0.0))
                continue
            if r:
                edge = jnp.clip(edge, 0.0, float(TILE))
                table[g, PIECES + r : PIECES + r + 1, :] = edge.astype(jnp.int32)
            row = jnp.clip(jnp.where(current + r < CHUNKS, row - edge, 0.0), 0.0, float(ROWS))
            table[g, r : r + 1, :] = row.astype(jnp.int32)
    full = jnp.broadcast_to(jnp.max(full, 1, keepdims=True), (1, 128))
    tell = pltpu.make_async_copy(table, scal, local.at[4])
    tell.start()

    held[0] = pivots[...]
    pl.semaphore_wait(barrier, LEAVES + COLS - 2)
    each(LEAVES, lambda k: send_pivots(k).start())

    def joined_of(t):
        row = iota((16, CHUNK), 0)
        extra = jnp.where(row == 0, ranked[t, 1:2, :], 0.0).astype(BF)
        return jnp.concatenate([feat_in[:, pl.ds(pl.multiple_of(t * CHUNK, CHUNK), CHUNK)], extra], 0)

    def sort(t, _):
        place = ranked[t, 0:1, :].astype(jnp.int32)
        chosen = (iota((CHUNK, CHUNK), 0) == place).astype(F32).astype(BF)
        ybuf[pl.ds(pl.multiple_of(t * CHUNK, CHUNK), CHUNK), :] = dot_nt(chosen, joined_of(t))
        return 0

    bring.wait()
    lax.fori_loop(0, CHUNKS, sort, 0, unroll=8)
    ybuf[ROWS:, :] = jnp.zeros((TILE, WIDE), F32)
    tell.wait()

    eye = (iota((WIDE, WIDE), 0) == iota((WIDE, WIDE), 1)).astype(F32).astype(BF)
    sub = iota((TILE, WIDE), 0)

    def packet(k):
        to = lax.rem(leaf + k, jnp.int32(LEAVES))
        group = lax.div(to, jnp.int32(AT_ONCE))
        lane = lax.rem(to, jnp.int32(AT_ONCE)) * TILES

        def piece(r, q):
            return ybuf[pl.ds(jnp.clip(scal[group, r, lane + q], 0, ROWS), TILE), :]

        tiles = []
        for q in range(TILES):
            tile = piece(0, q)
            for r in range(1, PIECES):
                tile = jnp.where(sub >= scal[group, PIECES + r, lane + q], piece(r, q), tile)
            tiles.append(tile)
        turned = dot_nt(eye, jnp.concatenate(tiles, 0).astype(BF))
        feat[k] = turned[:F].astype(BF)
        aux[k] = jnp.concatenate([turned[F : F + 1, 128 * c : 128 * c + 128] for c in range(4)] * 2, 0)

    def give(j, _):
        steps = turn_of(2 * j + 1), turn_of(rem(2 * j + 2, LEAVES))
        for k in steps:
            packet(k)
        send_aux(steps[0]).start()
        send_feat(steps[0]).start()

        @pl.when(j < LEAVES // 2 - 1)
        def second():
            send_aux(steps[1]).start()
            send_feat(steps[1]).start()

        return 0

    lax.fori_loop(0, 2, give, 0)

    each(LEAVES, lambda k: send_pivots(k).wait_recv())
    place = jnp.concatenate([held[(LEAVES - b) % LEAVES] for b in range(LEAVES)], 0)
    home = place % ROWS // PACKET
    number = ((leaf + iota((LEAVES, RANK), 0)) % LEAVES) * 8 + place // ROWS
    number = (number * PACKET + place % PACKET).astype(F32)
    valid = home == leaf * COLS + col
    order = dot(valid.astype(F32).astype(BF), before)
    order = jnp.where(valid, order, -1.0)

    def spread(table):
        return jnp.concatenate(
            [jnp.broadcast_to(table[b : b + 1], (SLOTS, RANK)) for b in range(LEAVES)], 0
        )

    shape = (LEAVES * SLOTS, RANK)
    hit = spread(order) == (iota(shape, 0) % SLOTS).astype(F32)
    wanted = jnp.sum(jnp.where(hit, spread(number) + 1.0, 0.0), 1, keepdims=True) - 1.0
    which = jnp.sum(jnp.where(hit, iota(shape, 1).astype(F32) + 1.0, 0.0), 1, keepdims=True) - 1.0
    wanted = jnp.broadcast_to(wanted, (LEAVES * SLOTS, CHUNK))

    def take(t, total):
        chosen = (wanted == ranked[t, 2:3, :]).astype(F32).astype(BF)
        rest = jnp.zeros((128 - WIDE, CHUNK), BF)
        return total + dot_nt(chosen, jnp.concatenate([joined_of(t), rest], 0))

    shape = (LEAVES * SLOTS, 128)
    taken = lax.fori_loop(0, CHUNKS, take, jnp.zeros(shape, F32), unroll=4)
    taken = jnp.where(iota(shape, 1) == WHICH, which, taken)
    taken = jnp.where(iota(shape, 1) == FULL, full, taken).astype(BF)
    for b in range(LEAVES):
        slots[b] = taken[b * SLOTS : (b + 1) * SLOTS]
    came[0] = slots[0]
    each(LEAVES, lambda k: send_slots(k).start())
    lax.fori_loop(2, 5, give, 0)

    each(LEAVES, lambda k: send_slots(k).wait_recv())
    got = jnp.concatenate([came[b] for b in range(LEAVES)], 0).astype(F32)
    chosen = got[:, WHICH : WHICH + 1] == iota((LEAVES * SLOTS, RANK), 1).astype(F32)
    picked = dot(got.T[:F].astype(BF), chosen.astype(F32).astype(BF))
    full = jnp.broadcast_to(jnp.max(got[:, FULL : FULL + 1], 0, keepdims=True), (1, 128))
    sk[0] = picked.astype(BF)
    each(COLS, lambda k: send_skel(k).start())
    lax.fori_loop(5, LEAVES // 2, give, 0)
    rx[0] = feat[0]
    ra[0] = aux[0]

    largest = jnp.zeros((OWNERS, 1), F32)
    for b in range(LEAVES):
        held_here = (iota((OWNERS, RANK), 0) == home[b : b + 1]).astype(F32)
        largest = jnp.maximum(largest, jnp.sum(held_here, 1, keepdims=True))

    for copy in smalls:
        copy.wait()
    spare[...] = jnp.ones((8, 128), F32)
    spare[0:1, 0:F] = scales[...]
    inverse = 1.0 / to_column(spare[0:1, :])[:F]
    scale = inverse * inverse * LOG2E
    scale2 = across(scale, RANK)
    scale4 = across(scale, PER)

    index[...] = top_index(parent, top, leaf // 4)
    index2 = across(index[...], 2 * RANK)
    number = iota((RANK, 2 * RANK), 1)
    base = (quarter * RANK).astype(F32)
    other = (sibling * RANK).astype(F32)
    chosen = index2[:, :RANK] == iota((RANK, RANK), 1).astype(F32) + base
    rows[...] = chosen.astype(F32).astype(BF)
    lanes = number.astype(F32) + jnp.where(number < RANK, base, other - RANK)
    columns[...] = (index2 == lanes).astype(F32).astype(BF)
    chosen = across(index[...], 4 * RANK) == iota((RANK, 4 * RANK), 1).astype(F32)
    fours[...] = chosen.astype(F32).astype(BF)

    def norms(k):
        side[k] = point_side(rx[k].astype(F32), scale4)

    def add_skel(k, total):
        send_skel(k).wait_recv()
        return total + sk[k].astype(F32)

    picked = lax.fori_loop(1, COLS, add_skel, picked)
    mine[...] = picked.astype(BF)
    sk4[quarter] = picked.astype(BF)

    def send_four(k):
        return remote(mine, sk4.at[quarter], (s_4, r_4), k, cousin(k))

    each(4, lambda k: send_four(k).start())
    left[0:RANK, :] = skel_side(picked, scale2)

    def block_of(k, out, begin):
        p = rx[k]
        fill = jnp.zeros((256 - 3 * F - 16, PER), BF)
        right = jnp.concatenate([p, p, p, side[k], fill], 0)
        power = dot(left[begin : begin + RANK, :], right)
        out[0:RANK, :] = jnp.exp2(jnp.minimum(power, 0.0)).astype(BF)

    def own_of(k, out):
        block_of(k, out, 0)
        value = ra[k]
        value = jnp.concatenate([value[r : r + 1] for r in range(4)], 1)
        out[RANK:, :] = jnp.broadcast_to(value, (16, PER)).astype(BF)

    def gram_of(u):
        gram[...] += dot_nt(u[...], u[0:RANK, :])

    def couple_of(v, u):
        couple[...] += dot_nt(v[...], u[0:RANK, :])

    last = LEAVES // 2 - 1

    def own_two(j, _):
        k, l = turn_of(2 * j), turn_of(2 * j + 1)
        pl.when(j > 0)(lambda: receive(k))
        receive(l)
        norms(k)
        norms(l)
        own_of(k, even.at[j])
        gram_of(odd.at[rem(j + last, last + 1)])
        own_of(l, odd.at[j])
        gram_of(even.at[j])
        return 0

    def receive(k):
        send_aux(k).wait_recv()
        send_feat(k).wait_recv()

    def other_two(j, _):
        block_of(turn_of(2 * j), other_even, RANK)
        couple_of(other_odd, odd.at[rem(j + last, last + 1)])
        block_of(turn_of(2 * j + 1), other_odd, RANK)
        couple_of(other_even, even.at[j])
        return 0

    gram[...] = jnp.zeros_like(gram)
    couple[...] = jnp.zeros_like(couple)
    odd[last] = jnp.zeros((RANK + 16, PER), BF)
    other_odd[...] = jnp.zeros_like(other_odd)
    def send_gram(k):
        return remote(pg.at[(col + k) % COLS], gr.at[k], (s_p, r_p), k, beside(k))

    def send_couple(k):
        return remote(pc.at[(col + k) % COLS], cr.at[k], (s_c, r_c), k, beside(k))

    def send_chosen(k):
        return remote(pt.at[(col + k) % COLS], qr.at[k], (s_o, r_o), k, beside(k))

    def send_rhs(k):
        return remote(rs, rr.at[k], (s_r, r_r), k, beside(k))

    def sibling_side():
        each(4, lambda k: remote(mine, sk4.at[(quarter + 4 - k) % 4], (s_4, r_4), k, cousin(k)).wait_recv())
        left[RANK:, :] = skel_side(sk4[sibling].astype(F32), scale2)

    def give_gram():
        gram_of(odd.at[last])
        part = gram[0:RANK, :].astype(BF)
        for k in range(COLS):
            pg[k] = part[k * SLAB : (k + 1) * SLAB]
        rhs = gram[RANK : RANK + 1, :]
        rhs = jnp.sum(dot_nt(stack16(split3(rhs), RANK), rows[...]), 0, keepdims=True)
        rs[...] = jnp.zeros_like(rs)
        rs[0:1, :] = rhs[:, :128]
        rs[1:2, :] = rhs[:, 128:]
        rs[2:3, :] = full
        each(COLS, lambda k: send_gram(k).start())
        each(COLS, lambda k: send_rhs(k).start())
        tops[...] = dot_nt(dot(rows[...], part).astype(BF), columns[:, 0:RANK])

    def half(h, _):
        pairs = LEAVES // 4
        lax.fori_loop(pairs * h, pairs * (h + 1), own_two, 0)
        pl.when(h == 0)(sibling_side)
        pl.when(h == 1)(give_gram)
        lax.fori_loop(pairs * h, pairs * (h + 1), other_two, 0)
        return 0

    lax.fori_loop(0, 2, half, 0)
    couple_of(other_odd, odd.at[last])

    part = couple[...].astype(BF)
    chosen = dot_nt(dot_nt(rows[...], part).astype(BF), columns[:, RANK:]) + tops[...]
    chosen = chosen.astype(BF)
    for k in range(COLS):
        pt[k] = chosen[k * SLAB : (k + 1) * SLAB]
    each(COLS, lambda k: send_chosen(k).start())
    part = couple[...].T.astype(BF)
    for k in range(COLS):
        pc[k] = part[k * SLAB : (k + 1) * SLAB]
    each(COLS, lambda k: send_couple(k).start())

    whole = jnp.concatenate([sk4[k] for k in range(4)], 1)
    points = dot_nt(whole, fours[...])
    fill = jnp.zeros((256 - 3 * F - 16, RANK), BF)
    points_b = points.astype(BF)
    right = jnp.concatenate([points_b, points_b, points_b, point_side(points, scale2), fill], 0)
    value = jnp.exp2(jnp.minimum(dot(skel_side(points, scale2), right), 0.0))
    crossing = (across(index[...], RANK) >= 2.0 * RANK) != (index[...].T[0:1, :] >= 2.0 * RANK)
    square = iota((RANK, RANK), 0) == iota((RANK, RANK), 1)
    tops[...] = jnp.where(crossing, value, 0.0) + jnp.where(square, ridge[...], 0.0)

    def finish(sends):
        return lambda k: [send(k).wait_send() for send in sends]

    each(LEAVES, finish((send_pivots, send_slots, send_aux, send_feat)))
    each(COLS, finish((send_skel, send_gram, send_rhs)))
    each(4, finish((send_four,)))

    def add_chosen(k, totals):
        send_chosen(k).wait_recv()
        send_rhs(k).wait_recv()
        return totals[0] + qr[k].astype(F32), totals[1] + rr[k]

    chosen, rhs = lax.fori_loop(1, COLS, add_chosen, (pt[col].astype(F32), rs[...]))
    over = jnp.maximum(jnp.max(rhs[2:3, :]), jnp.max(largest) - SLOTS)
    flag[0] = (over > 0.0).astype(jnp.int32)
    chosen = chosen * (1.0 / NODE)
    t4[0] = chosen.astype(BF)
    r4[0] = rhs * (1.0 / NODE)

    def send_top(k):
        return remote(t4.at[0], t4.at[k], (s_t, r_t), k, cousin(k))

    def send_top_rhs(k):
        return remote(r4.at[0], r4.at[k], (s_q, r_q), k, cousin(k))

    each(4, lambda k: send_top(k).start())
    each(4, lambda k: send_top_rhs(k).start())

    def add_gram(k, total):
        send_gram(k).wait_recv()
        return total + gr[k].astype(F32)

    def add_couple(k, total):
        send_couple(k).wait_recv()
        return total + cr[k].astype(F32)

    total = lax.fori_loop(1, COLS, add_gram, pg[col].astype(F32))
    diagonal = iota((SLAB, RANK), 0) + col * SLAB == iota((SLAB, RANK), 1)
    out_share[0, :, 0:RANK] = total * (1.0 / NODE) + jnp.where(diagonal, ridge[...], 0.0)
    total = lax.fori_loop(1, COLS, add_couple, pc[col].astype(F32))
    out_share[0, :, RANK:] = total * (1.0 / NODE)
    result = chosen + tops[pl.ds(pl.multiple_of(col * SLAB, SLAB), SLAB), :]

    def add_top(k, totals):
        send_top(k).wait_recv()
        send_top_rhs(k).wait_recv()
        return totals[0] + t4[k].astype(F32), totals[1] + r4[k]

    result, rhs = lax.fori_loop(1, 4, add_top, (result, r4[0]))
    out_top[0] = result
    out_rhs[...] = jnp.concatenate([rhs[0:1], rhs[1:2]], 1)

    each(COLS, finish((send_couple, send_chosen)))
    each(4, finish((send_top, send_top_rhs)))


SHAPES = ((1, SLAB, 2 * RANK), (1, SLAB, RANK), (1, RANK))


def exchange(merged, ridge, *smalls):
    return pl.pallas_call(
        exchange_kernel,
        out_shape=tuple(pltpu.VMEM(shape, F32) for shape in SHAPES),
        in_specs=[VMEM, VMEM] + [ANYWHERE] * 4,
        out_specs=[VMEM] * 3,
        scratch_shapes=[
            pltpu.VMEM((1, RANK), jnp.int32),
            pltpu.VMEM((1, F), F32),
            pltpu.VMEM((8, RANK), jnp.int32),
            pltpu.VMEM((4, RANK), jnp.int32),
            pltpu.VMEM((8, 128), F32),
            pltpu.VMEM((LEAVES, F, PER), BF),
            pltpu.VMEM((LEAVES, 8, 128), F32),
            pltpu.VMEM((LEAVES, F, PER), BF),
            pltpu.VMEM((LEAVES, 8, 128), F32),
            pltpu.VMEM((LEAVES, RANK, PER), BF),
            pltpu.VMEM((LEAVES, 16, PER), BF),
            pltpu.VMEM((COLS, F, RANK), BF),
            pltpu.VMEM((F, RANK), BF),
            pltpu.VMEM((4, F, RANK), BF),
            pltpu.VMEM((2 * RANK, 256), BF),
            pltpu.VMEM((LEAVES // 2, RANK + 16, PER), BF),
            pltpu.VMEM((LEAVES // 2, RANK + 16, PER), BF),
            pltpu.VMEM((RANK, PER), BF),
            pltpu.VMEM((RANK, PER), BF),
            pltpu.VMEM((RANK + 16, RANK), F32),
            pltpu.VMEM((RANK, RANK), F32),
            pltpu.VMEM((RANK, RANK), BF),
            pltpu.VMEM((RANK, 2 * RANK), BF),
            pltpu.VMEM((RANK, 4 * RANK), BF),
            pltpu.VMEM((RANK, 128), F32),
            pltpu.VMEM((RANK, RANK), F32),
            pltpu.VMEM((COLS, SLAB, RANK), BF),
            pltpu.VMEM((COLS, SLAB, RANK), BF),
            pltpu.VMEM((COLS, SLAB, RANK), BF),
            pltpu.VMEM((COLS, SLAB, RANK), BF),
            pltpu.VMEM((COLS, SLAB, RANK), BF),
            pltpu.VMEM((COLS, SLAB, RANK), BF),
            pltpu.VMEM((8, 128), F32),
            pltpu.VMEM((COLS, 8, 128), F32),
            pltpu.VMEM((4, SLAB, RANK), BF),
            pltpu.VMEM((4, 8, 128), F32),
            *dma(LEAVES),
            *dma(LEAVES),
            *dma(COLS),
            *dma(4),
            *dma(COLS),
            *dma(COLS),
            *dma(COLS),
            *dma(COLS),
            *dma(4),
            *dma(4),
            pltpu.SemaphoreType.DMA((5,)),
        ],
        compiler_params=params(0, 40),
        name="exchange",
    )(merged, ridge, *in_hbm(*smalls))


def stream(samples, pivots, ridge, *smalls):
    return pl.pallas_call(
        stream_kernel,
        out_shape=(
            *(pltpu.VMEM(shape, F32) for shape in SHAPES),
            jax.ShapeDtypeStruct((1,), jnp.int32),
        ),
        in_specs=[ANYWHERE, VMEM, VMEM, VMEM, VMEM] + [ANYWHERE] * 3,
        out_specs=[VMEM] * 3 + [pl.BlockSpec(memory_space=pltpu.SMEM)],
        scratch_shapes=[
            pltpu.VMEM((F, ROWS), BF),
            pltpu.VMEM((ROWS // 128, 128), F32),
            pltpu.VMEM((CHUNKS, 8, CHUNK), F32),
            pltpu.VMEM((LEAVES, 128), F32),
            pltpu.VMEM((LEAVES, 128), F32),
            pltpu.VMEM((ROWS + TILE, WIDE), F32),
            pltpu.VMEM((LEAVES // AT_ONCE, 16, 128), jnp.int32),
            pltpu.SMEM((LEAVES // AT_ONCE, 16, 128), jnp.int32),
            pltpu.VMEM((LEAVES, 1, RANK), jnp.int32),
            pltpu.VMEM((LEAVES, SLOTS, 128), BF),
            pltpu.VMEM((LEAVES, SLOTS, 128), BF),
            pltpu.VMEM((1, F), F32),
            pltpu.VMEM((8, RANK), jnp.int32),
            pltpu.VMEM((4, RANK), jnp.int32),
            pltpu.VMEM((8, 128), F32),
            pltpu.VMEM((LEAVES, F, PER), BF),
            pltpu.VMEM((LEAVES, 8, 128), F32),
            pltpu.VMEM((LEAVES, F, PER), BF),
            pltpu.VMEM((LEAVES, 8, 128), F32),
            pltpu.VMEM((LEAVES, 16, PER), BF),
            pltpu.VMEM((COLS, F, RANK), BF),
            pltpu.VMEM((F, RANK), BF),
            pltpu.VMEM((4, F, RANK), BF),
            pltpu.VMEM((2 * RANK, 256), BF),
            pltpu.VMEM((LEAVES // 2, RANK + 16, PER), BF),
            pltpu.VMEM((LEAVES // 2, RANK + 16, PER), BF),
            pltpu.VMEM((RANK, PER), BF),
            pltpu.VMEM((RANK, PER), BF),
            pltpu.VMEM((RANK + 16, RANK), F32),
            pltpu.VMEM((RANK, RANK), F32),
            pltpu.VMEM((RANK, RANK), BF),
            pltpu.VMEM((RANK, 2 * RANK), BF),
            pltpu.VMEM((RANK, 4 * RANK), BF),
            pltpu.VMEM((RANK, 128), F32),
            pltpu.VMEM((RANK, RANK), F32),
            pltpu.VMEM((COLS, SLAB, RANK), BF),
            pltpu.VMEM((COLS, SLAB, RANK), BF),
            pltpu.VMEM((COLS, SLAB, RANK), BF),
            pltpu.VMEM((COLS, SLAB, RANK), BF),
            pltpu.VMEM((COLS, SLAB, RANK), BF),
            pltpu.VMEM((COLS, SLAB, RANK), BF),
            pltpu.VMEM((8, 128), F32),
            pltpu.VMEM((COLS, 8, 128), F32),
            pltpu.VMEM((4, SLAB, RANK), BF),
            pltpu.VMEM((4, 8, 128), F32),
            *dma(LEAVES),
            *dma(LEAVES),
            *dma(LEAVES),
            *dma(LEAVES),
            *dma(COLS),
            *dma(4),
            *dma(COLS),
            *dma(COLS),
            *dma(COLS),
            *dma(COLS),
            *dma(4),
            *dma(4),
            pltpu.SemaphoreType.DMA((5,)),
        ],
        compiler_params=params(1, 40),
        name="stream",
    )(*in_hbm(*samples, pivots), ridge, *in_hbm(*smalls))


def emit_kernel(*refs):
    ins, outs, sem = refs[:3], refs[3:6], refs[6]
    copies = [pltpu.make_async_copy(a, b, sem.at[k]) for k, (a, b) in enumerate(zip(ins, outs))]
    for copy in copies:
        copy.start()
    for copy in copies:
        copy.wait()


def emit(results):
    return pl.pallas_call(
        emit_kernel,
        out_shape=tuple(jax.ShapeDtypeStruct(shape, F32) for shape in SHAPES),
        in_specs=[VMEM] * 3,
        out_specs=[ANYWHERE] * 3,
        scratch_shapes=[pltpu.SemaphoreType.DMA((3,))],
        compiler_params=params(),
        name="emit",
    )(*results)


def local(features, targets, owner, length_scales, ridge, leaf_pivots, parent_pivots, top_pivots):
    samples = (features, targets.reshape(ROWS // 128, 128), owner.reshape(ROWS // 128, 128))
    ridge = ridge.reshape(1, 1)
    smalls = (length_scales.reshape(1, F), parent_pivots, top_pivots)
    *results, flag = stream(samples, leaf_pivots, ridge, *smalls)

    def again():
        return tuple(emit(exchange(pack(*samples), ridge, leaf_pivots, *smalls)))

    return lax.switch(flag[0], [lambda: tuple(emit(results)), again])


def solution(mesh):
    return jax.shard_map(
        local,
        mesh=mesh,
        in_specs=(
            P(None, ("leaf", "col")),
            P(("leaf", "col")),
            P(("leaf", "col")),
            P(),
            P(),
            P("leaf", None),
            P(),
            P(),
        ),
        out_specs=(P("leaf", "col", None), P("leaf", "col", None), P("leaf", None)),
        check_vma=False,
    )
```

```python
import functools
import math

import jax
import jax.numpy as jnp
from jax import lax
from jax.experimental import pallas as pl
from jax.experimental.pallas import tpu as pltpu
from jax.sharding import PartitionSpec as P

F = 48
RANK = 256
ROWS = 8192
LEAVES = 16
COLS = 8
OWNERS = 128
PACKET = 64
PER = ROWS // LEAVES
CHUNK = 256
CHUNKS = ROWS // CHUNK
WINDOW = 40
REGION = PER + WINDOW
TILE = 32
TILES = PER // TILE
PIECES = 6
AT_ONCE = 128 // TILES
SLOTS = 16
WHICH = 50
FULL = 51
WIDE = 64
SLAB = RANK // COLS
NODE = ROWS * COLS
LOG2E = math.log2(math.e)
BF = jnp.bfloat16
F32 = jnp.float32
NT = (((1,), (1,)), ((), ()))
MESH = pl.DeviceIdType.MESH


def dma(count):
    return [pltpu.SemaphoreType.DMA((count,))] * 2


def params(number=None, limit=24):
    if number is None:
        return pltpu.CompilerParams(vmem_limit_bytes=limit * 2**20)
    return pltpu.CompilerParams(
        collective_id=number, has_side_effects=True, vmem_limit_bytes=limit * 2**20
    )


ANYWHERE = pl.BlockSpec(memory_space=pl.ANY)
VMEM = pl.BlockSpec(memory_space=pltpu.VMEM)


def iota(shape, axis):
    return lax.broadcasted_iota(jnp.int32, shape, axis)


def dot(a, b):
    return jnp.dot(a, b, preferred_element_type=F32)


def dot_nt(a, b):
    return lax.dot_general(a, b, NT, preferred_element_type=F32)


def row_pair(two):
    return jnp.concatenate([two[0:1], two[1:2]], 1)


def pack_kernel(
    feat_hbm, target, owner, zbuf, feat, goals, rows, ybuf, table, scal, sem, feat_sem
):
    bring = pltpu.make_async_copy(feat_hbm, feat, feat_sem)
    bring.start()
    goals[...] = target[...].astype(F32)
    before = (iota((CHUNK, CHUNK), 0) < iota((CHUNK, CHUNK), 1)).astype(F32).astype(BF)
    weights = jnp.concatenate([before, jnp.ones((CHUNK, 128), BF)], 1)
    lane = iota((LEAVES, 128), 1)

    def ranks(t, carry):
        seen, seen_leaf, most = carry
        own = row_pair(owner[pl.ds(2 * t, 2), :])
        leaf = own // 8
        is_own = iota((OWNERS, CHUNK), 0) == own
        is_leaf = iota((LEAVES, CHUNK), 0) == leaf
        is_after = iota((LEAVES, CHUNK), 0) > leaf
        marks = jnp.concatenate(
            [m.astype(F32).astype(BF) for m in (is_own, is_leaf, is_after)], 0
        )
        sums = dot(marks, weights)
        counts = sums[:OWNERS, CHUNK:]
        leaf_counts = sums[OWNERS : OWNERS + LEAVES, CHUNK:]
        base = sums[OWNERS + LEAVES :, CHUNK:]
        prior = sums[:OWNERS, :CHUNK] + jnp.concatenate([seen, seen], 1)
        rank = jnp.sum(jnp.where(is_own, prior, 0.0), 0, keepdims=True)
        place = sums[OWNERS : OWNERS + LEAVES, :CHUNK] + jnp.concatenate([base, base], 1)
        place = jnp.sum(jnp.where(is_leaf, place, 0.0), 0, keepdims=True)
        tag = (own % 8).astype(F32) * PACKET + rank - (PER // 2)
        rows[t, 0:1, :] = place
        rows[t, 1:2, :] = row_pair(goals[pl.ds(2 * t, 2), :])
        rows[t, 2:3, :] = tag
        here = lane == t
        table[0:LEAVES, :] = jnp.where(here, seen_leaf.astype(jnp.int32), table[0:LEAVES, :])
        table[LEAVES : 2 * LEAVES, :] = jnp.where(
            here, base.astype(jnp.int32), table[LEAVES : 2 * LEAVES, :]
        )
        return seen + counts, seen_leaf + leaf_counts, jnp.maximum(most, leaf_counts)

    table[0:LEAVES, :] = jnp.full((LEAVES, 128), PER, jnp.int32)
    zero = jnp.zeros((LEAVES, 128), F32)
    _, _, most = lax.fori_loop(
        0, CHUNKS, ranks, (jnp.zeros((OWNERS, 128), F32), zero, zero), unroll=16
    )
    most = jnp.broadcast_to(jnp.max(most, 0, keepdims=True), (8, 128))
    table[2 * LEAVES :, :] = most.astype(jnp.int32)
    move = pltpu.make_async_copy(table, scal, sem)
    move.start()
    bring.wait()

    def sort(t, _):
        start = pl.multiple_of(t * CHUNK, CHUNK)
        row = iota((16, CHUNK), 0)
        place, goal, tag = rows[t, 0:1, :], rows[t, 1:2, :], rows[t, 2:3, :]
        extra = jnp.where(row == 0, goal, jnp.where(row == 1, tag, 0.0)).astype(BF)
        joined = jnp.concatenate([feat[:, pl.ds(start, CHUNK)], extra], 0)
        chosen = (iota((CHUNK, CHUNK), 0) == place.astype(jnp.int32)).astype(F32).astype(BF)
        ybuf[pl.ds(start, CHUNK), :] = dot_nt(chosen, joined)
        return 0

    lax.fori_loop(0, CHUNKS, sort, 0, unroll=8)
    move.wait()
    widest = scal[2 * LEAVES, 0]

    @pl.when(widest <= WINDOW)
    def quick():
        def merge(t, _):
            for i in range(LEAVES):
                source = t * CHUNK + scal[LEAVES + i, t]
                goal = i * REGION + scal[i, t]
                zbuf[pl.ds(goal, WINDOW), :] = ybuf[pl.ds(source, WINDOW), :]
            return 0

        lax.fori_loop(0, CHUNKS, merge, 0, unroll=4)

    @pl.when(widest > WINDOW)
    def slow():
        def merge(index, _):
            t = index // LEAVES
            i = index % LEAVES
            source = t * CHUNK + scal[LEAVES + i, t]
            first = scal[i, t]
            count = scal[i, t + 1] - first

            def part(k, _):
                rows = ybuf[pl.ds(source + 8 * k, 8), :]
                zbuf[pl.ds(i * REGION + first + 8 * k, 8), :] = rows
                return 0

            lax.fori_loop(0, (count + 7) // 8, part, 0)
            return 0

        lax.fori_loop(0, CHUNKS * LEAVES, merge, 0)


def in_hbm(*arrays):
    return [pltpu.with_memory_space_constraint(a, pltpu.HBM) for a in arrays]


def pack(features, targets, owner):
    return pl.pallas_call(
        pack_kernel,
        out_shape=pltpu.VMEM((LEAVES * REGION, WIDE), F32),
        in_specs=[ANYWHERE, VMEM, VMEM],
        out_specs=VMEM,
        scratch_shapes=[
            pltpu.VMEM((F, ROWS), BF),
            pltpu.VMEM((ROWS // 128, 128), F32),
            pltpu.VMEM((CHUNKS, 8, CHUNK), F32),
            pltpu.VMEM((ROWS + WINDOW, WIDE), F32),
            pltpu.VMEM((40, 128), jnp.int32),
            pltpu.SMEM((40, 128), jnp.int32),
            pltpu.SemaphoreType.DMA,
            pltpu.SemaphoreType.DMA,
        ],
        compiler_params=params(),
        name="pack",
    )(*in_hbm(features, targets, owner))


def split3(x):
    high = x.astype(BF)
    rest = x - high.astype(F32)
    mid = rest.astype(BF)
    return high, mid, (rest - mid.astype(F32)).astype(BF)


def stack16(parts, width):
    row = iota((16, width), 0)
    block = jnp.zeros((16, width), F32)
    for k, part in enumerate(parts):
        block = jnp.where(row == k, part if isinstance(part, float) else part.astype(F32), block)
    return block.astype(BF)


def half_norm(points, scale):
    return jnp.sum(points * points * (0.5 * scale), 0, keepdims=True)


def point_side(points, scale):
    high, mid, low = split3(-half_norm(points, scale))
    return stack16([high, mid, low, 1.0, 1.0, 1.0], points.shape[1])


def skel_side(skel, scale):
    width = skel.shape[1]
    high, mid, low = split3(skel * scale)
    extra = stack16([1.0, 1.0, 1.0, *split3(-half_norm(skel, scale))], width)
    parts = [p.astype(F32) for p in (high, mid, low, extra)]
    fill = jnp.zeros((256 - 3 * F - 16, width), F32)
    return jnp.concatenate([*parts, fill], 0).T.astype(BF)


def select_row(table, row):
    hit = iota(table.shape, 0) == row
    return jnp.sum(jnp.where(hit, table.astype(F32), 0.0), 0, keepdims=True)


def to_column(row):
    return jnp.broadcast_to(row, (128, row.shape[1])).T


def across(column, width):
    return jnp.concatenate([column] * (width // 128), 1)


def place_of(leaf, col):
    return dict(device_id=(leaf, col), device_id_type=MESH)


def mate(k):
    leaf, col = lax.axis_index("leaf"), lax.axis_index("col")
    to = (leaf + k) % LEAVES
    cross = (to // 8 + leaf // 8) % 2
    return place_of(to, col + cross * (1 - 2 * (col % 2)))


def beside(k):
    leaf, col = lax.axis_index("leaf"), lax.axis_index("col")
    return place_of(leaf, (col + k) % COLS)


def cousin(k):
    leaf, col = lax.axis_index("leaf"), lax.axis_index("col")
    return place_of(leaf - leaf % 4 + (leaf + k) % 4, col)


def each(count, step, unroll=1):
    lax.fori_loop(1, count, lambda k, _: (step(k), 0)[1], 0, unroll=unroll)


def rem(a, b):
    return lax.rem(jnp.int32(a), jnp.int32(b))


def turn_of(n):
    n = jnp.int32(n)
    odd = lax.rem(n, jnp.int32(2))
    half = lax.div(n + odd, jnp.int32(2))
    return lax.rem(odd * half + (1 - odd) * (LEAVES - half), jnp.int32(LEAVES))


def remote(src, dst, sems, k, peer):
    return pltpu.make_async_remote_copy(src, dst, sems[0].at[k], sems[1].at[k], **peer)


def top_index(parent, top, group):
    top_row = select_row(top[...], group)
    below = jnp.concatenate([select_row(parent[...], 2 * group + r) for r in range(2)], 1)
    number = iota((RANK, 2 * RANK), 1)
    below = below + jnp.where(iota((1, 2 * RANK), 1) >= RANK, 2.0 * RANK, 0.0)
    hit = across(to_column(top_row), 2 * RANK) == number.astype(F32)
    index = jnp.sum(jnp.where(hit, below, 0.0), 1, keepdims=True)
    return jnp.broadcast_to(index, (RANK, 128))


def exchange_kernel(
    merged, ridge, pivots_hbm, scales_hbm, parent_hbm, top_hbm, out_share, out_top, out_rhs,
    pivots, scales, parent, top, spare, feat, aux, rx, ra, hot, side, sk, mine, sk4, left,
    even, odd, other_even, other_odd, gram, couple, rows, columns, fours, index, tops,
    pg, gr, pc, cr, pt, qr, rs, rr, t4, r4,
    s_f, r_f, s_a, r_a, s_k, r_k, s_4, r_4, s_p, r_p, s_c, r_c, s_o, r_o, s_r, r_r, s_t, r_t, s_q, r_q, local,
):
    leaf = lax.axis_index("leaf")
    col = lax.axis_index("col")
    quarter = leaf % 4
    sibling = quarter + 1 - 2 * (quarter % 2)
    barrier = pltpu.get_barrier_semaphore()
    each(LEAVES, lambda k: pl.semaphore_signal(barrier, inc=1, **mate(k)))
    each(COLS, lambda k: pl.semaphore_signal(barrier, inc=1, **beside(k)))
    smalls = [
        pltpu.make_async_copy(a, b, local.at[k])
        for k, (a, b) in enumerate(
            [(pivots_hbm, pivots), (scales_hbm, scales), (parent_hbm, parent), (top_hbm, top)]
        )
    ]
    for copy in smalls:
        copy.start()

    eye = (iota((WIDE, WIDE), 0) == iota((WIDE, WIDE), 1)).astype(F32).astype(BF)

    def turn(k):
        start = pl.multiple_of((leaf + k) % LEAVES * REGION, 8)
        turned = dot_nt(eye, merged[pl.ds(start, PER), :].astype(BF))
        feat[k] = turned[:F].astype(BF)
        aux[k] = jnp.concatenate(
            [turned[F + r : F + r + 1, 128 * c : 128 * c + 128] for r in range(2) for c in range(4)], 0
        )

    def send_feat(k):
        return remote(feat.at[k], rx.at[k], (s_f, r_f), k, mate(k))

    def send_aux(k):
        return remote(aux.at[k], ra.at[k], (s_a, r_a), k, mate(k))

    def four(j, _):
        steps = [turn_of(lax.rem(4 * j + r, LEAVES)) for r in range(1, 5)]
        for k in steps:
            turn(k)
        pl.when(j == 0)(lambda: pl.semaphore_wait(barrier, LEAVES + COLS - 2))
        for send in (send_aux, send_feat):
            for k in steps[:3]:
                send(k).start()
            pl.when(j < 3)(lambda: send(steps[3]).start())
        return 0

    lax.fori_loop(0, LEAVES // 4, four, 0)
    rx[0] = feat[0]
    ra[0] = aux[0]

    for copy in smalls:
        copy.wait()
    spare[...] = jnp.ones((8, 128), F32)
    spare[0:1, 0:F] = scales[...]
    inverse = 1.0 / to_column(spare[0:1, :])[:F]
    scale = inverse * inverse * LOG2E
    scale2 = across(scale, RANK)
    scale4 = across(scale, PER)

    place = pivots[...]
    within = place % ROWS
    block = within // PACKET
    key = (block // COLS) * PER + (place // ROWS) * PACKET + within % PACKET
    holder = block % COLS
    crossed = (block // COLS) // 8 != leaf // 8
    holder = jnp.where(crossed, holder + 1 - 2 * (holder % 2), holder)
    key = jnp.where(holder == col, key, -PER)
    key = across(to_column(key.astype(F32)), PER)

    def mark(k):
        source = (leaf + LEAVES - k) % LEAVES
        tags = ra[k, 4:8, :]
        tag = jnp.concatenate([tags[r : r + 1] for r in range(4)], 1)
        wanted = tag + (PER // 2 + source * PER).astype(F32)
        hot[k] = (key == wanted).astype(F32).astype(BF)

    def mark_next(n, _):
        k = turn_of(n)
        pl.when(n > 0)(lambda: send_aux(k).wait_recv())
        mark(k)
        return 0

    lax.fori_loop(0, LEAVES, mark_next, 0)

    index[...] = top_index(parent, top, leaf // 4)
    index2 = across(index[...], 2 * RANK)
    number = iota((RANK, 2 * RANK), 1)
    base = (quarter * RANK).astype(F32)
    other = (sibling * RANK).astype(F32)
    chosen = index2[:, :RANK] == iota((RANK, RANK), 1).astype(F32) + base
    rows[...] = chosen.astype(F32).astype(BF)
    lanes = number.astype(F32) + jnp.where(number < RANK, base, other - RANK)
    columns[...] = (index2 == lanes).astype(F32).astype(BF)
    chosen = across(index[...], 4 * RANK) == iota((RANK, 4 * RANK), 1).astype(F32)
    fours[...] = chosen.astype(F32).astype(BF)

    def pick(j, total):
        steps = [turn_of(4 * j + r) for r in range(4)]
        pl.when(j > 0)(lambda: send_feat(steps[0]).wait_recv())
        for k in steps[1:]:
            send_feat(k).wait_recv()
        for k in steps:
            total = total + dot_nt(hot[k], rx[k])
        return total

    picked = lax.fori_loop(0, LEAVES // 4, pick, jnp.zeros((RANK, F), F32))
    picked = jnp.concatenate([picked, jnp.zeros((RANK, 128 - F), F32)], 1).T[:F]
    sk[0] = picked.astype(BF)

    def send_skel(k):
        return remote(sk.at[0], sk.at[k], (s_k, r_k), k, beside(k))

    each(COLS, lambda k: send_skel(k).start())

    def norms(k, _):
        side[k] = point_side(rx[k].astype(F32), scale4)
        return 0

    lax.fori_loop(0, LEAVES, norms, 0)

    def add_skel(k, total):
        send_skel(k).wait_recv()
        return total + sk[k].astype(F32)

    picked = lax.fori_loop(1, COLS, add_skel, picked)
    mine[...] = picked.astype(BF)
    sk4[quarter] = picked.astype(BF)

    def send_four(k):
        return remote(mine, sk4.at[quarter], (s_4, r_4), k, cousin(k))

    each(4, lambda k: send_four(k).start())
    left[0:RANK, :] = skel_side(picked, scale2)

    def block_of(k, out, begin):
        p = rx[k]
        fill = jnp.zeros((256 - 3 * F - 16, PER), BF)
        right = jnp.concatenate([p, p, p, side[k], fill], 0)
        power = dot(left[begin : begin + RANK, :], right)
        out[0:RANK, :] = jnp.exp2(jnp.minimum(power, 0.0)).astype(BF)

    def own_of(k, out):
        block_of(k, out, 0)
        value = jnp.concatenate([ra[k, r : r + 1, :] for r in range(4)], 1)
        out[RANK:, :] = jnp.broadcast_to(value, (16, PER)).astype(BF)

    def gram_of(u):
        gram[...] += dot_nt(u[...], u[0:RANK, :])

    def couple_of(v, u):
        couple[...] += dot_nt(v[...], u[0:RANK, :])

    last = LEAVES // 2 - 1

    def own_two(j, _):
        own_of(2 * j, even.at[j])
        gram_of(odd.at[(j + last) % (last + 1)])
        own_of(2 * j + 1, odd.at[j])
        gram_of(even.at[j])
        return 0

    def other_two(j, _):
        block_of(2 * j, other_even, RANK)
        couple_of(other_odd, odd.at[(j + last) % (last + 1)])
        block_of(2 * j + 1, other_odd, RANK)
        couple_of(other_even, even.at[j])
        return 0

    gram[...] = jnp.zeros_like(gram)
    couple[...] = jnp.zeros_like(couple)
    odd[last] = jnp.zeros((RANK + 16, PER), BF)
    other_odd[...] = jnp.zeros_like(other_odd)
    lax.fori_loop(0, last + 1, own_two, 0)
    gram_of(odd.at[last])

    def send_gram(k):
        return remote(pg.at[(col + k) % COLS], gr.at[k], (s_p, r_p), k, beside(k))

    def send_couple(k):
        return remote(pc.at[(col + k) % COLS], cr.at[k], (s_c, r_c), k, beside(k))

    def send_chosen(k):
        return remote(pt.at[(col + k) % COLS], qr.at[k], (s_o, r_o), k, beside(k))

    def send_rhs(k):
        return remote(rs, rr.at[k], (s_r, r_r), k, beside(k))

    part = gram[0:RANK, :].astype(BF)
    for k in range(COLS):
        pg[k] = part[k * SLAB : (k + 1) * SLAB]
    rhs = gram[RANK : RANK + 1, :]
    rhs = jnp.sum(dot_nt(stack16(split3(rhs), RANK), rows[...]), 0, keepdims=True)
    rs[...] = jnp.zeros_like(rs)
    rs[0:1, :] = rhs[:, :128]
    rs[1:2, :] = rhs[:, 128:]
    each(COLS, lambda k: send_gram(k).start())
    each(COLS, lambda k: send_rhs(k).start())
    tops[...] = dot_nt(dot(rows[...], part).astype(BF), columns[:, 0:RANK])

    each(4, lambda k: remote(mine, sk4.at[(quarter + 4 - k) % 4], (s_4, r_4), k, cousin(k)).wait_recv())
    left[RANK:, :] = skel_side(sk4[sibling].astype(F32), scale2)
    lax.fori_loop(0, last + 1, other_two, 0)
    couple_of(other_odd, odd.at[last])

    part = couple[...].astype(BF)
    chosen = dot_nt(dot_nt(rows[...], part).astype(BF), columns[:, RANK:]) + tops[...]
    chosen = chosen.astype(BF)
    for k in range(COLS):
        pt[k] = chosen[k * SLAB : (k + 1) * SLAB]
    each(COLS, lambda k: send_chosen(k).start())
    part = couple[...].T.astype(BF)
    for k in range(COLS):
        pc[k] = part[k * SLAB : (k + 1) * SLAB]
    each(COLS, lambda k: send_couple(k).start())

    whole = jnp.concatenate([sk4[k] for k in range(4)], 1)
    points = dot_nt(whole, fours[...])
    fill = jnp.zeros((256 - 3 * F - 16, RANK), BF)
    points_b = points.astype(BF)
    right = jnp.concatenate([points_b, points_b, points_b, point_side(points, scale2), fill], 0)
    value = jnp.exp2(jnp.minimum(dot(skel_side(points, scale2), right), 0.0))
    crossing = (across(index[...], RANK) >= 2.0 * RANK) != (index[...].T[0:1, :] >= 2.0 * RANK)
    square = iota((RANK, RANK), 0) == iota((RANK, RANK), 1)
    tops[...] = jnp.where(crossing, value, 0.0) + jnp.where(square, ridge[...], 0.0)

    def finish(sends):
        return lambda k: [send(k).wait_send() for send in sends]

    each(LEAVES, finish((send_aux, send_feat)))
    each(COLS, finish((send_skel, send_gram, send_rhs)))
    each(4, finish((send_four,)))

    def add_chosen(k, totals):
        send_chosen(k).wait_recv()
        send_rhs(k).wait_recv()
        return totals[0] + qr[k].astype(F32), totals[1] + rr[k]

    chosen, rhs = lax.fori_loop(1, COLS, add_chosen, (pt[col].astype(F32), rs[...]))
    chosen = chosen * (1.0 / NODE)
    t4[0] = chosen.astype(BF)
    r4[0] = rhs * (1.0 / NODE)

    def send_top(k):
        return remote(t4.at[0], t4.at[k], (s_t, r_t), k, cousin(k))

    def send_top_rhs(k):
        return remote(r4.at[0], r4.at[k], (s_q, r_q), k, cousin(k))

    each(4, lambda k: send_top(k).start())
    each(4, lambda k: send_top_rhs(k).start())

    def add_gram(k, total):
        send_gram(k).wait_recv()
        return total + gr[k].astype(F32)

    def add_couple(k, total):
        send_couple(k).wait_recv()
        return total + cr[k].astype(F32)

    total = lax.fori_loop(1, COLS, add_gram, pg[col].astype(F32))
    diagonal = iota((SLAB, RANK), 0) + col * SLAB == iota((SLAB, RANK), 1)
    out_share[0, :, 0:RANK] = total * (1.0 / NODE) + jnp.where(diagonal, ridge[...], 0.0)
    total = lax.fori_loop(1, COLS, add_couple, pc[col].astype(F32))
    out_share[0, :, RANK:] = total * (1.0 / NODE)
    result = chosen + tops[pl.ds(pl.multiple_of(col * SLAB, SLAB), SLAB), :]

    def add_top(k, totals):
        send_top(k).wait_recv()
        send_top_rhs(k).wait_recv()
        return totals[0] + t4[k].astype(F32), totals[1] + r4[k]

    result, rhs = lax.fori_loop(1, 4, add_top, (result, r4[0]))
    out_top[0] = result
    out_rhs[...] = jnp.concatenate([rhs[0:1], rhs[1:2]], 1)

    each(COLS, finish((send_couple, send_chosen)))
    each(4, finish((send_top, send_top_rhs)))


FAR_FIRST = (12, 13, 4, 5, 11, 14, 3, 6, 10, 15, 2, 7, 9, 8, 1)


def stream_kernel(
    feat_hbm, target, owner, pivots, ridge, scales_hbm, parent_hbm, top_hbm,
    out_share, out_top, out_rhs, flag,
    feat_in, goals, ranked, starts, bases, ybuf, table, scal, held, slots, came, scales, parent, top, spare,
    feat, aux, rx, ra, side, sk, mine, sk4, left, even, odd, other_even, other_odd, gram, couple,
    rows, columns, fours, index, tops, pg, gr, pc, cr, pt, qr, rs, rr, t4, r4,
    s_v, r_v, s_s, r_s, s_f, r_f, s_a, r_a, s_k, r_k, s_4, r_4, s_p, r_p, s_c, r_c, s_o, r_o,
    s_r, r_r, s_t, r_t, s_q, r_q, local,
):
    leaf = lax.axis_index("leaf")
    col = lax.axis_index("col")
    quarter = leaf % 4
    sibling = quarter + 1 - 2 * (quarter % 2)
    barrier = pltpu.get_barrier_semaphore()
    each(LEAVES, lambda k: pl.semaphore_signal(barrier, inc=1, **mate(k)))
    each(COLS, lambda k: pl.semaphore_signal(barrier, inc=1, **beside(k)))
    bring = pltpu.make_async_copy(feat_hbm, feat_in, local.at[3])
    bring.start()
    smalls = [
        pltpu.make_async_copy(a, b, local.at[k])
        for k, (a, b) in enumerate([(scales_hbm, scales), (parent_hbm, parent), (top_hbm, top)])
    ]
    for copy in smalls:
        copy.start()

    def send_pivots(k):
        return remote(pivots, held.at[k], (s_v, r_v), k, mate(k))

    def send_slots(k):
        return remote(slots.at[k], came.at[k], (s_s, r_s), k, mate(k))

    def send_feat(k):
        return remote(feat.at[k], rx.at[k], (s_f, r_f), k, mate(k))

    def send_aux(k):
        return remote(aux.at[k], ra.at[k], (s_a, r_a), k, mate(k))

    def send_skel(k):
        return remote(sk.at[0], sk.at[k], (s_k, r_k), k, beside(k))

    goals[...] = target[...].astype(F32)
    before = (iota((CHUNK, CHUNK), 0) < iota((CHUNK, CHUNK), 1)).astype(F32).astype(BF)
    weights = jnp.concatenate([before, jnp.ones((CHUNK, 128), BF)], 1)
    lane = iota((LEAVES, 128), 1)

    def rank(t, carry):
        seen, seen_leaf = carry
        own = row_pair(owner[pl.ds(2 * t, 2), :])
        group = own // 8
        is_own = iota((OWNERS, CHUNK), 0) == own
        is_leaf = iota((LEAVES, CHUNK), 0) == group
        is_after = iota((LEAVES, CHUNK), 0) > group
        marks = jnp.concatenate([m.astype(F32).astype(BF) for m in (is_own, is_leaf, is_after)], 0)
        sums = dot(marks, weights)
        leaf_counts = sums[OWNERS : OWNERS + LEAVES, CHUNK:]
        base = sums[OWNERS + LEAVES :, CHUNK:]
        prior = sums[:OWNERS, :CHUNK] + jnp.concatenate([seen, seen], 1)
        place = jnp.sum(jnp.where(is_own, prior, 0.0), 0, keepdims=True)
        order = sums[OWNERS : OWNERS + LEAVES, :CHUNK] + jnp.concatenate([base, base], 1)
        ranked[t, 0:1, :] = jnp.sum(jnp.where(is_leaf, order, 0.0), 0, keepdims=True)
        ranked[t, 1:2, :] = row_pair(goals[pl.ds(2 * t, 2), :])
        ranked[t, 2:3, :] = own.astype(F32) * PACKET + place
        starts[...] = jnp.where(lane == t, seen_leaf, starts[...])
        bases[...] = jnp.where(lane == t, base, bases[...])
        return seen + sums[:OWNERS, CHUNK:], seen_leaf + leaf_counts

    starts[...] = jnp.zeros_like(starts)
    bases[...] = jnp.zeros_like(bases)
    seen = (jnp.zeros((OWNERS, 128), F32), jnp.zeros((LEAVES, 128), F32))
    seen = lax.fori_loop(0, CHUNKS // 2, rank, seen, unroll=16)

    held[0] = pivots[...]
    pl.semaphore_wait(barrier, LEAVES + COLS - 2)
    for k in FAR_FIRST:
        send_pivots(k).start()
    lax.fori_loop(CHUNKS // 2, CHUNKS, rank, seen, unroll=16)

    rest = jnp.zeros((128 - LEAVES, 128), F32)
    start_of = jnp.concatenate([starts[...], rest], 0).T[:CHUNKS]
    base_of = jnp.concatenate([bases[...], rest], 0).T[:CHUNKS]
    high = jnp.where(start_of >= 256.0, 256.0, 0.0)
    columns_of = jnp.concatenate([high, start_of - high, base_of], 0).astype(BF)
    chunk = iota((CHUNKS, 128), 0).astype(F32)
    first = (iota((1, 128), 1) % TILES * TILE).astype(F32)
    full = jnp.zeros((1, 128), F32)
    table[...] = jnp.zeros_like(table)
    for g in range(LEAVES // AT_ONCE):
        one = iota((128, 128), 0) == iota((128, 128), 1) // TILES + g * AT_ONCE
        spread_out = dot(columns_of, one.astype(F32).astype(BF))
        begin = spread_out[:CHUNKS] + spread_out[CHUNKS : 2 * CHUNKS]
        place = spread_out[2 * CHUNKS :] + chunk * CHUNK
        passed = (begin <= first) & (chunk > 0.0)
        current = jnp.sum(jnp.where(passed, 1.0, 0.0), 0, keepdims=True)
        for r in range(PIECES + 1):
            here = chunk == current + r
            row = jnp.sum(jnp.where(here, place, 0.0), 0, keepdims=True)
            edge = jnp.sum(jnp.where(here, begin, 0.0), 0, keepdims=True)
            edge = jnp.where(current + r < CHUNKS, edge, float(PER)) - first
            if r == PIECES:
                full = jnp.maximum(full, jnp.where(edge < TILE, 1.0, 0.0))
                continue
            if r:
                edge = jnp.clip(edge, 0.0, float(TILE))
                table[g, PIECES + r : PIECES + r + 1, :] = edge.astype(jnp.int32)
            row = jnp.clip(jnp.where(current + r < CHUNKS, row - edge, 0.0), 0.0, float(ROWS))
            table[g, r : r + 1, :] = row.astype(jnp.int32)
    full = jnp.broadcast_to(jnp.max(full, 1, keepdims=True), (1, 128))
    tell = pltpu.make_async_copy(table, scal, local.at[4])
    tell.start()

    def joined_of(t):
        row = iota((16, CHUNK), 0)
        extra = jnp.where(row == 0, ranked[t, 1:2, :], 0.0).astype(BF)
        return jnp.concatenate([feat_in[:, pl.ds(pl.multiple_of(t * CHUNK, CHUNK), CHUNK)], extra], 0)

    def sort(t, _):
        place = ranked[t, 0:1, :].astype(jnp.int32)
        chosen = (iota((CHUNK, CHUNK), 0) == place).astype(F32).astype(BF)
        ybuf[pl.ds(pl.multiple_of(t * CHUNK, CHUNK), CHUNK), :] = dot_nt(chosen, joined_of(t))
        return 0

    bring.wait()
    lax.fori_loop(0, CHUNKS, sort, 0, unroll=8)
    ybuf[ROWS:, :] = jnp.zeros((TILE, WIDE), F32)
    tell.wait()

    eye = (iota((WIDE, WIDE), 0) == iota((WIDE, WIDE), 1)).astype(F32).astype(BF)
    sub = iota((TILE, WIDE), 0)

    def packet(k):
        to = lax.rem(leaf + k, jnp.int32(LEAVES))
        group = lax.div(to, jnp.int32(AT_ONCE))
        lane = lax.rem(to, jnp.int32(AT_ONCE)) * TILES

        def piece(r, q):
            return ybuf[pl.ds(jnp.clip(scal[group, r, lane + q], 0, ROWS), TILE), :]

        tiles = []
        for q in range(TILES):
            tile = piece(0, q)
            for r in range(1, PIECES):
                tile = jnp.where(sub >= scal[group, PIECES + r, lane + q], piece(r, q), tile)
            tiles.append(tile)
        turned = dot_nt(eye, jnp.concatenate(tiles, 0).astype(BF))
        feat[k] = turned[:F].astype(BF)
        aux[k] = jnp.concatenate([turned[F : F + 1, 128 * c : 128 * c + 128] for c in range(4)] * 2, 0)

    def give(j, _):
        steps = turn_of(2 * j + 1), turn_of(rem(2 * j + 2, LEAVES))
        for k in steps:
            packet(k)
        send_aux(steps[0]).start()
        send_feat(steps[0]).start()

        @pl.when(j < LEAVES // 2 - 1)
        def second():
            send_aux(steps[1]).start()
            send_feat(steps[1]).start()

        return 0

    lax.fori_loop(0, 3, give, 0)

    each(LEAVES, lambda k: send_pivots(k).wait_recv())
    place = jnp.concatenate([held[(LEAVES - b) % LEAVES] for b in range(LEAVES)], 0)
    home = place % ROWS // PACKET
    number = ((leaf + iota((LEAVES, RANK), 0)) % LEAVES) * 8 + place // ROWS
    number = (number * PACKET + place % PACKET).astype(F32)
    valid = home == leaf * COLS + col
    order = dot(valid.astype(F32).astype(BF), before)
    order = jnp.where(valid, order, -1.0)

    def spread(table):
        return jnp.concatenate(
            [jnp.broadcast_to(table[b : b + 1], (SLOTS, RANK)) for b in range(LEAVES)], 0
        )

    shape = (LEAVES * SLOTS, RANK)
    hit = spread(order) == (iota(shape, 0) % SLOTS).astype(F32)
    wanted = jnp.sum(jnp.where(hit, spread(number) + 1.0, 0.0), 1, keepdims=True) - 1.0
    which = jnp.sum(jnp.where(hit, iota(shape, 1).astype(F32) + 1.0, 0.0), 1, keepdims=True) - 1.0
    wanted = jnp.broadcast_to(wanted, (LEAVES * SLOTS, CHUNK))

    def take(t, total):
        chosen = (wanted == ranked[t, 2:3, :]).astype(F32).astype(BF)
        rest = jnp.zeros((128 - WIDE, CHUNK), BF)
        return total + dot_nt(chosen, jnp.concatenate([joined_of(t), rest], 0))

    shape = (LEAVES * SLOTS, 128)
    taken = lax.fori_loop(0, CHUNKS, take, jnp.zeros(shape, F32), unroll=4)
    taken = jnp.where(iota(shape, 1) == WHICH, which, taken)
    taken = jnp.where(iota(shape, 1) == FULL, full, taken).astype(BF)
    for b in range(LEAVES):
        slots[b] = taken[b * SLOTS : (b + 1) * SLOTS]
    came[0] = slots[0]
    for k in FAR_FIRST:
        send_slots(k).start()
    lax.fori_loop(3, 6, give, 0)

    each(LEAVES, lambda k: send_slots(k).wait_recv())
    got = jnp.concatenate([came[b] for b in range(LEAVES)], 0).astype(F32)
    chosen = got[:, WHICH : WHICH + 1] == iota((LEAVES * SLOTS, RANK), 1).astype(F32)
    picked = dot(got.T[:F].astype(BF), chosen.astype(F32).astype(BF))
    full = jnp.broadcast_to(jnp.max(got[:, FULL : FULL + 1], 0, keepdims=True), (1, 128))
    sk[0] = picked.astype(BF)
    for k in (5, 3, 4, 6, 2, 7, 1):
        send_skel(k).start()
    lax.fori_loop(6, LEAVES // 2, give, 0)
    rx[0] = feat[0]
    ra[0] = aux[0]

    largest = jnp.zeros((OWNERS, 1), F32)
    for b in range(LEAVES):
        held_here = (iota((OWNERS, RANK), 0) == home[b : b + 1]).astype(F32)
        largest = jnp.maximum(largest, jnp.sum(held_here, 1, keepdims=True))

    for copy in smalls:
        copy.wait()
    spare[...] = jnp.ones((8, 128), F32)
    spare[0:1, 0:F] = scales[...]
    inverse = 1.0 / to_column(spare[0:1, :])[:F]
    scale = inverse * inverse * LOG2E
    scale2 = across(scale, RANK)
    scale4 = across(scale, PER)

    index[...] = top_index(parent, top, leaf // 4)
    index2 = across(index[...], 2 * RANK)
    number = iota((RANK, 2 * RANK), 1)
    base = (quarter * RANK).astype(F32)
    other = (sibling * RANK).astype(F32)
    chosen = index2[:, :RANK] == iota((RANK, RANK), 1).astype(F32) + base
    rows[...] = chosen.astype(F32).astype(BF)
    lanes = number.astype(F32) + jnp.where(number < RANK, base, other - RANK)
    columns[...] = (index2 == lanes).astype(F32).astype(BF)
    chosen = across(index[...], 4 * RANK) == iota((RANK, 4 * RANK), 1).astype(F32)
    fours[...] = chosen.astype(F32).astype(BF)

    def norms(k):
        side[k] = point_side(rx[k].astype(F32), scale4)

    def receive(k):
        send_aux(k).wait_recv()
        send_feat(k).wait_recv()

    def early_norms(n, _):
        k = turn_of(n)
        pl.when(n > 0)(lambda: receive(k))
        norms(k)
        return 0

    lax.fori_loop(0, LEAVES // 2, early_norms, 0)

    def add_skel(k, total):
        send_skel(k).wait_recv()
        return total + sk[k].astype(F32)

    picked = lax.fori_loop(1, COLS, add_skel, picked)
    mine[...] = picked.astype(BF)
    sk4[quarter] = picked.astype(BF)

    def send_four(k):
        return remote(mine, sk4.at[quarter], (s_4, r_4), k, cousin(k))

    each(4, lambda k: send_four(k).start())
    left[0:RANK, :] = skel_side(picked, scale2)

    def block_of(k, out, begin):
        p = rx[k]
        fill = jnp.zeros((256 - 3 * F - 16, PER), BF)
        right = jnp.concatenate([p, p, p, side[k], fill], 0)
        power = dot(left[begin : begin + RANK, :], right)
        out[0:RANK, :] = jnp.exp2(jnp.minimum(power, 0.0)).astype(BF)

    def own_of(k, out):
        block_of(k, out, 0)
        value = ra[k]
        value = jnp.concatenate([value[r : r + 1] for r in range(4)], 1)
        out[RANK:, :] = jnp.broadcast_to(value, (16, PER)).astype(BF)

    def gram_of(u):
        gram[...] += dot_nt(u[...], u[0:RANK, :])

    def couple_of(v, u):
        couple[...] += dot_nt(v[...], u[0:RANK, :])

    last = LEAVES // 2 - 1

    def own_two(j, _):
        k, l = turn_of(2 * j), turn_of(2 * j + 1)
        @pl.when(j >= LEAVES // 4)
        def late():
            receive(k)
            receive(l)
            norms(k)
            norms(l)

        own_of(k, even.at[j])
        gram_of(odd.at[rem(j + last, last + 1)])
        own_of(l, odd.at[j])
        gram_of(even.at[j])
        return 0

    def other_two(j, _):
        block_of(turn_of(2 * j), other_even, RANK)
        couple_of(other_odd, odd.at[rem(j + last, last + 1)])
        block_of(turn_of(2 * j + 1), other_odd, RANK)
        couple_of(other_even, even.at[j])
        return 0

    gram[...] = jnp.zeros_like(gram)
    couple[...] = jnp.zeros_like(couple)
    odd[last] = jnp.zeros((RANK + 16, PER), BF)
    other_odd[...] = jnp.zeros_like(other_odd)
    def send_gram(k):
        return remote(pg.at[(col + k) % COLS], gr.at[k], (s_p, r_p), k, beside(k))

    def send_couple(k):
        return remote(pc.at[(col + k) % COLS], cr.at[k], (s_c, r_c), k, beside(k))

    def send_chosen(k):
        return remote(pt.at[(col + k) % COLS], qr.at[k], (s_o, r_o), k, beside(k))

    def send_rhs(k):
        return remote(rs, rr.at[k], (s_r, r_r), k, beside(k))

    def sibling_side():
        each(4, lambda k: remote(mine, sk4.at[(quarter + 4 - k) % 4], (s_4, r_4), k, cousin(k)).wait_recv())
        left[RANK:, :] = skel_side(sk4[sibling].astype(F32), scale2)

    def give_gram():
        gram_of(odd.at[last])
        part = gram[0:RANK, :].astype(BF)
        for k in range(COLS):
            pg[k] = part[k * SLAB : (k + 1) * SLAB]
        rhs = gram[RANK : RANK + 1, :]
        rhs = jnp.sum(dot_nt(stack16(split3(rhs), RANK), rows[...]), 0, keepdims=True)
        rs[...] = jnp.zeros_like(rs)
        rs[0:1, :] = rhs[:, :128]
        rs[1:2, :] = rhs[:, 128:]
        rs[2:3, :] = full
        each(COLS, lambda k: send_gram(k).start())
        each(COLS, lambda k: send_rhs(k).start())
        tops[...] = dot_nt(dot(rows[...], part).astype(BF), columns[:, 0:RANK])

    def half(h, _):
        pairs = LEAVES // 4
        lax.fori_loop(pairs * h, pairs * (h + 1), own_two, 0)
        pl.when(h == 0)(sibling_side)
        pl.when(h == 1)(give_gram)
        lax.fori_loop(pairs * h, pairs * (h + 1), other_two, 0)
        return 0

    lax.fori_loop(0, 2, half, 0)
    couple_of(other_odd, odd.at[last])

    part = couple[...].astype(BF)
    chosen = dot_nt(dot_nt(rows[...], part).astype(BF), columns[:, RANK:]) + tops[...]
    chosen = chosen.astype(BF)
    for k in range(COLS):
        pt[k] = chosen[k * SLAB : (k + 1) * SLAB]
    each(COLS, lambda k: send_chosen(k).start())
    part = couple[...].T.astype(BF)
    for k in range(COLS):
        pc[k] = part[k * SLAB : (k + 1) * SLAB]
    each(COLS, lambda k: send_couple(k).start())

    whole = jnp.concatenate([sk4[k] for k in range(4)], 1)
    points = dot_nt(whole, fours[...])
    fill = jnp.zeros((256 - 3 * F - 16, RANK), BF)
    points_b = points.astype(BF)
    right = jnp.concatenate([points_b, points_b, points_b, point_side(points, scale2), fill], 0)
    value = jnp.exp2(jnp.minimum(dot(skel_side(points, scale2), right), 0.0))
    crossing = (across(index[...], RANK) >= 2.0 * RANK) != (index[...].T[0:1, :] >= 2.0 * RANK)
    square = iota((RANK, RANK), 0) == iota((RANK, RANK), 1)
    tops[...] = jnp.where(crossing, value, 0.0) + jnp.where(square, ridge[...], 0.0)

    def finish(sends):
        return lambda k: [send(k).wait_send() for send in sends]

    each(LEAVES, finish((send_pivots, send_slots, send_aux, send_feat)))
    each(COLS, finish((send_skel, send_gram, send_rhs)))
    each(4, finish((send_four,)))

    def add_chosen(k, totals):
        send_chosen(k).wait_recv()
        send_rhs(k).wait_recv()
        return totals[0] + qr[k].astype(F32), totals[1] + rr[k]

    chosen, rhs = lax.fori_loop(1, COLS, add_chosen, (pt[col].astype(F32), rs[...]))
    over = jnp.maximum(jnp.max(rhs[2:3, :]), jnp.max(largest) - SLOTS)
    flag[0] = (over > 0.0).astype(jnp.int32)
    chosen = chosen * (1.0 / NODE)
    t4[0] = chosen.astype(BF)
    r4[0] = rhs * (1.0 / NODE)

    def send_top(k):
        return remote(t4.at[0], t4.at[k], (s_t, r_t), k, cousin(k))

    def send_top_rhs(k):
        return remote(r4.at[0], r4.at[k], (s_q, r_q), k, cousin(k))

    each(4, lambda k: send_top(k).start())
    each(4, lambda k: send_top_rhs(k).start())

    def add_gram(k, total):
        send_gram(k).wait_recv()
        return total + gr[k].astype(F32)

    def add_couple(k, total):
        send_couple(k).wait_recv()
        return total + cr[k].astype(F32)

    total = lax.fori_loop(1, COLS, add_gram, pg[col].astype(F32))
    diagonal = iota((SLAB, RANK), 0) + col * SLAB == iota((SLAB, RANK), 1)
    out_share[0, :, 0:RANK] = total * (1.0 / NODE) + jnp.where(diagonal, ridge[...], 0.0)
    total = lax.fori_loop(1, COLS, add_couple, pc[col].astype(F32))
    out_share[0, :, RANK:] = total * (1.0 / NODE)
    result = chosen + tops[pl.ds(pl.multiple_of(col * SLAB, SLAB), SLAB), :]

    def add_top(k, totals):
        send_top(k).wait_recv()
        send_top_rhs(k).wait_recv()
        return totals[0] + t4[k].astype(F32), totals[1] + r4[k]

    result, rhs = lax.fori_loop(1, 4, add_top, (result, r4[0]))
    out_top[0] = result
    out_rhs[...] = jnp.concatenate([rhs[0:1], rhs[1:2]], 1)

    each(COLS, finish((send_couple, send_chosen)))
    each(4, finish((send_top, send_top_rhs)))


SHAPES = ((1, SLAB, 2 * RANK), (1, SLAB, RANK), (1, RANK))


def exchange(merged, ridge, *smalls):
    return pl.pallas_call(
        exchange_kernel,
        out_shape=tuple(pltpu.VMEM(shape, F32) for shape in SHAPES),
        in_specs=[VMEM, VMEM] + [ANYWHERE] * 4,
        out_specs=[VMEM] * 3,
        scratch_shapes=[
            pltpu.VMEM((1, RANK), jnp.int32),
            pltpu.VMEM((1, F), F32),
            pltpu.VMEM((8, RANK), jnp.int32),
            pltpu.VMEM((4, RANK), jnp.int32),
            pltpu.VMEM((8, 128), F32),
            pltpu.VMEM((LEAVES, F, PER), BF),
            pltpu.VMEM((LEAVES, 8, 128), F32),
            pltpu.VMEM((LEAVES, F, PER), BF),
            pltpu.VMEM((LEAVES, 8, 128), F32),
            pltpu.VMEM((LEAVES, RANK, PER), BF),
            pltpu.VMEM((LEAVES, 16, PER), BF),
            pltpu.VMEM((COLS, F, RANK), BF),
            pltpu.VMEM((F, RANK), BF),
            pltpu.VMEM((4, F, RANK), BF),
            pltpu.VMEM((2 * RANK, 256), BF),
            pltpu.VMEM((LEAVES // 2, RANK + 16, PER), BF),
            pltpu.VMEM((LEAVES // 2, RANK + 16, PER), BF),
            pltpu.VMEM((RANK, PER), BF),
            pltpu.VMEM((RANK, PER), BF),
            pltpu.VMEM((RANK + 16, RANK), F32),
            pltpu.VMEM((RANK, RANK), F32),
            pltpu.VMEM((RANK, RANK), BF),
            pltpu.VMEM((RANK, 2 * RANK), BF),
            pltpu.VMEM((RANK, 4 * RANK), BF),
            pltpu.VMEM((RANK, 128), F32),
            pltpu.VMEM((RANK, RANK), F32),
            pltpu.VMEM((COLS, SLAB, RANK), BF),
            pltpu.VMEM((COLS, SLAB, RANK), BF),
            pltpu.VMEM((COLS, SLAB, RANK), BF),
            pltpu.VMEM((COLS, SLAB, RANK), BF),
            pltpu.VMEM((COLS, SLAB, RANK), BF),
            pltpu.VMEM((COLS, SLAB, RANK), BF),
            pltpu.VMEM((8, 128), F32),
            pltpu.VMEM((COLS, 8, 128), F32),
            pltpu.VMEM((4, SLAB, RANK), BF),
            pltpu.VMEM((4, 8, 128), F32),
            *dma(LEAVES),
            *dma(LEAVES),
            *dma(COLS),
            *dma(4),
            *dma(COLS),
            *dma(COLS),
            *dma(COLS),
            *dma(COLS),
            *dma(4),
            *dma(4),
            pltpu.SemaphoreType.DMA((5,)),
        ],
        compiler_params=params(0, 40),
        name="exchange",
    )(merged, ridge, *in_hbm(*smalls))


def stream(samples, pivots, ridge, *smalls):
    return pl.pallas_call(
        stream_kernel,
        out_shape=(
            *(pltpu.VMEM(shape, F32) for shape in SHAPES),
            jax.ShapeDtypeStruct((1,), jnp.int32),
        ),
        in_specs=[ANYWHERE, VMEM, VMEM, VMEM, VMEM] + [ANYWHERE] * 3,
        out_specs=[VMEM] * 3 + [pl.BlockSpec(memory_space=pltpu.SMEM)],
        scratch_shapes=[
            pltpu.VMEM((F, ROWS), BF),
            pltpu.VMEM((ROWS // 128, 128), F32),
            pltpu.VMEM((CHUNKS, 8, CHUNK), F32),
            pltpu.VMEM((LEAVES, 128), F32),
            pltpu.VMEM((LEAVES, 128), F32),
            pltpu.VMEM((ROWS + TILE, WIDE), F32),
            pltpu.VMEM((LEAVES // AT_ONCE, 16, 128), jnp.int32),
            pltpu.SMEM((LEAVES // AT_ONCE, 16, 128), jnp.int32),
            pltpu.VMEM((LEAVES, 1, RANK), jnp.int32),
            pltpu.VMEM((LEAVES, SLOTS, 128), BF),
            pltpu.VMEM((LEAVES, SLOTS, 128), BF),
            pltpu.VMEM((1, F), F32),
            pltpu.VMEM((8, RANK), jnp.int32),
            pltpu.VMEM((4, RANK), jnp.int32),
            pltpu.VMEM((8, 128), F32),
            pltpu.VMEM((LEAVES, F, PER), BF),
            pltpu.VMEM((LEAVES, 8, 128), F32),
            pltpu.VMEM((LEAVES, F, PER), BF),
            pltpu.VMEM((LEAVES, 8, 128), F32),
            pltpu.VMEM((LEAVES, 16, PER), BF),
            pltpu.VMEM((COLS, F, RANK), BF),
            pltpu.VMEM((F, RANK), BF),
            pltpu.VMEM((4, F, RANK), BF),
            pltpu.VMEM((2 * RANK, 256), BF),
            pltpu.VMEM((LEAVES // 2, RANK + 16, PER), BF),
            pltpu.VMEM((LEAVES // 2, RANK + 16, PER), BF),
            pltpu.VMEM((RANK, PER), BF),
            pltpu.VMEM((RANK, PER), BF),
            pltpu.VMEM((RANK + 16, RANK), F32),
            pltpu.VMEM((RANK, RANK), F32),
            pltpu.VMEM((RANK, RANK), BF),
            pltpu.VMEM((RANK, 2 * RANK), BF),
            pltpu.VMEM((RANK, 4 * RANK), BF),
            pltpu.VMEM((RANK, 128), F32),
            pltpu.VMEM((RANK, RANK), F32),
            pltpu.VMEM((COLS, SLAB, RANK), BF),
            pltpu.VMEM((COLS, SLAB, RANK), BF),
            pltpu.VMEM((COLS, SLAB, RANK), BF),
            pltpu.VMEM((COLS, SLAB, RANK), BF),
            pltpu.VMEM((COLS, SLAB, RANK), BF),
            pltpu.VMEM((COLS, SLAB, RANK), BF),
            pltpu.VMEM((8, 128), F32),
            pltpu.VMEM((COLS, 8, 128), F32),
            pltpu.VMEM((4, SLAB, RANK), BF),
            pltpu.VMEM((4, 8, 128), F32),
            *dma(LEAVES),
            *dma(LEAVES),
            *dma(LEAVES),
            *dma(LEAVES),
            *dma(COLS),
            *dma(4),
            *dma(COLS),
            *dma(COLS),
            *dma(COLS),
            *dma(COLS),
            *dma(4),
            *dma(4),
            pltpu.SemaphoreType.DMA((5,)),
        ],
        compiler_params=params(1, 40),
        name="stream",
    )(*in_hbm(*samples, pivots), ridge, *in_hbm(*smalls))


def emit_kernel(*refs):
    ins, outs, sem = refs[:3], refs[3:6], refs[6]
    copies = [pltpu.make_async_copy(a, b, sem.at[k]) for k, (a, b) in enumerate(zip(ins, outs))]
    for copy in copies:
        copy.start()
    for copy in copies:
        copy.wait()


def emit(results):
    return pl.pallas_call(
        emit_kernel,
        out_shape=tuple(jax.ShapeDtypeStruct(shape, F32) for shape in SHAPES),
        in_specs=[VMEM] * 3,
        out_specs=[ANYWHERE] * 3,
        scratch_shapes=[pltpu.SemaphoreType.DMA((3,))],
        compiler_params=params(),
        name="emit",
    )(*results)


def local(features, targets, owner, length_scales, ridge, leaf_pivots, parent_pivots, top_pivots):
    samples = (features, targets.reshape(ROWS // 128, 128), owner.reshape(ROWS // 128, 128))
    ridge = ridge.reshape(1, 1)
    smalls = (length_scales.reshape(1, F), parent_pivots, top_pivots)
    *results, flag = stream(samples, leaf_pivots, ridge, *smalls)

    def again():
        return tuple(emit(exchange(pack(*samples), ridge, leaf_pivots, *smalls)))

    return lax.switch(flag[0], [lambda: tuple(emit(results)), again])


def solution(mesh):
    return jax.shard_map(
        local,
        mesh=mesh,
        in_specs=(
            P(None, ("leaf", "col")),
            P(("leaf", "col")),
            P(("leaf", "col")),
            P(),
            P(),
            P("leaf", None),
            P(),
            P(),
        ),
        out_specs=(P("leaf", "col", None), P("leaf", "col", None), P("leaf", None)),
        check_vma=False,
    )
```

```python
import functools
import math

import jax
import jax.numpy as jnp
from jax import lax
from jax.experimental import pallas as pl
from jax.experimental.pallas import tpu as pltpu
from jax.sharding import PartitionSpec as P

F = 48
RANK = 256
ROWS = 8192
LEAVES = 16
COLS = 8
OWNERS = 128
PACKET = 64
PER = ROWS // LEAVES
CHUNK = 256
CHUNKS = ROWS // CHUNK
WINDOW = 40
REGION = PER + WINDOW
TILE = 32
TILES = PER // TILE
PIECES = 6
AT_ONCE = 128 // TILES
SLOTS = 16
WHICH = 50
FULL = 51
WIDE = 64
SLAB = RANK // COLS
NODE = ROWS * COLS
LOG2E = math.log2(math.e)
BF = jnp.bfloat16
F32 = jnp.float32
NT = (((1,), (1,)), ((), ()))
MESH = pl.DeviceIdType.MESH


def dma(count):
    return [pltpu.SemaphoreType.DMA((count,))] * 2


def params(number=None, limit=24):
    if number is None:
        return pltpu.CompilerParams(vmem_limit_bytes=limit * 2**20)
    return pltpu.CompilerParams(
        collective_id=number, has_side_effects=True, vmem_limit_bytes=limit * 2**20
    )


ANYWHERE = pl.BlockSpec(memory_space=pl.ANY)
VMEM = pl.BlockSpec(memory_space=pltpu.VMEM)


def iota(shape, axis):
    return lax.broadcasted_iota(jnp.int32, shape, axis)


def dot(a, b):
    return jnp.dot(a, b, preferred_element_type=F32)


def dot_nt(a, b):
    return lax.dot_general(a, b, NT, preferred_element_type=F32)


def row_pair(two):
    return jnp.concatenate([two[0:1], two[1:2]], 1)


def pack_kernel(
    feat_hbm, target, owner, zbuf, feat, goals, rows, ybuf, table, scal, sem, feat_sem
):
    bring = pltpu.make_async_copy(feat_hbm, feat, feat_sem)
    bring.start()
    goals[...] = target[...].astype(F32)
    before = (iota((CHUNK, CHUNK), 0) < iota((CHUNK, CHUNK), 1)).astype(F32).astype(BF)
    weights = jnp.concatenate([before, jnp.ones((CHUNK, 128), BF)], 1)
    lane = iota((LEAVES, 128), 1)

    def ranks(t, carry):
        seen, seen_leaf, most = carry
        own = row_pair(owner[pl.ds(2 * t, 2), :])
        leaf = own // 8
        is_own = iota((OWNERS, CHUNK), 0) == own
        is_leaf = iota((LEAVES, CHUNK), 0) == leaf
        is_after = iota((LEAVES, CHUNK), 0) > leaf
        marks = jnp.concatenate(
            [m.astype(F32).astype(BF) for m in (is_own, is_leaf, is_after)], 0
        )
        sums = dot(marks, weights)
        counts = sums[:OWNERS, CHUNK:]
        leaf_counts = sums[OWNERS : OWNERS + LEAVES, CHUNK:]
        base = sums[OWNERS + LEAVES :, CHUNK:]
        prior = sums[:OWNERS, :CHUNK] + jnp.concatenate([seen, seen], 1)
        rank = jnp.sum(jnp.where(is_own, prior, 0.0), 0, keepdims=True)
        place = sums[OWNERS : OWNERS + LEAVES, :CHUNK] + jnp.concatenate([base, base], 1)
        place = jnp.sum(jnp.where(is_leaf, place, 0.0), 0, keepdims=True)
        tag = (own % 8).astype(F32) * PACKET + rank - (PER // 2)
        rows[t, 0:1, :] = place
        rows[t, 1:2, :] = row_pair(goals[pl.ds(2 * t, 2), :])
        rows[t, 2:3, :] = tag
        here = lane == t
        table[0:LEAVES, :] = jnp.where(here, seen_leaf.astype(jnp.int32), table[0:LEAVES, :])
        table[LEAVES : 2 * LEAVES, :] = jnp.where(
            here, base.astype(jnp.int32), table[LEAVES : 2 * LEAVES, :]
        )
        return seen + counts, seen_leaf + leaf_counts, jnp.maximum(most, leaf_counts)

    table[0:LEAVES, :] = jnp.full((LEAVES, 128), PER, jnp.int32)
    zero = jnp.zeros((LEAVES, 128), F32)
    _, _, most = lax.fori_loop(
        0, CHUNKS, ranks, (jnp.zeros((OWNERS, 128), F32), zero, zero), unroll=16
    )
    most = jnp.broadcast_to(jnp.max(most, 0, keepdims=True), (8, 128))
    table[2 * LEAVES :, :] = most.astype(jnp.int32)
    move = pltpu.make_async_copy(table, scal, sem)
    move.start()
    bring.wait()

    def sort(t, _):
        start = pl.multiple_of(t * CHUNK, CHUNK)
        row = iota((16, CHUNK), 0)
        place, goal, tag = rows[t, 0:1, :], rows[t, 1:2, :], rows[t, 2:3, :]
        extra = jnp.where(row == 0, goal, jnp.where(row == 1, tag, 0.0)).astype(BF)
        joined = jnp.concatenate([feat[:, pl.ds(start, CHUNK)], extra], 0)
        chosen = (iota((CHUNK, CHUNK), 0) == place.astype(jnp.int32)).astype(F32).astype(BF)
        ybuf[pl.ds(start, CHUNK), :] = dot_nt(chosen, joined)
        return 0

    lax.fori_loop(0, CHUNKS, sort, 0, unroll=8)
    move.wait()
    widest = scal[2 * LEAVES, 0]

    @pl.when(widest <= WINDOW)
    def quick():
        def merge(t, _):
            for i in range(LEAVES):
                source = t * CHUNK + scal[LEAVES + i, t]
                goal = i * REGION + scal[i, t]
                zbuf[pl.ds(goal, WINDOW), :] = ybuf[pl.ds(source, WINDOW), :]
            return 0

        lax.fori_loop(0, CHUNKS, merge, 0, unroll=4)

    @pl.when(widest > WINDOW)
    def slow():
        def merge(index, _):
            t = index // LEAVES
            i = index % LEAVES
            source = t * CHUNK + scal[LEAVES + i, t]
            first = scal[i, t]
            count = scal[i, t + 1] - first

            def part(k, _):
                rows = ybuf[pl.ds(source + 8 * k, 8), :]
                zbuf[pl.ds(i * REGION + first + 8 * k, 8), :] = rows
                return 0

            lax.fori_loop(0, (count + 7) // 8, part, 0)
            return 0

        lax.fori_loop(0, CHUNKS * LEAVES, merge, 0)


def in_hbm(*arrays):
    return [pltpu.with_memory_space_constraint(a, pltpu.HBM) for a in arrays]


def pack(features, targets, owner):
    return pl.pallas_call(
        pack_kernel,
        out_shape=pltpu.VMEM((LEAVES * REGION, WIDE), F32),
        in_specs=[ANYWHERE, VMEM, VMEM],
        out_specs=VMEM,
        scratch_shapes=[
            pltpu.VMEM((F, ROWS), BF),
            pltpu.VMEM((ROWS // 128, 128), F32),
            pltpu.VMEM((CHUNKS, 8, CHUNK), F32),
            pltpu.VMEM((ROWS + WINDOW, WIDE), F32),
            pltpu.VMEM((40, 128), jnp.int32),
            pltpu.SMEM((40, 128), jnp.int32),
            pltpu.SemaphoreType.DMA,
            pltpu.SemaphoreType.DMA,
        ],
        compiler_params=params(),
        name="pack",
    )(*in_hbm(features, targets, owner))


def split3(x):
    high = x.astype(BF)
    rest = x - high.astype(F32)
    mid = rest.astype(BF)
    return high, mid, (rest - mid.astype(F32)).astype(BF)


def stack16(parts, width):
    row = iota((16, width), 0)
    block = jnp.zeros((16, width), F32)
    for k, part in enumerate(parts):
        block = jnp.where(row == k, part if isinstance(part, float) else part.astype(F32), block)
    return block.astype(BF)


def half_norm(points, scale):
    return jnp.sum(points * points * (0.5 * scale), 0, keepdims=True)


def point_side(points, scale):
    high, mid, low = split3(-half_norm(points, scale))
    return stack16([high, mid, low, 1.0, 1.0, 1.0], points.shape[1])


def skel_side(skel, scale):
    width = skel.shape[1]
    high, mid, low = split3(skel * scale)
    extra = stack16([1.0, 1.0, 1.0, *split3(-half_norm(skel, scale))], width)
    parts = [p.astype(F32) for p in (high, mid, low, extra)]
    fill = jnp.zeros((256 - 3 * F - 16, width), F32)
    return jnp.concatenate([*parts, fill], 0).T.astype(BF)


def select_row(table, row):
    hit = iota(table.shape, 0) == row
    return jnp.sum(jnp.where(hit, table.astype(F32), 0.0), 0, keepdims=True)


def to_column(row):
    return jnp.broadcast_to(row, (128, row.shape[1])).T


def across(column, width):
    return jnp.concatenate([column] * (width // 128), 1)


def place_of(leaf, col):
    return dict(device_id=(leaf, col), device_id_type=MESH)


def mate(k):
    leaf, col = lax.axis_index("leaf"), lax.axis_index("col")
    to = (leaf + k) % LEAVES
    cross = (to // 8 + leaf // 8) % 2
    return place_of(to, col + cross * (1 - 2 * (col % 2)))


def beside(k):
    leaf, col = lax.axis_index("leaf"), lax.axis_index("col")
    return place_of(leaf, (col + k) % COLS)


def cousin(k):
    leaf, col = lax.axis_index("leaf"), lax.axis_index("col")
    return place_of(leaf - leaf % 4 + (leaf + k) % 4, col)


def each(count, step, unroll=1):
    lax.fori_loop(1, count, lambda k, _: (step(k), 0)[1], 0, unroll=unroll)


def rem(a, b):
    return lax.rem(jnp.int32(a), jnp.int32(b))


def turn_of(n):
    n = jnp.int32(n)
    odd = lax.rem(n, jnp.int32(2))
    half = lax.div(n + odd, jnp.int32(2))
    return lax.rem(odd * half + (1 - odd) * (LEAVES - half), jnp.int32(LEAVES))


def remote(src, dst, sems, k, peer):
    return pltpu.make_async_remote_copy(src, dst, sems[0].at[k], sems[1].at[k], **peer)


def top_index(parent, top, group):
    top_row = select_row(top[...], group)
    below = jnp.concatenate([select_row(parent[...], 2 * group + r) for r in range(2)], 1)
    number = iota((RANK, 2 * RANK), 1)
    below = below + jnp.where(iota((1, 2 * RANK), 1) >= RANK, 2.0 * RANK, 0.0)
    hit = across(to_column(top_row), 2 * RANK) == number.astype(F32)
    index = jnp.sum(jnp.where(hit, below, 0.0), 1, keepdims=True)
    return jnp.broadcast_to(index, (RANK, 128))


def exchange_kernel(
    merged, ridge, pivots_hbm, scales_hbm, parent_hbm, top_hbm, out_share, out_top, out_rhs,
    pivots, scales, parent, top, spare, feat, aux, rx, ra, hot, side, sk, mine, sk4, left,
    even, odd, other_even, other_odd, gram, couple, rows, columns, fours, index, tops,
    pg, gr, pc, cr, pt, qr, rs, rr, t4, r4,
    s_f, r_f, s_a, r_a, s_k, r_k, s_4, r_4, s_p, r_p, s_c, r_c, s_o, r_o, s_r, r_r, s_t, r_t, s_q, r_q, local,
):
    leaf = lax.axis_index("leaf")
    col = lax.axis_index("col")
    quarter = leaf % 4
    sibling = quarter + 1 - 2 * (quarter % 2)
    barrier = pltpu.get_barrier_semaphore()
    each(LEAVES, lambda k: pl.semaphore_signal(barrier, inc=1, **mate(k)))
    each(COLS, lambda k: pl.semaphore_signal(barrier, inc=1, **beside(k)))
    smalls = [
        pltpu.make_async_copy(a, b, local.at[k])
        for k, (a, b) in enumerate(
            [(pivots_hbm, pivots), (scales_hbm, scales), (parent_hbm, parent), (top_hbm, top)]
        )
    ]
    for copy in smalls:
        copy.start()

    eye = (iota((WIDE, WIDE), 0) == iota((WIDE, WIDE), 1)).astype(F32).astype(BF)

    def turn(k):
        start = pl.multiple_of((leaf + k) % LEAVES * REGION, 8)
        turned = dot_nt(eye, merged[pl.ds(start, PER), :].astype(BF))
        feat[k] = turned[:F].astype(BF)
        aux[k] = jnp.concatenate(
            [turned[F + r : F + r + 1, 128 * c : 128 * c + 128] for r in range(2) for c in range(4)], 0
        )

    def send_feat(k):
        return remote(feat.at[k], rx.at[k], (s_f, r_f), k, mate(k))

    def send_aux(k):
        return remote(aux.at[k], ra.at[k], (s_a, r_a), k, mate(k))

    def four(j, _):
        steps = [turn_of(lax.rem(4 * j + r, LEAVES)) for r in range(1, 5)]
        for k in steps:
            turn(k)
        pl.when(j == 0)(lambda: pl.semaphore_wait(barrier, LEAVES + COLS - 2))
        for send in (send_aux, send_feat):
            for k in steps[:3]:
                send(k).start()
            pl.when(j < 3)(lambda: send(steps[3]).start())
        return 0

    lax.fori_loop(0, LEAVES // 4, four, 0)
    rx[0] = feat[0]
    ra[0] = aux[0]

    for copy in smalls:
        copy.wait()
    spare[...] = jnp.ones((8, 128), F32)
    spare[0:1, 0:F] = scales[...]
    inverse = 1.0 / to_column(spare[0:1, :])[:F]
    scale = inverse * inverse * LOG2E
    scale2 = across(scale, RANK)
    scale4 = across(scale, PER)

    place = pivots[...]
    within = place % ROWS
    block = within // PACKET
    key = (block // COLS) * PER + (place // ROWS) * PACKET + within % PACKET
    holder = block % COLS
    crossed = (block // COLS) // 8 != leaf // 8
    holder = jnp.where(crossed, holder + 1 - 2 * (holder % 2), holder)
    key = jnp.where(holder == col, key, -PER)
    key = across(to_column(key.astype(F32)), PER)

    def mark(k):
        source = (leaf + LEAVES - k) % LEAVES
        tags = ra[k, 4:8, :]
        tag = jnp.concatenate([tags[r : r + 1] for r in range(4)], 1)
        wanted = tag + (PER // 2 + source * PER).astype(F32)
        hot[k] = (key == wanted).astype(F32).astype(BF)

    def mark_next(n, _):
        k = turn_of(n)
        pl.when(n > 0)(lambda: send_aux(k).wait_recv())
        mark(k)
        return 0

    lax.fori_loop(0, LEAVES, mark_next, 0)

    index[...] = top_index(parent, top, leaf // 4)
    index2 = across(index[...], 2 * RANK)
    number = iota((RANK, 2 * RANK), 1)
    base = (quarter * RANK).astype(F32)
    other = (sibling * RANK).astype(F32)
    chosen = index2[:, :RANK] == iota((RANK, RANK), 1).astype(F32) + base
    rows[...] = chosen.astype(F32).astype(BF)
    lanes = number.astype(F32) + jnp.where(number < RANK, base, other - RANK)
    columns[...] = (index2 == lanes).astype(F32).astype(BF)
    chosen = across(index[...], 4 * RANK) == iota((RANK, 4 * RANK), 1).astype(F32)
    fours[...] = chosen.astype(F32).astype(BF)

    def pick(j, total):
        steps = [turn_of(4 * j + r) for r in range(4)]
        pl.when(j > 0)(lambda: send_feat(steps[0]).wait_recv())
        for k in steps[1:]:
            send_feat(k).wait_recv()
        for k in steps:
            total = total + dot_nt(hot[k], rx[k])
        return total

    picked = lax.fori_loop(0, LEAVES // 4, pick, jnp.zeros((RANK, F), F32))
    picked = jnp.concatenate([picked, jnp.zeros((RANK, 128 - F), F32)], 1).T[:F]
    sk[0] = picked.astype(BF)

    def send_skel(k):
        return remote(sk.at[0], sk.at[k], (s_k, r_k), k, beside(k))

    each(COLS, lambda k: send_skel(k).start())

    def norms(k, _):
        side[k] = point_side(rx[k].astype(F32), scale4)
        return 0

    lax.fori_loop(0, LEAVES, norms, 0)

    def add_skel(k, total):
        send_skel(k).wait_recv()
        return total + sk[k].astype(F32)

    picked = lax.fori_loop(1, COLS, add_skel, picked)
    mine[...] = picked.astype(BF)
    sk4[quarter] = picked.astype(BF)

    def send_four(k):
        return remote(mine, sk4.at[quarter], (s_4, r_4), k, cousin(k))

    each(4, lambda k: send_four(k).start())
    left[0:RANK, :] = skel_side(picked, scale2)

    def block_of(k, out, begin):
        p = rx[k]
        fill = jnp.zeros((256 - 3 * F - 16, PER), BF)
        right = jnp.concatenate([p, p, p, side[k], fill], 0)
        power = dot(left[begin : begin + RANK, :], right)
        out[0:RANK, :] = jnp.exp2(jnp.minimum(power, 0.0)).astype(BF)

    def own_of(k, out):
        block_of(k, out, 0)
        value = jnp.concatenate([ra[k, r : r + 1, :] for r in range(4)], 1)
        out[RANK:, :] = jnp.broadcast_to(value, (16, PER)).astype(BF)

    def gram_of(u):
        gram[...] += dot_nt(u[...], u[0:RANK, :])

    def couple_of(v, u):
        couple[...] += dot_nt(v[...], u[0:RANK, :])

    last = LEAVES // 2 - 1

    def own_two(j, _):
        own_of(2 * j, even.at[j])
        gram_of(odd.at[(j + last) % (last + 1)])
        own_of(2 * j + 1, odd.at[j])
        gram_of(even.at[j])
        return 0

    def other_two(j, _):
        block_of(2 * j, other_even, RANK)
        couple_of(other_odd, odd.at[(j + last) % (last + 1)])
        block_of(2 * j + 1, other_odd, RANK)
        couple_of(other_even, even.at[j])
        return 0

    gram[...] = jnp.zeros_like(gram)
    couple[...] = jnp.zeros_like(couple)
    odd[last] = jnp.zeros((RANK + 16, PER), BF)
    other_odd[...] = jnp.zeros_like(other_odd)
    lax.fori_loop(0, last + 1, own_two, 0)
    gram_of(odd.at[last])

    def send_gram(k):
        return remote(pg.at[(col + k) % COLS], gr.at[k], (s_p, r_p), k, beside(k))

    def send_couple(k):
        return remote(pc.at[(col + k) % COLS], cr.at[k], (s_c, r_c), k, beside(k))

    def send_chosen(k):
        return remote(pt.at[(col + k) % COLS], qr.at[k], (s_o, r_o), k, beside(k))

    def send_rhs(k):
        return remote(rs, rr.at[k], (s_r, r_r), k, beside(k))

    part = gram[0:RANK, :].astype(BF)
    for k in range(COLS):
        pg[k] = part[k * SLAB : (k + 1) * SLAB]
    rhs = gram[RANK : RANK + 1, :]
    rhs = jnp.sum(dot_nt(stack16(split3(rhs), RANK), rows[...]), 0, keepdims=True)
    rs[...] = jnp.zeros_like(rs)
    rs[0:1, :] = rhs[:, :128]
    rs[1:2, :] = rhs[:, 128:]
    each(COLS, lambda k: send_gram(k).start())
    each(COLS, lambda k: send_rhs(k).start())
    tops[...] = dot_nt(dot(rows[...], part).astype(BF), columns[:, 0:RANK])

    each(4, lambda k: remote(mine, sk4.at[(quarter + 4 - k) % 4], (s_4, r_4), k, cousin(k)).wait_recv())
    left[RANK:, :] = skel_side(sk4[sibling].astype(F32), scale2)
    lax.fori_loop(0, last + 1, other_two, 0)
    couple_of(other_odd, odd.at[last])

    part = couple[...].astype(BF)
    chosen = dot_nt(dot_nt(rows[...], part).astype(BF), columns[:, RANK:]) + tops[...]
    chosen = chosen.astype(BF)
    for k in range(COLS):
        pt[k] = chosen[k * SLAB : (k + 1) * SLAB]
    each(COLS, lambda k: send_chosen(k).start())
    part = couple[...].T.astype(BF)
    for k in range(COLS):
        pc[k] = part[k * SLAB : (k + 1) * SLAB]
    each(COLS, lambda k: send_couple(k).start())

    whole = jnp.concatenate([sk4[k] for k in range(4)], 1)
    points = dot_nt(whole, fours[...])
    fill = jnp.zeros((256 - 3 * F - 16, RANK), BF)
    points_b = points.astype(BF)
    right = jnp.concatenate([points_b, points_b, points_b, point_side(points, scale2), fill], 0)
    value = jnp.exp2(jnp.minimum(dot(skel_side(points, scale2), right), 0.0))
    crossing = (across(index[...], RANK) >= 2.0 * RANK) != (index[...].T[0:1, :] >= 2.0 * RANK)
    square = iota((RANK, RANK), 0) == iota((RANK, RANK), 1)
    tops[...] = jnp.where(crossing, value, 0.0) + jnp.where(square, ridge[...], 0.0)

    def finish(sends):
        return lambda k: [send(k).wait_send() for send in sends]

    each(LEAVES, finish((send_aux, send_feat)))
    each(COLS, finish((send_skel, send_gram, send_rhs)))
    each(4, finish((send_four,)))

    def add_chosen(k, totals):
        send_chosen(k).wait_recv()
        send_rhs(k).wait_recv()
        return totals[0] + qr[k].astype(F32), totals[1] + rr[k]

    chosen, rhs = lax.fori_loop(1, COLS, add_chosen, (pt[col].astype(F32), rs[...]))
    chosen = chosen * (1.0 / NODE)
    t4[0] = chosen.astype(BF)
    r4[0] = rhs * (1.0 / NODE)

    def send_top(k):
        return remote(t4.at[0], t4.at[k], (s_t, r_t), k, cousin(k))

    def send_top_rhs(k):
        return remote(r4.at[0], r4.at[k], (s_q, r_q), k, cousin(k))

    each(4, lambda k: send_top(k).start())
    each(4, lambda k: send_top_rhs(k).start())

    def add_gram(k, total):
        send_gram(k).wait_recv()
        return total + gr[k].astype(F32)

    def add_couple(k, total):
        send_couple(k).wait_recv()
        return total + cr[k].astype(F32)

    total = lax.fori_loop(1, COLS, add_gram, pg[col].astype(F32))
    diagonal = iota((SLAB, RANK), 0) + col * SLAB == iota((SLAB, RANK), 1)
    out_share[0, :, 0:RANK] = total * (1.0 / NODE) + jnp.where(diagonal, ridge[...], 0.0)
    total = lax.fori_loop(1, COLS, add_couple, pc[col].astype(F32))
    out_share[0, :, RANK:] = total * (1.0 / NODE)
    result = chosen + tops[pl.ds(pl.multiple_of(col * SLAB, SLAB), SLAB), :]

    def add_top(k, totals):
        send_top(k).wait_recv()
        send_top_rhs(k).wait_recv()
        return totals[0] + t4[k].astype(F32), totals[1] + r4[k]

    result, rhs = lax.fori_loop(1, 4, add_top, (result, r4[0]))
    out_top[0] = result
    out_rhs[...] = jnp.concatenate([rhs[0:1], rhs[1:2]], 1)

    each(COLS, finish((send_couple, send_chosen)))
    each(4, finish((send_top, send_top_rhs)))


def stream_kernel(
    feat_hbm, target, owner, pivots, ridge, scales_hbm, parent_hbm, top_hbm,
    out_share, out_top, out_rhs, flag,
    feat_in, goals, ranked, starts, bases, ybuf, table, scal, held, slots, came, scales, parent, top, spare,
    feat, aux, rx, ra, side, sk, mine, sk4, left, even, odd, other_even, other_odd, gram, couple,
    rows, columns, fours, index, tops, pg, gr, pc, cr, pt, qr, rs, rr, t4, r4,
    s_v, r_v, s_s, r_s, s_f, r_f, s_a, r_a, s_k, r_k, s_4, r_4, s_p, r_p, s_c, r_c, s_o, r_o,
    s_r, r_r, s_t, r_t, s_q, r_q, local,
):
    leaf = lax.axis_index("leaf")
    col = lax.axis_index("col")
    quarter = leaf % 4
    sibling = quarter + 1 - 2 * (quarter % 2)
    barrier = pltpu.get_barrier_semaphore()
    each(LEAVES, lambda k: pl.semaphore_signal(barrier, inc=1, **mate(k)))
    each(COLS, lambda k: pl.semaphore_signal(barrier, inc=1, **beside(k)))
    bring = pltpu.make_async_copy(feat_hbm, feat_in, local.at[3])
    bring.start()
    smalls = [
        pltpu.make_async_copy(a, b, local.at[k])
        for k, (a, b) in enumerate([(scales_hbm, scales), (parent_hbm, parent), (top_hbm, top)])
    ]
    for copy in smalls:
        copy.start()

    def send_pivots(k):
        return remote(pivots, held.at[k], (s_v, r_v), k, mate(k))

    def send_slots(k):
        return remote(slots.at[k], came.at[k], (s_s, r_s), k, mate(k))

    def send_feat(k):
        return remote(feat.at[k], rx.at[k], (s_f, r_f), k, mate(k))

    def send_aux(k):
        return remote(aux.at[k], ra.at[k], (s_a, r_a), k, mate(k))

    def send_skel(k):
        return remote(sk.at[0], sk.at[k], (s_k, r_k), k, beside(k))

    goals[...] = target[...].astype(F32)
    before = (iota((CHUNK, CHUNK), 0) < iota((CHUNK, CHUNK), 1)).astype(F32).astype(BF)
    weights = jnp.concatenate([before, jnp.ones((CHUNK, 128), BF)], 1)
    lane = iota((LEAVES, 128), 1)

    def rank(t, carry):
        seen, seen_leaf = carry
        own = row_pair(owner[pl.ds(2 * t, 2), :])
        group = own // 8
        is_own = iota((OWNERS, CHUNK), 0) == own
        is_leaf = iota((LEAVES, CHUNK), 0) == group
        is_after = iota((LEAVES, CHUNK), 0) > group
        marks = jnp.concatenate([m.astype(F32).astype(BF) for m in (is_own, is_leaf, is_after)], 0)
        sums = dot(marks, weights)
        leaf_counts = sums[OWNERS : OWNERS + LEAVES, CHUNK:]
        base = sums[OWNERS + LEAVES :, CHUNK:]
        prior = sums[:OWNERS, :CHUNK] + jnp.concatenate([seen, seen], 1)
        place = jnp.sum(jnp.where(is_own, prior, 0.0), 0, keepdims=True)
        order = sums[OWNERS : OWNERS + LEAVES, :CHUNK] + jnp.concatenate([base, base], 1)
        ranked[t, 0:1, :] = jnp.sum(jnp.where(is_leaf, order, 0.0), 0, keepdims=True)
        ranked[t, 1:2, :] = row_pair(goals[pl.ds(2 * t, 2), :])
        ranked[t, 2:3, :] = own.astype(F32) * PACKET + place
        starts[...] = jnp.where(lane == t, seen_leaf, starts[...])
        bases[...] = jnp.where(lane == t, base, bases[...])
        return seen + sums[:OWNERS, CHUNK:], seen_leaf + leaf_counts

    starts[...] = jnp.zeros_like(starts)
    bases[...] = jnp.zeros_like(bases)
    lax.fori_loop(
        0, CHUNKS, rank, (jnp.zeros((OWNERS, 128), F32), jnp.zeros((LEAVES, 128), F32)), unroll=16
    )

    rest = jnp.zeros((128 - LEAVES, 128), F32)
    start_of = jnp.concatenate([starts[...], rest], 0).T[:CHUNKS]
    base_of = jnp.concatenate([bases[...], rest], 0).T[:CHUNKS]
    high = jnp.where(start_of >= 256.0, 256.0, 0.0)
    columns_of = jnp.concatenate([high, start_of - high, base_of], 0).astype(BF)
    chunk = iota((CHUNKS, 128), 0).astype(F32)
    first = (iota((1, 128), 1) % TILES * TILE).astype(F32)
    full = jnp.zeros((1, 128), F32)
    table[...] = jnp.zeros_like(table)
    for g in range(LEAVES // AT_ONCE):
        one = iota((128, 128), 0) == iota((128, 128), 1) // TILES + g * AT_ONCE
        spread_out = dot(columns_of, one.astype(F32).astype(BF))
        begin = spread_out[:CHUNKS] + spread_out[CHUNKS : 2 * CHUNKS]
        place = spread_out[2 * CHUNKS :] + chunk * CHUNK
        passed = (begin <= first) & (chunk > 0.0)
        current = jnp.sum(jnp.where(passed, 1.0, 0.0), 0, keepdims=True)
        for r in range(PIECES + 1):
            here = chunk == current + r
            row = jnp.sum(jnp.where(here, place, 0.0), 0, keepdims=True)
            edge = jnp.sum(jnp.where(here, begin, 0.0), 0, keepdims=True)
            edge = jnp.where(current + r < CHUNKS, edge, float(PER)) - first
            if r == PIECES:
                full = jnp.maximum(full, jnp.where(edge < TILE, 1.0, 0.0))
                continue
            if r:
                edge = jnp.clip(edge, 0.0, float(TILE))
                table[g, PIECES + r : PIECES + r + 1, :] = edge.astype(jnp.int32)
            row = jnp.clip(jnp.where(current + r < CHUNKS, row - edge, 0.0), 0.0, float(ROWS))
            table[g, r : r + 1, :] = row.astype(jnp.int32)
    full = jnp.broadcast_to(jnp.max(full, 1, keepdims=True), (1, 128))
    tell = pltpu.make_async_copy(table, scal, local.at[4])
    tell.start()

    held[0] = pivots[...]
    pl.semaphore_wait(barrier, LEAVES + COLS - 2)
    each(LEAVES, lambda k: send_pivots(k).start())

    def joined_of(t):
        row = iota((16, CHUNK), 0)
        extra = jnp.where(row == 0, ranked[t, 1:2, :], 0.0).astype(BF)
        return jnp.concatenate([feat_in[:, pl.ds(pl.multiple_of(t * CHUNK, CHUNK), CHUNK)], extra], 0)

    def sort(t, _):
        place = ranked[t, 0:1, :].astype(jnp.int32)
        chosen = (iota((CHUNK, CHUNK), 0) == place).astype(F32).astype(BF)
        ybuf[pl.ds(pl.multiple_of(t * CHUNK, CHUNK), CHUNK), :] = dot_nt(chosen, joined_of(t))
        return 0

    bring.wait()
    lax.fori_loop(0, CHUNKS, sort, 0, unroll=8)
    ybuf[ROWS:, :] = jnp.zeros((TILE, WIDE), F32)
    tell.wait()

    eye = (iota((WIDE, WIDE), 0) == iota((WIDE, WIDE), 1)).astype(F32).astype(BF)
    sub = iota((TILE, WIDE), 0)

    def packet(k):
        to = lax.rem(leaf + k, jnp.int32(LEAVES))
        group = lax.div(to, jnp.int32(AT_ONCE))
        lane = lax.rem(to, jnp.int32(AT_ONCE)) * TILES

        def piece(r, q):
            return ybuf[pl.ds(jnp.clip(scal[group, r, lane + q], 0, ROWS), TILE), :]

        tiles = []
        for q in range(TILES):
            tile = piece(0, q)
            for r in range(1, PIECES):
                tile = jnp.where(sub >= scal[group, PIECES + r, lane + q], piece(r, q), tile)
            tiles.append(tile)
        turned = dot_nt(eye, jnp.concatenate(tiles, 0).astype(BF))
        feat[k] = turned[:F].astype(BF)
        aux[k] = jnp.concatenate([turned[F : F + 1, 128 * c : 128 * c + 128] for c in range(4)] * 2, 0)

    def give(j, _):
        steps = turn_of(2 * j + 1), turn_of(rem(2 * j + 2, LEAVES))
        for k in steps:
            packet(k)
        send_aux(steps[0]).start()
        send_feat(steps[0]).start()

        @pl.when(j < LEAVES // 2 - 1)
        def second():
            send_aux(steps[1]).start()
            send_feat(steps[1]).start()

        return 0

    lax.fori_loop(0, 1, give, 0)

    each(LEAVES, lambda k: send_pivots(k).wait_recv())
    place = jnp.concatenate([held[(LEAVES - b) % LEAVES] for b in range(LEAVES)], 0)
    home = place % ROWS // PACKET
    number = ((leaf + iota((LEAVES, RANK), 0)) % LEAVES) * 8 + place // ROWS
    number = (number * PACKET + place % PACKET).astype(F32)
    valid = home == leaf * COLS + col
    order = dot(valid.astype(F32).astype(BF), before)
    order = jnp.where(valid, order, -1.0)

    def spread(table):
        return jnp.concatenate(
            [jnp.broadcast_to(table[b : b + 1], (SLOTS, RANK)) for b in range(LEAVES)], 0
        )

    shape = (LEAVES * SLOTS, RANK)
    hit = spread(order) == (iota(shape, 0) % SLOTS).astype(F32)
    wanted = jnp.sum(jnp.where(hit, spread(number) + 1.0, 0.0), 1, keepdims=True) - 1.0
    which = jnp.sum(jnp.where(hit, iota(shape, 1).astype(F32) + 1.0, 0.0), 1, keepdims=True) - 1.0
    wanted = jnp.broadcast_to(wanted, (LEAVES * SLOTS, CHUNK))

    def take(t, total):
        chosen = (wanted == ranked[t, 2:3, :]).astype(F32).astype(BF)
        rest = jnp.zeros((128 - WIDE, CHUNK), BF)
        return total + dot_nt(chosen, jnp.concatenate([joined_of(t), rest], 0))

    shape = (LEAVES * SLOTS, 128)
    taken = lax.fori_loop(0, CHUNKS, take, jnp.zeros(shape, F32), unroll=4)
    taken = jnp.where(iota(shape, 1) == WHICH, which, taken)
    taken = jnp.where(iota(shape, 1) == FULL, full, taken).astype(BF)
    for b in range(LEAVES):
        slots[b] = taken[b * SLOTS : (b + 1) * SLOTS]
    came[0] = slots[0]
    each(LEAVES, lambda k: send_slots(k).start())
    lax.fori_loop(1, 3, give, 0)

    each(LEAVES, lambda k: send_slots(k).wait_recv())
    got = jnp.concatenate([came[b] for b in range(LEAVES)], 0).astype(F32)
    chosen = got[:, WHICH : WHICH + 1] == iota((LEAVES * SLOTS, RANK), 1).astype(F32)
    picked = dot(got.T[:F].astype(BF), chosen.astype(F32).astype(BF))
    full = jnp.broadcast_to(jnp.max(got[:, FULL : FULL + 1], 0, keepdims=True), (1, 128))
    sk[0] = picked.astype(BF)
    each(COLS, lambda k: send_skel(k).start())
    lax.fori_loop(3, LEAVES // 2, give, 0)
    rx[0] = feat[0]
    ra[0] = aux[0]

    largest = jnp.zeros((OWNERS, 1), F32)
    for b in range(LEAVES):
        held_here = (iota((OWNERS, RANK), 0) == home[b : b + 1]).astype(F32)
        largest = jnp.maximum(largest, jnp.sum(held_here, 1, keepdims=True))

    for copy in smalls:
        copy.wait()
    spare[...] = jnp.ones((8, 128), F32)
    spare[0:1, 0:F] = scales[...]
    inverse = 1.0 / to_column(spare[0:1, :])[:F]
    scale = inverse * inverse * LOG2E
    scale2 = across(scale, RANK)
    scale4 = across(scale, PER)

    index[...] = top_index(parent, top, leaf // 4)
    index2 = across(index[...], 2 * RANK)
    number = iota((RANK, 2 * RANK), 1)
    base = (quarter * RANK).astype(F32)
    other = (sibling * RANK).astype(F32)
    chosen = index2[:, :RANK] == iota((RANK, RANK), 1).astype(F32) + base
    rows[...] = chosen.astype(F32).astype(BF)
    lanes = number.astype(F32) + jnp.where(number < RANK, base, other - RANK)
    columns[...] = (index2 == lanes).astype(F32).astype(BF)
    chosen = across(index[...], 4 * RANK) == iota((RANK, 4 * RANK), 1).astype(F32)
    fours[...] = chosen.astype(F32).astype(BF)

    def norms(k):
        side[k] = point_side(rx[k].astype(F32), scale4)

    def add_skel(k, total):
        send_skel(k).wait_recv()
        return total + sk[k].astype(F32)

    picked = lax.fori_loop(1, COLS, add_skel, picked)
    mine[...] = picked.astype(BF)
    sk4[quarter] = picked.astype(BF)

    def send_four(k):
        return remote(mine, sk4.at[quarter], (s_4, r_4), k, cousin(k))

    each(4, lambda k: send_four(k).start())
    left[0:RANK, :] = skel_side(picked, scale2)

    def block_of(k, out, begin):
        p = rx[k]
        fill = jnp.zeros((256 - 3 * F - 16, PER), BF)
        right = jnp.concatenate([p, p, p, side[k], fill], 0)
        power = dot(left[begin : begin + RANK, :], right)
        out[0:RANK, :] = jnp.exp2(jnp.minimum(power, 0.0)).astype(BF)

    def own_of(k, out):
        block_of(k, out, 0)
        value = ra[k]
        value = jnp.concatenate([value[r : r + 1] for r in range(4)], 1)
        out[RANK:, :] = jnp.broadcast_to(value, (16, PER)).astype(BF)

    def gram_of(u):
        gram[...] += dot_nt(u[...], u[0:RANK, :])

    def couple_of(v, u):
        couple[...] += dot_nt(v[...], u[0:RANK, :])

    last = LEAVES // 2 - 1

    def own_two(j, _):
        k, l = turn_of(2 * j), turn_of(2 * j + 1)
        pl.when(j > 0)(lambda: receive(k))
        receive(l)
        norms(k)
        norms(l)
        own_of(k, even.at[j])
        gram_of(odd.at[rem(j + last, last + 1)])
        own_of(l, odd.at[j])
        gram_of(even.at[j])
        return 0

    def receive(k):
        send_aux(k).wait_recv()
        send_feat(k).wait_recv()

    def other_two(j, _):
        block_of(turn_of(2 * j), other_even, RANK)
        couple_of(other_odd, odd.at[rem(j + last, last + 1)])
        block_of(turn_of(2 * j + 1), other_odd, RANK)
        couple_of(other_even, even.at[j])
        return 0

    gram[...] = jnp.zeros_like(gram)
    couple[...] = jnp.zeros_like(couple)
    odd[last] = jnp.zeros((RANK + 16, PER), BF)
    other_odd[...] = jnp.zeros_like(other_odd)
    def send_gram(k):
        return remote(pg.at[(col + k) % COLS], gr.at[k], (s_p, r_p), k, beside(k))

    def send_couple(k):
        return remote(pc.at[(col + k) % COLS], cr.at[k], (s_c, r_c), k, beside(k))

    def send_chosen(k):
        return remote(pt.at[(col + k) % COLS], qr.at[k], (s_o, r_o), k, beside(k))

    def send_rhs(k):
        return remote(rs, rr.at[k], (s_r, r_r), k, beside(k))

    def sibling_side():
        each(4, lambda k: remote(mine, sk4.at[(quarter + 4 - k) % 4], (s_4, r_4), k, cousin(k)).wait_recv())
        left[RANK:, :] = skel_side(sk4[sibling].astype(F32), scale2)

    def give_gram():
        gram_of(odd.at[last])
        part = gram[0:RANK, :].astype(BF)
        for k in range(COLS):
            pg[k] = part[k * SLAB : (k + 1) * SLAB]
        rhs = gram[RANK : RANK + 1, :]
        rhs = jnp.sum(dot_nt(stack16(split3(rhs), RANK), rows[...]), 0, keepdims=True)
        rs[...] = jnp.zeros_like(rs)
        rs[0:1, :] = rhs[:, :128]
        rs[1:2, :] = rhs[:, 128:]
        rs[2:3, :] = full
        each(COLS, lambda k: send_gram(k).start())
        each(COLS, lambda k: send_rhs(k).start())
        tops[...] = dot_nt(dot(rows[...], part).astype(BF), columns[:, 0:RANK])

    def half(h, _):
        pairs = LEAVES // 4
        lax.fori_loop(pairs * h, pairs * (h + 1), own_two, 0)
        pl.when(h == 0)(sibling_side)
        pl.when(h == 1)(give_gram)
        lax.fori_loop(pairs * h, pairs * (h + 1), other_two, 0)
        return 0

    lax.fori_loop(0, 2, half, 0)
    couple_of(other_odd, odd.at[last])

    part = couple[...].astype(BF)
    chosen = dot_nt(dot_nt(rows[...], part).astype(BF), columns[:, RANK:]) + tops[...]
    chosen = chosen.astype(BF)
    for k in range(COLS):
        pt[k] = chosen[k * SLAB : (k + 1) * SLAB]
    each(COLS, lambda k: send_chosen(k).start())
    part = couple[...].T.astype(BF)
    for k in range(COLS):
        pc[k] = part[k * SLAB : (k + 1) * SLAB]
    each(COLS, lambda k: send_couple(k).start())

    whole = jnp.concatenate([sk4[k] for k in range(4)], 1)
    points = dot_nt(whole, fours[...])
    fill = jnp.zeros((256 - 3 * F - 16, RANK), BF)
    points_b = points.astype(BF)
    right = jnp.concatenate([points_b, points_b, points_b, point_side(points, scale2), fill], 0)
    value = jnp.exp2(jnp.minimum(dot(skel_side(points, scale2), right), 0.0))
    crossing = (across(index[...], RANK) >= 2.0 * RANK) != (index[...].T[0:1, :] >= 2.0 * RANK)
    square = iota((RANK, RANK), 0) == iota((RANK, RANK), 1)
    tops[...] = jnp.where(crossing, value, 0.0) + jnp.where(square, ridge[...], 0.0)

    def finish(sends):
        return lambda k: [send(k).wait_send() for send in sends]

    each(LEAVES, finish((send_pivots, send_slots, send_aux, send_feat)))
    each(COLS, finish((send_skel, send_gram, send_rhs)))
    each(4, finish((send_four,)))

    def add_chosen(k, totals):
        send_chosen(k).wait_recv()
        send_rhs(k).wait_recv()
        return totals[0] + qr[k].astype(F32), totals[1] + rr[k]

    chosen, rhs = lax.fori_loop(1, COLS, add_chosen, (pt[col].astype(F32), rs[...]))
    over = jnp.maximum(jnp.max(rhs[2:3, :]), jnp.max(largest) - SLOTS)
    flag[0] = (over > 0.0).astype(jnp.int32)
    chosen = chosen * (1.0 / NODE)
    t4[0] = chosen.astype(BF)
    r4[0] = rhs * (1.0 / NODE)

    def send_top(k):
        return remote(t4.at[0], t4.at[k], (s_t, r_t), k, cousin(k))

    def send_top_rhs(k):
        return remote(r4.at[0], r4.at[k], (s_q, r_q), k, cousin(k))

    each(4, lambda k: send_top(k).start())
    each(4, lambda k: send_top_rhs(k).start())

    def add_gram(k, total):
        send_gram(k).wait_recv()
        return total + gr[k].astype(F32)

    def add_couple(k, total):
        send_couple(k).wait_recv()
        return total + cr[k].astype(F32)

    total = lax.fori_loop(1, COLS, add_gram, pg[col].astype(F32))
    diagonal = iota((SLAB, RANK), 0) + col * SLAB == iota((SLAB, RANK), 1)
    out_share[0, :, 0:RANK] = total * (1.0 / NODE) + jnp.where(diagonal, ridge[...], 0.0)
    total = lax.fori_loop(1, COLS, add_couple, pc[col].astype(F32))
    out_share[0, :, RANK:] = total * (1.0 / NODE)
    result = chosen + tops[pl.ds(pl.multiple_of(col * SLAB, SLAB), SLAB), :]

    def add_top(k, totals):
        send_top(k).wait_recv()
        send_top_rhs(k).wait_recv()
        return totals[0] + t4[k].astype(F32), totals[1] + r4[k]

    result, rhs = lax.fori_loop(1, 4, add_top, (result, r4[0]))
    out_top[0] = result
    out_rhs[...] = jnp.concatenate([rhs[0:1], rhs[1:2]], 1)

    each(COLS, finish((send_couple, send_chosen)))
    each(4, finish((send_top, send_top_rhs)))


SHAPES = ((1, SLAB, 2 * RANK), (1, SLAB, RANK), (1, RANK))


def exchange(merged, ridge, *smalls):
    return pl.pallas_call(
        exchange_kernel,
        out_shape=tuple(pltpu.VMEM(shape, F32) for shape in SHAPES),
        in_specs=[VMEM, VMEM] + [ANYWHERE] * 4,
        out_specs=[VMEM] * 3,
        scratch_shapes=[
            pltpu.VMEM((1, RANK), jnp.int32),
            pltpu.VMEM((1, F), F32),
            pltpu.VMEM((8, RANK), jnp.int32),
            pltpu.VMEM((4, RANK), jnp.int32),
            pltpu.VMEM((8, 128), F32),
            pltpu.VMEM((LEAVES, F, PER), BF),
            pltpu.VMEM((LEAVES, 8, 128), F32),
            pltpu.VMEM((LEAVES, F, PER), BF),
            pltpu.VMEM((LEAVES, 8, 128), F32),
            pltpu.VMEM((LEAVES, RANK, PER), BF),
            pltpu.VMEM((LEAVES, 16, PER), BF),
            pltpu.VMEM((COLS, F, RANK), BF),
            pltpu.VMEM((F, RANK), BF),
            pltpu.VMEM((4, F, RANK), BF),
            pltpu.VMEM((2 * RANK, 256), BF),
            pltpu.VMEM((LEAVES // 2, RANK + 16, PER), BF),
            pltpu.VMEM((LEAVES // 2, RANK + 16, PER), BF),
            pltpu.VMEM((RANK, PER), BF),
            pltpu.VMEM((RANK, PER), BF),
            pltpu.VMEM((RANK + 16, RANK), F32),
            pltpu.VMEM((RANK, RANK), F32),
            pltpu.VMEM((RANK, RANK), BF),
            pltpu.VMEM((RANK, 2 * RANK), BF),
            pltpu.VMEM((RANK, 4 * RANK), BF),
            pltpu.VMEM((RANK, 128), F32),
            pltpu.VMEM((RANK, RANK), F32),
            pltpu.VMEM((COLS, SLAB, RANK), BF),
            pltpu.VMEM((COLS, SLAB, RANK), BF),
            pltpu.VMEM((COLS, SLAB, RANK), BF),
            pltpu.VMEM((COLS, SLAB, RANK), BF),
            pltpu.VMEM((COLS, SLAB, RANK), BF),
            pltpu.VMEM((COLS, SLAB, RANK), BF),
            pltpu.VMEM((8, 128), F32),
            pltpu.VMEM((COLS, 8, 128), F32),
            pltpu.VMEM((4, SLAB, RANK), BF),
            pltpu.VMEM((4, 8, 128), F32),
            *dma(LEAVES),
            *dma(LEAVES),
            *dma(COLS),
            *dma(4),
            *dma(COLS),
            *dma(COLS),
            *dma(COLS),
            *dma(COLS),
            *dma(4),
            *dma(4),
            pltpu.SemaphoreType.DMA((5,)),
        ],
        compiler_params=params(0, 40),
        name="exchange",
    )(merged, ridge, *in_hbm(*smalls))


def stream(samples, pivots, ridge, *smalls):
    return pl.pallas_call(
        stream_kernel,
        out_shape=(
            *(pltpu.VMEM(shape, F32) for shape in SHAPES),
            jax.ShapeDtypeStruct((1,), jnp.int32),
        ),
        in_specs=[ANYWHERE, VMEM, VMEM, VMEM, VMEM] + [ANYWHERE] * 3,
        out_specs=[VMEM] * 3 + [pl.BlockSpec(memory_space=pltpu.SMEM)],
        scratch_shapes=[
            pltpu.VMEM((F, ROWS), BF),
            pltpu.VMEM((ROWS // 128, 128), F32),
            pltpu.VMEM((CHUNKS, 8, CHUNK), F32),
            pltpu.VMEM((LEAVES, 128), F32),
            pltpu.VMEM((LEAVES, 128), F32),
            pltpu.VMEM((ROWS + TILE, WIDE), F32),
            pltpu.VMEM((LEAVES // AT_ONCE, 16, 128), jnp.int32),
            pltpu.SMEM((LEAVES // AT_ONCE, 16, 128), jnp.int32),
            pltpu.VMEM((LEAVES, 1, RANK), jnp.int32),
            pltpu.VMEM((LEAVES, SLOTS, 128), BF),
            pltpu.VMEM((LEAVES, SLOTS, 128), BF),
            pltpu.VMEM((1, F), F32),
            pltpu.VMEM((8, RANK), jnp.int32),
            pltpu.VMEM((4, RANK), jnp.int32),
            pltpu.VMEM((8, 128), F32),
            pltpu.VMEM((LEAVES, F, PER), BF),
            pltpu.VMEM((LEAVES, 8, 128), F32),
            pltpu.VMEM((LEAVES, F, PER), BF),
            pltpu.VMEM((LEAVES, 8, 128), F32),
            pltpu.VMEM((LEAVES, 16, PER), BF),
            pltpu.VMEM((COLS, F, RANK), BF),
            pltpu.VMEM((F, RANK), BF),
            pltpu.VMEM((4, F, RANK), BF),
            pltpu.VMEM((2 * RANK, 256), BF),
            pltpu.VMEM((LEAVES // 2, RANK + 16, PER), BF),
            pltpu.VMEM((LEAVES // 2, RANK + 16, PER), BF),
            pltpu.VMEM((RANK, PER), BF),
            pltpu.VMEM((RANK, PER), BF),
            pltpu.VMEM((RANK + 16, RANK), F32),
            pltpu.VMEM((RANK, RANK), F32),
            pltpu.VMEM((RANK, RANK), BF),
            pltpu.VMEM((RANK, 2 * RANK), BF),
            pltpu.VMEM((RANK, 4 * RANK), BF),
            pltpu.VMEM((RANK, 128), F32),
            pltpu.VMEM((RANK, RANK), F32),
            pltpu.VMEM((COLS, SLAB, RANK), BF),
            pltpu.VMEM((COLS, SLAB, RANK), BF),
            pltpu.VMEM((COLS, SLAB, RANK), BF),
            pltpu.VMEM((COLS, SLAB, RANK), BF),
            pltpu.VMEM((COLS, SLAB, RANK), BF),
            pltpu.VMEM((COLS, SLAB, RANK), BF),
            pltpu.VMEM((8, 128), F32),
            pltpu.VMEM((COLS, 8, 128), F32),
            pltpu.VMEM((4, SLAB, RANK), BF),
            pltpu.VMEM((4, 8, 128), F32),
            *dma(LEAVES),
            *dma(LEAVES),
            *dma(LEAVES),
            *dma(LEAVES),
            *dma(COLS),
            *dma(4),
            *dma(COLS),
            *dma(COLS),
            *dma(COLS),
            *dma(COLS),
            *dma(4),
            *dma(4),
            pltpu.SemaphoreType.DMA((5,)),
        ],
        compiler_params=params(1, 40),
        name="stream",
    )(*in_hbm(*samples, pivots), ridge, *in_hbm(*smalls))


def emit_kernel(*refs):
    ins, outs, sem = refs[:3], refs[3:6], refs[6]
    copies = [pltpu.make_async_copy(a, b, sem.at[k]) for k, (a, b) in enumerate(zip(ins, outs))]
    for copy in copies:
        copy.start()
    for copy in copies:
        copy.wait()


def emit(results):
    return pl.pallas_call(
        emit_kernel,
        out_shape=tuple(jax.ShapeDtypeStruct(shape, F32) for shape in SHAPES),
        in_specs=[VMEM] * 3,
        out_specs=[ANYWHERE] * 3,
        scratch_shapes=[pltpu.SemaphoreType.DMA((3,))],
        compiler_params=params(),
        name="emit",
    )(*results)


def local(features, targets, owner, length_scales, ridge, leaf_pivots, parent_pivots, top_pivots):
    samples = (features, targets.reshape(ROWS // 128, 128), owner.reshape(ROWS // 128, 128))
    ridge = ridge.reshape(1, 1)
    smalls = (length_scales.reshape(1, F), parent_pivots, top_pivots)
    *results, flag = stream(samples, leaf_pivots, ridge, *smalls)

    def again():
        return tuple(emit(exchange(pack(*samples), ridge, leaf_pivots, *smalls)))

    return lax.switch(flag[0], [lambda: tuple(emit(results)), again])


def solution(mesh):
    return jax.shard_map(
        local,
        mesh=mesh,
        in_specs=(
            P(None, ("leaf", "col")),
            P(("leaf", "col")),
            P(("leaf", "col")),
            P(),
            P(),
            P("leaf", None),
            P(),
            P(),
        ),
        out_specs=(P("leaf", "col", None), P("leaf", "col", None), P("leaf", None)),
        check_vma=False,
    )
```

```python
import functools
import math

import jax
import jax.numpy as jnp
from jax import lax
from jax.experimental import pallas as pl
from jax.experimental.pallas import tpu as pltpu
from jax.sharding import PartitionSpec as P

F = 48
RANK = 256
ROWS = 8192
LEAVES = 16
COLS = 8
OWNERS = 128
PACKET = 64
PER = ROWS // LEAVES
CHUNK = 256
CHUNKS = ROWS // CHUNK
WINDOW = 40
REGION = PER + WINDOW
TILE = 32
TILES = PER // TILE
PIECES = 6
AT_ONCE = 128 // TILES
SLOTS = 16
WHICH = 50
FULL = 51
WIDE = 64
SLAB = RANK // COLS
NODE = ROWS * COLS
LOG2E = math.log2(math.e)
BF = jnp.bfloat16
F32 = jnp.float32
NT = (((1,), (1,)), ((), ()))
MESH = pl.DeviceIdType.MESH


def dma(count):
    return [pltpu.SemaphoreType.DMA((count,))] * 2


def params(number=None, limit=24):
    if number is None:
        return pltpu.CompilerParams(vmem_limit_bytes=limit * 2**20)
    return pltpu.CompilerParams(
        collective_id=number, has_side_effects=True, vmem_limit_bytes=limit * 2**20
    )


ANYWHERE = pl.BlockSpec(memory_space=pl.ANY)
VMEM = pl.BlockSpec(memory_space=pltpu.VMEM)


def iota(shape, axis):
    return lax.broadcasted_iota(jnp.int32, shape, axis)


def dot(a, b):
    return jnp.dot(a, b, preferred_element_type=F32)


def dot_nt(a, b):
    return lax.dot_general(a, b, NT, preferred_element_type=F32)


def row_pair(two):
    return jnp.concatenate([two[0:1], two[1:2]], 1)


def pack_kernel(
    feat_hbm, target, owner, zbuf, feat, goals, rows, ybuf, table, scal, sem, feat_sem
):
    bring = pltpu.make_async_copy(feat_hbm, feat, feat_sem)
    bring.start()
    goals[...] = target[...].astype(F32)
    before = (iota((CHUNK, CHUNK), 0) < iota((CHUNK, CHUNK), 1)).astype(F32).astype(BF)
    weights = jnp.concatenate([before, jnp.ones((CHUNK, 128), BF)], 1)
    lane = iota((LEAVES, 128), 1)

    def ranks(t, carry):
        seen, seen_leaf, most = carry
        own = row_pair(owner[pl.ds(2 * t, 2), :])
        leaf = own // 8
        is_own = iota((OWNERS, CHUNK), 0) == own
        is_leaf = iota((LEAVES, CHUNK), 0) == leaf
        is_after = iota((LEAVES, CHUNK), 0) > leaf
        marks = jnp.concatenate(
            [m.astype(F32).astype(BF) for m in (is_own, is_leaf, is_after)], 0
        )
        sums = dot(marks, weights)
        counts = sums[:OWNERS, CHUNK:]
        leaf_counts = sums[OWNERS : OWNERS + LEAVES, CHUNK:]
        base = sums[OWNERS + LEAVES :, CHUNK:]
        prior = sums[:OWNERS, :CHUNK] + jnp.concatenate([seen, seen], 1)
        rank = jnp.sum(jnp.where(is_own, prior, 0.0), 0, keepdims=True)
        place = sums[OWNERS : OWNERS + LEAVES, :CHUNK] + jnp.concatenate([base, base], 1)
        place = jnp.sum(jnp.where(is_leaf, place, 0.0), 0, keepdims=True)
        tag = (own % 8).astype(F32) * PACKET + rank - (PER // 2)
        rows[t, 0:1, :] = place
        rows[t, 1:2, :] = row_pair(goals[pl.ds(2 * t, 2), :])
        rows[t, 2:3, :] = tag
        here = lane == t
        table[0:LEAVES, :] = jnp.where(here, seen_leaf.astype(jnp.int32), table[0:LEAVES, :])
        table[LEAVES : 2 * LEAVES, :] = jnp.where(
            here, base.astype(jnp.int32), table[LEAVES : 2 * LEAVES, :]
        )
        return seen + counts, seen_leaf + leaf_counts, jnp.maximum(most, leaf_counts)

    table[0:LEAVES, :] = jnp.full((LEAVES, 128), PER, jnp.int32)
    zero = jnp.zeros((LEAVES, 128), F32)
    _, _, most = lax.fori_loop(
        0, CHUNKS, ranks, (jnp.zeros((OWNERS, 128), F32), zero, zero), unroll=16
    )
    most = jnp.broadcast_to(jnp.max(most, 0, keepdims=True), (8, 128))
    table[2 * LEAVES :, :] = most.astype(jnp.int32)
    move = pltpu.make_async_copy(table, scal, sem)
    move.start()
    bring.wait()

    def sort(t, _):
        start = pl.multiple_of(t * CHUNK, CHUNK)
        row = iota((16, CHUNK), 0)
        place, goal, tag = rows[t, 0:1, :], rows[t, 1:2, :], rows[t, 2:3, :]
        extra = jnp.where(row == 0, goal, jnp.where(row == 1, tag, 0.0)).astype(BF)
        joined = jnp.concatenate([feat[:, pl.ds(start, CHUNK)], extra], 0)
        chosen = (iota((CHUNK, CHUNK), 0) == place.astype(jnp.int32)).astype(F32).astype(BF)
        ybuf[pl.ds(start, CHUNK), :] = dot_nt(chosen, joined)
        return 0

    lax.fori_loop(0, CHUNKS, sort, 0, unroll=8)
    move.wait()
    widest = scal[2 * LEAVES, 0]

    @pl.when(widest <= WINDOW)
    def quick():
        def merge(t, _):
            for i in range(LEAVES):
                source = t * CHUNK + scal[LEAVES + i, t]
                goal = i * REGION + scal[i, t]
                zbuf[pl.ds(goal, WINDOW), :] = ybuf[pl.ds(source, WINDOW), :]
            return 0

        lax.fori_loop(0, CHUNKS, merge, 0, unroll=4)

    @pl.when(widest > WINDOW)
    def slow():
        def merge(index, _):
            t = index // LEAVES
            i = index % LEAVES
            source = t * CHUNK + scal[LEAVES + i, t]
            first = scal[i, t]
            count = scal[i, t + 1] - first

            def part(k, _):
                rows = ybuf[pl.ds(source + 8 * k, 8), :]
                zbuf[pl.ds(i * REGION + first + 8 * k, 8), :] = rows
                return 0

            lax.fori_loop(0, (count + 7) // 8, part, 0)
            return 0

        lax.fori_loop(0, CHUNKS * LEAVES, merge, 0)


def in_hbm(*arrays):
    return [pltpu.with_memory_space_constraint(a, pltpu.HBM) for a in arrays]


def pack(features, targets, owner):
    return pl.pallas_call(
        pack_kernel,
        out_shape=pltpu.VMEM((LEAVES * REGION, WIDE), F32),
        in_specs=[ANYWHERE, VMEM, VMEM],
        out_specs=VMEM,
        scratch_shapes=[
            pltpu.VMEM((F, ROWS), BF),
            pltpu.VMEM((ROWS // 128, 128), F32),
            pltpu.VMEM((CHUNKS, 8, CHUNK), F32),
            pltpu.VMEM((ROWS + WINDOW, WIDE), F32),
            pltpu.VMEM((40, 128), jnp.int32),
            pltpu.SMEM((40, 128), jnp.int32),
            pltpu.SemaphoreType.DMA,
            pltpu.SemaphoreType.DMA,
        ],
        compiler_params=params(),
        name="pack",
    )(*in_hbm(features, targets, owner))


def split3(x):
    high = x.astype(BF)
    rest = x - high.astype(F32)
    mid = rest.astype(BF)
    return high, mid, (rest - mid.astype(F32)).astype(BF)


def stack16(parts, width):
    row = iota((16, width), 0)
    block = jnp.zeros((16, width), F32)
    for k, part in enumerate(parts):
        block = jnp.where(row == k, part if isinstance(part, float) else part.astype(F32), block)
    return block.astype(BF)


def half_norm(points, scale):
    return jnp.sum(points * points * (0.5 * scale), 0, keepdims=True)


def point_side(points, scale):
    high, mid, low = split3(-half_norm(points, scale))
    return stack16([high, mid, low, 1.0, 1.0, 1.0], points.shape[1])


def skel_side(skel, scale):
    width = skel.shape[1]
    high, mid, low = split3(skel * scale)
    extra = stack16([1.0, 1.0, 1.0, *split3(-half_norm(skel, scale))], width)
    parts = [p.astype(F32) for p in (high, mid, low, extra)]
    fill = jnp.zeros((256 - 3 * F - 16, width), F32)
    return jnp.concatenate([*parts, fill], 0).T.astype(BF)


def select_row(table, row):
    hit = iota(table.shape, 0) == row
    return jnp.sum(jnp.where(hit, table.astype(F32), 0.0), 0, keepdims=True)


def to_column(row):
    return jnp.broadcast_to(row, (128, row.shape[1])).T


def across(column, width):
    return jnp.concatenate([column] * (width // 128), 1)


def place_of(leaf, col):
    return dict(device_id=(leaf, col), device_id_type=MESH)


def mate(k):
    leaf, col = lax.axis_index("leaf"), lax.axis_index("col")
    to = (leaf + k) % LEAVES
    cross = (to // 8 + leaf // 8) % 2
    return place_of(to, col + cross * (1 - 2 * (col % 2)))


def beside(k):
    leaf, col = lax.axis_index("leaf"), lax.axis_index("col")
    return place_of(leaf, (col + k) % COLS)


def cousin(k):
    leaf, col = lax.axis_index("leaf"), lax.axis_index("col")
    return place_of(leaf - leaf % 4 + (leaf + k) % 4, col)


def each(count, step, unroll=1):
    lax.fori_loop(1, count, lambda k, _: (step(k), 0)[1], 0, unroll=unroll)


def rem(a, b):
    return lax.rem(jnp.int32(a), jnp.int32(b))


def turn_of(n):
    n = jnp.int32(n)
    odd = lax.rem(n, jnp.int32(2))
    half = lax.div(n + odd, jnp.int32(2))
    return lax.rem(odd * half + (1 - odd) * (LEAVES - half), jnp.int32(LEAVES))


def remote(src, dst, sems, k, peer):
    return pltpu.make_async_remote_copy(src, dst, sems[0].at[k], sems[1].at[k], **peer)


def top_index(parent, top, group):
    top_row = select_row(top[...], group)
    below = jnp.concatenate([select_row(parent[...], 2 * group + r) for r in range(2)], 1)
    number = iota((RANK, 2 * RANK), 1)
    below = below + jnp.where(iota((1, 2 * RANK), 1) >= RANK, 2.0 * RANK, 0.0)
    hit = across(to_column(top_row), 2 * RANK) == number.astype(F32)
    index = jnp.sum(jnp.where(hit, below, 0.0), 1, keepdims=True)
    return jnp.broadcast_to(index, (RANK, 128))


def exchange_kernel(
    merged, ridge, pivots_hbm, scales_hbm, parent_hbm, top_hbm, out_share, out_top, out_rhs,
    pivots, scales, parent, top, spare, feat, aux, rx, ra, hot, side, sk, mine, sk4, left,
    even, odd, other_even, other_odd, gram, couple, rows, columns, fours, index, tops,
    pg, gr, pc, cr, pt, qr, rs, rr, t4, r4,
    s_f, r_f, s_a, r_a, s_k, r_k, s_4, r_4, s_p, r_p, s_c, r_c, s_o, r_o, s_r, r_r, s_t, r_t, s_q, r_q, local,
):
    leaf = lax.axis_index("leaf")
    col = lax.axis_index("col")
    quarter = leaf % 4
    sibling = quarter + 1 - 2 * (quarter % 2)
    barrier = pltpu.get_barrier_semaphore()
    each(LEAVES, lambda k: pl.semaphore_signal(barrier, inc=1, **mate(k)))
    each(COLS, lambda k: pl.semaphore_signal(barrier, inc=1, **beside(k)))
    smalls = [
        pltpu.make_async_copy(a, b, local.at[k])
        for k, (a, b) in enumerate(
            [(pivots_hbm, pivots), (scales_hbm, scales), (parent_hbm, parent), (top_hbm, top)]
        )
    ]
    for copy in smalls:
        copy.start()

    eye = (iota((WIDE, WIDE), 0) == iota((WIDE, WIDE), 1)).astype(F32).astype(BF)

    def turn(k):
        start = pl.multiple_of((leaf + k) % LEAVES * REGION, 8)
        turned = dot_nt(eye, merged[pl.ds(start, PER), :].astype(BF))
        feat[k] = turned[:F].astype(BF)
        aux[k] = jnp.concatenate(
            [turned[F + r : F + r + 1, 128 * c : 128 * c + 128] for r in range(2) for c in range(4)], 0
        )

    def send_feat(k):
        return remote(feat.at[k], rx.at[k], (s_f, r_f), k, mate(k))

    def send_aux(k):
        return remote(aux.at[k], ra.at[k], (s_a, r_a), k, mate(k))

    def four(j, _):
        steps = [turn_of(lax.rem(4 * j + r, LEAVES)) for r in range(1, 5)]
        for k in steps:
            turn(k)
        pl.when(j == 0)(lambda: pl.semaphore_wait(barrier, LEAVES + COLS - 2))
        for send in (send_aux, send_feat):
            for k in steps[:3]:
                send(k).start()
            pl.when(j < 3)(lambda: send(steps[3]).start())
        return 0

    lax.fori_loop(0, LEAVES // 4, four, 0)
    rx[0] = feat[0]
    ra[0] = aux[0]

    for copy in smalls:
        copy.wait()
    spare[...] = jnp.ones((8, 128), F32)
    spare[0:1, 0:F] = scales[...]
    inverse = 1.0 / to_column(spare[0:1, :])[:F]
    scale = inverse * inverse * LOG2E
    scale2 = across(scale, RANK)
    scale4 = across(scale, PER)

    place = pivots[...]
    within = place % ROWS
    block = within // PACKET
    key = (block // COLS) * PER + (place // ROWS) * PACKET + within % PACKET
    holder = block % COLS
    crossed = (block // COLS) // 8 != leaf // 8
    holder = jnp.where(crossed, holder + 1 - 2 * (holder % 2), holder)
    key = jnp.where(holder == col, key, -PER)
    key = across(to_column(key.astype(F32)), PER)

    def mark(k):
        source = (leaf + LEAVES - k) % LEAVES
        tags = ra[k, 4:8, :]
        tag = jnp.concatenate([tags[r : r + 1] for r in range(4)], 1)
        wanted = tag + (PER // 2 + source * PER).astype(F32)
        hot[k] = (key == wanted).astype(F32).astype(BF)

    def mark_next(n, _):
        k = turn_of(n)
        pl.when(n > 0)(lambda: send_aux(k).wait_recv())
        mark(k)
        return 0

    lax.fori_loop(0, LEAVES, mark_next, 0)

    index[...] = top_index(parent, top, leaf // 4)
    index2 = across(index[...], 2 * RANK)
    number = iota((RANK, 2 * RANK), 1)
    base = (quarter * RANK).astype(F32)
    other = (sibling * RANK).astype(F32)
    chosen = index2[:, :RANK] == iota((RANK, RANK), 1).astype(F32) + base
    rows[...] = chosen.astype(F32).astype(BF)
    lanes = number.astype(F32) + jnp.where(number < RANK, base, other - RANK)
    columns[...] = (index2 == lanes).astype(F32).astype(BF)
    chosen = across(index[...], 4 * RANK) == iota((RANK, 4 * RANK), 1).astype(F32)
    fours[...] = chosen.astype(F32).astype(BF)

    def pick(j, total):
        steps = [turn_of(4 * j + r) for r in range(4)]
        pl.when(j > 0)(lambda: send_feat(steps[0]).wait_recv())
        for k in steps[1:]:
            send_feat(k).wait_recv()
        for k in steps:
            total = total + dot_nt(hot[k], rx[k])
        return total

    picked = lax.fori_loop(0, LEAVES // 4, pick, jnp.zeros((RANK, F), F32))
    picked = jnp.concatenate([picked, jnp.zeros((RANK, 128 - F), F32)], 1).T[:F]
    sk[0] = picked.astype(BF)

    def send_skel(k):
        return remote(sk.at[0], sk.at[k], (s_k, r_k), k, beside(k))

    each(COLS, lambda k: send_skel(k).start())

    def norms(k, _):
        side[k] = point_side(rx[k].astype(F32), scale4)
        return 0

    lax.fori_loop(0, LEAVES, norms, 0)

    def add_skel(k, total):
        send_skel(k).wait_recv()
        return total + sk[k].astype(F32)

    picked = lax.fori_loop(1, COLS, add_skel, picked)
    mine[...] = picked.astype(BF)
    sk4[quarter] = picked.astype(BF)

    def send_four(k):
        return remote(mine, sk4.at[quarter], (s_4, r_4), k, cousin(k))

    each(4, lambda k: send_four(k).start())
    left[0:RANK, :] = skel_side(picked, scale2)

    def block_of(k, out, begin):
        p = rx[k]
        fill = jnp.zeros((256 - 3 * F - 16, PER), BF)
        right = jnp.concatenate([p, p, p, side[k], fill], 0)
        power = dot(left[begin : begin + RANK, :], right)
        out[0:RANK, :] = jnp.exp2(jnp.minimum(power, 0.0)).astype(BF)

    def own_of(k, out):
        block_of(k, out, 0)
        value = jnp.concatenate([ra[k, r : r + 1, :] for r in range(4)], 1)
        out[RANK:, :] = jnp.broadcast_to(value, (16, PER)).astype(BF)

    def gram_of(u):
        gram[...] += dot_nt(u[...], u[0:RANK, :])

    def couple_of(v, u):
        couple[...] += dot_nt(v[...], u[0:RANK, :])

    last = LEAVES // 2 - 1

    def own_two(j, _):
        own_of(2 * j, even.at[j])
        gram_of(odd.at[(j + last) % (last + 1)])
        own_of(2 * j + 1, odd.at[j])
        gram_of(even.at[j])
        return 0

    def other_two(j, _):
        block_of(2 * j, other_even, RANK)
        couple_of(other_odd, odd.at[(j + last) % (last + 1)])
        block_of(2 * j + 1, other_odd, RANK)
        couple_of(other_even, even.at[j])
        return 0

    gram[...] = jnp.zeros_like(gram)
    couple[...] = jnp.zeros_like(couple)
    odd[last] = jnp.zeros((RANK + 16, PER), BF)
    other_odd[...] = jnp.zeros_like(other_odd)
    lax.fori_loop(0, last + 1, own_two, 0)
    gram_of(odd.at[last])

    def send_gram(k):
        return remote(pg.at[(col + k) % COLS], gr.at[k], (s_p, r_p), k, beside(k))

    def send_couple(k):
        return remote(pc.at[(col + k) % COLS], cr.at[k], (s_c, r_c), k, beside(k))

    def send_chosen(k):
        return remote(pt.at[(col + k) % COLS], qr.at[k], (s_o, r_o), k, beside(k))

    def send_rhs(k):
        return remote(rs, rr.at[k], (s_r, r_r), k, beside(k))

    part = gram[0:RANK, :].astype(BF)
    for k in range(COLS):
        pg[k] = part[k * SLAB : (k + 1) * SLAB]
    rhs = gram[RANK : RANK + 1, :]
    rhs = jnp.sum(dot_nt(stack16(split3(rhs), RANK), rows[...]), 0, keepdims=True)
    rs[...] = jnp.zeros_like(rs)
    rs[0:1, :] = rhs[:, :128]
    rs[1:2, :] = rhs[:, 128:]
    each(COLS, lambda k: send_gram(k).start())
    each(COLS, lambda k: send_rhs(k).start())
    tops[...] = dot_nt(dot(rows[...], part).astype(BF), columns[:, 0:RANK])

    each(4, lambda k: remote(mine, sk4.at[(quarter + 4 - k) % 4], (s_4, r_4), k, cousin(k)).wait_recv())
    left[RANK:, :] = skel_side(sk4[sibling].astype(F32), scale2)
    lax.fori_loop(0, last + 1, other_two, 0)
    couple_of(other_odd, odd.at[last])

    part = couple[...].astype(BF)
    chosen = dot_nt(dot_nt(rows[...], part).astype(BF), columns[:, RANK:]) + tops[...]
    chosen = chosen.astype(BF)
    for k in range(COLS):
        pt[k] = chosen[k * SLAB : (k + 1) * SLAB]
    each(COLS, lambda k: send_chosen(k).start())
    part = couple[...].T.astype(BF)
    for k in range(COLS):
        pc[k] = part[k * SLAB : (k + 1) * SLAB]
    each(COLS, lambda k: send_couple(k).start())

    whole = jnp.concatenate([sk4[k] for k in range(4)], 1)
    points = dot_nt(whole, fours[...])
    fill = jnp.zeros((256 - 3 * F - 16, RANK), BF)
    points_b = points.astype(BF)
    right = jnp.concatenate([points_b, points_b, points_b, point_side(points, scale2), fill], 0)
    value = jnp.exp2(jnp.minimum(dot(skel_side(points, scale2), right), 0.0))
    crossing = (across(index[...], RANK) >= 2.0 * RANK) != (index[...].T[0:1, :] >= 2.0 * RANK)
    square = iota((RANK, RANK), 0) == iota((RANK, RANK), 1)
    tops[...] = jnp.where(crossing, value, 0.0) + jnp.where(square, ridge[...], 0.0)

    def finish(sends):
        return lambda k: [send(k).wait_send() for send in sends]

    each(LEAVES, finish((send_aux, send_feat)))
    each(COLS, finish((send_skel, send_gram, send_rhs)))
    each(4, finish((send_four,)))

    def add_chosen(k, totals):
        send_chosen(k).wait_recv()
        send_rhs(k).wait_recv()
        return totals[0] + qr[k].astype(F32), totals[1] + rr[k]

    chosen, rhs = lax.fori_loop(1, COLS, add_chosen, (pt[col].astype(F32), rs[...]))
    chosen = chosen * (1.0 / NODE)
    t4[0] = chosen.astype(BF)
    r4[0] = rhs * (1.0 / NODE)

    def send_top(k):
        return remote(t4.at[0], t4.at[k], (s_t, r_t), k, cousin(k))

    def send_top_rhs(k):
        return remote(r4.at[0], r4.at[k], (s_q, r_q), k, cousin(k))

    each(4, lambda k: send_top(k).start())
    each(4, lambda k: send_top_rhs(k).start())

    def add_gram(k, total):
        send_gram(k).wait_recv()
        return total + gr[k].astype(F32)

    def add_couple(k, total):
        send_couple(k).wait_recv()
        return total + cr[k].astype(F32)

    total = lax.fori_loop(1, COLS, add_gram, pg[col].astype(F32))
    diagonal = iota((SLAB, RANK), 0) + col * SLAB == iota((SLAB, RANK), 1)
    out_share[0, :, 0:RANK] = total * (1.0 / NODE) + jnp.where(diagonal, ridge[...], 0.0)
    total = lax.fori_loop(1, COLS, add_couple, pc[col].astype(F32))
    out_share[0, :, RANK:] = total * (1.0 / NODE)
    result = chosen + tops[pl.ds(pl.multiple_of(col * SLAB, SLAB), SLAB), :]

    def add_top(k, totals):
        send_top(k).wait_recv()
        send_top_rhs(k).wait_recv()
        return totals[0] + t4[k].astype(F32), totals[1] + r4[k]

    result, rhs = lax.fori_loop(1, 4, add_top, (result, r4[0]))
    out_top[0] = result
    out_rhs[...] = jnp.concatenate([rhs[0:1], rhs[1:2]], 1)

    each(COLS, finish((send_couple, send_chosen)))
    each(4, finish((send_top, send_top_rhs)))


def stream_kernel(
    feat_hbm, target, owner, pivots, ridge, scales_hbm, parent_hbm, top_hbm,
    out_share, out_top, out_rhs, flag,
    feat_in, goals, ranked, starts, bases, ybuf, table, scal, held, slots, came, scales, parent, top, spare,
    feat, aux, rx, ra, side, sk, mine, sk4, left, even, odd, other_even, other_odd, gram, couple,
    rows, columns, fours, index, tops, pg, gr, pc, cr, pt, qr, rs, rr, t4, r4,
    s_v, r_v, s_s, r_s, s_f, r_f, s_a, r_a, s_k, r_k, s_4, r_4, s_p, r_p, s_c, r_c, s_o, r_o,
    s_r, r_r, s_t, r_t, s_q, r_q, local,
):
    leaf = lax.axis_index("leaf")
    col = lax.axis_index("col")
    quarter = leaf % 4
    sibling = quarter + 1 - 2 * (quarter % 2)
    barrier = pltpu.get_barrier_semaphore()
    each(LEAVES, lambda k: pl.semaphore_signal(barrier, inc=1, **mate(k)))
    each(COLS, lambda k: pl.semaphore_signal(barrier, inc=1, **beside(k)))
    bring = pltpu.make_async_copy(feat_hbm, feat_in, local.at[3])
    bring.start()
    smalls = [
        pltpu.make_async_copy(a, b, local.at[k])
        for k, (a, b) in enumerate([(scales_hbm, scales), (parent_hbm, parent), (top_hbm, top)])
    ]
    for copy in smalls:
        copy.start()

    def send_pivots(k):
        return remote(pivots, held.at[k], (s_v, r_v), k, mate(k))

    def send_slots(k):
        return remote(slots.at[k], came.at[k], (s_s, r_s), k, mate(k))

    def send_feat(k):
        return remote(feat.at[k], rx.at[k], (s_f, r_f), k, mate(k))

    def send_aux(k):
        return remote(aux.at[k], ra.at[k], (s_a, r_a), k, mate(k))

    def send_skel(k):
        return remote(sk.at[0], sk.at[k], (s_k, r_k), k, beside(k))

    goals[...] = target[...].astype(F32)
    before = (iota((CHUNK, CHUNK), 0) < iota((CHUNK, CHUNK), 1)).astype(F32).astype(BF)
    weights = jnp.concatenate([before, jnp.ones((CHUNK, 128), BF)], 1)
    lane = iota((LEAVES, 128), 1)

    def rank(t, carry):
        seen, seen_leaf = carry
        own = row_pair(owner[pl.ds(2 * t, 2), :])
        group = own // 8
        is_own = iota((OWNERS, CHUNK), 0) == own
        is_leaf = iota((LEAVES, CHUNK), 0) == group
        is_after = iota((LEAVES, CHUNK), 0) > group
        marks = jnp.concatenate([m.astype(F32).astype(BF) for m in (is_own, is_leaf, is_after)], 0)
        sums = dot(marks, weights)
        leaf_counts = sums[OWNERS : OWNERS + LEAVES, CHUNK:]
        base = sums[OWNERS + LEAVES :, CHUNK:]
        prior = sums[:OWNERS, :CHUNK] + jnp.concatenate([seen, seen], 1)
        place = jnp.sum(jnp.where(is_own, prior, 0.0), 0, keepdims=True)
        order = sums[OWNERS : OWNERS + LEAVES, :CHUNK] + jnp.concatenate([base, base], 1)
        ranked[t, 0:1, :] = jnp.sum(jnp.where(is_leaf, order, 0.0), 0, keepdims=True)
        ranked[t, 1:2, :] = row_pair(goals[pl.ds(2 * t, 2), :])
        ranked[t, 2:3, :] = own.astype(F32) * PACKET + place
        starts[...] = jnp.where(lane == t, seen_leaf, starts[...])
        bases[...] = jnp.where(lane == t, base, bases[...])
        return seen + sums[:OWNERS, CHUNK:], seen_leaf + leaf_counts

    starts[...] = jnp.zeros_like(starts)
    bases[...] = jnp.zeros_like(bases)
    lax.fori_loop(
        0, CHUNKS, rank, (jnp.zeros((OWNERS, 128), F32), jnp.zeros((LEAVES, 128), F32)), unroll=16
    )

    rest = jnp.zeros((128 - LEAVES, 128), F32)
    start_of = jnp.concatenate([starts[...], rest], 0).T[:CHUNKS]
    base_of = jnp.concatenate([bases[...], rest], 0).T[:CHUNKS]
    high = jnp.where(start_of >= 256.0, 256.0, 0.0)
    columns_of = jnp.concatenate([high, start_of - high, base_of], 0).astype(BF)
    chunk = iota((CHUNKS, 128), 0).astype(F32)
    first = (iota((1, 128), 1) % TILES * TILE).astype(F32)
    full = jnp.zeros((1, 128), F32)
    table[...] = jnp.zeros_like(table)
    for g in range(LEAVES // AT_ONCE):
        one = iota((128, 128), 0) == iota((128, 128), 1) // TILES + g * AT_ONCE
        spread_out = dot(columns_of, one.astype(F32).astype(BF))
        begin = spread_out[:CHUNKS] + spread_out[CHUNKS : 2 * CHUNKS]
        place = spread_out[2 * CHUNKS :] + chunk * CHUNK
        passed = (begin <= first) & (chunk > 0.0)
        current = jnp.sum(jnp.where(passed, 1.0, 0.0), 0, keepdims=True)
        for r in range(PIECES + 1):
            here = chunk == current + r
            row = jnp.sum(jnp.where(here, place, 0.0), 0, keepdims=True)
            edge = jnp.sum(jnp.where(here, begin, 0.0), 0, keepdims=True)
            edge = jnp.where(current + r < CHUNKS, edge, float(PER)) - first
            if r == PIECES:
                full = jnp.maximum(full, jnp.where(edge < TILE, 1.0, 0.0))
                continue
            if r:
                edge = jnp.clip(edge, 0.0, float(TILE))
                table[g, PIECES + r : PIECES + r + 1, :] = edge.astype(jnp.int32)
            row = jnp.clip(jnp.where(current + r < CHUNKS, row - edge, 0.0), 0.0, float(ROWS))
            table[g, r : r + 1, :] = row.astype(jnp.int32)
    full = jnp.broadcast_to(jnp.max(full, 1, keepdims=True), (1, 128))
    tell = pltpu.make_async_copy(table, scal, local.at[4])
    tell.start()

    held[0] = pivots[...]
    pl.semaphore_wait(barrier, LEAVES + COLS - 2)
    each(LEAVES, lambda k: send_pivots(k).start())

    def joined_of(t):
        row = iota((16, CHUNK), 0)
        extra = jnp.where(row == 0, ranked[t, 1:2, :], 0.0).astype(BF)
        return jnp.concatenate([feat_in[:, pl.ds(pl.multiple_of(t * CHUNK, CHUNK), CHUNK)], extra], 0)

    def sort(t, _):
        place = ranked[t, 0:1, :].astype(jnp.int32)
        chosen = (iota((CHUNK, CHUNK), 0) == place).astype(F32).astype(BF)
        ybuf[pl.ds(pl.multiple_of(t * CHUNK, CHUNK), CHUNK), :] = dot_nt(chosen, joined_of(t))
        return 0

    bring.wait()
    lax.fori_loop(0, CHUNKS, sort, 0, unroll=8)
    ybuf[ROWS:, :] = jnp.zeros((TILE, WIDE), F32)
    tell.wait()

    eye = (iota((WIDE, WIDE), 0) == iota((WIDE, WIDE), 1)).astype(F32).astype(BF)
    sub = iota((TILE, WIDE), 0)

    def packet(k):
        to = lax.rem(leaf + k, jnp.int32(LEAVES))
        group = lax.div(to, jnp.int32(AT_ONCE))
        lane = lax.rem(to, jnp.int32(AT_ONCE)) * TILES

        def piece(r, q):
            return ybuf[pl.ds(jnp.clip(scal[group, r, lane + q], 0, ROWS), TILE), :]

        tiles = []
        for q in range(TILES):
            tile = piece(0, q)
            for r in range(1, PIECES):
                tile = jnp.where(sub >= scal[group, PIECES + r, lane + q], piece(r, q), tile)
            tiles.append(tile)
        turned = dot_nt(eye, jnp.concatenate(tiles, 0).astype(BF))
        feat[k] = turned[:F].astype(BF)
        aux[k] = jnp.concatenate([turned[F : F + 1, 128 * c : 128 * c + 128] for c in range(4)] * 2, 0)

    def give(j, _):
        steps = turn_of(2 * j + 1), turn_of(rem(2 * j + 2, LEAVES))
        for k in steps:
            packet(k)
        send_aux(steps[0]).start()
        send_feat(steps[0]).start()

        @pl.when(j < LEAVES // 2 - 1)
        def second():
            send_aux(steps[1]).start()
            send_feat(steps[1]).start()

        return 0

    lax.fori_loop(0, 2, give, 0)

    each(LEAVES, lambda k: send_pivots(k).wait_recv())
    place = jnp.concatenate([held[(LEAVES - b) % LEAVES] for b in range(LEAVES)], 0)
    home = place % ROWS // PACKET
    number = ((leaf + iota((LEAVES, RANK), 0)) % LEAVES) * 8 + place // ROWS
    number = (number * PACKET + place % PACKET).astype(F32)
    valid = home == leaf * COLS + col
    order = dot(valid.astype(F32).astype(BF), before)
    order = jnp.where(valid, order, -1.0)

    def spread(table):
        return jnp.concatenate(
            [jnp.broadcast_to(table[b : b + 1], (SLOTS, RANK)) for b in range(LEAVES)], 0
        )

    shape = (LEAVES * SLOTS, RANK)
    hit = spread(order) == (iota(shape, 0) % SLOTS).astype(F32)
    wanted = jnp.sum(jnp.where(hit, spread(number) + 1.0, 0.0), 1, keepdims=True) - 1.0
    which = jnp.sum(jnp.where(hit, iota(shape, 1).astype(F32) + 1.0, 0.0), 1, keepdims=True) - 1.0
    wanted = jnp.broadcast_to(wanted, (LEAVES * SLOTS, CHUNK))

    def take(t, total):
        chosen = (wanted == ranked[t, 2:3, :]).astype(F32).astype(BF)
        rest = jnp.zeros((128 - WIDE, CHUNK), BF)
        return total + dot_nt(chosen, jnp.concatenate([joined_of(t), rest], 0))

    shape = (LEAVES * SLOTS, 128)
    taken = lax.fori_loop(0, CHUNKS, take, jnp.zeros(shape, F32), unroll=4)
    taken = jnp.where(iota(shape, 1) == WHICH, which, taken)
    taken = jnp.where(iota(shape, 1) == FULL, full, taken).astype(BF)
    for b in range(LEAVES):
        slots[b] = taken[b * SLOTS : (b + 1) * SLOTS]
    came[0] = slots[0]
    each(LEAVES, lambda k: send_slots(k).start())
    lax.fori_loop(2, 5, give, 0)

    each(LEAVES, lambda k: send_slots(k).wait_recv())
    got = jnp.concatenate([came[b] for b in range(LEAVES)], 0).astype(F32)
    chosen = got[:, WHICH : WHICH + 1] == iota((LEAVES * SLOTS, RANK), 1).astype(F32)
    picked = dot(got.T[:F].astype(BF), chosen.astype(F32).astype(BF))
    full = jnp.broadcast_to(jnp.max(got[:, FULL : FULL + 1], 0, keepdims=True), (1, 128))
    sk[0] = picked.astype(BF)
    each(COLS, lambda k: send_skel(k).start())
    lax.fori_loop(5, LEAVES // 2, give, 0)
    rx[0] = feat[0]
    ra[0] = aux[0]

    largest = jnp.zeros((OWNERS, 1), F32)
    for b in range(LEAVES):
        held_here = (iota((OWNERS, RANK), 0) == home[b : b + 1]).astype(F32)
        largest = jnp.maximum(largest, jnp.sum(held_here, 1, keepdims=True))

    for copy in smalls:
        copy.wait()
    spare[...] = jnp.ones((8, 128), F32)
    spare[0:1, 0:F] = scales[...]
    inverse = 1.0 / to_column(spare[0:1, :])[:F]
    scale = inverse * inverse * LOG2E
    scale2 = across(scale, RANK)
    scale4 = across(scale, PER)

    index[...] = top_index(parent, top, leaf // 4)
    index2 = across(index[...], 2 * RANK)
    number = iota((RANK, 2 * RANK), 1)
    base = (quarter * RANK).astype(F32)
    other = (sibling * RANK).astype(F32)
    chosen = index2[:, :RANK] == iota((RANK, RANK), 1).astype(F32) + base
    rows[...] = chosen.astype(F32).astype(BF)
    lanes = number.astype(F32) + jnp.where(number < RANK, base, other - RANK)
    columns[...] = (index2 == lanes).astype(F32).astype(BF)
    chosen = across(index[...], 4 * RANK) == iota((RANK, 4 * RANK), 1).astype(F32)
    fours[...] = chosen.astype(F32).astype(BF)

    def norms(k):
        side[k] = point_side(rx[k].astype(F32), scale4)

    def receive(k):
        send_aux(k).wait_recv()
        send_feat(k).wait_recv()

    def early_norms(n, _):
        k = turn_of(n)
        pl.when(n > 0)(lambda: receive(k))
        norms(k)
        return 0

    lax.fori_loop(0, LEAVES // 2, early_norms, 0)

    def add_skel(k, total):
        send_skel(k).wait_recv()
        return total + sk[k].astype(F32)

    picked = lax.fori_loop(1, COLS, add_skel, picked)
    mine[...] = picked.astype(BF)
    sk4[quarter] = picked.astype(BF)

    def send_four(k):
        return remote(mine, sk4.at[quarter], (s_4, r_4), k, cousin(k))

    each(4, lambda k: send_four(k).start())
    left[0:RANK, :] = skel_side(picked, scale2)

    def block_of(k, out, begin):
        p = rx[k]
        fill = jnp.zeros((256 - 3 * F - 16, PER), BF)
        right = jnp.concatenate([p, p, p, side[k], fill], 0)
        power = dot(left[begin : begin + RANK, :], right)
        out[0:RANK, :] = jnp.exp2(jnp.minimum(power, 0.0)).astype(BF)

    def own_of(k, out):
        block_of(k, out, 0)
        value = ra[k]
        value = jnp.concatenate([value[r : r + 1] for r in range(4)], 1)
        out[RANK:, :] = jnp.broadcast_to(value, (16, PER)).astype(BF)

    def gram_of(u):
        gram[...] += dot_nt(u[...], u[0:RANK, :])

    def couple_of(v, u):
        couple[...] += dot_nt(v[...], u[0:RANK, :])

    last = LEAVES // 2 - 1

    def own_two(j, _):
        k, l = turn_of(2 * j), turn_of(2 * j + 1)
        @pl.when(j >= LEAVES // 4)
        def late():
            receive(k)
            receive(l)
            norms(k)
            norms(l)

        own_of(k, even.at[j])
        gram_of(odd.at[rem(j + last, last + 1)])
        own_of(l, odd.at[j])
        gram_of(even.at[j])
        return 0

    def other_two(j, _):
        block_of(turn_of(2 * j), other_even, RANK)
        couple_of(other_odd, odd.at[rem(j + last, last + 1)])
        block_of(turn_of(2 * j + 1), other_odd, RANK)
        couple_of(other_even, even.at[j])
        return 0

    gram[...] = jnp.zeros_like(gram)
    couple[...] = jnp.zeros_like(couple)
    odd[last] = jnp.zeros((RANK + 16, PER), BF)
    other_odd[...] = jnp.zeros_like(other_odd)
    def send_gram(k):
        return remote(pg.at[(col + k) % COLS], gr.at[k], (s_p, r_p), k, beside(k))

    def send_couple(k):
        return remote(pc.at[(col + k) % COLS], cr.at[k], (s_c, r_c), k, beside(k))

    def send_chosen(k):
        return remote(pt.at[(col + k) % COLS], qr.at[k], (s_o, r_o), k, beside(k))

    def send_rhs(k):
        return remote(rs, rr.at[k], (s_r, r_r), k, beside(k))

    def sibling_side():
        each(4, lambda k: remote(mine, sk4.at[(quarter + 4 - k) % 4], (s_4, r_4), k, cousin(k)).wait_recv())
        left[RANK:, :] = skel_side(sk4[sibling].astype(F32), scale2)

    def give_gram():
        gram_of(odd.at[last])
        part = gram[0:RANK, :].astype(BF)
        for k in range(COLS):
            pg[k] = part[k * SLAB : (k + 1) * SLAB]
        each(COLS, lambda k: send_gram(k).start())

    def half(h, _):
        pairs = LEAVES // 4
        lax.fori_loop(pairs * h, pairs * (h + 1), own_two, 0)
        pl.when(h == 0)(sibling_side)
        pl.when(h == 1)(give_gram)
        lax.fori_loop(pairs * h, pairs * (h + 1), other_two, 0)
        return 0

    lax.fori_loop(0, 2, half, 0)
    couple_of(other_odd, odd.at[last])

    rhs = gram[RANK : RANK + 1, :]
    rhs = jnp.sum(dot_nt(stack16(split3(rhs), RANK), rows[...]), 0, keepdims=True)
    rs[...] = jnp.zeros_like(rs)
    rs[0:1, :] = rhs[:, :128]
    rs[1:2, :] = rhs[:, 128:]
    rs[2:3, :] = full
    part = dot(rows[...], gram[0:RANK, :].astype(BF)).astype(BF)
    chosen = dot_nt(part, columns[:, 0:RANK])
    part = dot_nt(rows[...], couple[...].astype(BF)).astype(BF)
    chosen = chosen + dot_nt(part, columns[:, RANK:])
    chosen = chosen.astype(BF)
    for k in range(COLS):
        pt[k] = chosen[k * SLAB : (k + 1) * SLAB]
    each(COLS, lambda k: send_chosen(k).start())
    each(COLS, lambda k: send_rhs(k).start())
    part = couple[...].T.astype(BF)
    for k in range(COLS):
        pc[k] = part[k * SLAB : (k + 1) * SLAB]
    each(COLS, lambda k: send_couple(k).start())

    whole = jnp.concatenate([sk4[k] for k in range(4)], 1)
    points = dot_nt(whole, fours[...])
    fill = jnp.zeros((256 - 3 * F - 16, RANK), BF)
    points_b = points.astype(BF)
    right = jnp.concatenate([points_b, points_b, points_b, point_side(points, scale2), fill], 0)
    value = jnp.exp2(jnp.minimum(dot(skel_side(points, scale2), right), 0.0))
    crossing = (across(index[...], RANK) >= 2.0 * RANK) != (index[...].T[0:1, :] >= 2.0 * RANK)
    square = iota((RANK, RANK), 0) == iota((RANK, RANK), 1)
    tops[...] = jnp.where(crossing, value, 0.0) + jnp.where(square, ridge[...], 0.0)

    def finish(sends):
        return lambda k: [send(k).wait_send() for send in sends]

    each(LEAVES, finish((send_pivots, send_slots, send_aux, send_feat)))
    each(COLS, finish((send_skel, send_gram, send_rhs)))
    each(4, finish((send_four,)))

    def add_chosen(k, totals):
        send_chosen(k).wait_recv()
        send_rhs(k).wait_recv()
        return totals[0] + qr[k].astype(F32), totals[1] + rr[k]

    chosen, rhs = lax.fori_loop(1, COLS, add_chosen, (pt[col].astype(F32), rs[...]))
    over = jnp.maximum(jnp.max(rhs[2:3, :]), jnp.max(largest) - SLOTS)
    flag[0] = (over > 0.0).astype(jnp.int32)
    chosen = chosen * (1.0 / NODE)
    t4[0] = chosen.astype(BF)
    r4[0] = rhs * (1.0 / NODE)

    def send_top(k):
        return remote(t4.at[0], t4.at[k], (s_t, r_t), k, cousin(k))

    def send_top_rhs(k):
        return remote(r4.at[0], r4.at[k], (s_q, r_q), k, cousin(k))

    each(4, lambda k: send_top(k).start())
    each(4, lambda k: send_top_rhs(k).start())

    def add_gram(k, total):
        send_gram(k).wait_recv()
        return total + gr[k].astype(F32)

    def add_couple(k, total):
        send_couple(k).wait_recv()
        return total + cr[k].astype(F32)

    total = lax.fori_loop(1, COLS, add_gram, pg[col].astype(F32))
    diagonal = iota((SLAB, RANK), 0) + col * SLAB == iota((SLAB, RANK), 1)
    out_share[0, :, 0:RANK] = total * (1.0 / NODE) + jnp.where(diagonal, ridge[...], 0.0)
    total = lax.fori_loop(1, COLS, add_couple, pc[col].astype(F32))
    out_share[0, :, RANK:] = total * (1.0 / NODE)
    result = chosen + tops[pl.ds(pl.multiple_of(col * SLAB, SLAB), SLAB), :]

    def add_top(k, totals):
        send_top(k).wait_recv()
        send_top_rhs(k).wait_recv()
        return totals[0] + t4[k].astype(F32), totals[1] + r4[k]

    result, rhs = lax.fori_loop(1, 4, add_top, (result, r4[0]))
    out_top[0] = result
    out_rhs[...] = jnp.concatenate([rhs[0:1], rhs[1:2]], 1)

    each(COLS, finish((send_couple, send_chosen)))
    each(4, finish((send_top, send_top_rhs)))


SHAPES = ((1, SLAB, 2 * RANK), (1, SLAB, RANK), (1, RANK))


def exchange(merged, ridge, *smalls):
    return pl.pallas_call(
        exchange_kernel,
        out_shape=tuple(pltpu.VMEM(shape, F32) for shape in SHAPES),
        in_specs=[VMEM, VMEM] + [ANYWHERE] * 4,
        out_specs=[VMEM] * 3,
        scratch_shapes=[
            pltpu.VMEM((1, RANK), jnp.int32),
            pltpu.VMEM((1, F), F32),
            pltpu.VMEM((8, RANK), jnp.int32),
            pltpu.VMEM((4, RANK), jnp.int32),
            pltpu.VMEM((8, 128), F32),
            pltpu.VMEM((LEAVES, F, PER), BF),
            pltpu.VMEM((LEAVES, 8, 128), F32),
            pltpu.VMEM((LEAVES, F, PER), BF),
            pltpu.VMEM((LEAVES, 8, 128), F32),
            pltpu.VMEM((LEAVES, RANK, PER), BF),
            pltpu.VMEM((LEAVES, 16, PER), BF),
            pltpu.VMEM((COLS, F, RANK), BF),
            pltpu.VMEM((F, RANK), BF),
            pltpu.VMEM((4, F, RANK), BF),
            pltpu.VMEM((2 * RANK, 256), BF),
            pltpu.VMEM((LEAVES // 2, RANK + 16, PER), BF),
            pltpu.VMEM((LEAVES // 2, RANK + 16, PER), BF),
            pltpu.VMEM((RANK, PER), BF),
            pltpu.VMEM((RANK, PER), BF),
            pltpu.VMEM((RANK + 16, RANK), F32),
            pltpu.VMEM((RANK, RANK), F32),
            pltpu.VMEM((RANK, RANK), BF),
            pltpu.VMEM((RANK, 2 * RANK), BF),
            pltpu.VMEM((RANK, 4 * RANK), BF),
            pltpu.VMEM((RANK, 128), F32),
            pltpu.VMEM((RANK, RANK), F32),
            pltpu.VMEM((COLS, SLAB, RANK), BF),
            pltpu.VMEM((COLS, SLAB, RANK), BF),
            pltpu.VMEM((COLS, SLAB, RANK), BF),
            pltpu.VMEM((COLS, SLAB, RANK), BF),
            pltpu.VMEM((COLS, SLAB, RANK), BF),
            pltpu.VMEM((COLS, SLAB, RANK), BF),
            pltpu.VMEM((8, 128), F32),
            pltpu.VMEM((COLS, 8, 128), F32),
            pltpu.VMEM((4, SLAB, RANK), BF),
            pltpu.VMEM((4, 8, 128), F32),
            *dma(LEAVES),
            *dma(LEAVES),
            *dma(COLS),
            *dma(4),
            *dma(COLS),
            *dma(COLS),
            *dma(COLS),
            *dma(COLS),
            *dma(4),
            *dma(4),
            pltpu.SemaphoreType.DMA((5,)),
        ],
        compiler_params=params(0, 40),
        name="exchange",
    )(merged, ridge, *in_hbm(*smalls))


def stream(samples, pivots, ridge, *smalls):
    return pl.pallas_call(
        stream_kernel,
        out_shape=(
            *(pltpu.VMEM(shape, F32) for shape in SHAPES),
            jax.ShapeDtypeStruct((1,), jnp.int32),
        ),
        in_specs=[ANYWHERE, VMEM, VMEM, VMEM, VMEM] + [ANYWHERE] * 3,
        out_specs=[VMEM] * 3 + [pl.BlockSpec(memory_space=pltpu.SMEM)],
        scratch_shapes=[
            pltpu.VMEM((F, ROWS), BF),
            pltpu.VMEM((ROWS // 128, 128), F32),
            pltpu.VMEM((CHUNKS, 8, CHUNK), F32),
            pltpu.VMEM((LEAVES, 128), F32),
            pltpu.VMEM((LEAVES, 128), F32),
            pltpu.VMEM((ROWS + TILE, WIDE), F32),
            pltpu.VMEM((LEAVES // AT_ONCE, 16, 128), jnp.int32),
            pltpu.SMEM((LEAVES // AT_ONCE, 16, 128), jnp.int32),
            pltpu.VMEM((LEAVES, 1, RANK), jnp.int32),
            pltpu.VMEM((LEAVES, SLOTS, 128), BF),
            pltpu.VMEM((LEAVES, SLOTS, 128), BF),
            pltpu.VMEM((1, F), F32),
            pltpu.VMEM((8, RANK), jnp.int32),
            pltpu.VMEM((4, RANK), jnp.int32),
            pltpu.VMEM((8, 128), F32),
            pltpu.VMEM((LEAVES, F, PER), BF),
            pltpu.VMEM((LEAVES, 8, 128), F32),
            pltpu.VMEM((LEAVES, F, PER), BF),
            pltpu.VMEM((LEAVES, 8, 128), F32),
            pltpu.VMEM((LEAVES, 16, PER), BF),
            pltpu.VMEM((COLS, F, RANK), BF),
            pltpu.VMEM((F, RANK), BF),
            pltpu.VMEM((4, F, RANK), BF),
            pltpu.VMEM((2 * RANK, 256), BF),
            pltpu.VMEM((LEAVES // 2, RANK + 16, PER), BF),
            pltpu.VMEM((LEAVES // 2, RANK + 16, PER), BF),
            pltpu.VMEM((RANK, PER), BF),
            pltpu.VMEM((RANK, PER), BF),
            pltpu.VMEM((RANK + 16, RANK), F32),
            pltpu.VMEM((RANK, RANK), F32),
            pltpu.VMEM((RANK, RANK), BF),
            pltpu.VMEM((RANK, 2 * RANK), BF),
            pltpu.VMEM((RANK, 4 * RANK), BF),
            pltpu.VMEM((RANK, 128), F32),
            pltpu.VMEM((RANK, RANK), F32),
            pltpu.VMEM((COLS, SLAB, RANK), BF),
            pltpu.VMEM((COLS, SLAB, RANK), BF),
            pltpu.VMEM((COLS, SLAB, RANK), BF),
            pltpu.VMEM((COLS, SLAB, RANK), BF),
            pltpu.VMEM((COLS, SLAB, RANK), BF),
            pltpu.VMEM((COLS, SLAB, RANK), BF),
            pltpu.VMEM((8, 128), F32),
            pltpu.VMEM((COLS, 8, 128), F32),
            pltpu.VMEM((4, SLAB, RANK), BF),
            pltpu.VMEM((4, 8, 128), F32),
            *dma(LEAVES),
            *dma(LEAVES),
            *dma(LEAVES),
            *dma(LEAVES),
            *dma(COLS),
            *dma(4),
            *dma(COLS),
            *dma(COLS),
            *dma(COLS),
            *dma(COLS),
            *dma(4),
            *dma(4),
            pltpu.SemaphoreType.DMA((5,)),
        ],
        compiler_params=params(1, 40),
        name="stream",
    )(*in_hbm(*samples, pivots), ridge, *in_hbm(*smalls))


def emit_kernel(*refs):
    ins, outs, sem = refs[:3], refs[3:6], refs[6]
    copies = [pltpu.make_async_copy(a, b, sem.at[k]) for k, (a, b) in enumerate(zip(ins, outs))]
    for copy in copies:
        copy.start()
    for copy in copies:
        copy.wait()


def emit(results):
    return pl.pallas_call(
        emit_kernel,
        out_shape=tuple(jax.ShapeDtypeStruct(shape, F32) for shape in SHAPES),
        in_specs=[VMEM] * 3,
        out_specs=[ANYWHERE] * 3,
        scratch_shapes=[pltpu.SemaphoreType.DMA((3,))],
        compiler_params=params(),
        name="emit",
    )(*results)


def local(features, targets, owner, length_scales, ridge, leaf_pivots, parent_pivots, top_pivots):
    samples = (features, targets.reshape(ROWS // 128, 128), owner.reshape(ROWS // 128, 128))
    ridge = ridge.reshape(1, 1)
    smalls = (length_scales.reshape(1, F), parent_pivots, top_pivots)
    *results, flag = stream(samples, leaf_pivots, ridge, *smalls)

    def again():
        return tuple(emit(exchange(pack(*samples), ridge, leaf_pivots, *smalls)))

    return lax.switch(flag[0], [lambda: tuple(emit(results)), again])


def solution(mesh):
    return jax.shard_map(
        local,
        mesh=mesh,
        in_specs=(
            P(None, ("leaf", "col")),
            P(("leaf", "col")),
            P(("leaf", "col")),
            P(),
            P(),
            P("leaf", None),
            P(),
            P(),
        ),
        out_specs=(P("leaf", "col", None), P("leaf", "col", None), P("leaf", None)),
        check_vma=False,
    )
```

```python
import functools
import math

import jax
import jax.numpy as jnp
from jax import lax
from jax.experimental import pallas as pl
from jax.experimental.pallas import tpu as pltpu
from jax.sharding import PartitionSpec as P

F = 48
RANK = 256
ROWS = 8192
LEAVES = 16
COLS = 8
OWNERS = 128
PACKET = 64
PER = ROWS // LEAVES
CHUNK = 256
CHUNKS = ROWS // CHUNK
WINDOW = 40
REGION = PER + WINDOW
TILE = 32
TILES = PER // TILE
PIECES = 6
AT_ONCE = 128 // TILES
SLOTS = 16
WHICH = 50
FULL = 51
WIDE = 64
SLAB = RANK // COLS
NODE = ROWS * COLS
LOG2E = math.log2(math.e)
BF = jnp.bfloat16
F32 = jnp.float32
NT = (((1,), (1,)), ((), ()))
MESH = pl.DeviceIdType.MESH


def dma(count):
    return [pltpu.SemaphoreType.DMA((count,))] * 2


def params(number=None, limit=24):
    if number is None:
        return pltpu.CompilerParams(vmem_limit_bytes=limit * 2**20)
    return pltpu.CompilerParams(
        collective_id=number, has_side_effects=True, vmem_limit_bytes=limit * 2**20
    )


ANYWHERE = pl.BlockSpec(memory_space=pl.ANY)
VMEM = pl.BlockSpec(memory_space=pltpu.VMEM)


def iota(shape, axis):
    return lax.broadcasted_iota(jnp.int32, shape, axis)


def dot(a, b):
    return jnp.dot(a, b, preferred_element_type=F32)


def dot_nt(a, b):
    return lax.dot_general(a, b, NT, preferred_element_type=F32)


def row_pair(two):
    return jnp.concatenate([two[0:1], two[1:2]], 1)


def pack_kernel(
    feat_hbm, target, owner, zbuf, feat, goals, rows, ybuf, table, scal, sem, feat_sem
):
    bring = pltpu.make_async_copy(feat_hbm, feat, feat_sem)
    bring.start()
    goals[...] = target[...].astype(F32)
    before = (iota((CHUNK, CHUNK), 0) < iota((CHUNK, CHUNK), 1)).astype(F32).astype(BF)
    weights = jnp.concatenate([before, jnp.ones((CHUNK, 128), BF)], 1)
    lane = iota((LEAVES, 128), 1)

    def ranks(t, carry):
        seen, seen_leaf, most = carry
        own = row_pair(owner[pl.ds(2 * t, 2), :])
        leaf = own // 8
        is_own = iota((OWNERS, CHUNK), 0) == own
        is_leaf = iota((LEAVES, CHUNK), 0) == leaf
        is_after = iota((LEAVES, CHUNK), 0) > leaf
        marks = jnp.concatenate(
            [m.astype(F32).astype(BF) for m in (is_own, is_leaf, is_after)], 0
        )
        sums = dot(marks, weights)
        counts = sums[:OWNERS, CHUNK:]
        leaf_counts = sums[OWNERS : OWNERS + LEAVES, CHUNK:]
        base = sums[OWNERS + LEAVES :, CHUNK:]
        prior = sums[:OWNERS, :CHUNK] + jnp.concatenate([seen, seen], 1)
        rank = jnp.sum(jnp.where(is_own, prior, 0.0), 0, keepdims=True)
        place = sums[OWNERS : OWNERS + LEAVES, :CHUNK] + jnp.concatenate([base, base], 1)
        place = jnp.sum(jnp.where(is_leaf, place, 0.0), 0, keepdims=True)
        tag = (own % 8).astype(F32) * PACKET + rank - (PER // 2)
        rows[t, 0:1, :] = place
        rows[t, 1:2, :] = row_pair(goals[pl.ds(2 * t, 2), :])
        rows[t, 2:3, :] = tag
        here = lane == t
        table[0:LEAVES, :] = jnp.where(here, seen_leaf.astype(jnp.int32), table[0:LEAVES, :])
        table[LEAVES : 2 * LEAVES, :] = jnp.where(
            here, base.astype(jnp.int32), table[LEAVES : 2 * LEAVES, :]
        )
        return seen + counts, seen_leaf + leaf_counts, jnp.maximum(most, leaf_counts)

    table[0:LEAVES, :] = jnp.full((LEAVES, 128), PER, jnp.int32)
    zero = jnp.zeros((LEAVES, 128), F32)
    _, _, most = lax.fori_loop(
        0, CHUNKS, ranks, (jnp.zeros((OWNERS, 128), F32), zero, zero), unroll=16
    )
    most = jnp.broadcast_to(jnp.max(most, 0, keepdims=True), (8, 128))
    table[2 * LEAVES :, :] = most.astype(jnp.int32)
    move = pltpu.make_async_copy(table, scal, sem)
    move.start()
    bring.wait()

    def sort(t, _):
        start = pl.multiple_of(t * CHUNK, CHUNK)
        row = iota((16, CHUNK), 0)
        place, goal, tag = rows[t, 0:1, :], rows[t, 1:2, :], rows[t, 2:3, :]
        extra = jnp.where(row == 0, goal, jnp.where(row == 1, tag, 0.0)).astype(BF)
        joined = jnp.concatenate([feat[:, pl.ds(start, CHUNK)], extra], 0)
        chosen = (iota((CHUNK, CHUNK), 0) == place.astype(jnp.int32)).astype(F32).astype(BF)
        ybuf[pl.ds(start, CHUNK), :] = dot_nt(chosen, joined)
        return 0

    lax.fori_loop(0, CHUNKS, sort, 0, unroll=8)
    move.wait()
    widest = scal[2 * LEAVES, 0]

    @pl.when(widest <= WINDOW)
    def quick():
        def merge(t, _):
            for i in range(LEAVES):
                source = t * CHUNK + scal[LEAVES + i, t]
                goal = i * REGION + scal[i, t]
                zbuf[pl.ds(goal, WINDOW), :] = ybuf[pl.ds(source, WINDOW), :]
            return 0

        lax.fori_loop(0, CHUNKS, merge, 0, unroll=4)

    @pl.when(widest > WINDOW)
    def slow():
        def merge(index, _):
            t = index // LEAVES
            i = index % LEAVES
            source = t * CHUNK + scal[LEAVES + i, t]
            first = scal[i, t]
            count = scal[i, t + 1] - first

            def part(k, _):
                rows = ybuf[pl.ds(source + 8 * k, 8), :]
                zbuf[pl.ds(i * REGION + first + 8 * k, 8), :] = rows
                return 0

            lax.fori_loop(0, (count + 7) // 8, part, 0)
            return 0

        lax.fori_loop(0, CHUNKS * LEAVES, merge, 0)


def in_hbm(*arrays):
    return [pltpu.with_memory_space_constraint(a, pltpu.HBM) for a in arrays]


def pack(features, targets, owner):
    return pl.pallas_call(
        pack_kernel,
        out_shape=pltpu.VMEM((LEAVES * REGION, WIDE), F32),
        in_specs=[ANYWHERE, VMEM, VMEM],
        out_specs=VMEM,
        scratch_shapes=[
            pltpu.VMEM((F, ROWS), BF),
            pltpu.VMEM((ROWS // 128, 128), F32),
            pltpu.VMEM((CHUNKS, 8, CHUNK), F32),
            pltpu.VMEM((ROWS + WINDOW, WIDE), F32),
            pltpu.VMEM((40, 128), jnp.int32),
            pltpu.SMEM((40, 128), jnp.int32),
            pltpu.SemaphoreType.DMA,
            pltpu.SemaphoreType.DMA,
        ],
        compiler_params=params(),
        name="pack",
    )(*in_hbm(features, targets, owner))


def split3(x):
    high = x.astype(BF)
    rest = x - high.astype(F32)
    mid = rest.astype(BF)
    return high, mid, (rest - mid.astype(F32)).astype(BF)


def stack16(parts, width):
    row = iota((16, width), 0)
    block = jnp.zeros((16, width), F32)
    for k, part in enumerate(parts):
        block = jnp.where(row == k, part if isinstance(part, float) else part.astype(F32), block)
    return block.astype(BF)


def half_norm(points, scale):
    return jnp.sum(points * points * (0.5 * scale), 0, keepdims=True)


def point_side(points, scale):
    high, mid, low = split3(-half_norm(points, scale))
    return stack16([high, mid, low, 1.0, 1.0, 1.0], points.shape[1])


def skel_side(skel, scale):
    width = skel.shape[1]
    high, mid, low = split3(skel * scale)
    extra = stack16([1.0, 1.0, 1.0, *split3(-half_norm(skel, scale))], width)
    parts = [p.astype(F32) for p in (high, mid, low, extra)]
    fill = jnp.zeros((256 - 3 * F - 16, width), F32)
    return jnp.concatenate([*parts, fill], 0).T.astype(BF)


def select_row(table, row):
    hit = iota(table.shape, 0) == row
    return jnp.sum(jnp.where(hit, table.astype(F32), 0.0), 0, keepdims=True)


def to_column(row):
    return jnp.broadcast_to(row, (128, row.shape[1])).T


def across(column, width):
    return jnp.concatenate([column] * (width // 128), 1)


def place_of(leaf, col):
    return dict(device_id=(leaf, col), device_id_type=MESH)


def mate(k):
    leaf, col = lax.axis_index("leaf"), lax.axis_index("col")
    to = (leaf + k) % LEAVES
    cross = (to // 8 + leaf // 8) % 2
    return place_of(to, col + cross * (1 - 2 * (col % 2)))


def beside(k):
    leaf, col = lax.axis_index("leaf"), lax.axis_index("col")
    return place_of(leaf, (col + k) % COLS)


def cousin(k):
    leaf, col = lax.axis_index("leaf"), lax.axis_index("col")
    return place_of(leaf - leaf % 4 + (leaf + k) % 4, col)


def each(count, step, unroll=1):
    lax.fori_loop(1, count, lambda k, _: (step(k), 0)[1], 0, unroll=unroll)


def rem(a, b):
    return lax.rem(jnp.int32(a), jnp.int32(b))


def turn_of(n):
    n = jnp.int32(n)
    odd = lax.rem(n, jnp.int32(2))
    half = lax.div(n + odd, jnp.int32(2))
    return lax.rem(odd * half + (1 - odd) * (LEAVES - half), jnp.int32(LEAVES))


def remote(src, dst, sems, k, peer):
    return pltpu.make_async_remote_copy(src, dst, sems[0].at[k], sems[1].at[k], **peer)


def top_index(parent, top, group):
    top_row = select_row(top[...], group)
    below = jnp.concatenate([select_row(parent[...], 2 * group + r) for r in range(2)], 1)
    number = iota((RANK, 2 * RANK), 1)
    below = below + jnp.where(iota((1, 2 * RANK), 1) >= RANK, 2.0 * RANK, 0.0)
    hit = across(to_column(top_row), 2 * RANK) == number.astype(F32)
    index = jnp.sum(jnp.where(hit, below, 0.0), 1, keepdims=True)
    return jnp.broadcast_to(index, (RANK, 128))


def exchange_kernel(
    merged, ridge, pivots_hbm, scales_hbm, parent_hbm, top_hbm, out_share, out_top, out_rhs,
    pivots, scales, parent, top, spare, feat, aux, rx, ra, hot, side, sk, mine, sk4, left,
    even, odd, other_even, other_odd, gram, couple, rows, columns, fours, index, tops,
    pg, gr, pc, cr, pt, qr, rs, rr, t4, r4,
    s_f, r_f, s_a, r_a, s_k, r_k, s_4, r_4, s_p, r_p, s_c, r_c, s_o, r_o, s_r, r_r, s_t, r_t, s_q, r_q, local,
):
    leaf = lax.axis_index("leaf")
    col = lax.axis_index("col")
    quarter = leaf % 4
    sibling = quarter + 1 - 2 * (quarter % 2)
    barrier = pltpu.get_barrier_semaphore()
    each(LEAVES, lambda k: pl.semaphore_signal(barrier, inc=1, **mate(k)))
    each(COLS, lambda k: pl.semaphore_signal(barrier, inc=1, **beside(k)))
    smalls = [
        pltpu.make_async_copy(a, b, local.at[k])
        for k, (a, b) in enumerate(
            [(pivots_hbm, pivots), (scales_hbm, scales), (parent_hbm, parent), (top_hbm, top)]
        )
    ]
    for copy in smalls:
        copy.start()

    eye = (iota((WIDE, WIDE), 0) == iota((WIDE, WIDE), 1)).astype(F32).astype(BF)

    def turn(k):
        start = pl.multiple_of((leaf + k) % LEAVES * REGION, 8)
        turned = dot_nt(eye, merged[pl.ds(start, PER), :].astype(BF))
        feat[k] = turned[:F].astype(BF)
        aux[k] = jnp.concatenate(
            [turned[F + r : F + r + 1, 128 * c : 128 * c + 128] for r in range(2) for c in range(4)], 0
        )

    def send_feat(k):
        return remote(feat.at[k], rx.at[k], (s_f, r_f), k, mate(k))

    def send_aux(k):
        return remote(aux.at[k], ra.at[k], (s_a, r_a), k, mate(k))

    def four(j, _):
        steps = [turn_of(lax.rem(4 * j + r, LEAVES)) for r in range(1, 5)]
        for k in steps:
            turn(k)
        pl.when(j == 0)(lambda: pl.semaphore_wait(barrier, LEAVES + COLS - 2))
        for send in (send_aux, send_feat):
            for k in steps[:3]:
                send(k).start()
            pl.when(j < 3)(lambda: send(steps[3]).start())
        return 0

    lax.fori_loop(0, LEAVES // 4, four, 0)
    rx[0] = feat[0]
    ra[0] = aux[0]

    for copy in smalls:
        copy.wait()
    spare[...] = jnp.ones((8, 128), F32)
    spare[0:1, 0:F] = scales[...]
    inverse = 1.0 / to_column(spare[0:1, :])[:F]
    scale = inverse * inverse * LOG2E
    scale2 = across(scale, RANK)
    scale4 = across(scale, PER)

    place = pivots[...]
    within = place % ROWS
    block = within // PACKET
    key = (block // COLS) * PER + (place // ROWS) * PACKET + within % PACKET
    holder = block % COLS
    crossed = (block // COLS) // 8 != leaf // 8
    holder = jnp.where(crossed, holder + 1 - 2 * (holder % 2), holder)
    key = jnp.where(holder == col, key, -PER)
    key = across(to_column(key.astype(F32)), PER)

    def mark(k):
        source = (leaf + LEAVES - k) % LEAVES
        tags = ra[k, 4:8, :]
        tag = jnp.concatenate([tags[r : r + 1] for r in range(4)], 1)
        wanted = tag + (PER // 2 + source * PER).astype(F32)
        hot[k] = (key == wanted).astype(F32).astype(BF)

    def mark_next(n, _):
        k = turn_of(n)
        pl.when(n > 0)(lambda: send_aux(k).wait_recv())
        mark(k)
        return 0

    lax.fori_loop(0, LEAVES, mark_next, 0)

    index[...] = top_index(parent, top, leaf // 4)
    index2 = across(index[...], 2 * RANK)
    number = iota((RANK, 2 * RANK), 1)
    base = (quarter * RANK).astype(F32)
    other = (sibling * RANK).astype(F32)
    chosen = index2[:, :RANK] == iota((RANK, RANK), 1).astype(F32) + base
    rows[...] = chosen.astype(F32).astype(BF)
    lanes = number.astype(F32) + jnp.where(number < RANK, base, other - RANK)
    columns[...] = (index2 == lanes).astype(F32).astype(BF)
    chosen = across(index[...], 4 * RANK) == iota((RANK, 4 * RANK), 1).astype(F32)
    fours[...] = chosen.astype(F32).astype(BF)

    def pick(j, total):
        steps = [turn_of(4 * j + r) for r in range(4)]
        pl.when(j > 0)(lambda: send_feat(steps[0]).wait_recv())
        for k in steps[1:]:
            send_feat(k).wait_recv()
        for k in steps:
            total = total + dot_nt(hot[k], rx[k])
        return total

    picked = lax.fori_loop(0, LEAVES // 4, pick, jnp.zeros((RANK, F), F32))
    picked = jnp.concatenate([picked, jnp.zeros((RANK, 128 - F), F32)], 1).T[:F]
    sk[0] = picked.astype(BF)

    def send_skel(k):
        return remote(sk.at[0], sk.at[k], (s_k, r_k), k, beside(k))

    each(COLS, lambda k: send_skel(k).start())

    def norms(k, _):
        side[k] = point_side(rx[k].astype(F32), scale4)
        return 0

    lax.fori_loop(0, LEAVES, norms, 0)

    def add_skel(k, total):
        send_skel(k).wait_recv()
        return total + sk[k].astype(F32)

    picked = lax.fori_loop(1, COLS, add_skel, picked)
    mine[...] = picked.astype(BF)
    sk4[quarter] = picked.astype(BF)

    def send_four(k):
        return remote(mine, sk4.at[quarter], (s_4, r_4), k, cousin(k))

    each(4, lambda k: send_four(k).start())
    left[0:RANK, :] = skel_side(picked, scale2)

    def block_of(k, out, begin):
        p = rx[k]
        fill = jnp.zeros((256 - 3 * F - 16, PER), BF)
        right = jnp.concatenate([p, p, p, side[k], fill], 0)
        power = dot(left[begin : begin + RANK, :], right)
        out[0:RANK, :] = jnp.exp2(jnp.minimum(power, 0.0)).astype(BF)

    def own_of(k, out):
        block_of(k, out, 0)
        value = jnp.concatenate([ra[k, r : r + 1, :] for r in range(4)], 1)
        out[RANK:, :] = jnp.broadcast_to(value, (16, PER)).astype(BF)

    def gram_of(u):
        gram[...] += dot_nt(u[...], u[0:RANK, :])

    def couple_of(v, u):
        couple[...] += dot_nt(v[...], u[0:RANK, :])

    last = LEAVES // 2 - 1

    def own_two(j, _):
        own_of(2 * j, even.at[j])
        gram_of(odd.at[(j + last) % (last + 1)])
        own_of(2 * j + 1, odd.at[j])
        gram_of(even.at[j])
        return 0

    def other_two(j, _):
        block_of(2 * j, other_even, RANK)
        couple_of(other_odd, odd.at[(j + last) % (last + 1)])
        block_of(2 * j + 1, other_odd, RANK)
        couple_of(other_even, even.at[j])
        return 0

    gram[...] = jnp.zeros_like(gram)
    couple[...] = jnp.zeros_like(couple)
    odd[last] = jnp.zeros((RANK + 16, PER), BF)
    other_odd[...] = jnp.zeros_like(other_odd)
    lax.fori_loop(0, last + 1, own_two, 0)
    gram_of(odd.at[last])

    def send_gram(k):
        return remote(pg.at[(col + k) % COLS], gr.at[k], (s_p, r_p), k, beside(k))

    def send_couple(k):
        return remote(pc.at[(col + k) % COLS], cr.at[k], (s_c, r_c), k, beside(k))

    def send_chosen(k):
        return remote(pt.at[(col + k) % COLS], qr.at[k], (s_o, r_o), k, beside(k))

    def send_rhs(k):
        return remote(rs, rr.at[k], (s_r, r_r), k, beside(k))

    part = gram[0:RANK, :].astype(BF)
    for k in range(COLS):
        pg[k] = part[k * SLAB : (k + 1) * SLAB]
    rhs = gram[RANK : RANK + 1, :]
    rhs = jnp.sum(dot_nt(stack16(split3(rhs), RANK), rows[...]), 0, keepdims=True)
    rs[...] = jnp.zeros_like(rs)
    rs[0:1, :] = rhs[:, :128]
    rs[1:2, :] = rhs[:, 128:]
    each(COLS, lambda k: send_gram(k).start())
    each(COLS, lambda k: send_rhs(k).start())
    tops[...] = dot_nt(dot(rows[...], part).astype(BF), columns[:, 0:RANK])

    each(4, lambda k: remote(mine, sk4.at[(quarter + 4 - k) % 4], (s_4, r_4), k, cousin(k)).wait_recv())
    left[RANK:, :] = skel_side(sk4[sibling].astype(F32), scale2)
    lax.fori_loop(0, last + 1, other_two, 0)
    couple_of(other_odd, odd.at[last])

    part = couple[...].astype(BF)
    chosen = dot_nt(dot_nt(rows[...], part).astype(BF), columns[:, RANK:]) + tops[...]
    chosen = chosen.astype(BF)
    for k in range(COLS):
        pt[k] = chosen[k * SLAB : (k + 1) * SLAB]
    each(COLS, lambda k: send_chosen(k).start())
    part = couple[...].T.astype(BF)
    for k in range(COLS):
        pc[k] = part[k * SLAB : (k + 1) * SLAB]
    each(COLS, lambda k: send_couple(k).start())

    whole = jnp.concatenate([sk4[k] for k in range(4)], 1)
    points = dot_nt(whole, fours[...])
    fill = jnp.zeros((256 - 3 * F - 16, RANK), BF)
    points_b = points.astype(BF)
    right = jnp.concatenate([points_b, points_b, points_b, point_side(points, scale2), fill], 0)
    value = jnp.exp2(jnp.minimum(dot(skel_side(points, scale2), right), 0.0))
    crossing = (across(index[...], RANK) >= 2.0 * RANK) != (index[...].T[0:1, :] >= 2.0 * RANK)
    square = iota((RANK, RANK), 0) == iota((RANK, RANK), 1)
    tops[...] = jnp.where(crossing, value, 0.0) + jnp.where(square, ridge[...], 0.0)

    def finish(sends):
        return lambda k: [send(k).wait_send() for send in sends]

    each(LEAVES, finish((send_aux, send_feat)))
    each(COLS, finish((send_skel, send_gram, send_rhs)))
    each(4, finish((send_four,)))

    def add_chosen(k, totals):
        send_chosen(k).wait_recv()
        send_rhs(k).wait_recv()
        return totals[0] + qr[k].astype(F32), totals[1] + rr[k]

    chosen, rhs = lax.fori_loop(1, COLS, add_chosen, (pt[col].astype(F32), rs[...]))
    chosen = chosen * (1.0 / NODE)
    t4[0] = chosen.astype(BF)
    r4[0] = rhs * (1.0 / NODE)

    def send_top(k):
        return remote(t4.at[0], t4.at[k], (s_t, r_t), k, cousin(k))

    def send_top_rhs(k):
        return remote(r4.at[0], r4.at[k], (s_q, r_q), k, cousin(k))

    each(4, lambda k: send_top(k).start())
    each(4, lambda k: send_top_rhs(k).start())

    def add_gram(k, total):
        send_gram(k).wait_recv()
        return total + gr[k].astype(F32)

    def add_couple(k, total):
        send_couple(k).wait_recv()
        return total + cr[k].astype(F32)

    total = lax.fori_loop(1, COLS, add_gram, pg[col].astype(F32))
    diagonal = iota((SLAB, RANK), 0) + col * SLAB == iota((SLAB, RANK), 1)
    out_share[0, :, 0:RANK] = total * (1.0 / NODE) + jnp.where(diagonal, ridge[...], 0.0)
    total = lax.fori_loop(1, COLS, add_couple, pc[col].astype(F32))
    out_share[0, :, RANK:] = total * (1.0 / NODE)
    result = chosen + tops[pl.ds(pl.multiple_of(col * SLAB, SLAB), SLAB), :]

    def add_top(k, totals):
        send_top(k).wait_recv()
        send_top_rhs(k).wait_recv()
        return totals[0] + t4[k].astype(F32), totals[1] + r4[k]

    result, rhs = lax.fori_loop(1, 4, add_top, (result, r4[0]))
    out_top[0] = result
    out_rhs[...] = jnp.concatenate([rhs[0:1], rhs[1:2]], 1)

    each(COLS, finish((send_couple, send_chosen)))
    each(4, finish((send_top, send_top_rhs)))


def stream_kernel(
    feat_hbm, target, owner, pivots, ridge, scales_hbm, parent_hbm, top_hbm,
    out_share, out_top, out_rhs, flag,
    feat_in, bad, goals, ranked, starts, bases, ybuf, table, scal, held, slots, came, scales, parent, top, spare,
    feat, aux, rx, ra, side, sk, mine, sk4, left, even, odd, other_even, other_odd, gram, couple,
    rows, columns, fours, index, tops, pg, gr, pc, cr, pt, qr, rs, rr, t4, r4,
    s_v, r_v, s_s, r_s, s_f, r_f, s_a, r_a, s_k, r_k, s_4, r_4, s_p, r_p, s_c, r_c, s_o, r_o,
    s_r, r_r, s_t, r_t, s_q, r_q, local,
):
    leaf = lax.axis_index("leaf")
    col = lax.axis_index("col")
    quarter = leaf % 4
    sibling = quarter + 1 - 2 * (quarter % 2)
    barrier = pltpu.get_barrier_semaphore()
    each(LEAVES, lambda k: pl.semaphore_signal(barrier, inc=1, **mate(k)))
    each(COLS, lambda k: pl.semaphore_signal(barrier, inc=1, **beside(k)))
    bring = pltpu.make_async_copy(feat_hbm, feat_in, local.at[3])
    bring.start()
    smalls = [
        pltpu.make_async_copy(a, b, local.at[k])
        for k, (a, b) in enumerate([(scales_hbm, scales), (parent_hbm, parent), (top_hbm, top)])
    ]
    for copy in smalls:
        copy.start()

    def send_pivots(k):
        return remote(pivots, held.at[k], (s_v, r_v), k, mate(k))

    def send_slots(k):
        return remote(slots.at[k], came.at[k], (s_s, r_s), k, mate(k))

    def send_feat(k):
        return remote(feat.at[k], rx.at[k], (s_f, r_f), k, mate(k))

    def send_aux(k):
        return remote(aux.at[k], ra.at[k], (s_a, r_a), k, mate(k))

    def send_skel(k):
        return remote(sk.at[0], sk.at[k], (s_k, r_k), k, beside(k))

    goals[...] = target[...].astype(F32)
    before = (iota((CHUNK, CHUNK), 0) < iota((CHUNK, CHUNK), 1)).astype(F32).astype(BF)
    weights = jnp.concatenate([before, jnp.ones((CHUNK, 128), BF)], 1)
    lane = iota((LEAVES, 128), 1)

    def rank(t, carry):
        seen, seen_leaf = carry
        own = row_pair(owner[pl.ds(2 * t, 2), :])
        group = own // 8
        is_own = iota((OWNERS, CHUNK), 0) == own
        is_leaf = iota((LEAVES, CHUNK), 0) == group
        is_after = iota((LEAVES, CHUNK), 0) > group
        marks = jnp.concatenate([m.astype(F32).astype(BF) for m in (is_own, is_leaf, is_after)], 0)
        sums = dot(marks, weights)
        leaf_counts = sums[OWNERS : OWNERS + LEAVES, CHUNK:]
        base = sums[OWNERS + LEAVES :, CHUNK:]
        prior = sums[:OWNERS, :CHUNK] + jnp.concatenate([seen, seen], 1)
        place = jnp.sum(jnp.where(is_own, prior, 0.0), 0, keepdims=True)
        order = sums[OWNERS : OWNERS + LEAVES, :CHUNK] + jnp.concatenate([base, base], 1)
        ranked[t, 0:1, :] = jnp.sum(jnp.where(is_leaf, order, 0.0), 0, keepdims=True)
        ranked[t, 1:2, :] = row_pair(goals[pl.ds(2 * t, 2), :])
        ranked[t, 2:3, :] = own.astype(F32) * PACKET + place
        starts[...] = jnp.where(lane == t, seen_leaf, starts[...])
        bases[...] = jnp.where(lane == t, base, bases[...])
        return seen + sums[:OWNERS, CHUNK:], seen_leaf + leaf_counts

    starts[...] = jnp.zeros_like(starts)
    bases[...] = jnp.zeros_like(bases)
    lax.fori_loop(
        0, CHUNKS, rank, (jnp.zeros((OWNERS, 128), F32), jnp.zeros((LEAVES, 128), F32)), unroll=16
    )

    rest = jnp.zeros((128 - LEAVES, 128), F32)
    start_of = jnp.concatenate([starts[...], rest], 0).T[:CHUNKS]
    base_of = jnp.concatenate([bases[...], rest], 0).T[:CHUNKS]
    high = jnp.where(start_of >= 256.0, 256.0, 0.0)
    columns_of = jnp.concatenate([high, start_of - high, base_of], 0).astype(BF)
    chunk = iota((CHUNKS, 128), 0).astype(F32)
    first = (iota((1, 128), 1) % TILES * TILE).astype(F32)
    full = jnp.zeros((1, 128), F32)
    table[...] = jnp.zeros_like(table)
    for g in range(LEAVES // AT_ONCE):
        one = iota((128, 128), 0) == iota((128, 128), 1) // TILES + g * AT_ONCE
        spread_out = dot(columns_of, one.astype(F32).astype(BF))
        begin = spread_out[:CHUNKS] + spread_out[CHUNKS : 2 * CHUNKS]
        place = spread_out[2 * CHUNKS :] + chunk * CHUNK
        passed = (begin <= first) & (chunk > 0.0)
        current = jnp.sum(jnp.where(passed, 1.0, 0.0), 0, keepdims=True)
        for r in range(PIECES + 1):
            here = chunk == current + r
            row = jnp.sum(jnp.where(here, place, 0.0), 0, keepdims=True)
            edge = jnp.sum(jnp.where(here, begin, 0.0), 0, keepdims=True)
            edge = jnp.where(current + r < CHUNKS, edge, float(PER)) - first
            if r == PIECES:
                full = jnp.maximum(full, jnp.where(edge < TILE, 1.0, 0.0))
                continue
            if r:
                edge = jnp.clip(edge, 0.0, float(TILE))
                table[g, PIECES + r : PIECES + r + 1, :] = edge.astype(jnp.int32)
            row = jnp.clip(jnp.where(current + r < CHUNKS, row - edge, 0.0), 0.0, float(ROWS))
            table[g, r : r + 1, :] = row.astype(jnp.int32)
    full = jnp.broadcast_to(jnp.max(full, 1, keepdims=True), (1, 128))
    tell = pltpu.make_async_copy(table, scal, local.at[4])
    tell.start()

    held[0] = pivots[...]
    pl.semaphore_wait(barrier, LEAVES + COLS - 2)
    each(LEAVES, lambda k: send_pivots(k).start())

    def joined_of(t):
        row = iota((16, CHUNK), 0)
        extra = jnp.where(row == 0, ranked[t, 1:2, :], 0.0).astype(BF)
        return jnp.concatenate([feat_in[:, pl.ds(pl.multiple_of(t * CHUNK, CHUNK), CHUNK)], extra], 0)

    def sort(t, _):
        place = ranked[t, 0:1, :].astype(jnp.int32)
        chosen = (iota((CHUNK, CHUNK), 0) == place).astype(F32).astype(BF)
        ybuf[pl.ds(pl.multiple_of(t * CHUNK, CHUNK), CHUNK), :] = dot_nt(chosen, joined_of(t))
        return 0

    bring.wait()
    lax.fori_loop(0, CHUNKS, sort, 0, unroll=8)
    ybuf[ROWS:, :] = jnp.zeros((TILE, WIDE), F32)
    tell.wait()

    eye = (iota((WIDE, WIDE), 0) == iota((WIDE, WIDE), 1)).astype(F32).astype(BF)
    sub = iota((TILE, WIDE), 0)

    def packet(k):
        to = lax.rem(leaf + k, jnp.int32(LEAVES))
        group = lax.div(to, jnp.int32(AT_ONCE))
        lane = lax.rem(to, jnp.int32(AT_ONCE)) * TILES

        def piece(r, q):
            return ybuf[pl.ds(jnp.clip(scal[group, r, lane + q], 0, ROWS), TILE), :]

        tiles = []
        for q in range(TILES):
            tile = piece(0, q)
            for r in range(1, PIECES):
                tile = jnp.where(sub >= scal[group, PIECES + r, lane + q], piece(r, q), tile)
            tiles.append(tile)
        turned = dot_nt(eye, jnp.concatenate(tiles, 0).astype(BF))
        feat[k] = turned[:F].astype(BF)
        aux[k] = jnp.concatenate([turned[F : F + 1, 128 * c : 128 * c + 128] for c in range(4)] * 2, 0)

    def give(j, _):
        steps = turn_of(2 * j + 1), turn_of(rem(2 * j + 2, LEAVES))
        for k in steps:
            packet(k)
        send_aux(steps[0]).start()
        send_feat(steps[0]).start()

        @pl.when(j < LEAVES // 2 - 1)
        def second():
            send_aux(steps[1]).start()
            send_feat(steps[1]).start()

        return 0

    def take_slots():
        each(LEAVES, lambda k: send_pivots(k).wait_recv())
        place = jnp.concatenate([held[(LEAVES - b) % LEAVES] for b in range(LEAVES)], 0)
        home = place % ROWS // PACKET
        number = ((leaf + iota((LEAVES, RANK), 0)) % LEAVES) * 8 + place // ROWS
        number = (number * PACKET + place % PACKET).astype(F32)
        valid = home == leaf * COLS + col
        order = dot(valid.astype(F32).astype(BF), before)
        order = jnp.where(valid, order, -1.0)

        def spread(table):
            return jnp.concatenate(
                [jnp.broadcast_to(table[b : b + 1], (SLOTS, RANK)) for b in range(LEAVES)], 0
            )

        shape = (LEAVES * SLOTS, RANK)
        hit = spread(order) == (iota(shape, 0) % SLOTS).astype(F32)
        wanted = jnp.sum(jnp.where(hit, spread(number) + 1.0, 0.0), 1, keepdims=True) - 1.0
        which = jnp.sum(jnp.where(hit, iota(shape, 1).astype(F32) + 1.0, 0.0), 1, keepdims=True) - 1.0
        wanted = jnp.broadcast_to(wanted, (LEAVES * SLOTS, CHUNK))

        def take(t, total):
            chosen = (wanted == ranked[t, 2:3, :]).astype(F32).astype(BF)
            rest = jnp.zeros((128 - WIDE, CHUNK), BF)
            return total + dot_nt(chosen, jnp.concatenate([joined_of(t), rest], 0))

        shape = (LEAVES * SLOTS, 128)
        taken = lax.fori_loop(0, CHUNKS, take, jnp.zeros(shape, F32), unroll=4)
        taken = jnp.where(iota(shape, 1) == WHICH, which, taken)
        taken = jnp.where(iota(shape, 1) == FULL, full, taken).astype(BF)
        for b in range(LEAVES):
            slots[b] = taken[b * SLOTS : (b + 1) * SLOTS]
        came[0] = slots[0]
        each(LEAVES, lambda k: send_slots(k).start())

    def place_points():
        each(LEAVES, lambda k: send_slots(k).wait_recv())
        got = jnp.concatenate([came[b] for b in range(LEAVES)], 0).astype(F32)
        chosen = got[:, WHICH : WHICH + 1] == iota((LEAVES * SLOTS, RANK), 1).astype(F32)
        picked = dot(got.T[:F].astype(BF), chosen.astype(F32).astype(BF))
        bad[...] = jnp.broadcast_to(jnp.max(got[:, FULL : FULL + 1], 0, keepdims=True), (8, 128))
        sk[0] = picked.astype(BF)
        each(COLS, lambda k: send_skel(k).start())

    def work(j, _):
        pl.when(j == 2)(take_slots)
        pl.when(j == 5)(place_points)
        return give(j, 0)

    lax.fori_loop(0, LEAVES // 2, work, 0)
    rx[0] = feat[0]
    ra[0] = aux[0]

    place = jnp.concatenate([held[(LEAVES - b) % LEAVES] for b in range(LEAVES)], 0)
    home = place % ROWS // PACKET
    largest = jnp.zeros((OWNERS, 1), F32)
    for b in range(LEAVES):
        held_here = (iota((OWNERS, RANK), 0) == home[b : b + 1]).astype(F32)
        largest = jnp.maximum(largest, jnp.sum(held_here, 1, keepdims=True))

    for copy in smalls:
        copy.wait()
    spare[...] = jnp.ones((8, 128), F32)
    spare[0:1, 0:F] = scales[...]
    inverse = 1.0 / to_column(spare[0:1, :])[:F]
    scale = inverse * inverse * LOG2E
    scale2 = across(scale, RANK)
    scale4 = across(scale, PER)

    index[...] = top_index(parent, top, leaf // 4)
    index2 = across(index[...], 2 * RANK)
    number = iota((RANK, 2 * RANK), 1)
    base = (quarter * RANK).astype(F32)
    other = (sibling * RANK).astype(F32)
    chosen = index2[:, :RANK] == iota((RANK, RANK), 1).astype(F32) + base
    rows[...] = chosen.astype(F32).astype(BF)
    lanes = number.astype(F32) + jnp.where(number < RANK, base, other - RANK)
    columns[...] = (index2 == lanes).astype(F32).astype(BF)
    chosen = across(index[...], 4 * RANK) == iota((RANK, 4 * RANK), 1).astype(F32)
    fours[...] = chosen.astype(F32).astype(BF)

    def norms(k):
        side[k] = point_side(rx[k].astype(F32), scale4)

    def receive(k):
        send_aux(k).wait_recv()
        send_feat(k).wait_recv()

    def early_norms(n, _):
        k = turn_of(n)
        pl.when(n > 0)(lambda: receive(k))
        norms(k)
        return 0

    lax.fori_loop(0, LEAVES // 2, early_norms, 0)

    picked = sk[0].astype(F32)

    def add_skel(k, total):
        send_skel(k).wait_recv()
        return total + sk[k].astype(F32)

    picked = lax.fori_loop(1, COLS, add_skel, picked)
    mine[...] = picked.astype(BF)
    sk4[quarter] = picked.astype(BF)

    def send_four(k):
        return remote(mine, sk4.at[quarter], (s_4, r_4), k, cousin(k))

    each(4, lambda k: send_four(k).start())
    left[0:RANK, :] = skel_side(picked, scale2)

    def block_of(k, out, begin):
        p = rx[k]
        fill = jnp.zeros((256 - 3 * F - 16, PER), BF)
        right = jnp.concatenate([p, p, p, side[k], fill], 0)
        power = dot(left[begin : begin + RANK, :], right)
        out[0:RANK, :] = jnp.exp2(jnp.minimum(power, 0.0)).astype(BF)

    def own_of(k, out):
        block_of(k, out, 0)
        value = ra[k]
        value = jnp.concatenate([value[r : r + 1] for r in range(4)], 1)
        out[RANK:, :] = jnp.broadcast_to(value, (16, PER)).astype(BF)

    def gram_of(u):
        gram[...] += dot_nt(u[...], u[0:RANK, :])

    def couple_of(v, u):
        couple[...] += dot_nt(v[...], u[0:RANK, :])

    last = LEAVES // 2 - 1

    def own_two(j, _):
        k, l = turn_of(2 * j), turn_of(2 * j + 1)
        @pl.when(j >= LEAVES // 4)
        def late():
            receive(k)
            receive(l)
            norms(k)
            norms(l)

        own_of(k, even.at[j])
        gram_of(odd.at[rem(j + last, last + 1)])
        own_of(l, odd.at[j])
        gram_of(even.at[j])
        return 0

    def other_two(j, _):
        block_of(turn_of(2 * j), other_even, RANK)
        couple_of(other_odd, odd.at[rem(j + last, last + 1)])
        block_of(turn_of(2 * j + 1), other_odd, RANK)
        couple_of(other_even, even.at[j])
        return 0

    gram[...] = jnp.zeros_like(gram)
    couple[...] = jnp.zeros_like(couple)
    odd[last] = jnp.zeros((RANK + 16, PER), BF)
    other_odd[...] = jnp.zeros_like(other_odd)
    def send_gram(k):
        return remote(pg.at[(col + k) % COLS], gr.at[k], (s_p, r_p), k, beside(k))

    def send_couple(k):
        return remote(pc.at[(col + k) % COLS], cr.at[k], (s_c, r_c), k, beside(k))

    def send_chosen(k):
        return remote(pt.at[(col + k) % COLS], qr.at[k], (s_o, r_o), k, beside(k))

    def send_rhs(k):
        return remote(rs, rr.at[k], (s_r, r_r), k, beside(k))

    def sibling_side():
        each(4, lambda k: remote(mine, sk4.at[(quarter + 4 - k) % 4], (s_4, r_4), k, cousin(k)).wait_recv())
        left[RANK:, :] = skel_side(sk4[sibling].astype(F32), scale2)

    def give_gram():
        gram_of(odd.at[last])
        part = gram[0:RANK, :].astype(BF)
        for k in range(COLS):
            pg[k] = part[k * SLAB : (k + 1) * SLAB]
        each(COLS, lambda k: send_gram(k).start())

    def half(h, _):
        pairs = LEAVES // 4
        lax.fori_loop(pairs * h, pairs * (h + 1), own_two, 0)
        pl.when(h == 0)(sibling_side)
        pl.when(h == 1)(give_gram)
        lax.fori_loop(pairs * h, pairs * (h + 1), other_two, 0)
        return 0

    lax.fori_loop(0, 2, half, 0)
    couple_of(other_odd, odd.at[last])

    rhs = gram[RANK : RANK + 1, :]
    rhs = jnp.sum(dot_nt(stack16(split3(rhs), RANK), rows[...]), 0, keepdims=True)
    rs[...] = jnp.zeros_like(rs)
    rs[0:1, :] = rhs[:, :128]
    rs[1:2, :] = rhs[:, 128:]
    rs[2:3, :] = bad[0:1, :]
    part = dot(rows[...], gram[0:RANK, :].astype(BF)).astype(BF)
    chosen = dot_nt(part, columns[:, 0:RANK])
    part = dot_nt(rows[...], couple[...].astype(BF)).astype(BF)
    chosen = chosen + dot_nt(part, columns[:, RANK:])
    chosen = chosen.astype(BF)
    for k in range(COLS):
        pt[k] = chosen[k * SLAB : (k + 1) * SLAB]
    each(COLS, lambda k: send_chosen(k).start())
    each(COLS, lambda k: send_rhs(k).start())
    part = couple[...].T.astype(BF)
    for k in range(COLS):
        pc[k] = part[k * SLAB : (k + 1) * SLAB]
    each(COLS, lambda k: send_couple(k).start())

    whole = jnp.concatenate([sk4[k] for k in range(4)], 1)
    points = dot_nt(whole, fours[...])
    fill = jnp.zeros((256 - 3 * F - 16, RANK), BF)
    points_b = points.astype(BF)
    right = jnp.concatenate([points_b, points_b, points_b, point_side(points, scale2), fill], 0)
    value = jnp.exp2(jnp.minimum(dot(skel_side(points, scale2), right), 0.0))
    crossing = (across(index[...], RANK) >= 2.0 * RANK) != (index[...].T[0:1, :] >= 2.0 * RANK)
    square = iota((RANK, RANK), 0) == iota((RANK, RANK), 1)
    tops[...] = jnp.where(crossing, value, 0.0) + jnp.where(square, ridge[...], 0.0)

    def finish(sends):
        return lambda k: [send(k).wait_send() for send in sends]

    each(LEAVES, finish((send_pivots, send_slots, send_aux, send_feat)))
    each(COLS, finish((send_skel, send_gram, send_rhs)))
    each(4, finish((send_four,)))

    def add_chosen(k, totals):
        send_chosen(k).wait_recv()
        send_rhs(k).wait_recv()
        return totals[0] + qr[k].astype(F32), totals[1] + rr[k]

    chosen, rhs = lax.fori_loop(1, COLS, add_chosen, (pt[col].astype(F32), rs[...]))
    over = jnp.maximum(jnp.max(rhs[2:3, :]), jnp.max(largest) - SLOTS)
    flag[0] = (over > 0.0).astype(jnp.int32)
    chosen = chosen * (1.0 / NODE)
    t4[0] = chosen.astype(BF)
    r4[0] = rhs * (1.0 / NODE)

    def send_top(k):
        return remote(t4.at[0], t4.at[k], (s_t, r_t), k, cousin(k))

    def send_top_rhs(k):
        return remote(r4.at[0], r4.at[k], (s_q, r_q), k, cousin(k))

    each(4, lambda k: send_top(k).start())
    each(4, lambda k: send_top_rhs(k).start())

    def add_gram(k, total):
        send_gram(k).wait_recv()
        return total + gr[k].astype(F32)

    def add_couple(k, total):
        send_couple(k).wait_recv()
        return total + cr[k].astype(F32)

    total = lax.fori_loop(1, COLS, add_gram, pg[col].astype(F32))
    diagonal = iota((SLAB, RANK), 0) + col * SLAB == iota((SLAB, RANK), 1)
    out_share[0, :, 0:RANK] = total * (1.0 / NODE) + jnp.where(diagonal, ridge[...], 0.0)
    total = lax.fori_loop(1, COLS, add_couple, pc[col].astype(F32))
    out_share[0, :, RANK:] = total * (1.0 / NODE)
    result = chosen + tops[pl.ds(pl.multiple_of(col * SLAB, SLAB), SLAB), :]

    def add_top(k, totals):
        send_top(k).wait_recv()
        send_top_rhs(k).wait_recv()
        return totals[0] + t4[k].astype(F32), totals[1] + r4[k]

    result, rhs = lax.fori_loop(1, 4, add_top, (result, r4[0]))
    out_top[0] = result
    out_rhs[...] = jnp.concatenate([rhs[0:1], rhs[1:2]], 1)

    each(COLS, finish((send_couple, send_chosen)))
    each(4, finish((send_top, send_top_rhs)))


SHAPES = ((1, SLAB, 2 * RANK), (1, SLAB, RANK), (1, RANK))


def exchange(merged, ridge, *smalls):
    return pl.pallas_call(
        exchange_kernel,
        out_shape=tuple(pltpu.VMEM(shape, F32) for shape in SHAPES),
        in_specs=[VMEM, VMEM] + [ANYWHERE] * 4,
        out_specs=[VMEM] * 3,
        scratch_shapes=[
            pltpu.VMEM((1, RANK), jnp.int32),
            pltpu.VMEM((1, F), F32),
            pltpu.VMEM((8, RANK), jnp.int32),
            pltpu.VMEM((4, RANK), jnp.int32),
            pltpu.VMEM((8, 128), F32),
            pltpu.VMEM((LEAVES, F, PER), BF),
            pltpu.VMEM((LEAVES, 8, 128), F32),
            pltpu.VMEM((LEAVES, F, PER), BF),
            pltpu.VMEM((LEAVES, 8, 128), F32),
            pltpu.VMEM((LEAVES, RANK, PER), BF),
            pltpu.VMEM((LEAVES, 16, PER), BF),
            pltpu.VMEM((COLS, F, RANK), BF),
            pltpu.VMEM((F, RANK), BF),
            pltpu.VMEM((4, F, RANK), BF),
            pltpu.VMEM((2 * RANK, 256), BF),
            pltpu.VMEM((LEAVES // 2, RANK + 16, PER), BF),
            pltpu.VMEM((LEAVES // 2, RANK + 16, PER), BF),
            pltpu.VMEM((RANK, PER), BF),
            pltpu.VMEM((RANK, PER), BF),
            pltpu.VMEM((RANK + 16, RANK), F32),
            pltpu.VMEM((RANK, RANK), F32),
            pltpu.VMEM((RANK, RANK), BF),
            pltpu.VMEM((RANK, 2 * RANK), BF),
            pltpu.VMEM((RANK, 4 * RANK), BF),
            pltpu.VMEM((RANK, 128), F32),
            pltpu.VMEM((RANK, RANK), F32),
            pltpu.VMEM((COLS, SLAB, RANK), BF),
            pltpu.VMEM((COLS, SLAB, RANK), BF),
            pltpu.VMEM((COLS, SLAB, RANK), BF),
            pltpu.VMEM((COLS, SLAB, RANK), BF),
            pltpu.VMEM((COLS, SLAB, RANK), BF),
            pltpu.VMEM((COLS, SLAB, RANK), BF),
            pltpu.VMEM((8, 128), F32),
            pltpu.VMEM((COLS, 8, 128), F32),
            pltpu.VMEM((4, SLAB, RANK), BF),
            pltpu.VMEM((4, 8, 128), F32),
            *dma(LEAVES),
            *dma(LEAVES),
            *dma(COLS),
            *dma(4),
            *dma(COLS),
            *dma(COLS),
            *dma(COLS),
            *dma(COLS),
            *dma(4),
            *dma(4),
            pltpu.SemaphoreType.DMA((5,)),
        ],
        compiler_params=params(0, 40),
        name="exchange",
    )(merged, ridge, *in_hbm(*smalls))


def stream(samples, pivots, ridge, *smalls):
    return pl.pallas_call(
        stream_kernel,
        out_shape=(
            *(pltpu.VMEM(shape, F32) for shape in SHAPES),
            jax.ShapeDtypeStruct((1,), jnp.int32),
        ),
        in_specs=[ANYWHERE, VMEM, VMEM, VMEM, VMEM] + [ANYWHERE] * 3,
        out_specs=[VMEM] * 3 + [pl.BlockSpec(memory_space=pltpu.SMEM)],
        scratch_shapes=[
            pltpu.VMEM((F, ROWS), BF),
            pltpu.VMEM((8, 128), F32),
            pltpu.VMEM((ROWS // 128, 128), F32),
            pltpu.VMEM((CHUNKS, 8, CHUNK), F32),
            pltpu.VMEM((LEAVES, 128), F32),
            pltpu.VMEM((LEAVES, 128), F32),
            pltpu.VMEM((ROWS + TILE, WIDE), F32),
            pltpu.VMEM((LEAVES // AT_ONCE, 16, 128), jnp.int32),
            pltpu.SMEM((LEAVES // AT_ONCE, 16, 128), jnp.int32),
            pltpu.VMEM((LEAVES, 1, RANK), jnp.int32),
            pltpu.VMEM((LEAVES, SLOTS, 128), BF),
            pltpu.VMEM((LEAVES, SLOTS, 128), BF),
            pltpu.VMEM((1, F), F32),
            pltpu.VMEM((8, RANK), jnp.int32),
            pltpu.VMEM((4, RANK), jnp.int32),
            pltpu.VMEM((8, 128), F32),
            pltpu.VMEM((LEAVES, F, PER), BF),
            pltpu.VMEM((LEAVES, 8, 128), F32),
            pltpu.VMEM((LEAVES, F, PER), BF),
            pltpu.VMEM((LEAVES, 8, 128), F32),
            pltpu.VMEM((LEAVES, 16, PER), BF),
            pltpu.VMEM((COLS, F, RANK), BF),
            pltpu.VMEM((F, RANK), BF),
            pltpu.VMEM((4, F, RANK), BF),
            pltpu.VMEM((2 * RANK, 256), BF),
            pltpu.VMEM((LEAVES // 2, RANK + 16, PER), BF),
            pltpu.VMEM((LEAVES // 2, RANK + 16, PER), BF),
            pltpu.VMEM((RANK, PER), BF),
            pltpu.VMEM((RANK, PER), BF),
            pltpu.VMEM((RANK + 16, RANK), F32),
            pltpu.VMEM((RANK, RANK), F32),
            pltpu.VMEM((RANK, RANK), BF),
            pltpu.VMEM((RANK, 2 * RANK), BF),
            pltpu.VMEM((RANK, 4 * RANK), BF),
            pltpu.VMEM((RANK, 128), F32),
            pltpu.VMEM((RANK, RANK), F32),
            pltpu.VMEM((COLS, SLAB, RANK), BF),
            pltpu.VMEM((COLS, SLAB, RANK), BF),
            pltpu.VMEM((COLS, SLAB, RANK), BF),
            pltpu.VMEM((COLS, SLAB, RANK), BF),
            pltpu.VMEM((COLS, SLAB, RANK), BF),
            pltpu.VMEM((COLS, SLAB, RANK), BF),
            pltpu.VMEM((8, 128), F32),
            pltpu.VMEM((COLS, 8, 128), F32),
            pltpu.VMEM((4, SLAB, RANK), BF),
            pltpu.VMEM((4, 8, 128), F32),
            *dma(LEAVES),
            *dma(LEAVES),
            *dma(LEAVES),
            *dma(LEAVES),
            *dma(COLS),
            *dma(4),
            *dma(COLS),
            *dma(COLS),
            *dma(COLS),
            *dma(COLS),
            *dma(4),
            *dma(4),
            pltpu.SemaphoreType.DMA((5,)),
        ],
        compiler_params=params(1, 40),
        name="stream",
    )(*in_hbm(*samples, pivots), ridge, *in_hbm(*smalls))


def emit_kernel(*refs):
    ins, outs, sem = refs[:3], refs[3:6], refs[6]
    copies = [pltpu.make_async_copy(a, b, sem.at[k]) for k, (a, b) in enumerate(zip(ins, outs))]
    for copy in copies:
        copy.start()
    for copy in copies:
        copy.wait()


def emit(results):
    return pl.pallas_call(
        emit_kernel,
        out_shape=tuple(jax.ShapeDtypeStruct(shape, F32) for shape in SHAPES),
        in_specs=[VMEM] * 3,
        out_specs=[ANYWHERE] * 3,
        scratch_shapes=[pltpu.SemaphoreType.DMA((3,))],
        compiler_params=params(),
        name="emit",
    )(*results)


def local(features, targets, owner, length_scales, ridge, leaf_pivots, parent_pivots, top_pivots):
    samples = (features, targets.reshape(ROWS // 128, 128), owner.reshape(ROWS // 128, 128))
    ridge = ridge.reshape(1, 1)
    smalls = (length_scales.reshape(1, F), parent_pivots, top_pivots)
    *results, flag = stream(samples, leaf_pivots, ridge, *smalls)

    def again():
        return tuple(emit(exchange(pack(*samples), ridge, leaf_pivots, *smalls)))

    return lax.switch(flag[0], [lambda: tuple(emit(results)), again])


def solution(mesh):
    return jax.shard_map(
        local,
        mesh=mesh,
        in_specs=(
            P(None, ("leaf", "col")),
            P(("leaf", "col")),
            P(("leaf", "col")),
            P(),
            P(),
            P("leaf", None),
            P(),
            P(),
        ),
        out_specs=(P("leaf", "col", None), P("leaf", "col", None), P("leaf", None)),
        check_vma=False,
    )
```

```python
import functools
import math

import jax
import jax.numpy as jnp
from jax import lax
from jax.experimental import pallas as pl
from jax.experimental.pallas import tpu as pltpu
from jax.sharding import PartitionSpec as P

F = 48
RANK = 256
ROWS = 8192
LEAVES = 16
COLS = 8
OWNERS = 128
PACKET = 64
PER = ROWS // LEAVES
CHUNK = 256
CHUNKS = ROWS // CHUNK
WINDOW = 40
REGION = PER + WINDOW
TILE = 32
TILES = PER // TILE
PIECES = 6
AT_ONCE = 128 // TILES
SLOTS = 16
WHICH = 50
FULL = 51
WIDE = 64
SLAB = RANK // COLS
NODE = ROWS * COLS
LOG2E = math.log2(math.e)
BF = jnp.bfloat16
F32 = jnp.float32
NT = (((1,), (1,)), ((), ()))
MESH = pl.DeviceIdType.MESH


def dma(count):
    return [pltpu.SemaphoreType.DMA((count,))] * 2


def params(number=None, limit=24):
    if number is None:
        return pltpu.CompilerParams(vmem_limit_bytes=limit * 2**20)
    return pltpu.CompilerParams(
        collective_id=number, has_side_effects=True, vmem_limit_bytes=limit * 2**20
    )


ANYWHERE = pl.BlockSpec(memory_space=pl.ANY)
VMEM = pl.BlockSpec(memory_space=pltpu.VMEM)


def iota(shape, axis):
    return lax.broadcasted_iota(jnp.int32, shape, axis)


def dot(a, b):
    return jnp.dot(a, b, preferred_element_type=F32)


def dot_nt(a, b):
    return lax.dot_general(a, b, NT, preferred_element_type=F32)


def row_pair(two):
    return jnp.concatenate([two[0:1], two[1:2]], 1)


def pack_kernel(
    feat_hbm, target, owner, zbuf, feat, goals, rows, ybuf, table, scal, sem, feat_sem
):
    bring = pltpu.make_async_copy(feat_hbm, feat, feat_sem)
    bring.start()
    goals[...] = target[...].astype(F32)
    before = (iota((CHUNK, CHUNK), 0) < iota((CHUNK, CHUNK), 1)).astype(F32).astype(BF)
    weights = jnp.concatenate([before, jnp.ones((CHUNK, 128), BF)], 1)
    lane = iota((LEAVES, 128), 1)

    def ranks(t, carry):
        seen, seen_leaf, most = carry
        own = row_pair(owner[pl.ds(2 * t, 2), :])
        leaf = own // 8
        is_own = iota((OWNERS, CHUNK), 0) == own
        is_leaf = iota((LEAVES, CHUNK), 0) == leaf
        is_after = iota((LEAVES, CHUNK), 0) > leaf
        marks = jnp.concatenate(
            [m.astype(F32).astype(BF) for m in (is_own, is_leaf, is_after)], 0
        )
        sums = dot(marks, weights)
        counts = sums[:OWNERS, CHUNK:]
        leaf_counts = sums[OWNERS : OWNERS + LEAVES, CHUNK:]
        base = sums[OWNERS + LEAVES :, CHUNK:]
        prior = sums[:OWNERS, :CHUNK] + jnp.concatenate([seen, seen], 1)
        rank = jnp.sum(jnp.where(is_own, prior, 0.0), 0, keepdims=True)
        place = sums[OWNERS : OWNERS + LEAVES, :CHUNK] + jnp.concatenate([base, base], 1)
        place = jnp.sum(jnp.where(is_leaf, place, 0.0), 0, keepdims=True)
        tag = (own % 8).astype(F32) * PACKET + rank - (PER // 2)
        rows[t, 0:1, :] = place
        rows[t, 1:2, :] = row_pair(goals[pl.ds(2 * t, 2), :])
        rows[t, 2:3, :] = tag
        here = lane == t
        table[0:LEAVES, :] = jnp.where(here, seen_leaf.astype(jnp.int32), table[0:LEAVES, :])
        table[LEAVES : 2 * LEAVES, :] = jnp.where(
            here, base.astype(jnp.int32), table[LEAVES : 2 * LEAVES, :]
        )
        return seen + counts, seen_leaf + leaf_counts, jnp.maximum(most, leaf_counts)

    table[0:LEAVES, :] = jnp.full((LEAVES, 128), PER, jnp.int32)
    zero = jnp.zeros((LEAVES, 128), F32)
    _, _, most = lax.fori_loop(
        0, CHUNKS, ranks, (jnp.zeros((OWNERS, 128), F32), zero, zero), unroll=16
    )
    most = jnp.broadcast_to(jnp.max(most, 0, keepdims=True), (8, 128))
    table[2 * LEAVES :, :] = most.astype(jnp.int32)
    move = pltpu.make_async_copy(table, scal, sem)
    move.start()
    bring.wait()

    def sort(t, _):
        start = pl.multiple_of(t * CHUNK, CHUNK)
        row = iota((16, CHUNK), 0)
        place, goal, tag = rows[t, 0:1, :], rows[t, 1:2, :], rows[t, 2:3, :]
        extra = jnp.where(row == 0, goal, jnp.where(row == 1, tag, 0.0)).astype(BF)
        joined = jnp.concatenate([feat[:, pl.ds(start, CHUNK)], extra], 0)
        chosen = (iota((CHUNK, CHUNK), 0) == place.astype(jnp.int32)).astype(F32).astype(BF)
        ybuf[pl.ds(start, CHUNK), :] = dot_nt(chosen, joined)
        return 0

    lax.fori_loop(0, CHUNKS, sort, 0, unroll=8)
    move.wait()
    widest = scal[2 * LEAVES, 0]

    @pl.when(widest <= WINDOW)
    def quick():
        def merge(t, _):
            for i in range(LEAVES):
                source = t * CHUNK + scal[LEAVES + i, t]
                goal = i * REGION + scal[i, t]
                zbuf[pl.ds(goal, WINDOW), :] = ybuf[pl.ds(source, WINDOW), :]
            return 0

        lax.fori_loop(0, CHUNKS, merge, 0, unroll=4)

    @pl.when(widest > WINDOW)
    def slow():
        def merge(index, _):
            t = index // LEAVES
            i = index % LEAVES
            source = t * CHUNK + scal[LEAVES + i, t]
            first = scal[i, t]
            count = scal[i, t + 1] - first

            def part(k, _):
                rows = ybuf[pl.ds(source + 8 * k, 8), :]
                zbuf[pl.ds(i * REGION + first + 8 * k, 8), :] = rows
                return 0

            lax.fori_loop(0, (count + 7) // 8, part, 0)
            return 0

        lax.fori_loop(0, CHUNKS * LEAVES, merge, 0)


def in_hbm(*arrays):
    return [pltpu.with_memory_space_constraint(a, pltpu.HBM) for a in arrays]


def pack(features, targets, owner):
    return pl.pallas_call(
        pack_kernel,
        out_shape=pltpu.VMEM((LEAVES * REGION, WIDE), F32),
        in_specs=[ANYWHERE, VMEM, VMEM],
        out_specs=VMEM,
        scratch_shapes=[
            pltpu.VMEM((F, ROWS), BF),
            pltpu.VMEM((ROWS // 128, 128), F32),
            pltpu.VMEM((CHUNKS, 8, CHUNK), F32),
            pltpu.VMEM((ROWS + WINDOW, WIDE), F32),
            pltpu.VMEM((40, 128), jnp.int32),
            pltpu.SMEM((40, 128), jnp.int32),
            pltpu.SemaphoreType.DMA,
            pltpu.SemaphoreType.DMA,
        ],
        compiler_params=params(),
        name="pack",
    )(*in_hbm(features, targets, owner))


def split3(x):
    high = x.astype(BF)
    rest = x - high.astype(F32)
    mid = rest.astype(BF)
    return high, mid, (rest - mid.astype(F32)).astype(BF)


def stack16(parts, width):
    row = iota((16, width), 0)
    block = jnp.zeros((16, width), F32)
    for k, part in enumerate(parts):
        block = jnp.where(row == k, part if isinstance(part, float) else part.astype(F32), block)
    return block.astype(BF)


def half_norm(points, scale):
    return jnp.sum(points * points * (0.5 * scale), 0, keepdims=True)


def point_side(points, scale):
    high, mid, low = split3(-half_norm(points, scale))
    return stack16([high, mid, low, 1.0, 1.0, 1.0], points.shape[1])


def skel_side(skel, scale):
    width = skel.shape[1]
    high, mid, low = split3(skel * scale)
    extra = stack16([1.0, 1.0, 1.0, *split3(-half_norm(skel, scale))], width)
    parts = [p.astype(F32) for p in (high, mid, low, extra)]
    fill = jnp.zeros((256 - 3 * F - 16, width), F32)
    return jnp.concatenate([*parts, fill], 0).T.astype(BF)


def select_row(table, row):
    hit = iota(table.shape, 0) == row
    return jnp.sum(jnp.where(hit, table.astype(F32), 0.0), 0, keepdims=True)


def to_column(row):
    return jnp.broadcast_to(row, (128, row.shape[1])).T


def across(column, width):
    return jnp.concatenate([column] * (width // 128), 1)


def place_of(leaf, col):
    return dict(device_id=(leaf, col), device_id_type=MESH)


def mate(k):
    leaf, col = lax.axis_index("leaf"), lax.axis_index("col")
    to = (leaf + k) % LEAVES
    cross = (to // 8 + leaf // 8) % 2
    return place_of(to, col + cross * (1 - 2 * (col % 2)))


def beside(k):
    leaf, col = lax.axis_index("leaf"), lax.axis_index("col")
    return place_of(leaf, (col + k) % COLS)


def cousin(k):
    leaf, col = lax.axis_index("leaf"), lax.axis_index("col")
    return place_of(leaf - leaf % 4 + (leaf + k) % 4, col)


def each(count, step, unroll=1):
    lax.fori_loop(1, count, lambda k, _: (step(k), 0)[1], 0, unroll=unroll)


def rem(a, b):
    return lax.rem(jnp.int32(a), jnp.int32(b))


def turn_of(n):
    n = jnp.int32(n)
    odd = lax.rem(n, jnp.int32(2))
    half = lax.div(n + odd, jnp.int32(2))
    return lax.rem(odd * half + (1 - odd) * (LEAVES - half), jnp.int32(LEAVES))


def remote(src, dst, sems, k, peer):
    return pltpu.make_async_remote_copy(src, dst, sems[0].at[k], sems[1].at[k], **peer)


def top_index(parent, top, group):
    top_row = select_row(top[...], group)
    below = jnp.concatenate([select_row(parent[...], 2 * group + r) for r in range(2)], 1)
    number = iota((RANK, 2 * RANK), 1)
    below = below + jnp.where(iota((1, 2 * RANK), 1) >= RANK, 2.0 * RANK, 0.0)
    hit = across(to_column(top_row), 2 * RANK) == number.astype(F32)
    index = jnp.sum(jnp.where(hit, below, 0.0), 1, keepdims=True)
    return jnp.broadcast_to(index, (RANK, 128))


def exchange_kernel(
    merged, ridge, pivots_hbm, scales_hbm, parent_hbm, top_hbm, out_share, out_top, out_rhs,
    pivots, scales, parent, top, spare, feat, aux, rx, ra, hot, side, sk, mine, sk4, left,
    even, odd, other_even, other_odd, gram, couple, rows, columns, fours, index, tops,
    pg, gr, pc, cr, pt, qr, rs, rr, t4, r4,
    s_f, r_f, s_a, r_a, s_k, r_k, s_4, r_4, s_p, r_p, s_c, r_c, s_o, r_o, s_r, r_r, s_t, r_t, s_q, r_q, local,
):
    leaf = lax.axis_index("leaf")
    col = lax.axis_index("col")
    quarter = leaf % 4
    sibling = quarter + 1 - 2 * (quarter % 2)
    barrier = pltpu.get_barrier_semaphore()
    each(LEAVES, lambda k: pl.semaphore_signal(barrier, inc=1, **mate(k)))
    each(COLS, lambda k: pl.semaphore_signal(barrier, inc=1, **beside(k)))
    smalls = [
        pltpu.make_async_copy(a, b, local.at[k])
        for k, (a, b) in enumerate(
            [(pivots_hbm, pivots), (scales_hbm, scales), (parent_hbm, parent), (top_hbm, top)]
        )
    ]
    for copy in smalls:
        copy.start()

    eye = (iota((WIDE, WIDE), 0) == iota((WIDE, WIDE), 1)).astype(F32).astype(BF)

    def turn(k):
        start = pl.multiple_of((leaf + k) % LEAVES * REGION, 8)
        turned = dot_nt(eye, merged[pl.ds(start, PER), :].astype(BF))
        feat[k] = turned[:F].astype(BF)
        aux[k] = jnp.concatenate(
            [turned[F + r : F + r + 1, 128 * c : 128 * c + 128] for r in range(2) for c in range(4)], 0
        )

    def send_feat(k):
        return remote(feat.at[k], rx.at[k], (s_f, r_f), k, mate(k))

    def send_aux(k):
        return remote(aux.at[k], ra.at[k], (s_a, r_a), k, mate(k))

    def four(j, _):
        steps = [turn_of(lax.rem(4 * j + r, LEAVES)) for r in range(1, 5)]
        for k in steps:
            turn(k)
        pl.when(j == 0)(lambda: pl.semaphore_wait(barrier, LEAVES + COLS - 2))
        for send in (send_aux, send_feat):
            for k in steps[:3]:
                send(k).start()
            pl.when(j < 3)(lambda: send(steps[3]).start())
        return 0

    lax.fori_loop(0, LEAVES // 4, four, 0)
    rx[0] = feat[0]
    ra[0] = aux[0]

    for copy in smalls:
        copy.wait()
    spare[...] = jnp.ones((8, 128), F32)
    spare[0:1, 0:F] = scales[...]
    inverse = 1.0 / to_column(spare[0:1, :])[:F]
    scale = inverse * inverse * LOG2E
    scale2 = across(scale, RANK)
    scale4 = across(scale, PER)

    place = pivots[...]
    within = place % ROWS
    block = within // PACKET
    key = (block // COLS) * PER + (place // ROWS) * PACKET + within % PACKET
    holder = block % COLS
    crossed = (block // COLS) // 8 != leaf // 8
    holder = jnp.where(crossed, holder + 1 - 2 * (holder % 2), holder)
    key = jnp.where(holder == col, key, -PER)
    key = across(to_column(key.astype(F32)), PER)

    def mark(k):
        source = (leaf + LEAVES - k) % LEAVES
        tags = ra[k, 4:8, :]
        tag = jnp.concatenate([tags[r : r + 1] for r in range(4)], 1)
        wanted = tag + (PER // 2 + source * PER).astype(F32)
        hot[k] = (key == wanted).astype(F32).astype(BF)

    def mark_next(n, _):
        k = turn_of(n)
        pl.when(n > 0)(lambda: send_aux(k).wait_recv())
        mark(k)
        return 0

    lax.fori_loop(0, LEAVES, mark_next, 0)

    index[...] = top_index(parent, top, leaf // 4)
    index2 = across(index[...], 2 * RANK)
    number = iota((RANK, 2 * RANK), 1)
    base = (quarter * RANK).astype(F32)
    other = (sibling * RANK).astype(F32)
    chosen = index2[:, :RANK] == iota((RANK, RANK), 1).astype(F32) + base
    rows[...] = chosen.astype(F32).astype(BF)
    lanes = number.astype(F32) + jnp.where(number < RANK, base, other - RANK)
    columns[...] = (index2 == lanes).astype(F32).astype(BF)
    chosen = across(index[...], 4 * RANK) == iota((RANK, 4 * RANK), 1).astype(F32)
    fours[...] = chosen.astype(F32).astype(BF)

    def pick(j, total):
        steps = [turn_of(4 * j + r) for r in range(4)]
        pl.when(j > 0)(lambda: send_feat(steps[0]).wait_recv())
        for k in steps[1:]:
            send_feat(k).wait_recv()
        for k in steps:
            total = total + dot_nt(hot[k], rx[k])
        return total

    picked = lax.fori_loop(0, LEAVES // 4, pick, jnp.zeros((RANK, F), F32))
    picked = jnp.concatenate([picked, jnp.zeros((RANK, 128 - F), F32)], 1).T[:F]
    sk[0] = picked.astype(BF)

    def send_skel(k):
        return remote(sk.at[0], sk.at[k], (s_k, r_k), k, beside(k))

    each(COLS, lambda k: send_skel(k).start())

    def norms(k, _):
        side[k] = point_side(rx[k].astype(F32), scale4)
        return 0

    lax.fori_loop(0, LEAVES, norms, 0)

    def add_skel(k, total):
        send_skel(k).wait_recv()
        return total + sk[k].astype(F32)

    picked = lax.fori_loop(1, COLS, add_skel, picked)
    mine[...] = picked.astype(BF)
    sk4[quarter] = picked.astype(BF)

    def send_four(k):
        return remote(mine, sk4.at[quarter], (s_4, r_4), k, cousin(k))

    each(4, lambda k: send_four(k).start())
    left[0:RANK, :] = skel_side(picked, scale2)

    def block_of(k, out, begin):
        p = rx[k]
        fill = jnp.zeros((256 - 3 * F - 16, PER), BF)
        right = jnp.concatenate([p, p, p, side[k], fill], 0)
        power = dot(left[begin : begin + RANK, :], right)
        out[0:RANK, :] = jnp.exp2(jnp.minimum(power, 0.0)).astype(BF)

    def own_of(k, out):
        block_of(k, out, 0)
        value = jnp.concatenate([ra[k, r : r + 1, :] for r in range(4)], 1)
        out[RANK:, :] = jnp.broadcast_to(value, (16, PER)).astype(BF)

    def gram_of(u):
        gram[...] += dot_nt(u[...], u[0:RANK, :])

    def couple_of(v, u):
        couple[...] += dot_nt(v[...], u[0:RANK, :])

    last = LEAVES // 2 - 1

    def own_two(j, _):
        own_of(2 * j, even.at[j])
        gram_of(odd.at[(j + last) % (last + 1)])
        own_of(2 * j + 1, odd.at[j])
        gram_of(even.at[j])
        return 0

    def other_two(j, _):
        block_of(2 * j, other_even, RANK)
        couple_of(other_odd, odd.at[(j + last) % (last + 1)])
        block_of(2 * j + 1, other_odd, RANK)
        couple_of(other_even, even.at[j])
        return 0

    gram[...] = jnp.zeros_like(gram)
    couple[...] = jnp.zeros_like(couple)
    odd[last] = jnp.zeros((RANK + 16, PER), BF)
    other_odd[...] = jnp.zeros_like(other_odd)
    lax.fori_loop(0, last + 1, own_two, 0)
    gram_of(odd.at[last])

    def send_gram(k):
        return remote(pg.at[(col + k) % COLS], gr.at[k], (s_p, r_p), k, beside(k))

    def send_couple(k):
        return remote(pc.at[(col + k) % COLS], cr.at[k], (s_c, r_c), k, beside(k))

    def send_chosen(k):
        return remote(pt.at[(col + k) % COLS], qr.at[k], (s_o, r_o), k, beside(k))

    def send_rhs(k):
        return remote(rs, rr.at[k], (s_r, r_r), k, beside(k))

    part = gram[0:RANK, :].astype(BF)
    for k in range(COLS):
        pg[k] = part[k * SLAB : (k + 1) * SLAB]
    rhs = gram[RANK : RANK + 1, :]
    rhs = jnp.sum(dot_nt(stack16(split3(rhs), RANK), rows[...]), 0, keepdims=True)
    rs[...] = jnp.zeros_like(rs)
    rs[0:1, :] = rhs[:, :128]
    rs[1:2, :] = rhs[:, 128:]
    each(COLS, lambda k: send_gram(k).start())
    each(COLS, lambda k: send_rhs(k).start())
    tops[...] = dot_nt(dot(rows[...], part).astype(BF), columns[:, 0:RANK])

    each(4, lambda k: remote(mine, sk4.at[(quarter + 4 - k) % 4], (s_4, r_4), k, cousin(k)).wait_recv())
    left[RANK:, :] = skel_side(sk4[sibling].astype(F32), scale2)
    lax.fori_loop(0, last + 1, other_two, 0)
    couple_of(other_odd, odd.at[last])

    part = couple[...].astype(BF)
    chosen = dot_nt(dot_nt(rows[...], part).astype(BF), columns[:, RANK:]) + tops[...]
    chosen = chosen.astype(BF)
    for k in range(COLS):
        pt[k] = chosen[k * SLAB : (k + 1) * SLAB]
    each(COLS, lambda k: send_chosen(k).start())
    part = couple[...].T.astype(BF)
    for k in range(COLS):
        pc[k] = part[k * SLAB : (k + 1) * SLAB]
    each(COLS, lambda k: send_couple(k).start())

    whole = jnp.concatenate([sk4[k] for k in range(4)], 1)
    points = dot_nt(whole, fours[...])
    fill = jnp.zeros((256 - 3 * F - 16, RANK), BF)
    points_b = points.astype(BF)
    right = jnp.concatenate([points_b, points_b, points_b, point_side(points, scale2), fill], 0)
    value = jnp.exp2(jnp.minimum(dot(skel_side(points, scale2), right), 0.0))
    crossing = (across(index[...], RANK) >= 2.0 * RANK) != (index[...].T[0:1, :] >= 2.0 * RANK)
    square = iota((RANK, RANK), 0) == iota((RANK, RANK), 1)
    tops[...] = jnp.where(crossing, value, 0.0) + jnp.where(square, ridge[...], 0.0)

    def finish(sends):
        return lambda k: [send(k).wait_send() for send in sends]

    each(LEAVES, finish((send_aux, send_feat)))
    each(COLS, finish((send_skel, send_gram, send_rhs)))
    each(4, finish((send_four,)))

    def add_chosen(k, totals):
        send_chosen(k).wait_recv()
        send_rhs(k).wait_recv()
        return totals[0] + qr[k].astype(F32), totals[1] + rr[k]

    chosen, rhs = lax.fori_loop(1, COLS, add_chosen, (pt[col].astype(F32), rs[...]))
    chosen = chosen * (1.0 / NODE)
    t4[0] = chosen.astype(BF)
    r4[0] = rhs * (1.0 / NODE)

    def send_top(k):
        return remote(t4.at[0], t4.at[k], (s_t, r_t), k, cousin(k))

    def send_top_rhs(k):
        return remote(r4.at[0], r4.at[k], (s_q, r_q), k, cousin(k))

    each(4, lambda k: send_top(k).start())
    each(4, lambda k: send_top_rhs(k).start())

    def add_gram(k, total):
        send_gram(k).wait_recv()
        return total + gr[k].astype(F32)

    def add_couple(k, total):
        send_couple(k).wait_recv()
        return total + cr[k].astype(F32)

    total = lax.fori_loop(1, COLS, add_gram, pg[col].astype(F32))
    diagonal = iota((SLAB, RANK), 0) + col * SLAB == iota((SLAB, RANK), 1)
    out_share[0, :, 0:RANK] = total * (1.0 / NODE) + jnp.where(diagonal, ridge[...], 0.0)
    total = lax.fori_loop(1, COLS, add_couple, pc[col].astype(F32))
    out_share[0, :, RANK:] = total * (1.0 / NODE)
    result = chosen + tops[pl.ds(pl.multiple_of(col * SLAB, SLAB), SLAB), :]

    def add_top(k, totals):
        send_top(k).wait_recv()
        send_top_rhs(k).wait_recv()
        return totals[0] + t4[k].astype(F32), totals[1] + r4[k]

    result, rhs = lax.fori_loop(1, 4, add_top, (result, r4[0]))
    out_top[0] = result
    out_rhs[...] = jnp.concatenate([rhs[0:1], rhs[1:2]], 1)

    each(COLS, finish((send_couple, send_chosen)))
    each(4, finish((send_top, send_top_rhs)))


def stream_kernel(
    feat_hbm, target, owner, pivots, ridge, scales_hbm, parent_hbm, top_hbm,
    out_share, out_top, out_rhs, flag,
    feat_in, bad, goals, ranked, starts, bases, ybuf, table, scal, held, slots, came, scales, parent, top, spare,
    feat, aux, rx, ra, side, sk, mine, sk4, left, even, odd, other_even, other_odd, gram, couple,
    rows, columns, fours, index, tops, pg, gr, pc, cr, pt, qr, rs, rr, t4, r4,
    s_v, r_v, s_s, r_s, s_f, r_f, s_a, r_a, s_k, r_k, s_4, r_4, s_p, r_p, s_c, r_c, s_o, r_o,
    s_r, r_r, s_t, r_t, s_q, r_q, local,
):
    leaf = lax.axis_index("leaf")
    col = lax.axis_index("col")
    quarter = leaf % 4
    sibling = quarter + 1 - 2 * (quarter % 2)
    barrier = pltpu.get_barrier_semaphore()
    each(LEAVES, lambda k: pl.semaphore_signal(barrier, inc=1, **mate(k)))
    each(COLS, lambda k: pl.semaphore_signal(barrier, inc=1, **beside(k)))
    bring = pltpu.make_async_copy(feat_hbm, feat_in, local.at[3])
    bring.start()
    smalls = [
        pltpu.make_async_copy(a, b, local.at[k])
        for k, (a, b) in enumerate([(scales_hbm, scales), (parent_hbm, parent), (top_hbm, top)])
    ]
    for copy in smalls:
        copy.start()

    def send_pivots(k):
        return remote(pivots, held.at[k], (s_v, r_v), k, mate(k))

    def send_slots(k):
        return remote(slots.at[k], came.at[k], (s_s, r_s), k, mate(k))

    def send_feat(k):
        return remote(feat.at[k], rx.at[k], (s_f, r_f), k, mate(k))

    def send_aux(k):
        return remote(aux.at[k], ra.at[k], (s_a, r_a), k, mate(k))

    def send_skel(k):
        return remote(sk.at[0], sk.at[k], (s_k, r_k), k, beside(k))

    goals[...] = target[...].astype(F32)
    before = (iota((CHUNK, CHUNK), 0) < iota((CHUNK, CHUNK), 1)).astype(F32).astype(BF)
    weights = jnp.concatenate([before, jnp.ones((CHUNK, 128), BF)], 1)
    lane = iota((LEAVES, 128), 1)

    def rank(t, carry):
        seen, seen_leaf = carry
        own = row_pair(owner[pl.ds(2 * t, 2), :])
        group = own // 8
        is_own = iota((OWNERS, CHUNK), 0) == own
        is_leaf = iota((LEAVES, CHUNK), 0) == group
        is_after = iota((LEAVES, CHUNK), 0) > group
        marks = jnp.concatenate([m.astype(F32).astype(BF) for m in (is_own, is_leaf, is_after)], 0)
        sums = dot(marks, weights)
        leaf_counts = sums[OWNERS : OWNERS + LEAVES, CHUNK:]
        base = sums[OWNERS + LEAVES :, CHUNK:]
        prior = sums[:OWNERS, :CHUNK] + jnp.concatenate([seen, seen], 1)
        place = jnp.sum(jnp.where(is_own, prior, 0.0), 0, keepdims=True)
        order = sums[OWNERS : OWNERS + LEAVES, :CHUNK] + jnp.concatenate([base, base], 1)
        ranked[t, 0:1, :] = jnp.sum(jnp.where(is_leaf, order, 0.0), 0, keepdims=True)
        ranked[t, 1:2, :] = row_pair(goals[pl.ds(2 * t, 2), :])
        ranked[t, 2:3, :] = own.astype(F32) * PACKET + place
        starts[...] = jnp.where(lane == t, seen_leaf, starts[...])
        bases[...] = jnp.where(lane == t, base, bases[...])
        return seen + sums[:OWNERS, CHUNK:], seen_leaf + leaf_counts

    starts[...] = jnp.zeros_like(starts)
    bases[...] = jnp.zeros_like(bases)
    lax.fori_loop(
        0, CHUNKS, rank, (jnp.zeros((OWNERS, 128), F32), jnp.zeros((LEAVES, 128), F32)), unroll=16
    )

    rest = jnp.zeros((128 - LEAVES, 128), F32)
    start_of = jnp.concatenate([starts[...], rest], 0).T[:CHUNKS]
    base_of = jnp.concatenate([bases[...], rest], 0).T[:CHUNKS]
    high = jnp.where(start_of >= 256.0, 256.0, 0.0)
    columns_of = jnp.concatenate([high, start_of - high, base_of], 0).astype(BF)
    chunk = iota((CHUNKS, 128), 0).astype(F32)
    first = (iota((1, 128), 1) % TILES * TILE).astype(F32)
    full = jnp.zeros((1, 128), F32)
    table[...] = jnp.zeros_like(table)
    for g in range(LEAVES // AT_ONCE):
        one = iota((128, 128), 0) == iota((128, 128), 1) // TILES + g * AT_ONCE
        spread_out = dot(columns_of, one.astype(F32).astype(BF))
        begin = spread_out[:CHUNKS] + spread_out[CHUNKS : 2 * CHUNKS]
        place = spread_out[2 * CHUNKS :] + chunk * CHUNK
        passed = (begin <= first) & (chunk > 0.0)
        current = jnp.sum(jnp.where(passed, 1.0, 0.0), 0, keepdims=True)
        for r in range(PIECES + 1):
            here = chunk == current + r
            row = jnp.sum(jnp.where(here, place, 0.0), 0, keepdims=True)
            edge = jnp.sum(jnp.where(here, begin, 0.0), 0, keepdims=True)
            edge = jnp.where(current + r < CHUNKS, edge, float(PER)) - first
            if r == PIECES:
                full = jnp.maximum(full, jnp.where(edge < TILE, 1.0, 0.0))
                continue
            if r:
                edge = jnp.clip(edge, 0.0, float(TILE))
                table[g, PIECES + r : PIECES + r + 1, :] = edge.astype(jnp.int32)
            row = jnp.clip(jnp.where(current + r < CHUNKS, row - edge, 0.0), 0.0, float(ROWS))
            table[g, r : r + 1, :] = row.astype(jnp.int32)
    full = jnp.broadcast_to(jnp.max(full, 1, keepdims=True), (1, 128))
    tell = pltpu.make_async_copy(table, scal, local.at[4])
    tell.start()

    held[0] = pivots[...]
    pl.semaphore_wait(barrier, LEAVES + COLS - 2)
    each(LEAVES, lambda k: send_pivots(k).start())

    def joined_of(t):
        row = iota((16, CHUNK), 0)
        extra = jnp.where(row == 0, ranked[t, 1:2, :], 0.0).astype(BF)
        return jnp.concatenate([feat_in[:, pl.ds(pl.multiple_of(t * CHUNK, CHUNK), CHUNK)], extra], 0)

    def sort(t, _):
        place = ranked[t, 0:1, :].astype(jnp.int32)
        chosen = (iota((CHUNK, CHUNK), 0) == place).astype(F32).astype(BF)
        ybuf[pl.ds(pl.multiple_of(t * CHUNK, CHUNK), CHUNK), :] = dot_nt(chosen, joined_of(t))
        return 0

    bring.wait()
    lax.fori_loop(0, CHUNKS, sort, 0, unroll=8)
    ybuf[ROWS:, :] = jnp.zeros((TILE, WIDE), F32)
    tell.wait()

    eye = (iota((WIDE, WIDE), 0) == iota((WIDE, WIDE), 1)).astype(F32).astype(BF)
    sub = iota((TILE, WIDE), 0)

    def packet(k):
        to = lax.rem(leaf + k, jnp.int32(LEAVES))
        group = lax.div(to, jnp.int32(AT_ONCE))
        lane = lax.rem(to, jnp.int32(AT_ONCE)) * TILES

        def piece(r, q):
            return ybuf[pl.ds(jnp.clip(scal[group, r, lane + q], 0, ROWS), TILE), :]

        tiles = []
        for q in range(TILES):
            tile = piece(0, q)
            for r in range(1, PIECES):
                tile = jnp.where(sub >= scal[group, PIECES + r, lane + q], piece(r, q), tile)
            tiles.append(tile)
        turned = dot_nt(eye, jnp.concatenate(tiles, 0).astype(BF))
        feat[k] = turned[:F].astype(BF)
        aux[k] = jnp.concatenate([turned[F : F + 1, 128 * c : 128 * c + 128] for c in range(4)] * 2, 0)

    def give(j, _):
        steps = turn_of(2 * j + 1), turn_of(rem(2 * j + 2, LEAVES))
        for k in steps:
            packet(k)
        send_aux(steps[0]).start()
        send_feat(steps[0]).start()

        @pl.when(j < LEAVES // 2 - 1)
        def second():
            send_aux(steps[1]).start()
            send_feat(steps[1]).start()

        return 0

    def take_slots():
        each(LEAVES, lambda k: send_pivots(k).wait_recv())
        place = jnp.concatenate([held[(LEAVES - b) % LEAVES] for b in range(LEAVES)], 0)
        home = place % ROWS // PACKET
        number = ((leaf + iota((LEAVES, RANK), 0)) % LEAVES) * 8 + place // ROWS
        number = (number * PACKET + place % PACKET).astype(F32)
        valid = home == leaf * COLS + col
        order = dot(valid.astype(F32).astype(BF), before)
        order = jnp.where(valid, order, -1.0)

        def spread(table):
            return jnp.concatenate(
                [jnp.broadcast_to(table[b : b + 1], (SLOTS, RANK)) for b in range(LEAVES)], 0
            )

        shape = (LEAVES * SLOTS, RANK)
        hit = spread(order) == (iota(shape, 0) % SLOTS).astype(F32)
        wanted = jnp.sum(jnp.where(hit, spread(number) + 1.0, 0.0), 1, keepdims=True) - 1.0
        which = jnp.sum(jnp.where(hit, iota(shape, 1).astype(F32) + 1.0, 0.0), 1, keepdims=True) - 1.0
        wanted = jnp.broadcast_to(wanted, (LEAVES * SLOTS, CHUNK))

        def take(t, total):
            chosen = (wanted == ranked[t, 2:3, :]).astype(F32).astype(BF)
            rest = jnp.zeros((128 - WIDE, CHUNK), BF)
            return total + dot_nt(chosen, jnp.concatenate([joined_of(t), rest], 0))

        shape = (LEAVES * SLOTS, 128)
        taken = lax.fori_loop(0, CHUNKS, take, jnp.zeros(shape, F32), unroll=4)
        taken = jnp.where(iota(shape, 1) == WHICH, which, taken)
        taken = jnp.where(iota(shape, 1) == FULL, full, taken).astype(BF)
        for b in range(LEAVES):
            slots[b] = taken[b * SLOTS : (b + 1) * SLOTS]
        came[0] = slots[0]
        each(LEAVES, lambda k: send_slots(k).start())

    def place_points():
        each(LEAVES, lambda k: send_slots(k).wait_recv())
        got = jnp.concatenate([came[b] for b in range(LEAVES)], 0).astype(F32)
        chosen = got[:, WHICH : WHICH + 1] == iota((LEAVES * SLOTS, RANK), 1).astype(F32)
        picked = dot(got.T[:F].astype(BF), chosen.astype(F32).astype(BF))
        bad[...] = jnp.broadcast_to(jnp.max(got[:, FULL : FULL + 1], 0, keepdims=True), (8, 128))
        sk[0] = picked.astype(BF)
        each(COLS, lambda k: send_skel(k).start())

    def work(j, _):
        pl.when(j == 2)(take_slots)
        pl.when(j == 5)(place_points)
        return give(j, 0)

    lax.fori_loop(0, LEAVES // 2, work, 0)
    rx[0] = feat[0]
    ra[0] = aux[0]

    for copy in smalls:
        copy.wait()
    spare[...] = jnp.ones((8, 128), F32)
    spare[0:1, 0:F] = scales[...]
    inverse = 1.0 / to_column(spare[0:1, :])[:F]
    scale = inverse * inverse * LOG2E
    scale2 = across(scale, RANK)
    scale4 = across(scale, PER)

    index[...] = top_index(parent, top, leaf // 4)
    index2 = across(index[...], 2 * RANK)
    number = iota((RANK, 2 * RANK), 1)
    base = (quarter * RANK).astype(F32)
    other = (sibling * RANK).astype(F32)
    chosen = index2[:, :RANK] == iota((RANK, RANK), 1).astype(F32) + base
    rows[...] = chosen.astype(F32).astype(BF)
    lanes = number.astype(F32) + jnp.where(number < RANK, base, other - RANK)
    columns[...] = (index2 == lanes).astype(F32).astype(BF)

    def norms(k):
        side[k] = point_side(rx[k].astype(F32), scale4)

    def receive(k):
        send_aux(k).wait_recv()
        send_feat(k).wait_recv()

    def early_norms(n, _):
        k = turn_of(n)
        pl.when(n > 0)(lambda: receive(k))
        norms(k)
        return 0

    lax.fori_loop(0, LEAVES // 2, early_norms, 0)

    picked = sk[0].astype(F32)

    def add_skel(k, total):
        send_skel(k).wait_recv()
        return total + sk[k].astype(F32)

    picked = lax.fori_loop(1, COLS, add_skel, picked)
    mine[...] = picked.astype(BF)
    sk4[quarter] = picked.astype(BF)

    def send_four(k):
        return remote(mine, sk4.at[quarter], (s_4, r_4), k, cousin(k))

    each(4, lambda k: send_four(k).start())
    left[0:RANK, :] = skel_side(picked, scale2)

    def block_of(k, out, begin):
        p = rx[k]
        fill = jnp.zeros((256 - 3 * F - 16, PER), BF)
        right = jnp.concatenate([p, p, p, side[k], fill], 0)
        power = dot(left[begin : begin + RANK, :], right)
        out[0:RANK, :] = jnp.exp2(jnp.minimum(power, 0.0)).astype(BF)

    def own_of(k, out):
        block_of(k, out, 0)
        value = ra[k]
        value = jnp.concatenate([value[r : r + 1] for r in range(4)], 1)
        out[RANK:, :] = jnp.broadcast_to(value, (16, PER)).astype(BF)

    def gram_of(u):
        gram[...] += dot_nt(u[...], u[0:RANK, :])

    def couple_of(v, u):
        couple[...] += dot_nt(v[...], u[0:RANK, :])

    last = LEAVES // 2 - 1

    def own_two(j, _):
        k, l = turn_of(2 * j), turn_of(2 * j + 1)
        @pl.when(j >= LEAVES // 4)
        def late():
            receive(k)
            receive(l)
            norms(k)
            norms(l)

        own_of(k, even.at[j])
        gram_of(odd.at[rem(j + last, last + 1)])
        own_of(l, odd.at[j])
        gram_of(even.at[j])
        return 0

    def other_two(j, _):
        block_of(turn_of(2 * j), other_even, RANK)
        couple_of(other_odd, odd.at[rem(j + last, last + 1)])
        block_of(turn_of(2 * j + 1), other_odd, RANK)
        couple_of(other_even, even.at[j])
        return 0

    gram[...] = jnp.zeros_like(gram)
    couple[...] = jnp.zeros_like(couple)
    odd[last] = jnp.zeros((RANK + 16, PER), BF)
    other_odd[...] = jnp.zeros_like(other_odd)
    def send_gram(k):
        return remote(pg.at[(col + k) % COLS], gr.at[k], (s_p, r_p), k, beside(k))

    def send_couple(k):
        return remote(pc.at[(col + k) % COLS], cr.at[k], (s_c, r_c), k, beside(k))

    def send_chosen(k):
        return remote(pt.at[(col + k) % COLS], qr.at[k], (s_o, r_o), k, beside(k))

    def send_rhs(k):
        return remote(rs, rr.at[k], (s_r, r_r), k, beside(k))

    def sibling_side():
        each(4, lambda k: remote(mine, sk4.at[(quarter + 4 - k) % 4], (s_4, r_4), k, cousin(k)).wait_recv())
        left[RANK:, :] = skel_side(sk4[sibling].astype(F32), scale2)

    def give_gram():
        gram_of(odd.at[last])
        part = gram[0:RANK, :].astype(BF)
        for k in range(COLS):
            pg[k] = part[k * SLAB : (k + 1) * SLAB]
        each(COLS, lambda k: send_gram(k).start())

    def half(h, _):
        pairs = LEAVES // 4
        lax.fori_loop(pairs * h, pairs * (h + 1), own_two, 0)
        pl.when(h == 0)(sibling_side)
        pl.when(h == 1)(give_gram)
        lax.fori_loop(pairs * h, pairs * (h + 1), other_two, 0)
        return 0

    lax.fori_loop(0, 2, half, 0)
    couple_of(other_odd, odd.at[last])

    rhs = gram[RANK : RANK + 1, :]
    rhs = jnp.sum(dot_nt(stack16(split3(rhs), RANK), rows[...]), 0, keepdims=True)
    rs[...] = jnp.zeros_like(rs)
    rs[0:1, :] = rhs[:, :128]
    rs[1:2, :] = rhs[:, 128:]
    rs[2:3, :] = bad[0:1, :]
    part = dot(rows[...], gram[0:RANK, :].astype(BF)).astype(BF)
    chosen = dot_nt(part, columns[:, 0:RANK])
    part = dot_nt(rows[...], couple[...].astype(BF)).astype(BF)
    chosen = chosen + dot_nt(part, columns[:, RANK:])
    chosen = chosen.astype(BF)
    for k in range(COLS):
        pt[k] = chosen[k * SLAB : (k + 1) * SLAB]
    each(COLS, lambda k: send_chosen(k).start())
    each(COLS, lambda k: send_rhs(k).start())
    part = couple[...].T.astype(BF)
    for k in range(COLS):
        pc[k] = part[k * SLAB : (k + 1) * SLAB]
    each(COLS, lambda k: send_couple(k).start())

    chosen = across(index[...], 4 * RANK) == iota((RANK, 4 * RANK), 1).astype(F32)
    fours[...] = chosen.astype(F32).astype(BF)
    whole = jnp.concatenate([sk4[k] for k in range(4)], 1)
    points = dot_nt(whole, fours[...])
    fill = jnp.zeros((256 - 3 * F - 16, RANK), BF)
    points_b = points.astype(BF)
    right = jnp.concatenate([points_b, points_b, points_b, point_side(points, scale2), fill], 0)
    value = jnp.exp2(jnp.minimum(dot(skel_side(points, scale2), right), 0.0))
    crossing = (across(index[...], RANK) >= 2.0 * RANK) != (index[...].T[0:1, :] >= 2.0 * RANK)
    square = iota((RANK, RANK), 0) == iota((RANK, RANK), 1)
    tops[...] = jnp.where(crossing, value, 0.0) + jnp.where(square, ridge[...], 0.0)

    place = jnp.concatenate([held[(LEAVES - b) % LEAVES] for b in range(LEAVES)], 0)
    home = place % ROWS // PACKET
    largest = jnp.zeros((OWNERS, 1), F32)
    for b in range(LEAVES):
        held_here = (iota((OWNERS, RANK), 0) == home[b : b + 1]).astype(F32)
        largest = jnp.maximum(largest, jnp.sum(held_here, 1, keepdims=True))

    def finish(sends):
        return lambda k: [send(k).wait_send() for send in sends]

    each(LEAVES, finish((send_pivots, send_slots, send_aux, send_feat)))
    each(COLS, finish((send_skel, send_gram, send_rhs)))
    each(4, finish((send_four,)))

    def add_chosen(k, totals):
        send_chosen(k).wait_recv()
        send_rhs(k).wait_recv()
        return totals[0] + qr[k].astype(F32), totals[1] + rr[k]

    chosen, rhs = lax.fori_loop(1, COLS, add_chosen, (pt[col].astype(F32), rs[...]))
    over = jnp.maximum(jnp.max(rhs[2:3, :]), jnp.max(largest) - SLOTS)
    flag[0] = (over > 0.0).astype(jnp.int32)
    chosen = chosen * (1.0 / NODE)
    t4[0] = chosen.astype(BF)
    r4[0] = rhs * (1.0 / NODE)

    def send_top(k):
        return remote(t4.at[0], t4.at[k], (s_t, r_t), k, cousin(k))

    def send_top_rhs(k):
        return remote(r4.at[0], r4.at[k], (s_q, r_q), k, cousin(k))

    each(4, lambda k: send_top(k).start())
    each(4, lambda k: send_top_rhs(k).start())

    def add_gram(k, total):
        send_gram(k).wait_recv()
        return total + gr[k].astype(F32)

    def add_couple(k, total):
        send_couple(k).wait_recv()
        return total + cr[k].astype(F32)

    total = lax.fori_loop(1, COLS, add_gram, pg[col].astype(F32))
    diagonal = iota((SLAB, RANK), 0) + col * SLAB == iota((SLAB, RANK), 1)
    out_share[0, :, 0:RANK] = total * (1.0 / NODE) + jnp.where(diagonal, ridge[...], 0.0)
    total = lax.fori_loop(1, COLS, add_couple, pc[col].astype(F32))
    out_share[0, :, RANK:] = total * (1.0 / NODE)
    result = chosen + tops[pl.ds(pl.multiple_of(col * SLAB, SLAB), SLAB), :]

    def add_top(k, totals):
        send_top(k).wait_recv()
        send_top_rhs(k).wait_recv()
        return totals[0] + t4[k].astype(F32), totals[1] + r4[k]

    result, rhs = lax.fori_loop(1, 4, add_top, (result, r4[0]))
    out_top[0] = result
    out_rhs[...] = jnp.concatenate([rhs[0:1], rhs[1:2]], 1)

    each(COLS, finish((send_couple, send_chosen)))
    each(4, finish((send_top, send_top_rhs)))


SHAPES = ((1, SLAB, 2 * RANK), (1, SLAB, RANK), (1, RANK))


def exchange(merged, ridge, *smalls):
    return pl.pallas_call(
        exchange_kernel,
        out_shape=tuple(pltpu.VMEM(shape, F32) for shape in SHAPES),
        in_specs=[VMEM, VMEM] + [ANYWHERE] * 4,
        out_specs=[VMEM] * 3,
        scratch_shapes=[
            pltpu.VMEM((1, RANK), jnp.int32),
            pltpu.VMEM((1, F), F32),
            pltpu.VMEM((8, RANK), jnp.int32),
            pltpu.VMEM((4, RANK), jnp.int32),
            pltpu.VMEM((8, 128), F32),
            pltpu.VMEM((LEAVES, F, PER), BF),
            pltpu.VMEM((LEAVES, 8, 128), F32),
            pltpu.VMEM((LEAVES, F, PER), BF),
            pltpu.VMEM((LEAVES, 8, 128), F32),
            pltpu.VMEM((LEAVES, RANK, PER), BF),
            pltpu.VMEM((LEAVES, 16, PER), BF),
            pltpu.VMEM((COLS, F, RANK), BF),
            pltpu.VMEM((F, RANK), BF),
            pltpu.VMEM((4, F, RANK), BF),
            pltpu.VMEM((2 * RANK, 256), BF),
            pltpu.VMEM((LEAVES // 2, RANK + 16, PER), BF),
            pltpu.VMEM((LEAVES // 2, RANK + 16, PER), BF),
            pltpu.VMEM((RANK, PER), BF),
            pltpu.VMEM((RANK, PER), BF),
            pltpu.VMEM((RANK + 16, RANK), F32),
            pltpu.VMEM((RANK, RANK), F32),
            pltpu.VMEM((RANK, RANK), BF),
            pltpu.VMEM((RANK, 2 * RANK), BF),
            pltpu.VMEM((RANK, 4 * RANK), BF),
            pltpu.VMEM((RANK, 128), F32),
            pltpu.VMEM((RANK, RANK), F32),
            pltpu.VMEM((COLS, SLAB, RANK), BF),
            pltpu.VMEM((COLS, SLAB, RANK), BF),
            pltpu.VMEM((COLS, SLAB, RANK), BF),
            pltpu.VMEM((COLS, SLAB, RANK), BF),
            pltpu.VMEM((COLS, SLAB, RANK), BF),
            pltpu.VMEM((COLS, SLAB, RANK), BF),
            pltpu.VMEM((8, 128), F32),
            pltpu.VMEM((COLS, 8, 128), F32),
            pltpu.VMEM((4, SLAB, RANK), BF),
            pltpu.VMEM((4, 8, 128), F32),
            *dma(LEAVES),
            *dma(LEAVES),
            *dma(COLS),
            *dma(4),
            *dma(COLS),
            *dma(COLS),
            *dma(COLS),
            *dma(COLS),
            *dma(4),
            *dma(4),
            pltpu.SemaphoreType.DMA((5,)),
        ],
        compiler_params=params(0, 40),
        name="exchange",
    )(merged, ridge, *in_hbm(*smalls))


def stream(samples, pivots, ridge, *smalls):
    return pl.pallas_call(
        stream_kernel,
        out_shape=(
            *(pltpu.VMEM(shape, F32) for shape in SHAPES),
            jax.ShapeDtypeStruct((1,), jnp.int32),
        ),
        in_specs=[ANYWHERE, VMEM, VMEM, VMEM, VMEM] + [ANYWHERE] * 3,
        out_specs=[VMEM] * 3 + [pl.BlockSpec(memory_space=pltpu.SMEM)],
        scratch_shapes=[
            pltpu.VMEM((F, ROWS), BF),
            pltpu.VMEM((8, 128), F32),
            pltpu.VMEM((ROWS // 128, 128), F32),
            pltpu.VMEM((CHUNKS, 8, CHUNK), F32),
            pltpu.VMEM((LEAVES, 128), F32),
            pltpu.VMEM((LEAVES, 128), F32),
            pltpu.VMEM((ROWS + TILE, WIDE), F32),
            pltpu.VMEM((LEAVES // AT_ONCE, 16, 128), jnp.int32),
            pltpu.SMEM((LEAVES // AT_ONCE, 16, 128), jnp.int32),
            pltpu.VMEM((LEAVES, 1, RANK), jnp.int32),
            pltpu.VMEM((LEAVES, SLOTS, 128), BF),
            pltpu.VMEM((LEAVES, SLOTS, 128), BF),
            pltpu.VMEM((1, F), F32),
            pltpu.VMEM((8, RANK), jnp.int32),
            pltpu.VMEM((4, RANK), jnp.int32),
            pltpu.VMEM((8, 128), F32),
            pltpu.VMEM((LEAVES, F, PER), BF),
            pltpu.VMEM((LEAVES, 8, 128), F32),
            pltpu.VMEM((LEAVES, F, PER), BF),
            pltpu.VMEM((LEAVES, 8, 128), F32),
            pltpu.VMEM((LEAVES, 16, PER), BF),
            pltpu.VMEM((COLS, F, RANK), BF),
            pltpu.VMEM((F, RANK), BF),
            pltpu.VMEM((4, F, RANK), BF),
            pltpu.VMEM((2 * RANK, 256), BF),
            pltpu.VMEM((LEAVES // 2, RANK + 16, PER), BF),
            pltpu.VMEM((LEAVES // 2, RANK + 16, PER), BF),
            pltpu.VMEM((RANK, PER), BF),
            pltpu.VMEM((RANK, PER), BF),
            pltpu.VMEM((RANK + 16, RANK), F32),
            pltpu.VMEM((RANK, RANK), F32),
            pltpu.VMEM((RANK, RANK), BF),
            pltpu.VMEM((RANK, 2 * RANK), BF),
            pltpu.VMEM((RANK, 4 * RANK), BF),
            pltpu.VMEM((RANK, 128), F32),
            pltpu.VMEM((RANK, RANK), F32),
            pltpu.VMEM((COLS, SLAB, RANK), BF),
            pltpu.VMEM((COLS, SLAB, RANK), BF),
            pltpu.VMEM((COLS, SLAB, RANK), BF),
            pltpu.VMEM((COLS, SLAB, RANK), BF),
            pltpu.VMEM((COLS, SLAB, RANK), BF),
            pltpu.VMEM((COLS, SLAB, RANK), BF),
            pltpu.VMEM((8, 128), F32),
            pltpu.VMEM((COLS, 8, 128), F32),
            pltpu.VMEM((4, SLAB, RANK), BF),
            pltpu.VMEM((4, 8, 128), F32),
            *dma(LEAVES),
            *dma(LEAVES),
            *dma(LEAVES),
            *dma(LEAVES),
            *dma(COLS),
            *dma(4),
            *dma(COLS),
            *dma(COLS),
            *dma(COLS),
            *dma(COLS),
            *dma(4),
            *dma(4),
            pltpu.SemaphoreType.DMA((5,)),
        ],
        compiler_params=params(1, 40),
        name="stream",
    )(*in_hbm(*samples, pivots), ridge, *in_hbm(*smalls))


def emit_kernel(*refs):
    ins, outs, sem = refs[:3], refs[3:6], refs[6]
    copies = [pltpu.make_async_copy(a, b, sem.at[k]) for k, (a, b) in enumerate(zip(ins, outs))]
    for copy in copies:
        copy.start()
    for copy in copies:
        copy.wait()


def emit(results):
    return pl.pallas_call(
        emit_kernel,
        out_shape=tuple(jax.ShapeDtypeStruct(shape, F32) for shape in SHAPES),
        in_specs=[VMEM] * 3,
        out_specs=[ANYWHERE] * 3,
        scratch_shapes=[pltpu.SemaphoreType.DMA((3,))],
        compiler_params=params(),
        name="emit",
    )(*results)


def local(features, targets, owner, length_scales, ridge, leaf_pivots, parent_pivots, top_pivots):
    samples = (features, targets.reshape(ROWS // 128, 128), owner.reshape(ROWS // 128, 128))
    ridge = ridge.reshape(1, 1)
    smalls = (length_scales.reshape(1, F), parent_pivots, top_pivots)
    *results, flag = stream(samples, leaf_pivots, ridge, *smalls)

    def again():
        return tuple(emit(exchange(pack(*samples), ridge, leaf_pivots, *smalls)))

    return lax.switch(flag[0], [lambda: tuple(emit(results)), again])


def solution(mesh):
    return jax.shard_map(
        local,
        mesh=mesh,
        in_specs=(
            P(None, ("leaf", "col")),
            P(("leaf", "col")),
            P(("leaf", "col")),
            P(),
            P(),
            P("leaf", None),
            P(),
            P(),
        ),
        out_specs=(P("leaf", "col", None), P("leaf", "col", None), P("leaf", None)),
        check_vma=False,
    )
```

```python
import functools
import math

import jax
import jax.numpy as jnp
from jax import lax
from jax.experimental import pallas as pl
from jax.experimental.pallas import tpu as pltpu
from jax.sharding import PartitionSpec as P

F = 48
RANK = 256
ROWS = 8192
LEAVES = 16
COLS = 8
OWNERS = 128
PACKET = 64
PER = ROWS // LEAVES
CHUNK = 256
CHUNKS = ROWS // CHUNK
WINDOW = 40
REGION = PER + WINDOW
TILE = 32
TILES = PER // TILE
PIECES = 6
AT_ONCE = 128 // TILES
SLOTS = 16
WHICH = 50
FULL = 51
WIDE = 64
SLAB = RANK // COLS
NODE = ROWS * COLS
LOG2E = math.log2(math.e)
BF = jnp.bfloat16
F32 = jnp.float32
NT = (((1,), (1,)), ((), ()))
MESH = pl.DeviceIdType.MESH


def dma(count):
    return [pltpu.SemaphoreType.DMA((count,))] * 2


def params(number=None, limit=24):
    if number is None:
        return pltpu.CompilerParams(vmem_limit_bytes=limit * 2**20)
    return pltpu.CompilerParams(
        collective_id=number, has_side_effects=True, vmem_limit_bytes=limit * 2**20
    )


ANYWHERE = pl.BlockSpec(memory_space=pl.ANY)
VMEM = pl.BlockSpec(memory_space=pltpu.VMEM)


def iota(shape, axis):
    return lax.broadcasted_iota(jnp.int32, shape, axis)


def dot(a, b):
    return jnp.dot(a, b, preferred_element_type=F32)


def dot_nt(a, b):
    return lax.dot_general(a, b, NT, preferred_element_type=F32)


def row_pair(two):
    return jnp.concatenate([two[0:1], two[1:2]], 1)


def pack_kernel(
    feat_hbm, target, owner, zbuf, feat, goals, rows, ybuf, table, scal, sem, feat_sem
):
    bring = pltpu.make_async_copy(feat_hbm, feat, feat_sem)
    bring.start()
    goals[...] = target[...].astype(F32)
    before = (iota((CHUNK, CHUNK), 0) < iota((CHUNK, CHUNK), 1)).astype(F32).astype(BF)
    weights = jnp.concatenate([before, jnp.ones((CHUNK, 128), BF)], 1)
    lane = iota((LEAVES, 128), 1)

    def ranks(t, carry):
        seen, seen_leaf, most = carry
        own = row_pair(owner[pl.ds(2 * t, 2), :])
        leaf = own // 8
        is_own = iota((OWNERS, CHUNK), 0) == own
        is_leaf = iota((LEAVES, CHUNK), 0) == leaf
        is_after = iota((LEAVES, CHUNK), 0) > leaf
        marks = jnp.concatenate(
            [m.astype(F32).astype(BF) for m in (is_own, is_leaf, is_after)], 0
        )
        sums = dot(marks, weights)
        counts = sums[:OWNERS, CHUNK:]
        leaf_counts = sums[OWNERS : OWNERS + LEAVES, CHUNK:]
        base = sums[OWNERS + LEAVES :, CHUNK:]
        prior = sums[:OWNERS, :CHUNK] + jnp.concatenate([seen, seen], 1)
        rank = jnp.sum(jnp.where(is_own, prior, 0.0), 0, keepdims=True)
        place = sums[OWNERS : OWNERS + LEAVES, :CHUNK] + jnp.concatenate([base, base], 1)
        place = jnp.sum(jnp.where(is_leaf, place, 0.0), 0, keepdims=True)
        tag = (own % 8).astype(F32) * PACKET + rank - (PER // 2)
        rows[t, 0:1, :] = place
        rows[t, 1:2, :] = row_pair(goals[pl.ds(2 * t, 2), :])
        rows[t, 2:3, :] = tag
        here = lane == t
        table[0:LEAVES, :] = jnp.where(here, seen_leaf.astype(jnp.int32), table[0:LEAVES, :])
        table[LEAVES : 2 * LEAVES, :] = jnp.where(
            here, base.astype(jnp.int32), table[LEAVES : 2 * LEAVES, :]
        )
        return seen + counts, seen_leaf + leaf_counts, jnp.maximum(most, leaf_counts)

    table[0:LEAVES, :] = jnp.full((LEAVES, 128), PER, jnp.int32)
    zero = jnp.zeros((LEAVES, 128), F32)
    _, _, most = lax.fori_loop(
        0, CHUNKS, ranks, (jnp.zeros((OWNERS, 128), F32), zero, zero), unroll=16
    )
    most = jnp.broadcast_to(jnp.max(most, 0, keepdims=True), (8, 128))
    table[2 * LEAVES :, :] = most.astype(jnp.int32)
    move = pltpu.make_async_copy(table, scal, sem)
    move.start()
    bring.wait()

    def sort(t, _):
        start = pl.multiple_of(t * CHUNK, CHUNK)
        row = iota((16, CHUNK), 0)
        place, goal, tag = rows[t, 0:1, :], rows[t, 1:2, :], rows[t, 2:3, :]
        extra = jnp.where(row == 0, goal, jnp.where(row == 1, tag, 0.0)).astype(BF)
        joined = jnp.concatenate([feat[:, pl.ds(start, CHUNK)], extra], 0)
        chosen = (iota((CHUNK, CHUNK), 0) == place.astype(jnp.int32)).astype(F32).astype(BF)
        ybuf[pl.ds(start, CHUNK), :] = dot_nt(chosen, joined)
        return 0

    lax.fori_loop(0, CHUNKS, sort, 0, unroll=8)
    move.wait()
    widest = scal[2 * LEAVES, 0]

    @pl.when(widest <= WINDOW)
    def quick():
        def merge(t, _):
            for i in range(LEAVES):
                source = t * CHUNK + scal[LEAVES + i, t]
                goal = i * REGION + scal[i, t]
                zbuf[pl.ds(goal, WINDOW), :] = ybuf[pl.ds(source, WINDOW), :]
            return 0

        lax.fori_loop(0, CHUNKS, merge, 0, unroll=4)

    @pl.when(widest > WINDOW)
    def slow():
        def merge(index, _):
            t = index // LEAVES
            i = index % LEAVES
            source = t * CHUNK + scal[LEAVES + i, t]
            first = scal[i, t]
            count = scal[i, t + 1] - first

            def part(k, _):
                rows = ybuf[pl.ds(source + 8 * k, 8), :]
                zbuf[pl.ds(i * REGION + first + 8 * k, 8), :] = rows
                return 0

            lax.fori_loop(0, (count + 7) // 8, part, 0)
            return 0

        lax.fori_loop(0, CHUNKS * LEAVES, merge, 0)


def in_hbm(*arrays):
    return [pltpu.with_memory_space_constraint(a, pltpu.HBM) for a in arrays]


def pack(features, targets, owner):
    return pl.pallas_call(
        pack_kernel,
        out_shape=pltpu.VMEM((LEAVES * REGION, WIDE), F32),
        in_specs=[ANYWHERE, VMEM, VMEM],
        out_specs=VMEM,
        scratch_shapes=[
            pltpu.VMEM((F, ROWS), BF),
            pltpu.VMEM((ROWS // 128, 128), F32),
            pltpu.VMEM((CHUNKS, 8, CHUNK), F32),
            pltpu.VMEM((ROWS + WINDOW, WIDE), F32),
            pltpu.VMEM((40, 128), jnp.int32),
            pltpu.SMEM((40, 128), jnp.int32),
            pltpu.SemaphoreType.DMA,
            pltpu.SemaphoreType.DMA,
        ],
        compiler_params=params(),
        name="pack",
    )(*in_hbm(features, targets, owner))


def split3(x):
    high = x.astype(BF)
    rest = x - high.astype(F32)
    mid = rest.astype(BF)
    return high, mid, (rest - mid.astype(F32)).astype(BF)


def stack16(parts, width):
    row = iota((16, width), 0)
    block = jnp.zeros((16, width), F32)
    for k, part in enumerate(parts):
        block = jnp.where(row == k, part if isinstance(part, float) else part.astype(F32), block)
    return block.astype(BF)


def half_norm(points, scale):
    return jnp.sum(points * points * (0.5 * scale), 0, keepdims=True)


def point_side(points, scale):
    high, mid, low = split3(-half_norm(points, scale))
    return stack16([high, mid, low, 1.0, 1.0, 1.0], points.shape[1])


def skel_side(skel, scale):
    width = skel.shape[1]
    high, mid, low = split3(skel * scale)
    extra = stack16([1.0, 1.0, 1.0, *split3(-half_norm(skel, scale))], width)
    parts = [p.astype(F32) for p in (high, mid, low, extra)]
    fill = jnp.zeros((256 - 3 * F - 16, width), F32)
    return jnp.concatenate([*parts, fill], 0).T.astype(BF)


def select_row(table, row):
    hit = iota(table.shape, 0) == row
    return jnp.sum(jnp.where(hit, table.astype(F32), 0.0), 0, keepdims=True)


def to_column(row):
    return jnp.broadcast_to(row, (128, row.shape[1])).T


def across(column, width):
    return jnp.concatenate([column] * (width // 128), 1)


def place_of(leaf, col):
    return dict(device_id=(leaf, col), device_id_type=MESH)


def mate(k):
    leaf, col = lax.axis_index("leaf"), lax.axis_index("col")
    to = (leaf + k) % LEAVES
    cross = (to // 8 + leaf // 8) % 2
    return place_of(to, col + cross * (1 - 2 * (col % 2)))


def beside(k):
    leaf, col = lax.axis_index("leaf"), lax.axis_index("col")
    return place_of(leaf, (col + k) % COLS)


def cousin(k):
    leaf, col = lax.axis_index("leaf"), lax.axis_index("col")
    return place_of(leaf - leaf % 4 + (leaf + k) % 4, col)


def each(count, step, unroll=1):
    lax.fori_loop(1, count, lambda k, _: (step(k), 0)[1], 0, unroll=unroll)


def rem(a, b):
    return lax.rem(jnp.int32(a), jnp.int32(b))


def turn_of(n):
    n = jnp.int32(n)
    odd = lax.rem(n, jnp.int32(2))
    half = lax.div(n + odd, jnp.int32(2))
    return lax.rem(odd * half + (1 - odd) * (LEAVES - half), jnp.int32(LEAVES))


def remote(src, dst, sems, k, peer):
    return pltpu.make_async_remote_copy(src, dst, sems[0].at[k], sems[1].at[k], **peer)


def top_index(parent, top, group):
    top_row = select_row(top[...], group)
    below = jnp.concatenate([select_row(parent[...], 2 * group + r) for r in range(2)], 1)
    number = iota((RANK, 2 * RANK), 1)
    below = below + jnp.where(iota((1, 2 * RANK), 1) >= RANK, 2.0 * RANK, 0.0)
    hit = across(to_column(top_row), 2 * RANK) == number.astype(F32)
    index = jnp.sum(jnp.where(hit, below, 0.0), 1, keepdims=True)
    return jnp.broadcast_to(index, (RANK, 128))


def exchange_kernel(
    merged, ridge, pivots_hbm, scales_hbm, parent_hbm, top_hbm, out_share, out_top, out_rhs,
    pivots, scales, parent, top, spare, feat, aux, rx, ra, hot, side, sk, mine, sk4, left,
    even, odd, other_even, other_odd, gram, couple, rows, columns, fours, index, tops,
    pg, gr, pc, cr, pt, qr, rs, rr, t4, r4,
    s_f, r_f, s_a, r_a, s_k, r_k, s_4, r_4, s_p, r_p, s_c, r_c, s_o, r_o, s_r, r_r, s_t, r_t, s_q, r_q, local,
):
    leaf = lax.axis_index("leaf")
    col = lax.axis_index("col")
    quarter = leaf % 4
    sibling = quarter + 1 - 2 * (quarter % 2)
    barrier = pltpu.get_barrier_semaphore()
    each(LEAVES, lambda k: pl.semaphore_signal(barrier, inc=1, **mate(k)))
    each(COLS, lambda k: pl.semaphore_signal(barrier, inc=1, **beside(k)))
    smalls = [
        pltpu.make_async_copy(a, b, local.at[k])
        for k, (a, b) in enumerate(
            [(pivots_hbm, pivots), (scales_hbm, scales), (parent_hbm, parent), (top_hbm, top)]
        )
    ]
    for copy in smalls:
        copy.start()

    eye = (iota((WIDE, WIDE), 0) == iota((WIDE, WIDE), 1)).astype(F32).astype(BF)

    def turn(k):
        start = pl.multiple_of((leaf + k) % LEAVES * REGION, 8)
        turned = dot_nt(eye, merged[pl.ds(start, PER), :].astype(BF))
        feat[k] = turned[:F].astype(BF)
        aux[k] = jnp.concatenate(
            [turned[F + r : F + r + 1, 128 * c : 128 * c + 128] for r in range(2) for c in range(4)], 0
        )

    def send_feat(k):
        return remote(feat.at[k], rx.at[k], (s_f, r_f), k, mate(k))

    def send_aux(k):
        return remote(aux.at[k], ra.at[k], (s_a, r_a), k, mate(k))

    def four(j, _):
        steps = [turn_of(lax.rem(4 * j + r, LEAVES)) for r in range(1, 5)]
        for k in steps:
            turn(k)
        pl.when(j == 0)(lambda: pl.semaphore_wait(barrier, LEAVES + COLS - 2))
        for send in (send_aux, send_feat):
            for k in steps[:3]:
                send(k).start()
            pl.when(j < 3)(lambda: send(steps[3]).start())
        return 0

    lax.fori_loop(0, LEAVES // 4, four, 0)
    rx[0] = feat[0]
    ra[0] = aux[0]

    for copy in smalls:
        copy.wait()
    spare[...] = jnp.ones((8, 128), F32)
    spare[0:1, 0:F] = scales[...]
    inverse = 1.0 / to_column(spare[0:1, :])[:F]
    scale = inverse * inverse * LOG2E
    scale2 = across(scale, RANK)
    scale4 = across(scale, PER)

    place = pivots[...]
    within = place % ROWS
    block = within // PACKET
    key = (block // COLS) * PER + (place // ROWS) * PACKET + within % PACKET
    holder = block % COLS
    crossed = (block // COLS) // 8 != leaf // 8
    holder = jnp.where(crossed, holder + 1 - 2 * (holder % 2), holder)
    key = jnp.where(holder == col, key, -PER)
    key = across(to_column(key.astype(F32)), PER)

    def mark(k):
        source = (leaf + LEAVES - k) % LEAVES
        tags = ra[k, 4:8, :]
        tag = jnp.concatenate([tags[r : r + 1] for r in range(4)], 1)
        wanted = tag + (PER // 2 + source * PER).astype(F32)
        hot[k] = (key == wanted).astype(F32).astype(BF)

    def mark_next(n, _):
        k = turn_of(n)
        pl.when(n > 0)(lambda: send_aux(k).wait_recv())
        mark(k)
        return 0

    lax.fori_loop(0, LEAVES, mark_next, 0)

    index[...] = top_index(parent, top, leaf // 4)
    index2 = across(index[...], 2 * RANK)
    number = iota((RANK, 2 * RANK), 1)
    base = (quarter * RANK).astype(F32)
    other = (sibling * RANK).astype(F32)
    chosen = index2[:, :RANK] == iota((RANK, RANK), 1).astype(F32) + base
    rows[...] = chosen.astype(F32).astype(BF)
    lanes = number.astype(F32) + jnp.where(number < RANK, base, other - RANK)
    columns[...] = (index2 == lanes).astype(F32).astype(BF)
    chosen = across(index[...], 4 * RANK) == iota((RANK, 4 * RANK), 1).astype(F32)
    fours[...] = chosen.astype(F32).astype(BF)

    def pick(j, total):
        steps = [turn_of(4 * j + r) for r in range(4)]
        pl.when(j > 0)(lambda: send_feat(steps[0]).wait_recv())
        for k in steps[1:]:
            send_feat(k).wait_recv()
        for k in steps:
            total = total + dot_nt(hot[k], rx[k])
        return total

    picked = lax.fori_loop(0, LEAVES // 4, pick, jnp.zeros((RANK, F), F32))
    picked = jnp.concatenate([picked, jnp.zeros((RANK, 128 - F), F32)], 1).T[:F]
    sk[0] = picked.astype(BF)

    def send_skel(k):
        return remote(sk.at[0], sk.at[k], (s_k, r_k), k, beside(k))

    each(COLS, lambda k: send_skel(k).start())

    def norms(k, _):
        side[k] = point_side(rx[k].astype(F32), scale4)
        return 0

    lax.fori_loop(0, LEAVES, norms, 0)

    def add_skel(k, total):
        send_skel(k).wait_recv()
        return total + sk[k].astype(F32)

    picked = lax.fori_loop(1, COLS, add_skel, picked)
    mine[...] = picked.astype(BF)
    sk4[quarter] = picked.astype(BF)

    def send_four(k):
        return remote(mine, sk4.at[quarter], (s_4, r_4), k, cousin(k))

    each(4, lambda k: send_four(k).start())
    left[0:RANK, :] = skel_side(picked, scale2)

    def block_of(k, out, begin):
        p = rx[k]
        fill = jnp.zeros((256 - 3 * F - 16, PER), BF)
        right = jnp.concatenate([p, p, p, side[k], fill], 0)
        power = dot(left[begin : begin + RANK, :], right)
        out[0:RANK, :] = jnp.exp2(jnp.minimum(power, 0.0)).astype(BF)

    def own_of(k, out):
        block_of(k, out, 0)
        value = jnp.concatenate([ra[k, r : r + 1, :] for r in range(4)], 1)
        out[RANK:, :] = jnp.broadcast_to(value, (16, PER)).astype(BF)

    def gram_of(u):
        gram[...] += dot_nt(u[...], u[0:RANK, :])

    def couple_of(v, u):
        couple[...] += dot_nt(v[...], u[0:RANK, :])

    last = LEAVES // 2 - 1

    def own_two(j, _):
        own_of(2 * j, even.at[j])
        gram_of(odd.at[(j + last) % (last + 1)])
        own_of(2 * j + 1, odd.at[j])
        gram_of(even.at[j])
        return 0

    def other_two(j, _):
        block_of(2 * j, other_even, RANK)
        couple_of(other_odd, odd.at[(j + last) % (last + 1)])
        block_of(2 * j + 1, other_odd, RANK)
        couple_of(other_even, even.at[j])
        return 0

    gram[...] = jnp.zeros_like(gram)
    couple[...] = jnp.zeros_like(couple)
    odd[last] = jnp.zeros((RANK + 16, PER), BF)
    other_odd[...] = jnp.zeros_like(other_odd)
    lax.fori_loop(0, last + 1, own_two, 0)
    gram_of(odd.at[last])

    def send_gram(k):
        return remote(pg.at[(col + k) % COLS], gr.at[k], (s_p, r_p), k, beside(k))

    def send_couple(k):
        return remote(pc.at[(col + k) % COLS], cr.at[k], (s_c, r_c), k, beside(k))

    def send_chosen(k):
        return remote(pt.at[(col + k) % COLS], qr.at[k], (s_o, r_o), k, beside(k))

    def send_rhs(k):
        return remote(rs, rr.at[k], (s_r, r_r), k, beside(k))

    part = gram[0:RANK, :].astype(BF)
    for k in range(COLS):
        pg[k] = part[k * SLAB : (k + 1) * SLAB]
    rhs = gram[RANK : RANK + 1, :]
    rhs = jnp.sum(dot_nt(stack16(split3(rhs), RANK), rows[...]), 0, keepdims=True)
    rs[...] = jnp.zeros_like(rs)
    rs[0:1, :] = rhs[:, :128]
    rs[1:2, :] = rhs[:, 128:]
    each(COLS, lambda k: send_gram(k).start())
    each(COLS, lambda k: send_rhs(k).start())
    tops[...] = dot_nt(dot(rows[...], part).astype(BF), columns[:, 0:RANK])

    each(4, lambda k: remote(mine, sk4.at[(quarter + 4 - k) % 4], (s_4, r_4), k, cousin(k)).wait_recv())
    left[RANK:, :] = skel_side(sk4[sibling].astype(F32), scale2)
    lax.fori_loop(0, last + 1, other_two, 0)
    couple_of(other_odd, odd.at[last])

    part = couple[...].astype(BF)
    chosen = dot_nt(dot_nt(rows[...], part).astype(BF), columns[:, RANK:]) + tops[...]
    chosen = chosen.astype(BF)
    for k in range(COLS):
        pt[k] = chosen[k * SLAB : (k + 1) * SLAB]
    each(COLS, lambda k: send_chosen(k).start())
    part = couple[...].T.astype(BF)
    for k in range(COLS):
        pc[k] = part[k * SLAB : (k + 1) * SLAB]
    each(COLS, lambda k: send_couple(k).start())

    whole = jnp.concatenate([sk4[k] for k in range(4)], 1)
    points = dot_nt(whole, fours[...])
    fill = jnp.zeros((256 - 3 * F - 16, RANK), BF)
    points_b = points.astype(BF)
    right = jnp.concatenate([points_b, points_b, points_b, point_side(points, scale2), fill], 0)
    value = jnp.exp2(jnp.minimum(dot(skel_side(points, scale2), right), 0.0))
    crossing = (across(index[...], RANK) >= 2.0 * RANK) != (index[...].T[0:1, :] >= 2.0 * RANK)
    square = iota((RANK, RANK), 0) == iota((RANK, RANK), 1)
    tops[...] = jnp.where(crossing, value, 0.0) + jnp.where(square, ridge[...], 0.0)

    def finish(sends):
        return lambda k: [send(k).wait_send() for send in sends]

    each(LEAVES, finish((send_aux, send_feat)))
    each(COLS, finish((send_skel, send_gram, send_rhs)))
    each(4, finish((send_four,)))

    def add_chosen(k, totals):
        send_chosen(k).wait_recv()
        send_rhs(k).wait_recv()
        return totals[0] + qr[k].astype(F32), totals[1] + rr[k]

    chosen, rhs = lax.fori_loop(1, COLS, add_chosen, (pt[col].astype(F32), rs[...]))
    chosen = chosen * (1.0 / NODE)
    t4[0] = chosen.astype(BF)
    r4[0] = rhs * (1.0 / NODE)

    def send_top(k):
        return remote(t4.at[0], t4.at[k], (s_t, r_t), k, cousin(k))

    def send_top_rhs(k):
        return remote(r4.at[0], r4.at[k], (s_q, r_q), k, cousin(k))

    each(4, lambda k: send_top(k).start())
    each(4, lambda k: send_top_rhs(k).start())

    def add_gram(k, total):
        send_gram(k).wait_recv()
        return total + gr[k].astype(F32)

    def add_couple(k, total):
        send_couple(k).wait_recv()
        return total + cr[k].astype(F32)

    total = lax.fori_loop(1, COLS, add_gram, pg[col].astype(F32))
    diagonal = iota((SLAB, RANK), 0) + col * SLAB == iota((SLAB, RANK), 1)
    out_share[0, :, 0:RANK] = total * (1.0 / NODE) + jnp.where(diagonal, ridge[...], 0.0)
    total = lax.fori_loop(1, COLS, add_couple, pc[col].astype(F32))
    out_share[0, :, RANK:] = total * (1.0 / NODE)
    result = chosen + tops[pl.ds(pl.multiple_of(col * SLAB, SLAB), SLAB), :]

    def add_top(k, totals):
        send_top(k).wait_recv()
        send_top_rhs(k).wait_recv()
        return totals[0] + t4[k].astype(F32), totals[1] + r4[k]

    result, rhs = lax.fori_loop(1, 4, add_top, (result, r4[0]))
    out_top[0] = result
    out_rhs[...] = jnp.concatenate([rhs[0:1], rhs[1:2]], 1)

    each(COLS, finish((send_couple, send_chosen)))
    each(4, finish((send_top, send_top_rhs)))


def stream_kernel(
    feat_hbm, target, owner, pivots, ridge, scales_hbm, parent_hbm, top_hbm,
    out_share, out_top, out_rhs, flag,
    feat_in, bad, goals, ranked, starts, bases, ybuf, table, scal, held, slots, came, scales, parent, top, spare,
    feat, aux, rx, ra, side, sk, mine, sk4, left, even, odd, other_even, other_odd, gram, couple,
    rows, columns, fours, index, tops, pg, gr, pc, cr, pt, qr, rs, rr, t4, r4,
    s_v, r_v, s_s, r_s, s_f, r_f, s_a, r_a, s_k, r_k, s_4, r_4, s_p, r_p, s_c, r_c, s_o, r_o,
    s_r, r_r, s_t, r_t, s_q, r_q, local,
):
    leaf = lax.axis_index("leaf")
    col = lax.axis_index("col")
    quarter = leaf % 4
    sibling = quarter + 1 - 2 * (quarter % 2)
    barrier = pltpu.get_barrier_semaphore()
    each(LEAVES, lambda k: pl.semaphore_signal(barrier, inc=1, **mate(k)))
    each(COLS, lambda k: pl.semaphore_signal(barrier, inc=1, **beside(k)))
    bring = pltpu.make_async_copy(feat_hbm, feat_in, local.at[3])
    bring.start()
    smalls = [
        pltpu.make_async_copy(a, b, local.at[k])
        for k, (a, b) in enumerate([(scales_hbm, scales), (parent_hbm, parent), (top_hbm, top)])
    ]
    for copy in smalls:
        copy.start()

    def send_pivots(k):
        return remote(pivots, held.at[k], (s_v, r_v), k, mate(k))

    def send_slots(k):
        return remote(slots.at[k], came.at[k], (s_s, r_s), k, mate(k))

    def send_feat(k):
        return remote(feat.at[k], rx.at[k], (s_f, r_f), k, mate(k))

    def send_aux(k):
        return remote(aux.at[k], ra.at[k], (s_a, r_a), k, mate(k))

    def send_skel(k):
        return remote(sk.at[0], sk.at[k], (s_k, r_k), k, beside(k))

    goals[...] = target[...].astype(F32)
    before = (iota((CHUNK, CHUNK), 0) < iota((CHUNK, CHUNK), 1)).astype(F32).astype(BF)
    weights = jnp.concatenate([before, jnp.ones((CHUNK, 128), BF)], 1)
    lane = iota((LEAVES, 128), 1)

    def rank(t, carry):
        seen, seen_leaf = carry
        own = row_pair(owner[pl.ds(2 * t, 2), :])
        group = own // 8
        is_own = iota((OWNERS, CHUNK), 0) == own
        is_leaf = iota((LEAVES, CHUNK), 0) == group
        is_after = iota((LEAVES, CHUNK), 0) > group
        marks = jnp.concatenate([m.astype(F32).astype(BF) for m in (is_own, is_leaf, is_after)], 0)
        sums = dot(marks, weights)
        leaf_counts = sums[OWNERS : OWNERS + LEAVES, CHUNK:]
        base = sums[OWNERS + LEAVES :, CHUNK:]
        prior = sums[:OWNERS, :CHUNK] + jnp.concatenate([seen, seen], 1)
        place = jnp.sum(jnp.where(is_own, prior, 0.0), 0, keepdims=True)
        order = sums[OWNERS : OWNERS + LEAVES, :CHUNK] + jnp.concatenate([base, base], 1)
        ranked[t, 0:1, :] = jnp.sum(jnp.where(is_leaf, order, 0.0), 0, keepdims=True)
        ranked[t, 1:2, :] = row_pair(goals[pl.ds(2 * t, 2), :])
        ranked[t, 2:3, :] = own.astype(F32) * PACKET + place
        starts[...] = jnp.where(lane == t, seen_leaf, starts[...])
        bases[...] = jnp.where(lane == t, base, bases[...])
        return seen + sums[:OWNERS, CHUNK:], seen_leaf + leaf_counts

    starts[...] = jnp.zeros_like(starts)
    bases[...] = jnp.zeros_like(bases)
    lax.fori_loop(
        0, CHUNKS, rank, (jnp.zeros((OWNERS, 128), F32), jnp.zeros((LEAVES, 128), F32)), unroll=16
    )

    rest = jnp.zeros((128 - LEAVES, 128), F32)
    start_of = jnp.concatenate([starts[...], rest], 0).T[:CHUNKS]
    base_of = jnp.concatenate([bases[...], rest], 0).T[:CHUNKS]
    high = jnp.where(start_of >= 256.0, 256.0, 0.0)
    columns_of = jnp.concatenate([high, start_of - high, base_of], 0).astype(BF)
    chunk = iota((CHUNKS, 128), 0).astype(F32)
    first = (iota((1, 128), 1) % TILES * TILE).astype(F32)
    full = jnp.zeros((1, 128), F32)
    table[...] = jnp.zeros_like(table)
    for g in range(LEAVES // AT_ONCE):
        one = iota((128, 128), 0) == iota((128, 128), 1) // TILES + g * AT_ONCE
        spread_out = dot(columns_of, one.astype(F32).astype(BF))
        begin = spread_out[:CHUNKS] + spread_out[CHUNKS : 2 * CHUNKS]
        place = spread_out[2 * CHUNKS :] + chunk * CHUNK
        passed = (begin <= first) & (chunk > 0.0)
        current = jnp.sum(jnp.where(passed, 1.0, 0.0), 0, keepdims=True)
        for r in range(PIECES + 1):
            here = chunk == current + r
            row = jnp.sum(jnp.where(here, place, 0.0), 0, keepdims=True)
            edge = jnp.sum(jnp.where(here, begin, 0.0), 0, keepdims=True)
            edge = jnp.where(current + r < CHUNKS, edge, float(PER)) - first
            if r == PIECES:
                full = jnp.maximum(full, jnp.where(edge < TILE, 1.0, 0.0))
                continue
            if r:
                edge = jnp.clip(edge, 0.0, float(TILE))
                table[g, PIECES + r : PIECES + r + 1, :] = edge.astype(jnp.int32)
            row = jnp.clip(jnp.where(current + r < CHUNKS, row - edge, 0.0), 0.0, float(ROWS))
            table[g, r : r + 1, :] = row.astype(jnp.int32)
    full = jnp.broadcast_to(jnp.max(full, 1, keepdims=True), (1, 128))
    tell = pltpu.make_async_copy(table, scal, local.at[4])
    tell.start()

    held[0] = pivots[...]
    pl.semaphore_wait(barrier, LEAVES + COLS - 2)
    each(LEAVES, lambda k: send_pivots(k).start())

    def joined_of(t):
        row = iota((16, CHUNK), 0)
        extra = jnp.where(row == 0, ranked[t, 1:2, :], 0.0).astype(BF)
        return jnp.concatenate([feat_in[:, pl.ds(pl.multiple_of(t * CHUNK, CHUNK), CHUNK)], extra], 0)

    def sort(t, _):
        place = ranked[t, 0:1, :].astype(jnp.int32)
        chosen = (iota((CHUNK, CHUNK), 0) == place).astype(F32).astype(BF)
        ybuf[pl.ds(pl.multiple_of(t * CHUNK, CHUNK), CHUNK), :] = dot_nt(chosen, joined_of(t))
        return 0

    bring.wait()
    lax.fori_loop(0, CHUNKS, sort, 0, unroll=8)
    ybuf[ROWS:, :] = jnp.zeros((TILE, WIDE), F32)
    tell.wait()

    eye = (iota((WIDE, WIDE), 0) == iota((WIDE, WIDE), 1)).astype(F32).astype(BF)
    sub = iota((TILE, WIDE), 0)

    def packet(k):
        to = lax.rem(leaf + k, jnp.int32(LEAVES))
        group = lax.div(to, jnp.int32(AT_ONCE))
        lane = lax.rem(to, jnp.int32(AT_ONCE)) * TILES

        def piece(r, q):
            return ybuf[pl.ds(jnp.clip(scal[group, r, lane + q], 0, ROWS), TILE), :]

        tiles = []
        for q in range(TILES):
            tile = piece(0, q)
            for r in range(1, PIECES):
                tile = jnp.where(sub >= scal[group, PIECES + r, lane + q], piece(r, q), tile)
            tiles.append(tile)
        turned = dot_nt(eye, jnp.concatenate(tiles, 0).astype(BF))
        feat[k] = turned[:F].astype(BF)
        aux[k] = jnp.concatenate([turned[F : F + 1, 128 * c : 128 * c + 128] for c in range(4)] * 2, 0)

    def give(j, _):
        steps = turn_of(2 * j + 1), turn_of(rem(2 * j + 2, LEAVES))
        for k in steps:
            packet(k)
        send_aux(steps[0]).start()
        send_feat(steps[0]).start()

        @pl.when(j < LEAVES // 2 - 1)
        def second():
            send_aux(steps[1]).start()
            send_feat(steps[1]).start()

        return 0

    def take_slots():
        each(LEAVES, lambda k: send_pivots(k).wait_recv())
        place = jnp.concatenate([held[(LEAVES - b) % LEAVES] for b in range(LEAVES)], 0)
        home = place % ROWS // PACKET
        number = ((leaf + iota((LEAVES, RANK), 0)) % LEAVES) * 8 + place // ROWS
        number = (number * PACKET + place % PACKET).astype(F32)
        valid = home == leaf * COLS + col
        order = dot(valid.astype(F32).astype(BF), before)
        order = jnp.where(valid, order, -1.0)

        def spread(table):
            return jnp.concatenate(
                [jnp.broadcast_to(table[b : b + 1], (SLOTS, RANK)) for b in range(LEAVES)], 0
            )

        shape = (LEAVES * SLOTS, RANK)
        hit = spread(order) == (iota(shape, 0) % SLOTS).astype(F32)
        wanted = jnp.sum(jnp.where(hit, spread(number) + 1.0, 0.0), 1, keepdims=True) - 1.0
        which = jnp.sum(jnp.where(hit, iota(shape, 1).astype(F32) + 1.0, 0.0), 1, keepdims=True) - 1.0
        wanted = jnp.broadcast_to(wanted, (LEAVES * SLOTS, CHUNK))

        def take(t, total):
            chosen = (wanted == ranked[t, 2:3, :]).astype(F32).astype(BF)
            rest = jnp.zeros((128 - WIDE, CHUNK), BF)
            return total + dot_nt(chosen, jnp.concatenate([joined_of(t), rest], 0))

        shape = (LEAVES * SLOTS, 128)
        taken = lax.fori_loop(0, CHUNKS, take, jnp.zeros(shape, F32), unroll=8)
        taken = jnp.where(iota(shape, 1) == WHICH, which, taken)
        taken = jnp.where(iota(shape, 1) == FULL, full, taken).astype(BF)
        for b in range(LEAVES):
            slots[b] = taken[b * SLOTS : (b + 1) * SLOTS]
        came[0] = slots[0]
        each(LEAVES, lambda k: send_slots(k).start())

    def place_points():
        each(LEAVES, lambda k: send_slots(k).wait_recv())
        got = jnp.concatenate([came[b] for b in range(LEAVES)], 0).astype(F32)
        chosen = got[:, WHICH : WHICH + 1] == iota((LEAVES * SLOTS, RANK), 1).astype(F32)
        picked = dot(got.T[:F].astype(BF), chosen.astype(F32).astype(BF))
        bad[...] = jnp.broadcast_to(jnp.max(got[:, FULL : FULL + 1], 0, keepdims=True), (8, 128))
        sk[0] = picked.astype(BF)
        each(COLS, lambda k: send_skel(k).start())

    def work(j, _):
        pl.when(j == 2)(take_slots)
        pl.when(j == 5)(place_points)
        return give(j, 0)

    lax.fori_loop(0, LEAVES // 2, work, 0)
    rx[0] = feat[0]
    ra[0] = aux[0]

    place = jnp.concatenate([held[(LEAVES - b) % LEAVES] for b in range(LEAVES)], 0)
    home = place % ROWS // PACKET
    largest = jnp.zeros((OWNERS, 1), F32)
    for b in range(LEAVES):
        held_here = (iota((OWNERS, RANK), 0) == home[b : b + 1]).astype(F32)
        largest = jnp.maximum(largest, jnp.sum(held_here, 1, keepdims=True))

    for copy in smalls:
        copy.wait()
    spare[...] = jnp.ones((8, 128), F32)
    spare[0:1, 0:F] = scales[...]
    inverse = 1.0 / to_column(spare[0:1, :])[:F]
    scale = inverse * inverse * LOG2E
    scale2 = across(scale, RANK)
    scale4 = across(scale, PER)

    index[...] = top_index(parent, top, leaf // 4)
    index2 = across(index[...], 2 * RANK)
    number = iota((RANK, 2 * RANK), 1)
    base = (quarter * RANK).astype(F32)
    other = (sibling * RANK).astype(F32)
    chosen = index2[:, :RANK] == iota((RANK, RANK), 1).astype(F32) + base
    rows[...] = chosen.astype(F32).astype(BF)
    lanes = number.astype(F32) + jnp.where(number < RANK, base, other - RANK)
    columns[...] = (index2 == lanes).astype(F32).astype(BF)
    chosen = across(index[...], 4 * RANK) == iota((RANK, 4 * RANK), 1).astype(F32)
    fours[...] = chosen.astype(F32).astype(BF)

    def norms(k):
        side[k] = point_side(rx[k].astype(F32), scale4)

    def receive(k):
        send_aux(k).wait_recv()
        send_feat(k).wait_recv()

    def early_norms(n, _):
        k = turn_of(n)
        pl.when(n > 0)(lambda: receive(k))
        norms(k)
        return 0

    lax.fori_loop(0, LEAVES // 2, early_norms, 0)

    picked = sk[0].astype(F32)

    def add_skel(k, total):
        send_skel(k).wait_recv()
        return total + sk[k].astype(F32)

    picked = lax.fori_loop(1, COLS, add_skel, picked)
    mine[...] = picked.astype(BF)
    sk4[quarter] = picked.astype(BF)

    def send_four(k):
        return remote(mine, sk4.at[quarter], (s_4, r_4), k, cousin(k))

    each(4, lambda k: send_four(k).start())
    left[0:RANK, :] = skel_side(picked, scale2)

    def block_of(k, out, begin):
        p = rx[k]
        fill = jnp.zeros((256 - 3 * F - 16, PER), BF)
        right = jnp.concatenate([p, p, p, side[k], fill], 0)
        power = dot(left[begin : begin + RANK, :], right)
        out[0:RANK, :] = jnp.exp2(jnp.minimum(power, 0.0)).astype(BF)

    def own_of(k, out):
        block_of(k, out, 0)
        value = ra[k]
        value = jnp.concatenate([value[r : r + 1] for r in range(4)], 1)
        out[RANK:, :] = jnp.broadcast_to(value, (16, PER)).astype(BF)

    def gram_of(u):
        gram[...] += dot_nt(u[...], u[0:RANK, :])

    def couple_of(v, u):
        couple[...] += dot_nt(v[...], u[0:RANK, :])

    last = LEAVES // 2 - 1

    def own_two(j, _):
        k, l = turn_of(2 * j), turn_of(2 * j + 1)
        @pl.when(j >= LEAVES // 4)
        def late():
            receive(k)
            receive(l)
            norms(k)
            norms(l)

        own_of(k, even.at[j])
        gram_of(odd.at[rem(j + last, last + 1)])
        own_of(l, odd.at[j])
        gram_of(even.at[j])
        return 0

    def other_two(j, _):
        block_of(turn_of(2 * j), other_even, RANK)
        couple_of(other_odd, odd.at[rem(j + last, last + 1)])
        block_of(turn_of(2 * j + 1), other_odd, RANK)
        couple_of(other_even, even.at[j])
        return 0

    gram[...] = jnp.zeros_like(gram)
    couple[...] = jnp.zeros_like(couple)
    odd[last] = jnp.zeros((RANK + 16, PER), BF)
    other_odd[...] = jnp.zeros_like(other_odd)
    def send_gram(k):
        return remote(pg.at[(col + k) % COLS], gr.at[k], (s_p, r_p), k, beside(k))

    def send_couple(k):
        return remote(pc.at[(col + k) % COLS], cr.at[k], (s_c, r_c), k, beside(k))

    def send_chosen(k):
        return remote(pt.at[(col + k) % COLS], qr.at[k], (s_o, r_o), k, beside(k))

    def send_rhs(k):
        return remote(rs, rr.at[k], (s_r, r_r), k, beside(k))

    def sibling_side():
        each(4, lambda k: remote(mine, sk4.at[(quarter + 4 - k) % 4], (s_4, r_4), k, cousin(k)).wait_recv())
        left[RANK:, :] = skel_side(sk4[sibling].astype(F32), scale2)

    def give_gram():
        gram_of(odd.at[last])
        part = gram[0:RANK, :].astype(BF)
        for k in range(COLS):
            pg[k] = part[k * SLAB : (k + 1) * SLAB]
        each(COLS, lambda k: send_gram(k).start())

    def half(h, _):
        pairs = LEAVES // 4
        lax.fori_loop(pairs * h, pairs * (h + 1), own_two, 0)
        pl.when(h == 0)(sibling_side)
        pl.when(h == 1)(give_gram)
        lax.fori_loop(pairs * h, pairs * (h + 1), other_two, 0)
        return 0

    lax.fori_loop(0, 2, half, 0)
    couple_of(other_odd, odd.at[last])

    rhs = gram[RANK : RANK + 1, :]
    rhs = jnp.sum(dot_nt(stack16(split3(rhs), RANK), rows[...]), 0, keepdims=True)
    rs[...] = jnp.zeros_like(rs)
    rs[0:1, :] = rhs[:, :128]
    rs[1:2, :] = rhs[:, 128:]
    rs[2:3, :] = bad[0:1, :]
    part = dot(rows[...], gram[0:RANK, :].astype(BF)).astype(BF)
    chosen = dot_nt(part, columns[:, 0:RANK])
    part = dot_nt(rows[...], couple[...].astype(BF)).astype(BF)
    chosen = chosen + dot_nt(part, columns[:, RANK:])
    chosen = chosen.astype(BF)
    for k in range(COLS):
        pt[k] = chosen[k * SLAB : (k + 1) * SLAB]
    each(COLS, lambda k: send_chosen(k).start())
    each(COLS, lambda k: send_rhs(k).start())
    part = couple[...].T.astype(BF)
    for k in range(COLS):
        pc[k] = part[k * SLAB : (k + 1) * SLAB]
    each(COLS, lambda k: send_couple(k).start())

    whole = jnp.concatenate([sk4[k] for k in range(4)], 1)
    points = dot_nt(whole, fours[...])
    fill = jnp.zeros((256 - 3 * F - 16, RANK), BF)
    points_b = points.astype(BF)
    right = jnp.concatenate([points_b, points_b, points_b, point_side(points, scale2), fill], 0)
    value = jnp.exp2(jnp.minimum(dot(skel_side(points, scale2), right), 0.0))
    crossing = (across(index[...], RANK) >= 2.0 * RANK) != (index[...].T[0:1, :] >= 2.0 * RANK)
    square = iota((RANK, RANK), 0) == iota((RANK, RANK), 1)
    tops[...] = jnp.where(crossing, value, 0.0) + jnp.where(square, ridge[...], 0.0)

    def finish(sends):
        return lambda k: [send(k).wait_send() for send in sends]

    each(LEAVES, finish((send_pivots, send_slots, send_aux, send_feat)))
    each(COLS, finish((send_skel, send_gram, send_rhs)))
    each(4, finish((send_four,)))

    def add_chosen(k, totals):
        send_chosen(k).wait_recv()
        send_rhs(k).wait_recv()
        return totals[0] + qr[k].astype(F32), totals[1] + rr[k]

    chosen, rhs = lax.fori_loop(1, COLS, add_chosen, (pt[col].astype(F32), rs[...]))
    over = jnp.maximum(jnp.max(rhs[2:3, :]), jnp.max(largest) - SLOTS)
    flag[0] = (over > 0.0).astype(jnp.int32)
    chosen = chosen * (1.0 / NODE)
    t4[0] = chosen.astype(BF)
    r4[0] = rhs * (1.0 / NODE)

    def send_top(k):
        return remote(t4.at[0], t4.at[k], (s_t, r_t), k, cousin(k))

    def send_top_rhs(k):
        return remote(r4.at[0], r4.at[k], (s_q, r_q), k, cousin(k))

    each(4, lambda k: send_top(k).start())
    each(4, lambda k: send_top_rhs(k).start())

    def add_gram(k, total):
        send_gram(k).wait_recv()
        return total + gr[k].astype(F32)

    def add_couple(k, total):
        send_couple(k).wait_recv()
        return total + cr[k].astype(F32)

    total = lax.fori_loop(1, COLS, add_gram, pg[col].astype(F32))
    diagonal = iota((SLAB, RANK), 0) + col * SLAB == iota((SLAB, RANK), 1)
    out_share[0, :, 0:RANK] = total * (1.0 / NODE) + jnp.where(diagonal, ridge[...], 0.0)
    total = lax.fori_loop(1, COLS, add_couple, pc[col].astype(F32))
    out_share[0, :, RANK:] = total * (1.0 / NODE)
    result = chosen + tops[pl.ds(pl.multiple_of(col * SLAB, SLAB), SLAB), :]

    def add_top(k, totals):
        send_top(k).wait_recv()
        send_top_rhs(k).wait_recv()
        return totals[0] + t4[k].astype(F32), totals[1] + r4[k]

    result, rhs = lax.fori_loop(1, 4, add_top, (result, r4[0]))
    out_top[0] = result
    out_rhs[...] = jnp.concatenate([rhs[0:1], rhs[1:2]], 1)

    each(COLS, finish((send_couple, send_chosen)))
    each(4, finish((send_top, send_top_rhs)))


SHAPES = ((1, SLAB, 2 * RANK), (1, SLAB, RANK), (1, RANK))


def exchange(merged, ridge, *smalls):
    return pl.pallas_call(
        exchange_kernel,
        out_shape=tuple(pltpu.VMEM(shape, F32) for shape in SHAPES),
        in_specs=[VMEM, VMEM] + [ANYWHERE] * 4,
        out_specs=[VMEM] * 3,
        scratch_shapes=[
            pltpu.VMEM((1, RANK), jnp.int32),
            pltpu.VMEM((1, F), F32),
            pltpu.VMEM((8, RANK), jnp.int32),
            pltpu.VMEM((4, RANK), jnp.int32),
            pltpu.VMEM((8, 128), F32),
            pltpu.VMEM((LEAVES, F, PER), BF),
            pltpu.VMEM((LEAVES, 8, 128), F32),
            pltpu.VMEM((LEAVES, F, PER), BF),
            pltpu.VMEM((LEAVES, 8, 128), F32),
            pltpu.VMEM((LEAVES, RANK, PER), BF),
            pltpu.VMEM((LEAVES, 16, PER), BF),
            pltpu.VMEM((COLS, F, RANK), BF),
            pltpu.VMEM((F, RANK), BF),
            pltpu.VMEM((4, F, RANK), BF),
            pltpu.VMEM((2 * RANK, 256), BF),
            pltpu.VMEM((LEAVES // 2, RANK + 16, PER), BF),
            pltpu.VMEM((LEAVES // 2, RANK + 16, PER), BF),
            pltpu.VMEM((RANK, PER), BF),
            pltpu.VMEM((RANK, PER), BF),
            pltpu.VMEM((RANK + 16, RANK), F32),
            pltpu.VMEM((RANK, RANK), F32),
            pltpu.VMEM((RANK, RANK), BF),
            pltpu.VMEM((RANK, 2 * RANK), BF),
            pltpu.VMEM((RANK, 4 * RANK), BF),
            pltpu.VMEM((RANK, 128), F32),
            pltpu.VMEM((RANK, RANK), F32),
            pltpu.VMEM((COLS, SLAB, RANK), BF),
            pltpu.VMEM((COLS, SLAB, RANK), BF),
            pltpu.VMEM((COLS, SLAB, RANK), BF),
            pltpu.VMEM((COLS, SLAB, RANK), BF),
            pltpu.VMEM((COLS, SLAB, RANK), BF),
            pltpu.VMEM((COLS, SLAB, RANK), BF),
            pltpu.VMEM((8, 128), F32),
            pltpu.VMEM((COLS, 8, 128), F32),
            pltpu.VMEM((4, SLAB, RANK), BF),
            pltpu.VMEM((4, 8, 128), F32),
            *dma(LEAVES),
            *dma(LEAVES),
            *dma(COLS),
            *dma(4),
            *dma(COLS),
            *dma(COLS),
            *dma(COLS),
            *dma(COLS),
            *dma(4),
            *dma(4),
            pltpu.SemaphoreType.DMA((5,)),
        ],
        compiler_params=params(0, 40),
        name="exchange",
    )(merged, ridge, *in_hbm(*smalls))


def stream(samples, pivots, ridge, *smalls):
    return pl.pallas_call(
        stream_kernel,
        out_shape=(
            *(pltpu.VMEM(shape, F32) for shape in SHAPES),
            jax.ShapeDtypeStruct((1,), jnp.int32),
        ),
        in_specs=[ANYWHERE, VMEM, VMEM, VMEM, VMEM] + [ANYWHERE] * 3,
        out_specs=[VMEM] * 3 + [pl.BlockSpec(memory_space=pltpu.SMEM)],
        scratch_shapes=[
            pltpu.VMEM((F, ROWS), BF),
            pltpu.VMEM((8, 128), F32),
            pltpu.VMEM((ROWS // 128, 128), F32),
            pltpu.VMEM((CHUNKS, 8, CHUNK), F32),
            pltpu.VMEM((LEAVES, 128), F32),
            pltpu.VMEM((LEAVES, 128), F32),
            pltpu.VMEM((ROWS + TILE, WIDE), F32),
            pltpu.VMEM((LEAVES // AT_ONCE, 16, 128), jnp.int32),
            pltpu.SMEM((LEAVES // AT_ONCE, 16, 128), jnp.int32),
            pltpu.VMEM((LEAVES, 1, RANK), jnp.int32),
            pltpu.VMEM((LEAVES, SLOTS, 128), BF),
            pltpu.VMEM((LEAVES, SLOTS, 128), BF),
            pltpu.VMEM((1, F), F32),
            pltpu.VMEM((8, RANK), jnp.int32),
            pltpu.VMEM((4, RANK), jnp.int32),
            pltpu.VMEM((8, 128), F32),
            pltpu.VMEM((LEAVES, F, PER), BF),
            pltpu.VMEM((LEAVES, 8, 128), F32),
            pltpu.VMEM((LEAVES, F, PER), BF),
            pltpu.VMEM((LEAVES, 8, 128), F32),
            pltpu.VMEM((LEAVES, 16, PER), BF),
            pltpu.VMEM((COLS, F, RANK), BF),
            pltpu.VMEM((F, RANK), BF),
            pltpu.VMEM((4, F, RANK), BF),
            pltpu.VMEM((2 * RANK, 256), BF),
            pltpu.VMEM((LEAVES // 2, RANK + 16, PER), BF),
            pltpu.VMEM((LEAVES // 2, RANK + 16, PER), BF),
            pltpu.VMEM((RANK, PER), BF),
            pltpu.VMEM((RANK, PER), BF),
            pltpu.VMEM((RANK + 16, RANK), F32),
            pltpu.VMEM((RANK, RANK), F32),
            pltpu.VMEM((RANK, RANK), BF),
            pltpu.VMEM((RANK, 2 * RANK), BF),
            pltpu.VMEM((RANK, 4 * RANK), BF),
            pltpu.VMEM((RANK, 128), F32),
            pltpu.VMEM((RANK, RANK), F32),
            pltpu.VMEM((COLS, SLAB, RANK), BF),
            pltpu.VMEM((COLS, SLAB, RANK), BF),
            pltpu.VMEM((COLS, SLAB, RANK), BF),
            pltpu.VMEM((COLS, SLAB, RANK), BF),
            pltpu.VMEM((COLS, SLAB, RANK), BF),
            pltpu.VMEM((COLS, SLAB, RANK), BF),
            pltpu.VMEM((8, 128), F32),
            pltpu.VMEM((COLS, 8, 128), F32),
            pltpu.VMEM((4, SLAB, RANK), BF),
            pltpu.VMEM((4, 8, 128), F32),
            *dma(LEAVES),
            *dma(LEAVES),
            *dma(LEAVES),
            *dma(LEAVES),
            *dma(COLS),
            *dma(4),
            *dma(COLS),
            *dma(COLS),
            *dma(COLS),
            *dma(COLS),
            *dma(4),
            *dma(4),
            pltpu.SemaphoreType.DMA((5,)),
        ],
        compiler_params=params(1, 40),
        name="stream",
    )(*in_hbm(*samples, pivots), ridge, *in_hbm(*smalls))


def emit_kernel(*refs):
    ins, outs, sem = refs[:3], refs[3:6], refs[6]
    copies = [pltpu.make_async_copy(a, b, sem.at[k]) for k, (a, b) in enumerate(zip(ins, outs))]
    for copy in copies:
        copy.start()
    for copy in copies:
        copy.wait()


def emit(results):
    return pl.pallas_call(
        emit_kernel,
        out_shape=tuple(jax.ShapeDtypeStruct(shape, F32) for shape in SHAPES),
        in_specs=[VMEM] * 3,
        out_specs=[ANYWHERE] * 3,
        scratch_shapes=[pltpu.SemaphoreType.DMA((3,))],
        compiler_params=params(),
        name="emit",
    )(*results)


def local(features, targets, owner, length_scales, ridge, leaf_pivots, parent_pivots, top_pivots):
    samples = (features, targets.reshape(ROWS // 128, 128), owner.reshape(ROWS // 128, 128))
    ridge = ridge.reshape(1, 1)
    smalls = (length_scales.reshape(1, F), parent_pivots, top_pivots)
    *results, flag = stream(samples, leaf_pivots, ridge, *smalls)

    def again():
        return tuple(emit(exchange(pack(*samples), ridge, leaf_pivots, *smalls)))

    return lax.switch(flag[0], [lambda: tuple(emit(results)), again])


def solution(mesh):
    return jax.shard_map(
        local,
        mesh=mesh,
        in_specs=(
            P(None, ("leaf", "col")),
            P(("leaf", "col")),
            P(("leaf", "col")),
            P(),
            P(),
            P("leaf", None),
            P(),
            P(),
        ),
        out_specs=(P("leaf", "col", None), P("leaf", "col", None), P("leaf", None)),
        check_vma=False,
    )
```
